32 devices in a mesh: slab: 4 (over y, core), ray: 8 (over z, x).
Axes of the slice: x: 2, y: 2, z: 4, core: 2. Of those that a mesh axis runs over, the one named last changes fastest.
Arguments:
- intensity: float32 [4, 8, 256, 2048], P('slab', 'ray'), may hold values from 0.2 to 1
- angles: float32 [4, 8], replicated, may hold values from 0 to 3.14159
- volume: float32 [256, 64, 256], P('slab', 'ray'), may hold values from -3 to 3
- vol_list: int32 [64], replicated, may hold values from 0 to 63, as said below
Outputs:
- reconstruction: float32 [256, 64, 256], P('slab', 'ray')
- residual: float32 [4, 8, 256, 2048], P(None, 'ray', 'slab')
The draws below stay inside these ranges and needn't reach their ends.
Inputs may be any that keep to these rules, and one draw needn't show every extreme that they name: vol_list is a permutation of the patch ids that follows a Hilbert curve over the 8 x 8 grid of patches.
All inputs are finite; a program needn't handle non-finite values.
Results may differ from the reference program's by a relative error of at most 0.0003.
Values sent between devices are 32-bit elements; how exact they have to be, the bound alone decides.
No kernel may reach another device: no remote copies, remote signals or barrier semaphores. Data moves between devices by JAX's collectives and lax.ppermute only.
A program may use at most 192 MiB of HBM per device.

```python
import jax
import jax.numpy as jnp
from jax import lax

NCOL = 2048
NSLICE = 256
BAND = 2048
HLEV = 3
TR = 32
ANG_RAY = 4
PGRID = 8
ROI = 128
PATCHES = 64
N_RAY = 8


def draw_intensity(key, part):
    key_list = jax.random.split(jax.random.fold_in(key, 23), 10)
    lead_shape = (ANG_RAY, N_RAY)
    mode_count = 6
    row_pos = jnp.arange(NSLICE, dtype=jnp.float32)[:, None] / NSLICE
    col_pos = jnp.arange(NCOL, dtype=jnp.float32)[None, :] / NCOL
    row_int = jnp.arange(NSLICE, dtype=jnp.int32)[:, None]
    col_int = jnp.arange(NCOL, dtype=jnp.int32)[None, :]
    offsets = 0.6 * jax.random.normal(key_list[0], lead_shape, jnp.float32)
    mode_scale = 0.6
    roughness = jax.random.uniform(key_list[1], lead_shape + (NSLICE, NCOL), jnp.float32, -0.8, 0.8)
    row_freq = jax.random.randint(key_list[2], lead_shape + (mode_count,), 0, 3).astype(jnp.float32)
    col_freq = jax.random.randint(key_list[3], lead_shape + (mode_count,), 0, 9).astype(jnp.float32)
    amplitude = mode_scale * jax.random.normal(key_list[4], lead_shape + (mode_count,), jnp.float32)
    phases = jax.random.uniform(key_list[5], lead_shape + (mode_count,), jnp.float32, -jnp.pi, jnp.pi)
    col_edges = jax.random.randint(key_list[6], lead_shape + (3,), 0, NCOL)
    col_steps = 0.8 * jax.random.normal(key_list[7], lead_shape + (3,), jnp.float32)
    row_edges = jax.random.randint(key_list[8], lead_shape, 0, NSLICE)
    row_steps = 0.8 * jax.random.normal(key_list[9], lead_shape, jnp.float32)
    field_sum = roughness + offsets[:, :, None, None]
    for mode_idx in range(mode_count):
        phase_map = 2.0 * jnp.pi * (row_freq[:, :, mode_idx, None, None] * row_pos + col_freq[:, :, mode_idx, None, None] * col_pos) + phases[:, :, mode_idx, None, None]
        field_sum = field_sum + amplitude[:, :, mode_idx, None, None] * jnp.cos(phase_map)
    for edge_idx in range(3):
        upper_part = (col_int >= col_edges[:, :, edge_idx, None, None]).astype(jnp.float32)
        field_sum = field_sum + col_steps[:, :, edge_idx, None, None] * upper_part
    lower_rows = (row_int >= row_edges[:, :, None, None]).astype(jnp.float32)
    field_sum = field_sum + row_steps[:, :, None, None] * lower_rows
    return 0.2 + 0.8 * jax.nn.sigmoid(field_sum)


def draw_vol_list(key, part):
    keys = jax.random.split(jax.random.fold_in(key, 11), 2)
    grid_side = 2 ** HLEV
    total = grid_side * grid_side
    shift = jax.random.randint(keys[0], (), 0, total)
    flips = jax.random.randint(keys[1], (3,), 0, 2)
    remain = (jnp.arange(total, dtype=jnp.int32) + shift) % total
    position_across = jnp.zeros((total,), jnp.int32)
    position_down = jnp.zeros((total,), jnp.int32)
    current_edge_length = 1
    for level_idx in range(HLEV):
        bit_x = remain // 2 % 2
        bit_y = (remain + bit_x) % 2
        rotated_flag = bit_y == 0
        reflect_flag = jnp.logical_and(rotated_flag, bit_x == 1)
        reflected_across = jnp.where(reflect_flag, current_edge_length - 1 - position_across, position_across)
        reflected_down = jnp.where(reflect_flag, current_edge_length - 1 - position_down, position_down)
        updated_across = jnp.where(rotated_flag, reflected_down, reflected_across)
        updated_down = jnp.where(rotated_flag, reflected_across, reflected_down)
        position_across = updated_across + current_edge_length * bit_x
        position_down = updated_down + current_edge_length * bit_y
        remain = remain // 4
        current_edge_length = current_edge_length * 2
    x_swap = jnp.where(flips[0] == 1, position_down, position_across)
    y_swap = jnp.where(flips[0] == 1, position_across, position_down)
    x_fin = jnp.where(flips[1] == 1, grid_side - 1 - x_swap, x_swap)
    y_fin = jnp.where(flips[2] == 1, grid_side - 1 - y_swap, y_swap)
    return (x_fin * grid_side + y_fin).astype(jnp.int32)


def shard_levels(stream_key, dims, cuts, least, top_value):
    gain = 1.0
    for dim, blocks in cuts:
        draws = jax.random.uniform(jax.random.fold_in(jax.random.fold_in(stream_key, 6), dim), (blocks,), jnp.float32, least / len(cuts), top_value / len(cuts))
        gain = gain * jnp.repeat(jnp.exp(draws), dims[dim] // blocks).reshape((-1,) + (1,) * (len(dims) - 1 - dim))
    return gain


def centred(own_key, shape, scale, bound, pieces=(), held_as=jnp.bfloat16):
    loudness = shard_levels(own_key, shape, pieces, -0.22, 0.18) if pieces else 1.0
    drawn = jax.random.normal(own_key, shape, jnp.float32) * scale * loudness
    return jnp.minimum(jnp.maximum(drawn, -bound), bound).astype(held_as)


def setup_inputs(seed: int = 0) -> dict:
    splits = jax.random.split(jax.random.key(seed), 5)
    return {
        "intensity": draw_intensity(jax.random.fold_in(splits[4], 71), 0),
        "angles": jnp.clip(jax.random.uniform(splits[1], (ANG_RAY, N_RAY), jnp.float32, 0.0, 3.14159), 0.0, 3.14159),
        "volume": centred(splits[2], (NSLICE, PATCHES, 256), 0.5, 3.0, ((0, 4), (1, 8)), jnp.float32),
        "vol_list": draw_vol_list(jax.random.fold_in(splits[4], 71), 0),
    }


paganin_strength = 10.0
relax = 1.8
row_floor = 0.25
highest = lax.Precision.HIGHEST


def paganin_gain(height, width_px):
    freq_rows = 2.0 - 2.0 * jnp.cos(2.0 * jnp.pi * jnp.arange(height).astype(jnp.float32) / height)
    freq_cols = 2.0 - 2.0 * jnp.cos(2.0 * jnp.pi * jnp.arange(width_px).astype(jnp.float32) / width_px)
    return 1.0 / (1.0 + paganin_strength * (freq_rows[:, None] + freq_cols[None, :]))


def ray_windows(patch_ids, theta):
    half_roi = (ROI - 1) / 2.0
    half_band = (BAND - 1) / 2.0
    centre_x = (patch_ids // PGRID).astype(jnp.float32) * 16.0 + 7.5 - half_roi
    centre_y = (patch_ids % PGRID).astype(jnp.float32) * 16.0 + 7.5 - half_roi
    centre = half_band + centre_x[:, None] * jnp.cos(theta)[None, :] + centre_y[:, None] * jnp.sin(theta)[None, :]
    starts = jnp.floor(centre).astype(jnp.int32) - 15
    return starts[:, :, None] + jnp.arange(TR).astype(jnp.int32)[None, None, :]


def patch_weights(patch_ids, theta_one):
    half_roi = (ROI - 1) / 2.0
    half_band = (BAND - 1) / 2.0
    ray_index = ray_windows(patch_ids, theta_one[None])[:, 0, :]
    voxels = jnp.arange(256).astype(jnp.int32)
    voxel_x = (patch_ids // PGRID).astype(jnp.float32)[:, None] * 16.0 + (voxels // 16).astype(jnp.float32)[None, :] - half_roi
    voxel_y = (patch_ids % PGRID).astype(jnp.float32)[:, None] * 16.0 + (voxels % 16).astype(jnp.float32)[None, :] - half_roi
    along = voxel_x * jnp.cos(theta_one) + voxel_y * jnp.sin(theta_one)
    distance = (ray_index.astype(jnp.float32) - half_band)[:, None, :] - along[:, :, None]
    weights = jnp.maximum(0.0, 1.0 - jnp.abs(distance)) / ROI
    return weights, ray_index


def reference(intensity, angles, volume, vol_list):
    gain_table = paganin_gain(NSLICE, NCOL)
    spectrum = jnp.fft.fft2(intensity)
    filtered = jnp.real(jnp.fft.ifft2(spectrum * gain_table))
    offset = (NCOL - BAND) // 2
    projected = -jnp.log(filtered[..., offset:offset + BAND])
    all_angles = angles.reshape(-1)
    sinogram = projected.reshape(ANG_RAY * N_RAY, NSLICE, BAND)
    step_size = relax * ROI / (ANG_RAY * N_RAY)

    def forward(current):
        def project_one(theta_one):
            weights, ray_index = patch_weights(vol_list, theta_one)
            contrib = jnp.einsum("smv,mvj->smj", current, weights, precision=highest)
            predicted = jnp.zeros((NSLICE, BAND), jnp.float32).at[:, ray_index].add(contrib)
            sums = jnp.zeros((BAND,), jnp.float32).at[ray_index].add(jnp.sum(weights, axis=1))
            return predicted, sums
        return lax.map(project_one, all_angles)

    def backward(scaled):
        def accumulate(total, member):
            theta_one, sino_one = member
            weights, ray_index = patch_weights(vol_list, theta_one)
            windows = sino_one[:, ray_index]
            return total + jnp.einsum("smj,mvj->smv", windows, weights, precision=highest), None
        total, _ = lax.scan(accumulate, jnp.zeros(volume.shape, jnp.float32), (all_angles, scaled))
        return total

    predicted, row_sums = forward(volume)
    row_weight = 1.0 / jnp.maximum(row_sums, row_floor)
    difference = sinogram - predicted
    first_iterate = volume + step_size * backward(difference * row_weight[:, None, :])
    predicted_next, _ = forward(first_iterate)
    residual = sinogram - predicted_next
    reconstruction = first_iterate + step_size * backward(residual * row_weight[:, None, :])
    return reconstruction, residual.reshape(ANG_RAY, N_RAY, NSLICE, BAND)
```

```python
import functools
import math

import jax
import jax.numpy as jnp
import ml_dtypes
import numpy as np
from jax import lax
from jax.experimental import pallas as pl
from jax.experimental.pallas import tpu as pltpu
from jax.sharding import PartitionSpec as P

BAND = 2048
PGRID = 8
ROI = 128
SIDE = 16
VOX = SIDE * SIDE
WIN = 24
ACTIVE = 256
LANES = 128
ROWS = 8
SPLIT = 64

paganin_strength = 10.0
relax = 1.8
row_floor = 0.25

bf16 = jnp.bfloat16
f32 = jnp.float32


def halves(values):
    high = values.astype(bf16)
    low = (values - high.astype(f32)).astype(bf16)
    return high, low


def thirds(values):
    high = values.astype(bf16)
    rest = values - high.astype(f32)
    middle = rest.astype(bf16)
    low = (rest - middle.astype(f32)).astype(bf16)
    return high, middle, low


def dot(left, right):
    return jnp.dot(left, right, preferred_element_type=f32)


def numpy_halves(table):
    high = table.astype(ml_dtypes.bfloat16)
    low = (table - high.astype(np.float64)).astype(ml_dtypes.bfloat16)
    return high, low


def filter_tables(height):
    index = np.arange(height)
    phase = 2.0 * np.pi * (np.outer(index, index) % height) / height
    cas = (np.cos(phase) + np.sin(phase)) / math.sqrt(height)
    cas_high, cas_low = numpy_halves(cas)
    row_freq = 2.0 - 2.0 * np.cos(2.0 * np.pi * index / height)
    middle = (1.0 + paganin_strength * row_freq) / paganin_strength + 2.0
    rho = (middle - np.sqrt(middle * middle - 4.0)) / 2.0
    rho_wide = np.repeat(rho[:, None], LANES, axis=1).astype(np.float32)
    return cas_high, cas_low, rho_wide


def circular_decay(parts, rho, forward, lane):
    count = len(parts)
    step = 1
    power = rho
    while step < LANES:
        shift = step if forward else LANES - step
        turned = [pltpu.roll(part, shift, 1) for part in parts]
        if forward:
            keep = lane >= step
            moved = [jnp.where(keep, turned[i], turned[i - 1]) for i in range(count)]
        else:
            keep = lane < LANES - step
            moved = [jnp.where(keep, turned[i], turned[(i + 1) % count]) for i in range(count)]
        parts = [part + power * other for part, other in zip(parts, moved)]
        power = power * power
        step *= 2
    order = list(range(count)) if forward else list(range(count - 1, -1, -1))
    wrapped = parts[order[0]]
    for position in order[1:]:
        wrapped = parts[position] + power * wrapped
    whole = power
    for _ in range(int(math.log2(count))):
        whole = whole * whole
    carry = wrapped / (1.0 - whole)
    results = [None] * count
    for position in order:
        carry = parts[position] + power * carry
        results[position] = carry
    return results


def filter_kernel(image_ref, high_ref, low_ref, rho_ref, out_ref, active_ref, spec_ref):
    height, width = image_ref.shape
    tile = 256
    cas_high = high_ref[...]
    cas_low = low_ref[...]

    def transform(values):
        high, low = halves(values)
        return dot(cas_high, high) + dot(cas_high, low) + dot(cas_low, high)

    for start in range(0, width, tile):
        spec_ref[:, start : start + tile] = transform(1.0 - image_ref[:, start : start + tile])

    lane = lax.broadcasted_iota(jnp.int32, (ROWS, LANES), 1)

    def solve(index, carry):
        row = pl.ds(pl.multiple_of(index * ROWS, ROWS), ROWS)
        rho = rho_ref[row, :]
        scale = rho / paganin_strength
        parts = [
            spec_ref[row, start : start + LANES] * scale for start in range(0, width, LANES)
        ]
        parts = circular_decay(parts, rho, True, lane)
        parts = circular_decay(parts, rho, False, lane)
        for position, part in enumerate(parts):
            spec_ref[row, position * LANES : (position + 1) * LANES] = part
        return carry

    lax.fori_loop(0, height // ROWS, solve, 0)
    offset = (width - ACTIVE) // 2
    for start in range(0, width, tile):
        values = -jnp.log(1.0 - transform(spec_ref[:, start : start + tile]))
        out_ref[:, start : start + tile] = values
    active_ref[...] = out_ref[:, offset : offset + ACTIVE]


def paganin(image):
    height, width = image.shape
    tables = filter_tables(height)
    return pl.pallas_call(
        filter_kernel,
        out_shape=(
            jax.ShapeDtypeStruct((height, width), f32),
            jax.ShapeDtypeStruct((height, ACTIVE), f32),
        ),
        in_specs=[pl.BlockSpec(memory_space=pltpu.VMEM)] * 4,
        out_specs=[pl.BlockSpec(memory_space=pltpu.VMEM)] * 2,
        scratch_shapes=[pltpu.VMEM((height, width), f32)],
        compiler_params=pltpu.CompilerParams(vmem_limit_bytes=32 * 2**20),
        cost_estimate=pl.CostEstimate(
            flops=12 * height * height * width,
            bytes_accessed=8 * height * width,
            transcendentals=height * width,
        ),
        name="paganin",
    )(image, *[jnp.asarray(table) for table in tables])


def sirt_kernel(
    step_size,
    chunk,
    offset_ref,
    tile_ref,
    turn_ref,
    place_ref,
    slot_ref,
    cos_ref,
    sin_ref,
    vol_ref,
    sino_ref,
    flip_ref,
    shift_x_ref,
    shift_y_ref,
    out_ref,
    res_ref,
    weight_ref,
    acc_ref,
    along_ref,
    start_ref,
    update_ref,
    diff_ref,
    gain_ref,
    window_ref,
):
    patches, slices, _ = vol_ref.shape
    angles = sino_ref.shape[0]
    pairs = patches // 2
    both = 2 * slices
    chunks = angles // chunk
    cached = chunks == 1
    width = chunk * WIN
    flip = flip_ref[...]
    lane_rows = lax.broadcasted_iota(jnp.int32, (both, LANES), 1)

    def reversed_exact(values):
        return sum(dot(part, flip) for part in thirds(values))

    def along_angle(t, carry):
        along_ref[t] = shift_x_ref[...] * cos_ref[t] + shift_y_ref[...] * sin_ref[t]
        return carry

    lax.fori_loop(0, angles, along_angle, 0)

    def first_order(q, carry):
        diff_ref[q] = vol_ref[slot_ref[patches - 1 - q]]
        return carry

    lax.fori_loop(0, pairs, first_order, 0)
    turned = reversed_exact(diff_ref[0:pairs].reshape(pairs * slices, VOX))
    start_ref[:, slices:both, :] = turned.reshape(pairs, slices, VOX)

    def second_order(q, carry):
        start_ref[q, 0:slices, :] = vol_ref[slot_ref[q]]
        return carry

    lax.fori_loop(0, pairs, second_order, 0)

    ray = lax.broadcasted_iota(jnp.int32, (ROWS, VOX), 0).astype(f32)

    def make_weights(q, c):
        held = q if cached else 0
        for two in range(chunk // 2):
            pieces = []
            for t in (2 * two, 2 * two + 1):
                angle = c * chunk + t
                base = ray - (along_ref[angle] + place_ref[q * angles + angle])
                for group in range(WIN // ROWS):
                    distance = base + float(group * ROWS)
                    pieces.append(jnp.maximum(0.0, 1.0 - jnp.abs(distance)))
            high, low = halves(jnp.concatenate(pieces, axis=0))
            weight_ref[held, 2 * two * WIN : (2 * two + 2) * WIN, 0:VOX] = high
            weight_ref[held, 2 * two * WIN : (2 * two + 2) * WIN, VOX : 2 * VOX] = low

    def forward(first):
        acc_ref[...] = jnp.zeros(acc_ref.shape, f32)

        def pair(q, carry):
            values = start_ref[q]
            if not first:
                values = values + step_size * update_ref[q]
            high, low = halves(values)
            operand = jnp.concatenate(
                [
                    jnp.concatenate([high, high], axis=1),
                    jnp.concatenate([low, jnp.zeros_like(low)], axis=1),
                    jnp.ones((both, 2 * VOX), bf16),
                ],
                axis=0,
            )
            for c in range(chunks):
                if first or not cached:
                    make_weights(q, c)
                held = q if cached else 0
                sums = lax.dot_general(
                    weight_ref[held],
                    operand,
                    (((1,), (1,)), ((), ())),
                    preferred_element_type=f32,
                )
                for t in range(chunk):
                    angle = c * chunk + t
                    rows = pl.ds(offset_ref[q * angles + angle], WIN)
                    acc_ref[angle, rows, :] = (
                        acc_ref[angle, rows, :] + sums[t * WIN : (t + 1) * WIN, :]
                    )
            return carry

        lax.fori_loop(0, pairs, pair, 0)

        def spread(t, carry):
            rows = jnp.transpose(acc_ref[t]) * (1.0 / ROI)
            diff_ref[t] = rows[0:slices] + rows[both : both + slices]
            res_ref[t] = rows[slices:both] + rows[both + slices : 2 * both]
            if first:
                gain_ref[t] = rows[2 * both : 2 * both + slices]
            return carry

        lax.fori_loop(0, angles, spread, 0)
        flat = (angles * slices, ACTIVE)
        full = (angles, slices, ACTIVE)
        mirrored = reversed_exact(res_ref[...].reshape(flat)).reshape(full)
        res_ref[...] = sino_ref[...] - diff_ref[0:angles] - mirrored
        if first:
            direct = gain_ref[...]
            total = direct + reversed_exact(direct.reshape(flat)).reshape(full)
            gain_ref[...] = 1.0 / jnp.maximum(total, row_floor)

    def backward(first):
        weighted = res_ref[...] * gain_ref[...] * (1.0 / ROI)
        flat = (angles * slices, ACTIVE)
        full = (angles, slices, ACTIVE)
        high, low = halves(weighted.reshape(flat))
        mirrored = (dot(high, flip) + dot(low, flip)).reshape(full)
        lane = lax.broadcasted_iota(jnp.int32, (angles, slices, LANES), 2)
        for part, source in enumerate((weighted, mirrored)):
            rows = slice(part * slices, (part + 1) * slices)
            left = source[:, :, 0:LANES]
            right = source[:, :, LANES : 2 * LANES]
            window_ref[:, 0, rows, :] = left
            window_ref[:, 2, rows, :] = right
            mixed = jnp.where(lane >= SPLIT, left, right)
            window_ref[:, 1, rows, :] = pltpu.roll(mixed, SPLIT, 2)

        def pair(q, carry):
            total = None
            for c in range(chunks):
                if not cached:
                    make_weights(q, c)
                held = q if cached else 0
                tiles = [None] * (-(-width // LANES))
                for t in range(chunk):
                    index = q * angles + c * chunk + t
                    piece = pltpu.roll(
                        window_ref[c * chunk + t, tile_ref[index]], turn_ref[index], 1
                    )
                    begin = t * WIN
                    for place in range(begin // LANES, (begin + WIN - 1) // LANES + 1):
                        if tiles[place] is None:
                            tiles[place] = piece
                        else:
                            tiles[place] = jnp.where(
                                lane_rows >= begin - place * LANES, piece, tiles[place]
                            )
                high, low = halves(jnp.concatenate(tiles, axis=1))
                operand = jnp.concatenate([high, low], axis=0)
                sums = dot(operand, weight_ref[held])
                piece = sums[0:both, 0:VOX] + sums[both:, 0:VOX] + sums[0:both, VOX:]
                total = piece if total is None else total + piece
            update_ref[q] = total if first else update_ref[q] + total
            return carry

        lax.fori_loop(0, pairs, pair, 0)

    forward(True)
    backward(True)
    forward(False)
    backward(False)
    turned = reversed_exact(update_ref[:, slices:both, :].reshape(pairs * slices, VOX))
    diff_ref[0:pairs] = turned.reshape(pairs, slices, VOX)

    def finish(q, carry):
        direct = slot_ref[q]
        mirror = slot_ref[patches - 1 - q]
        out_ref[direct] = vol_ref[direct] + step_size * update_ref[q, 0:slices, :]
        out_ref[mirror] = vol_ref[mirror] + step_size * diff_ref[q]
        return carry

    lax.fori_loop(0, pairs, finish, 0)


def sirt(volume, sino, theta, vol_list, step_size):
    patches, slices, _ = volume.shape
    angles = sino.shape[0]
    pairs = patches // 2
    chunk = math.gcd(angles, 32)
    held = pairs if angles == chunk else 1
    centre = (ROI - 1) / 2.0
    ids = np.arange(pairs)
    centre_x = (ids // PGRID * float(SIDE) + (SIDE - 1) / 2.0 - centre).astype(np.float32)
    centre_y = (ids % PGRID * float(SIDE) + (SIDE - 1) / 2.0 - centre).astype(np.float32)
    cosine = jnp.cos(theta)
    sine = jnp.sin(theta)
    along = centre_x[:, None] * cosine[None, :] + centre_y[:, None] * sine[None, :] + 0.5
    whole = jnp.floor(along)
    lead = WIN // 2 - 1
    place = along - whole + float(lead)
    offset = whole.astype(jnp.int32) + (ACTIVE // 2 - 1 - lead)
    tile = jnp.minimum(offset // SPLIT, 2)
    local = jnp.arange(angles, dtype=jnp.int32) % chunk * WIN
    turn = (local[None, :] - offset + tile * SPLIT) % LANES
    slot = jnp.sum(
        jnp.where(
            vol_list[None, :] == jnp.arange(patches, dtype=jnp.int32)[:, None],
            jnp.arange(patches, dtype=jnp.int32)[None, :],
            0,
        ),
        axis=1,
    )
    voxel = np.arange(VOX)
    shift_x = np.repeat((voxel // SIDE - (SIDE - 1) / 2.0)[None, :], ROWS, axis=0)
    shift_y = np.repeat((voxel % SIDE - (SIDE - 1) / 2.0)[None, :], ROWS, axis=0)
    flip = np.eye(ACTIVE)[::-1].astype(ml_dtypes.bfloat16)
    smem = pl.BlockSpec(memory_space=pltpu.SMEM)
    vmem = pl.BlockSpec(memory_space=pltpu.VMEM)
    both = 2 * slices
    macs = 3 * patches * VOX * angles * WIN * slices
    return pl.pallas_call(
        functools.partial(sirt_kernel, step_size, chunk),
        out_shape=(
            jax.ShapeDtypeStruct(volume.shape, f32),
            jax.ShapeDtypeStruct(sino.shape, f32),
        ),
        in_specs=[smem] * 7 + [vmem] * 5,
        out_specs=[vmem] * 2,
        scratch_shapes=[
            pltpu.VMEM((held, chunk * WIN, 2 * VOX), bf16),
            pltpu.VMEM((angles, ACTIVE, 3 * both), f32),
            pltpu.VMEM((angles, ROWS, VOX), f32),
            pltpu.VMEM((pairs, both, VOX), f32),
            pltpu.VMEM((pairs, both, VOX), f32),
            pltpu.VMEM((max(pairs, angles), slices, ACTIVE), f32),
            pltpu.VMEM((angles, slices, ACTIVE), f32),
            pltpu.VMEM((angles, 3, both, LANES), f32),
        ],
        compiler_params=pltpu.CompilerParams(vmem_limit_bytes=56 * 2**20),
        cost_estimate=pl.CostEstimate(
            flops=8 * macs, bytes_accessed=4 * volume.size * 4, transcendentals=0
        ),
        name="sirt",
    )(
        offset.reshape(-1),
        tile.reshape(-1),
        turn.reshape(-1),
        place.reshape(-1),
        slot,
        cosine,
        sine,
        volume,
        sino,
        jnp.asarray(flip),
        jnp.asarray(shift_x, f32),
        jnp.asarray(shift_y, f32),
    )


def local(intensity, angles, volume, vol_list):
    n_slab = lax.axis_size("slab")
    n_ray = lax.axis_size("ray")
    devices = n_slab * n_ray
    height, band = intensity.shape[2:]
    slab_rows = height // n_slab
    slices = height // devices
    slots = volume.shape[1]
    count = angles.shape[0] * angles.shape[1]
    step_size = relax * ROI / count
    theta = angles.reshape(-1)

    spread = jnp.transpose(volume.reshape(n_ray, slices, slots, VOX), (0, 2, 1, 3))
    spread = lax.all_to_all(spread, "ray", split_axis=0, concat_axis=0, tiled=True)
    own_volume = spread.reshape(n_ray * slots, slices, VOX)

    projected, active = paganin(intensity.reshape(height, band))
    own_rays = lax.all_to_all(
        active.reshape(devices, slices, ACTIVE),
        ("slab", "ray"),
        split_axis=0,
        concat_axis=0,
        tiled=True,
    )
    pieces = projected.reshape(n_slab, slab_rows, band)
    sinogram = lax.all_to_all(pieces, "slab", split_axis=0, concat_axis=0, tiled=True)

    padded = -(-slices // ROWS) * ROWS
    if padded != slices:
        widen = ((0, 0), (0, padded - slices), (0, 0))
        own_volume = jnp.pad(own_volume, widen)
        own_rays = jnp.pad(own_rays, widen)
    result, residual = sirt(own_volume, own_rays, theta, vol_list, step_size)
    result = result[:, :slices].reshape(n_ray, slots, slices, VOX)
    residual = residual[:, :slices].reshape(n_slab, n_ray, slices, ACTIVE)

    result = lax.all_to_all(result, "ray", split_axis=0, concat_axis=0, tiled=True)
    reconstruction = jnp.transpose(result, (0, 2, 1, 3)).reshape(volume.shape)
    residual = lax.all_to_all(residual, "ray", split_axis=1, concat_axis=1, tiled=True)
    residual = residual.reshape(n_slab, slab_rows, ACTIVE)
    offset = (band - ACTIVE) // 2
    residual_out = lax.dynamic_update_slice(sinogram, residual, (0, 0, offset))
    return (reconstruction, residual_out[:, None])


def solution(mesh):
    placed = (P("slab", "ray", None, None), P(), P("slab", "ray", None), P())
    return jax.shard_map(
        local,
        mesh=mesh,
        in_specs=placed,
        out_specs=(P("slab", "ray", None), P(None, "ray", "slab", None)),
        check_vma=False,
    )
```

```python
import functools
import math

import jax
import jax.numpy as jnp
import ml_dtypes
import numpy as np
from jax import lax
from jax.experimental import pallas as pl
from jax.experimental.pallas import tpu as pltpu
from jax.sharding import PartitionSpec as P

BAND = 2048
PGRID = 8
ROI = 128
SIDE = 16
VOX = SIDE * SIDE
WIN = 24
ACTIVE = 256
LANES = 128
ROWS = 8
SPLIT = 64

paganin_strength = 10.0
relax = 1.8
row_floor = 0.25

bf16 = jnp.bfloat16
f32 = jnp.float32


def halves(values):
    high = values.astype(bf16)
    low = (values - high.astype(f32)).astype(bf16)
    return high, low


def thirds(values):
    high = values.astype(bf16)
    rest = values - high.astype(f32)
    middle = rest.astype(bf16)
    low = (rest - middle.astype(f32)).astype(bf16)
    return high, middle, low


def dot(left, right):
    return jnp.dot(left, right, preferred_element_type=f32)


def filter_tables(height):
    index = np.arange(height)
    phase = 2.0 * np.pi * (np.outer(index, index) % height) / height
    cas = (np.cos(phase) + np.sin(phase)) / math.sqrt(height)
    row_freq = 2.0 - 2.0 * np.cos(2.0 * np.pi * index / height)
    middle = (1.0 + paganin_strength * row_freq) / paganin_strength + 2.0
    rho = (middle - np.sqrt(middle * middle - 4.0)) / 2.0
    return np.concatenate([cas, np.repeat(rho[None, :], ROWS, axis=0)], axis=0).astype(np.float32)


def chunk_carry(ends, power, forward):
    shift = 1
    for _ in range(3):
        ends = ends + power * pltpu.roll(ends, shift if forward else ROWS - shift, 0)
        power = power * power
        shift *= 2
    return pltpu.roll(ends, 1 if forward else ROWS - 1, 0) / (1.0 - power)


def filter_kernel(rank_ref, image_ref, table_ref, *refs):
    *part_refs, active_ref, out_ref, spec_ref, up_ref, down_ref = refs
    height, width = image_ref.shape
    rank = rank_ref[0]
    share = height // len(part_refs)
    length = width // ROWS
    blocks = height // LANES
    unroll = 8
    cas_high, cas_low = halves(table_ref[0:height, :])
    rho_all = table_ref[height : height + ROWS, :]
    rhos = [rho_all[:, b * LANES : (b + 1) * LANES] for b in range(blocks)]
    zeros = [jnp.zeros((ROWS, LANES), f32)] * blocks

    def transform(values):
        high, low = halves(values)
        return dot(high, cas_high) + dot(low, cas_high) + dot(high, cas_low)

    for c in range(ROWS):
        image = 1.0 - image_ref[:, c * length : (c + 1) * length]
        spectrum = transform(jnp.transpose(image))
        for b in range(blocks):
            spec_ref[b, pl.ds(c, length, stride=ROWS), :] = spectrum[
                :, b * LANES : (b + 1) * LANES
            ]

    def rows(position):
        return pl.ds(pl.multiple_of(position * ROWS, ROWS), ROWS)

    def advance(position, ups, downs):
        ups = [spec_ref[b, rows(position), :] + rhos[b] * ups[b] for b in range(blocks)]
        back = length - 1 - position
        downs = [spec_ref[b, rows(back), :] + rhos[b] * downs[b] for b in range(blocks)]
        return ups, downs

    def sweep(index, carry):
        ups, downs = carry
        for step in range(unroll):
            ups, downs = advance(index * unroll + step, ups, downs)
        return ups, downs

    ups, downs = lax.fori_loop(0, length // unroll, sweep, (zeros, zeros))
    powers = list(rhos)
    for _ in range(int(math.log2(length))):
        powers = [power * power for power in powers]
    ups = [chunk_carry(ups[b], powers[b], True) for b in range(blocks)]
    downs = [chunk_carry(downs[b], powers[b], False) for b in range(blocks)]
    scales = [rho / (paganin_strength * (1.0 - rho * rho)) for rho in rhos]

    def outer(index, carry):
        ups, downs = carry
        for step in range(unroll):
            position = index * unroll + step
            ups, downs = advance(position, ups, downs)
            for b in range(blocks):
                up_ref[b, rows(position), :] = ups[b]
                down_ref[b, rows(position), :] = downs[b]
        return ups, downs

    def inner(index, carry):
        ups, downs = carry
        for step in range(unroll):
            position = index * unroll + step
            back = length - 1 - position
            ups, downs = advance(position, ups, downs)
            for b in range(blocks):
                here = ups[b] + down_ref[b, rows(back), :] - spec_ref[b, rows(position), :]
                there = downs[b] + up_ref[b, rows(back), :] - spec_ref[b, rows(back), :]
                up_ref[b, rows(position), :] = here * scales[b]
                up_ref[b, rows(back), :] = there * scales[b]
        return ups, downs

    half = length // 2 // unroll
    carry = lax.fori_loop(0, half, outer, (ups, downs))
    lax.fori_loop(half, 2 * half, inner, carry)

    offset = (width - ACTIVE) // 2
    for c in range(ROWS):
        spectrum = jnp.concatenate(
            [up_ref[b, pl.ds(c, length, stride=ROWS), :] for b in range(blocks)], axis=1
        )
        filtered = 1.0 - jnp.transpose(transform(spectrum))
        out_ref[:, c * length : (c + 1) * length] = -jnp.log(filtered)
    active_ref[...] = out_ref[:, offset : offset + ACTIVE]
    for d, part_ref in enumerate(part_refs):
        part_ref[...] = out_ref[pl.ds(pl.multiple_of((rank ^ d) * share, share), share), :]


def paganin(image, rank, parts):
    height, width = image.shape
    blocks = height // LANES
    return pl.pallas_call(
        filter_kernel,
        out_shape=[jax.ShapeDtypeStruct((height // parts, width), f32)] * parts
        + [jax.ShapeDtypeStruct((height, ACTIVE), f32)],
        in_specs=[pl.BlockSpec(memory_space=pltpu.SMEM)]
        + [pl.BlockSpec(memory_space=pltpu.VMEM)] * 2,
        out_specs=[pl.BlockSpec(memory_space=pltpu.VMEM)] * (parts + 1),
        scratch_shapes=[
            pltpu.VMEM((height, width), f32),
            pltpu.VMEM((blocks, width, LANES), f32),
            pltpu.VMEM((blocks, width, LANES), f32),
            pltpu.VMEM((blocks, width // 2, LANES), f32),
        ],
        compiler_params=pltpu.CompilerParams(vmem_limit_bytes=32 * 2**20),
        cost_estimate=pl.CostEstimate(
            flops=64 * height * height * width,
            bytes_accessed=8 * height * width,
            transcendentals=height * width,
        ),
        name="paganin",
    )(rank.reshape(1), image, jnp.asarray(filter_tables(height)))


def sirt_kernel(
    step_size,
    chunk,
    offset_ref,
    tile_ref,
    turn_ref,
    place_ref,
    slot_ref,
    cos_ref,
    sin_ref,
    vol_ref,
    sino_ref,
    flip_ref,
    shift_x_ref,
    shift_y_ref,
    out_ref,
    weight_ref,
    acc_ref,
    along_ref,
    start_ref,
    update_ref,
    diff_ref,
    res_ref,
    gain_ref,
    window_ref,
    half_ref,
):
    rays, held_rows, _ = vol_ref.shape
    patches = slot_ref.shape[0]
    slots = patches // rays
    slices = held_rows // slots
    angles = sino_ref.shape[0]
    pairs = patches // 2
    both = 2 * slices
    chunks = angles // chunk
    cached = chunks == 1
    width = chunk * WIN
    flip = flip_ref[...]
    lane_rows = lax.broadcasted_iota(jnp.int32, (both, LANES), 1)

    def reversed_exact(values):
        return sum(dot(part, flip) for part in thirds(values))

    def slot_rows(patch):
        slot = slot_ref[patch]
        return slot // slots, pl.ds(slot % slots, slices, stride=slots)

    def slot_values(patch):
        ray, rows = slot_rows(patch)
        return jnp.concatenate(
            [half_ref[0, ray, rows, :], half_ref[1, ray, rows, :]], axis=1
        )

    for part in range(2):
        half_ref[part] = vol_ref[:, :, part * LANES : (part + 1) * LANES]

    def along_angle(t, carry):
        along_ref[t] = shift_x_ref[...] * cos_ref[t] + shift_y_ref[...] * sin_ref[t]
        return carry

    lax.fori_loop(0, angles, along_angle, 0)

    def first_order(q, carry):
        diff_ref[q] = slot_values(patches - 1 - q)
        return carry

    lax.fori_loop(0, pairs, first_order, 0)
    turned = reversed_exact(diff_ref[0:pairs].reshape(pairs * slices, VOX))
    start_ref[:, slices:both, :] = turned.reshape(pairs, slices, VOX)

    def second_order(q, carry):
        start_ref[q, 0:slices, :] = slot_values(q)
        return carry

    lax.fori_loop(0, pairs, second_order, 0)

    ray = lax.broadcasted_iota(jnp.int32, (ROWS, VOX), 0).astype(f32)

    def make_weights(q, c):
        held = q if cached else 0
        for two in range(chunk // 2):
            pieces = []
            for t in (2 * two, 2 * two + 1):
                angle = c * chunk + t
                base = ray - (along_ref[angle] + place_ref[q * angles + angle])
                for group in range(WIN // ROWS):
                    distance = base + float(group * ROWS)
                    pieces.append(jnp.maximum(0.0, 1.0 - jnp.abs(distance)))
            high, low = halves(jnp.concatenate(pieces, axis=0))
            weight_ref[held, 2 * two * WIN : (2 * two + 2) * WIN, 0:VOX] = high
            weight_ref[held, 2 * two * WIN : (2 * two + 2) * WIN, VOX : 2 * VOX] = low

    def forward(first):
        acc_ref[...] = jnp.zeros(acc_ref.shape, f32)

        def pair(q, carry):
            values = start_ref[q]
            if not first:
                values = values + step_size * update_ref[q]
            high, low = halves(values)
            operand = jnp.concatenate(
                [
                    jnp.concatenate([high, high], axis=1),
                    jnp.concatenate([low, jnp.zeros_like(low)], axis=1),
                    jnp.ones((both, 2 * VOX), bf16),
                ],
                axis=0,
            )
            for c in range(chunks):
                if first or not cached:
                    make_weights(q, c)
                held = q if cached else 0
                sums = lax.dot_general(
                    weight_ref[held],
                    operand,
                    (((1,), (1,)), ((), ())),
                    preferred_element_type=f32,
                )
                for t in range(chunk):
                    angle = c * chunk + t
                    rows = pl.ds(offset_ref[q * angles + angle], WIN)
                    acc_ref[angle, rows, :] = (
                        acc_ref[angle, rows, :] + sums[t * WIN : (t + 1) * WIN, :]
                    )
            return carry

        lax.fori_loop(0, pairs, pair, 0)

        def spread(t, carry):
            rows = jnp.transpose(acc_ref[t]) * (1.0 / ROI)
            diff_ref[t] = rows[0:slices] + rows[both : both + slices]
            res_ref[t] = rows[slices:both] + rows[both + slices : 2 * both]
            if first:
                gain_ref[t] = rows[2 * both : 2 * both + slices]
            return carry

        lax.fori_loop(0, angles, spread, 0)
        flat = (angles * slices, ACTIVE)
        full = (angles, slices, ACTIVE)
        mirrored = reversed_exact(res_ref[...].reshape(flat)).reshape(full)
        res_ref[...] = sino_ref[...] - diff_ref[0:angles] - mirrored
        if first:
            direct = gain_ref[...]
            total = direct + reversed_exact(direct.reshape(flat)).reshape(full)
            gain_ref[...] = 1.0 / jnp.maximum(total, row_floor)

    def backward(first):
        weighted = res_ref[...] * gain_ref[...] * (1.0 / ROI)
        flat = (angles * slices, ACTIVE)
        full = (angles, slices, ACTIVE)
        high, low = halves(weighted.reshape(flat))
        mirrored = (dot(high, flip) + dot(low, flip)).reshape(full)
        lane = lax.broadcasted_iota(jnp.int32, (angles, slices, LANES), 2)
        for part, source in enumerate((weighted, mirrored)):
            rows = slice(part * slices, (part + 1) * slices)
            left = source[:, :, 0:LANES]
            right = source[:, :, LANES : 2 * LANES]
            window_ref[:, 0, rows, :] = left
            window_ref[:, 2, rows, :] = right
            mixed = jnp.where(lane >= SPLIT, left, right)
            window_ref[:, 1, rows, :] = pltpu.roll(mixed, SPLIT, 2)

        def pair(q, carry):
            total = None
            for c in range(chunks):
                if not cached:
                    make_weights(q, c)
                held = q if cached else 0
                tiles = [None] * (-(-width // LANES))
                for t in range(chunk):
                    index = q * angles + c * chunk + t
                    piece = pltpu.roll(
                        window_ref[c * chunk + t, tile_ref[index]], turn_ref[index], 1
                    )
                    begin = t * WIN
                    for place in range(begin // LANES, (begin + WIN - 1) // LANES + 1):
                        if tiles[place] is None:
                            tiles[place] = piece
                        else:
                            tiles[place] = jnp.where(
                                lane_rows >= begin - place * LANES, piece, tiles[place]
                            )
                high, low = halves(jnp.concatenate(tiles, axis=1))
                operand = jnp.concatenate([high, low], axis=0)
                sums = dot(operand, weight_ref[held])
                piece = sums[0:both, 0:VOX] + sums[both:, 0:VOX] + sums[0:both, VOX:]
                total = piece if total is None else total + piece
            update_ref[q] = total if first else update_ref[q] + total
            return carry

        lax.fori_loop(0, pairs, pair, 0)

    forward(True)
    backward(True)
    forward(False)
    backward(False)
    turned = reversed_exact(update_ref[:, slices:both, :].reshape(pairs * slices, VOX))
    diff_ref[0:pairs] = turned.reshape(pairs, slices, VOX)

    def finish(q, carry):
        for patch, update in (
            (q, update_ref[q, 0:slices, :]),
            (patches - 1 - q, diff_ref[q]),
        ):
            ray, rows = slot_rows(patch)
            values = slot_values(patch) + step_size * update
            half_ref[0, ray, rows, :] = values[:, 0:LANES]
            half_ref[1, ray, rows, :] = values[:, LANES : 2 * LANES]
        return carry

    lax.fori_loop(0, pairs, finish, 0)
    for part in range(2):
        out_ref[:, 0:held_rows, part * LANES : (part + 1) * LANES] = half_ref[part]
    for t in range(angles):
        begin = held_rows + t // rays * slices
        out_ref[t % rays, begin : begin + slices, :] = res_ref[t]


def sirt(volume, sino, theta, vol_list, step_size):
    rays, held_rows, _ = volume.shape
    patches = vol_list.shape[0]
    angles, slices, _ = sino.shape
    pairs = patches // 2
    sent_rows = held_rows + angles // rays * slices
    chunk = math.gcd(angles, 32)
    held = pairs if angles == chunk else 1
    centre = (ROI - 1) / 2.0
    ids = np.arange(pairs)
    centre_x = (ids // PGRID * float(SIDE) + (SIDE - 1) / 2.0 - centre).astype(np.float32)
    centre_y = (ids % PGRID * float(SIDE) + (SIDE - 1) / 2.0 - centre).astype(np.float32)
    cosine = jnp.cos(theta)
    sine = jnp.sin(theta)
    along = centre_x[:, None] * cosine[None, :] + centre_y[:, None] * sine[None, :] + 0.5
    whole = jnp.floor(along)
    lead = WIN // 2 - 1
    place = along - whole + float(lead)
    offset = whole.astype(jnp.int32) + (ACTIVE // 2 - 1 - lead)
    tile = jnp.minimum(offset // SPLIT, 2)
    local = jnp.arange(angles, dtype=jnp.int32) % chunk * WIN
    turn = (local[None, :] - offset + tile * SPLIT) % LANES
    slot = jnp.sum(
        jnp.where(
            vol_list[None, :] == jnp.arange(patches, dtype=jnp.int32)[:, None],
            jnp.arange(patches, dtype=jnp.int32)[None, :],
            0,
        ),
        axis=1,
    )
    voxel = np.arange(VOX)
    shift_x = np.repeat((voxel // SIDE - (SIDE - 1) / 2.0)[None, :], ROWS, axis=0)
    shift_y = np.repeat((voxel % SIDE - (SIDE - 1) / 2.0)[None, :], ROWS, axis=0)
    flip = np.eye(ACTIVE)[::-1].astype(ml_dtypes.bfloat16)
    smem = pl.BlockSpec(memory_space=pltpu.SMEM)
    vmem = pl.BlockSpec(memory_space=pltpu.VMEM)
    both = 2 * slices
    macs = 3 * patches * VOX * angles * WIN * slices
    return pl.pallas_call(
        functools.partial(sirt_kernel, step_size, chunk),
        out_shape=jax.ShapeDtypeStruct((rays, sent_rows, VOX), f32),
        in_specs=[smem] * 7 + [vmem] * 5,
        out_specs=vmem,
        scratch_shapes=[
            pltpu.VMEM((held, chunk * WIN, 2 * VOX), bf16),
            pltpu.VMEM((angles, ACTIVE, 3 * both), f32),
            pltpu.VMEM((angles, ROWS, VOX), f32),
            pltpu.VMEM((pairs, both, VOX), f32),
            pltpu.VMEM((pairs, both, VOX), f32),
            pltpu.VMEM((max(pairs, angles), slices, ACTIVE), f32),
            pltpu.VMEM((angles, slices, ACTIVE), f32),
            pltpu.VMEM((angles, slices, ACTIVE), f32),
            pltpu.VMEM((angles, 3, both, LANES), f32),
            pltpu.VMEM((2, rays, held_rows, LANES), f32),
        ],
        compiler_params=pltpu.CompilerParams(vmem_limit_bytes=56 * 2**20),
        cost_estimate=pl.CostEstimate(
            flops=128 * macs, bytes_accessed=4 * volume.size * 4, transcendentals=0
        ),
        name="sirt",
    )(
        offset.reshape(-1),
        tile.reshape(-1),
        turn.reshape(-1),
        place.reshape(-1),
        slot,
        cosine,
        sine,
        volume,
        sino,
        jnp.asarray(flip),
        jnp.asarray(shift_x, f32),
        jnp.asarray(shift_y, f32),
    )


def gather_kernel(rank_ref, *refs):
    *part_refs, out_ref, sems = refs
    rank = rank_ref[0]
    copies = [
        pltpu.make_async_copy(part_ref, out_ref.at[rank ^ d], sems.at[d])
        for d, part_ref in enumerate(part_refs)
    ]
    for copy in copies:
        copy.start()
    for copy in copies:
        copy.wait()


def gather_parts(parts, rank):
    count = len(parts)
    return pl.pallas_call(
        gather_kernel,
        out_shape=jax.ShapeDtypeStruct((count,) + parts[0].shape, f32),
        in_specs=[pl.BlockSpec(memory_space=pltpu.SMEM)]
        + [pl.BlockSpec(memory_space=pl.ANY)] * count,
        out_specs=pl.BlockSpec(memory_space=pl.ANY),
        scratch_shapes=[pltpu.SemaphoreType.DMA((count,))],
        cost_estimate=pl.CostEstimate(
            flops=0, bytes_accessed=8 * count * parts[0].size, transcendentals=0
        ),
        name="gather_parts",
    )(rank.reshape(1), *parts)


def finish_kernel(slots, got_ref, sino_ref, rec_ref, out_ref, values_ref, active_ref, sems):
    rays, rows, _ = got_ref.shape
    slabs = active_ref.shape[0]
    held = rows * slots // (slots + slabs)
    slices = held // slots
    for ray in range(rays):
        values_ref[ray * slices : (ray + 1) * slices] = got_ref[ray, 0:held, :].reshape(
            slices, slots, VOX
        )
        for k in range(slabs):
            begin = held + k * slices
            active_ref[k, ray * slices : (ray + 1) * slices, :] = got_ref[
                ray, begin : begin + slices, :
            ]
    offset = (out_ref.shape[2] - ACTIVE) // 2
    copies = [
        pltpu.make_async_copy(values_ref, rec_ref, sems.at[0]),
        pltpu.make_async_copy(
            active_ref, out_ref.at[:, :, offset : offset + ACTIVE], sems.at[1]
        ),
    ]
    for copy in copies:
        copy.start()
    for copy in copies:
        copy.wait()


def finish(got, sinogram, shape):
    slabs, slab_rows, _ = sinogram.shape
    any_space = pl.BlockSpec(memory_space=pl.ANY)
    return pl.pallas_call(
        functools.partial(finish_kernel, shape[1]),
        out_shape=(
            jax.ShapeDtypeStruct(shape, f32),
            jax.ShapeDtypeStruct(sinogram.shape, f32),
        ),
        in_specs=[pl.BlockSpec(memory_space=pltpu.VMEM), any_space],
        out_specs=[any_space, any_space],
        scratch_shapes=[
            pltpu.VMEM(shape, f32),
            pltpu.VMEM((slabs, slab_rows, ACTIVE), f32),
            pltpu.SemaphoreType.DMA((2,)),
        ],
        input_output_aliases={1: 1},
        compiler_params=pltpu.CompilerParams(vmem_limit_bytes=32 * 2**20),
        cost_estimate=pl.CostEstimate(
            flops=0, bytes_accessed=8 * got.size, transcendentals=0
        ),
        name="finish",
    )(got, sinogram)


def local(intensity, angles, volume, vol_list):
    n_slab = lax.axis_size("slab")
    n_ray = lax.axis_size("ray")
    devices = n_slab * n_ray
    height, band = intensity.shape[2:]
    slab_rows = height // n_slab
    slices = height // devices
    slots = volume.shape[1]
    count = angles.shape[0] * angles.shape[1]
    step_size = relax * ROI / count
    theta = angles.reshape(-1)
    rank = lax.axis_index("slab")

    spread = volume.reshape(n_ray, slices * slots, VOX)
    own_volume = lax.all_to_all(spread, "ray", split_axis=0, concat_axis=0, tiled=True)

    *parts, active = paganin(intensity.reshape(height, band), rank, n_slab)
    own_rays = lax.all_to_all(
        active.reshape(devices, slices, ACTIVE),
        ("slab", "ray"),
        split_axis=0,
        concat_axis=0,
        tiled=True,
    )
    parts = [
        lax.ppermute(part, "slab", [(i, i ^ d) for i in range(n_slab)]) if d else part
        for d, part in enumerate(parts)
    ]

    padded = -(-slices // ROWS) * ROWS
    if padded != slices:
        widen = ((0, 0), (0, padded - slices), (0, 0))
        own_volume = jnp.pad(own_volume, ((0, 0), (0, (padded - slices) * slots), (0, 0)))
        own_rays = jnp.pad(own_rays, widen)
    result = sirt(own_volume, own_rays, theta, vol_list, step_size)
    if padded != slices:
        lower = result[:, padded * slots :].reshape(n_ray, n_slab, padded, ACTIVE)
        lower = lower[:, :, :slices].reshape(n_ray, n_slab * slices, ACTIVE)
        result = jnp.concatenate([result[:, : slices * slots], lower], axis=1)
    result = lax.all_to_all(result, "ray", split_axis=0, concat_axis=0, tiled=True)
    sinogram = gather_parts(parts, rank)
    reconstruction, residual = finish(result, sinogram, volume.shape)
    return (reconstruction, residual[:, None])


def solution(mesh):
    placed = (P("slab", "ray", None, None), P(), P("slab", "ray", None), P())
    return jax.shard_map(
        local,
        mesh=mesh,
        in_specs=placed,
        out_specs=(P("slab", "ray", None), P(None, "ray", "slab", None)),
        check_vma=False,
    )
```

```python
import functools
import math

import jax
import jax.numpy as jnp
import ml_dtypes
import numpy as np
from jax import lax
from jax.experimental import pallas as pl
from jax.experimental.pallas import tpu as pltpu
from jax.sharding import PartitionSpec as P

BAND = 2048
PGRID = 8
ROI = 128
SIDE = 16
VOX = SIDE * SIDE
WIN = 24
ACTIVE = 256
LANES = 128
ROWS = 8
SPLIT = 64
GROUP = 8
PAIR_UNROLL = 2

paganin_strength = 10.0
relax = 1.8
row_floor = 0.25

bf16 = jnp.bfloat16
f32 = jnp.float32


def halves(values):
    high = values.astype(bf16)
    low = (values - high.astype(f32)).astype(bf16)
    return high, low


def thirds(values):
    high = values.astype(bf16)
    rest = values - high.astype(f32)
    middle = rest.astype(bf16)
    low = (rest - middle.astype(f32)).astype(bf16)
    return high, middle, low


def dot(left, right):
    return jnp.dot(left, right, preferred_element_type=f32)


def repeat(count, body, unroll):
    unroll = math.gcd(count, unroll)

    def several(index, carry):
        for step in range(unroll):
            body(index * unroll + step)
        return carry

    lax.fori_loop(0, count // unroll, several, 0)


def filter_tables(height):
    index = np.arange(height)
    phase = 2.0 * np.pi * (np.outer(index, index) % height) / height
    cas = (np.cos(phase) + np.sin(phase)) / math.sqrt(height)
    row_freq = 2.0 - 2.0 * np.cos(2.0 * np.pi * index / height)
    middle = (1.0 + paganin_strength * row_freq) / paganin_strength + 2.0
    rho = (middle - np.sqrt(middle * middle - 4.0)) / 2.0
    return np.concatenate([cas, np.repeat(rho[None, :], ROWS, axis=0)], axis=0).astype(np.float32)


def chunk_carry(ends, power, forward):
    shift = 1
    for _ in range(3):
        ends = ends + power * pltpu.roll(ends, shift if forward else ROWS - shift, 0)
        power = power * power
        shift *= 2
    return pltpu.roll(ends, 1 if forward else ROWS - 1, 0) / (1.0 - power)


def filter_kernel(rank_ref, image_ref, table_ref, *refs):
    *part_refs, active_ref, out_ref, spec_ref, up_ref, down_ref = refs
    height, width = image_ref.shape
    rank = rank_ref[0]
    share = height // len(part_refs)
    length = width // ROWS
    blocks = height // LANES
    unroll = 8
    cas_high, cas_low = halves(table_ref[0:height, :])
    rho_all = table_ref[height : height + ROWS, :]
    rhos = [rho_all[:, b * LANES : (b + 1) * LANES] for b in range(blocks)]
    zeros = [jnp.zeros((ROWS, LANES), f32)] * blocks

    def transform(values):
        high, low = halves(values)
        return dot(high, cas_high) + dot(low, cas_high) + dot(high, cas_low)

    for c in range(ROWS):
        image = 1.0 - image_ref[:, c * length : (c + 1) * length]
        spectrum = transform(jnp.transpose(image))
        for b in range(blocks):
            spec_ref[b, pl.ds(c, length, stride=ROWS), :] = spectrum[
                :, b * LANES : (b + 1) * LANES
            ]

    def rows(position):
        return pl.ds(pl.multiple_of(position * ROWS, ROWS), ROWS)

    def advance(position, ups, downs):
        ups = [spec_ref[b, rows(position), :] + rhos[b] * ups[b] for b in range(blocks)]
        back = length - 1 - position
        downs = [spec_ref[b, rows(back), :] + rhos[b] * downs[b] for b in range(blocks)]
        return ups, downs

    def sweep(index, carry):
        ups, downs = carry
        for step in range(unroll):
            ups, downs = advance(index * unroll + step, ups, downs)
        return ups, downs

    ups, downs = lax.fori_loop(0, length // unroll, sweep, (zeros, zeros))
    powers = list(rhos)
    for _ in range(int(math.log2(length))):
        powers = [power * power for power in powers]
    ups = [chunk_carry(ups[b], powers[b], True) for b in range(blocks)]
    downs = [chunk_carry(downs[b], powers[b], False) for b in range(blocks)]
    scales = [rho / (paganin_strength * (1.0 - rho * rho)) for rho in rhos]

    def outer(index, carry):
        ups, downs = carry
        for step in range(unroll):
            position = index * unroll + step
            ups, downs = advance(position, ups, downs)
            for b in range(blocks):
                up_ref[b, rows(position), :] = ups[b]
                down_ref[b, rows(position), :] = downs[b]
        return ups, downs

    def inner(index, carry):
        ups, downs = carry
        for step in range(unroll):
            position = index * unroll + step
            back = length - 1 - position
            ups, downs = advance(position, ups, downs)
            for b in range(blocks):
                here = ups[b] + down_ref[b, rows(back), :] - spec_ref[b, rows(position), :]
                there = downs[b] + up_ref[b, rows(back), :] - spec_ref[b, rows(back), :]
                up_ref[b, rows(position), :] = here * scales[b]
                up_ref[b, rows(back), :] = there * scales[b]
        return ups, downs

    half = length // 2 // unroll
    carry = lax.fori_loop(0, half, outer, (ups, downs))
    lax.fori_loop(half, 2 * half, inner, carry)

    offset = (width - ACTIVE) // 2
    for c in range(ROWS):
        spectrum = jnp.concatenate(
            [up_ref[b, pl.ds(c, length, stride=ROWS), :] for b in range(blocks)], axis=1
        )
        filtered = 1.0 - jnp.transpose(transform(spectrum))
        out_ref[:, c * length : (c + 1) * length] = -jnp.log(filtered)
    active_ref[...] = out_ref[:, offset : offset + ACTIVE]
    for d, part_ref in enumerate(part_refs):
        part_ref[...] = out_ref[pl.ds(pl.multiple_of((rank ^ d) * share, share), share), :]


def paganin(image, rank, parts):
    height, width = image.shape
    blocks = height // LANES
    return pl.pallas_call(
        filter_kernel,
        out_shape=[jax.ShapeDtypeStruct((height // parts, width), f32)] * parts
        + [jax.ShapeDtypeStruct((height, ACTIVE), f32)],
        in_specs=[pl.BlockSpec(memory_space=pltpu.SMEM)]
        + [pl.BlockSpec(memory_space=pltpu.VMEM)] * 2,
        out_specs=[pl.BlockSpec(memory_space=pltpu.VMEM)] * (parts + 1),
        scratch_shapes=[
            pltpu.VMEM((height, width), f32),
            pltpu.VMEM((blocks, width, LANES), f32),
            pltpu.VMEM((blocks, width, LANES), f32),
            pltpu.VMEM((blocks, width // 2, LANES), f32),
        ],
        compiler_params=pltpu.CompilerParams(vmem_limit_bytes=32 * 2**20),
        cost_estimate=pl.CostEstimate(
            flops=64 * height * height * width,
            bytes_accessed=8 * height * width,
            transcendentals=height * width,
        ),
        name="paganin",
    )(rank.reshape(1), image, jnp.asarray(filter_tables(height)))


def sirt_kernel(
    step_size,
    chunk,
    offset_ref,
    tile_ref,
    turn_ref,
    place_ref,
    slot_ref,
    cos_ref,
    sin_ref,
    vol_ref,
    sino_ref,
    flip_ref,
    shift_x_ref,
    shift_y_ref,
    out_ref,
    weight_ref,
    acc_ref,
    along_ref,
    start_ref,
    update_ref,
    diff_ref,
    res_ref,
    gain_ref,
    window_ref,
    half_ref,
):
    rays, held_rows, _ = vol_ref.shape
    patches = slot_ref.shape[0]
    slots = patches // rays
    slices = held_rows // slots
    angles = sino_ref.shape[0]
    pairs = patches // 2
    both = 2 * slices
    chunks = angles // chunk
    cached = chunks == 1
    width = chunk * WIN
    flip = flip_ref[...]
    lane_rows = lax.broadcasted_iota(jnp.int32, (both, LANES), 1)

    def reversed_exact(values):
        return sum(dot(part, flip) for part in thirds(values))

    def slot_rows(patch):
        slot = slot_ref[patch]
        return slot // slots, pl.ds(slot % slots, slices, stride=slots)

    def slot_values(patch):
        ray, rows = slot_rows(patch)
        return jnp.concatenate(
            [half_ref[0, ray, rows, :], half_ref[1, ray, rows, :]], axis=1
        )

    for part in range(2):
        half_ref[part] = vol_ref[:, :, part * LANES : (part + 1) * LANES]

    def along_angle(t):
        along_ref[t] = shift_x_ref[...] * cos_ref[t] + shift_y_ref[...] * sin_ref[t]

    repeat(angles, along_angle, 8)

    def first_order(q):
        diff_ref[q] = slot_values(patches - 1 - q)

    repeat(pairs, first_order, 8)
    turned = reversed_exact(diff_ref[0:pairs].reshape(pairs * slices, VOX))
    start_ref[:, slices:both, :] = turned.reshape(pairs, slices, VOX)

    def second_order(q):
        start_ref[q, 0:slices, :] = slot_values(q)

    repeat(pairs, second_order, 8)

    ray = lax.broadcasted_iota(jnp.int32, (ROWS, VOX), 0).astype(f32)

    def make_weights(q, c):
        held = q if cached else 0
        for two in range(chunk // 2):
            pieces = []
            for t in (2 * two, 2 * two + 1):
                angle = c * chunk + t
                base = ray - (along_ref[angle] + place_ref[q * angles + angle])
                for group in range(WIN // ROWS):
                    distance = base + float(group * ROWS)
                    pieces.append(jnp.maximum(0.0, 1.0 - jnp.abs(distance)))
            high, low = halves(jnp.concatenate(pieces, axis=0))
            weight_ref[held, 2 * two * WIN : (2 * two + 2) * WIN, 0:VOX] = high
            weight_ref[held, 2 * two * WIN : (2 * two + 2) * WIN, VOX : 2 * VOX] = low

    def forward(first):
        acc_ref[...] = jnp.zeros(acc_ref.shape, f32)

        def pair(q):
            values = start_ref[q]
            if not first:
                values = values + step_size * update_ref[q]
            high, low = halves(values)
            operand = jnp.concatenate(
                [
                    jnp.concatenate([high, high], axis=1),
                    jnp.concatenate([low, jnp.zeros_like(low)], axis=1),
                    jnp.ones((both, 2 * VOX), bf16),
                    jnp.zeros((LANES - 3 * both, 2 * VOX), bf16),
                ],
                axis=0,
            )
            for c in range(chunks):
                if first or not cached:
                    make_weights(q, c)
                held = q if cached else 0
                sums = lax.dot_general(
                    weight_ref[held],
                    operand,
                    (((1,), (1,)), ((), ())),
                    preferred_element_type=f32,
                )
                for begin in range(0, chunk, GROUP):
                    places = []
                    for t in range(begin, min(begin + GROUP, chunk)):
                        angle = c * chunk + t
                        rows = pl.ds(offset_ref[q * angles + angle], WIN)
                        values = acc_ref[angle, rows, :] + sums[t * WIN : (t + 1) * WIN, :]
                        places.append((angle, rows, values))
                    for angle, rows, values in places:
                        acc_ref[angle, rows, :] = values

        repeat(pairs, pair, PAIR_UNROLL)

        def spread(t):
            rows = jnp.transpose(acc_ref[t]) * (1.0 / ROI)
            diff_ref[t] = rows[0:slices] + rows[both : both + slices]
            res_ref[t] = rows[slices:both] + rows[both + slices : 2 * both]
            if first:
                gain_ref[t] = rows[2 * both : 2 * both + slices]

        repeat(angles, spread, 8)
        flat = (angles * slices, ACTIVE)
        full = (angles, slices, ACTIVE)
        mirrored = reversed_exact(res_ref[...].reshape(flat)).reshape(full)
        res_ref[...] = sino_ref[...] - diff_ref[0:angles] - mirrored
        if first:
            direct = gain_ref[...]
            total = direct + reversed_exact(direct.reshape(flat)).reshape(full)
            gain_ref[...] = 1.0 / jnp.maximum(total, row_floor)

    def backward(first):
        weighted = res_ref[...] * gain_ref[...] * (1.0 / ROI)
        flat = (angles * slices, ACTIVE)
        full = (angles, slices, ACTIVE)
        high, low = halves(weighted.reshape(flat))
        mirrored = (dot(high, flip) + dot(low, flip)).reshape(full)
        lane = lax.broadcasted_iota(jnp.int32, (angles, slices, LANES), 2)
        for part, source in enumerate((weighted, mirrored)):
            rows = slice(part * slices, (part + 1) * slices)
            left = source[:, :, 0:LANES]
            right = source[:, :, LANES : 2 * LANES]
            window_ref[:, 0, rows, :] = left
            window_ref[:, 2, rows, :] = right
            mixed = jnp.where(lane >= SPLIT, left, right)
            window_ref[:, 1, rows, :] = pltpu.roll(mixed, SPLIT, 2)

        def pair(q):
            total = None
            for c in range(chunks):
                if not cached:
                    make_weights(q, c)
                held = q if cached else 0
                tiles = [None] * (-(-width // LANES))
                for t in range(chunk):
                    index = q * angles + c * chunk + t
                    piece = pltpu.roll(
                        window_ref[c * chunk + t, tile_ref[index]], turn_ref[index], 1
                    )
                    begin = t * WIN
                    for place in range(begin // LANES, (begin + WIN - 1) // LANES + 1):
                        if tiles[place] is None:
                            tiles[place] = piece
                        else:
                            tiles[place] = jnp.where(
                                lane_rows >= begin - place * LANES, piece, tiles[place]
                            )
                high, low = halves(jnp.concatenate(tiles, axis=1))
                operand = jnp.concatenate([high, low], axis=0)
                sums = dot(operand, weight_ref[held])
                piece = sums[0:both, 0:VOX] + sums[both:, 0:VOX] + sums[0:both, VOX:]
                total = piece if total is None else total + piece
            update_ref[q] = total if first else update_ref[q] + total

        repeat(pairs, pair, PAIR_UNROLL)

    forward(True)
    backward(True)
    forward(False)
    backward(False)
    turned = reversed_exact(update_ref[:, slices:both, :].reshape(pairs * slices, VOX))
    diff_ref[0:pairs] = turned.reshape(pairs, slices, VOX)

    def finish(q):
        for patch, update in (
            (q, update_ref[q, 0:slices, :]),
            (patches - 1 - q, diff_ref[q]),
        ):
            ray, rows = slot_rows(patch)
            values = slot_values(patch) + step_size * update
            half_ref[0, ray, rows, :] = values[:, 0:LANES]
            half_ref[1, ray, rows, :] = values[:, LANES : 2 * LANES]

    repeat(pairs, finish, 8)
    for part in range(2):
        out_ref[:, 0:held_rows, part * LANES : (part + 1) * LANES] = half_ref[part]
    for t in range(angles):
        begin = held_rows + t // rays * slices
        out_ref[t % rays, begin : begin + slices, :] = res_ref[t]


def sirt(volume, sino, theta, vol_list, step_size):
    rays, held_rows, _ = volume.shape
    patches = vol_list.shape[0]
    angles, slices, _ = sino.shape
    pairs = patches // 2
    sent_rows = held_rows + angles // rays * slices
    chunk = math.gcd(angles, 32)
    held = pairs if angles == chunk else 1
    centre = (ROI - 1) / 2.0
    ids = np.arange(pairs)
    centre_x = (ids // PGRID * float(SIDE) + (SIDE - 1) / 2.0 - centre).astype(np.float32)
    centre_y = (ids % PGRID * float(SIDE) + (SIDE - 1) / 2.0 - centre).astype(np.float32)
    cosine = jnp.cos(theta)
    sine = jnp.sin(theta)
    along = centre_x[:, None] * cosine[None, :] + centre_y[:, None] * sine[None, :] + 0.5
    whole = jnp.floor(along)
    lead = WIN // 2 - 1
    place = along - whole + float(lead)
    offset = whole.astype(jnp.int32) + (ACTIVE // 2 - 1 - lead)
    tile = jnp.minimum(offset // SPLIT, 2)
    local = jnp.arange(angles, dtype=jnp.int32) % chunk * WIN
    turn = (local[None, :] - offset + tile * SPLIT) % LANES
    slot = jnp.sum(
        jnp.where(
            vol_list[None, :] == jnp.arange(patches, dtype=jnp.int32)[:, None],
            jnp.arange(patches, dtype=jnp.int32)[None, :],
            0,
        ),
        axis=1,
    )
    voxel = np.arange(VOX)
    shift_x = np.repeat((voxel // SIDE - (SIDE - 1) / 2.0)[None, :], ROWS, axis=0)
    shift_y = np.repeat((voxel % SIDE - (SIDE - 1) / 2.0)[None, :], ROWS, axis=0)
    flip = np.eye(ACTIVE)[::-1].astype(ml_dtypes.bfloat16)
    smem = pl.BlockSpec(memory_space=pltpu.SMEM)
    vmem = pl.BlockSpec(memory_space=pltpu.VMEM)
    both = 2 * slices
    macs = 3 * patches * VOX * angles * WIN * slices
    return pl.pallas_call(
        functools.partial(sirt_kernel, step_size, chunk),
        out_shape=jax.ShapeDtypeStruct((rays, sent_rows, VOX), f32),
        in_specs=[smem] * 7 + [vmem] * 5,
        out_specs=vmem,
        scratch_shapes=[
            pltpu.VMEM((held, chunk * WIN, 2 * VOX), bf16),
            pltpu.VMEM((angles, ACTIVE, LANES), f32),
            pltpu.VMEM((angles, ROWS, VOX), f32),
            pltpu.VMEM((pairs, both, VOX), f32),
            pltpu.VMEM((pairs, both, VOX), f32),
            pltpu.VMEM((max(pairs, angles), slices, ACTIVE), f32),
            pltpu.VMEM((angles, slices, ACTIVE), f32),
            pltpu.VMEM((angles, slices, ACTIVE), f32),
            pltpu.VMEM((angles, 3, both, LANES), f32),
            pltpu.VMEM((2, rays, held_rows, LANES), f32),
        ],
        compiler_params=pltpu.CompilerParams(vmem_limit_bytes=56 * 2**20),
        cost_estimate=pl.CostEstimate(
            flops=128 * macs, bytes_accessed=4 * volume.size * 4, transcendentals=0
        ),
        name="sirt",
    )(
        offset.reshape(-1),
        tile.reshape(-1),
        turn.reshape(-1),
        place.reshape(-1),
        slot,
        cosine,
        sine,
        volume,
        sino,
        jnp.asarray(flip),
        jnp.asarray(shift_x, f32),
        jnp.asarray(shift_y, f32),
    )


def gather_kernel(rank_ref, *refs):
    *part_refs, out_ref, sems = refs
    rank = rank_ref[0]
    copies = [
        pltpu.make_async_copy(part_ref, out_ref.at[rank ^ d], sems.at[d])
        for d, part_ref in enumerate(part_refs)
    ]
    for copy in copies:
        copy.start()
    for copy in copies:
        copy.wait()


def gather_parts(parts, rank):
    count = len(parts)
    return pl.pallas_call(
        gather_kernel,
        out_shape=jax.ShapeDtypeStruct((count,) + parts[0].shape, f32),
        in_specs=[pl.BlockSpec(memory_space=pltpu.SMEM)]
        + [pl.BlockSpec(memory_space=pltpu.VMEM)] * count,
        out_specs=pl.BlockSpec(memory_space=pl.ANY),
        scratch_shapes=[pltpu.SemaphoreType.DMA((count,))],
        cost_estimate=pl.CostEstimate(
            flops=0, bytes_accessed=8 * count * parts[0].size, transcendentals=0
        ),
        name="gather_parts",
    )(rank.reshape(1), *parts)


def finish_kernel(slots, got_ref, sino_ref, rec_ref, out_ref, values_ref, active_ref, sems):
    rays, rows, _ = got_ref.shape
    slabs = active_ref.shape[0]
    held = rows * slots // (slots + slabs)
    slices = held // slots
    for ray in range(rays):
        values_ref[ray * slices : (ray + 1) * slices] = got_ref[ray, 0:held, :].reshape(
            slices, slots, VOX
        )
        for k in range(slabs):
            begin = held + k * slices
            active_ref[k, ray * slices : (ray + 1) * slices, :] = got_ref[
                ray, begin : begin + slices, :
            ]
    offset = (out_ref.shape[2] - ACTIVE) // 2
    copies = [
        pltpu.make_async_copy(values_ref, rec_ref, sems.at[0]),
        pltpu.make_async_copy(
            active_ref, out_ref.at[:, :, offset : offset + ACTIVE], sems.at[1]
        ),
    ]
    for copy in copies:
        copy.start()
    for copy in copies:
        copy.wait()


def finish(got, sinogram, shape):
    slabs, slab_rows, _ = sinogram.shape
    any_space = pl.BlockSpec(memory_space=pl.ANY)
    return pl.pallas_call(
        functools.partial(finish_kernel, shape[1]),
        out_shape=(
            jax.ShapeDtypeStruct(shape, f32),
            jax.ShapeDtypeStruct(sinogram.shape, f32),
        ),
        in_specs=[pl.BlockSpec(memory_space=pltpu.VMEM), any_space],
        out_specs=[any_space, any_space],
        scratch_shapes=[
            pltpu.VMEM(shape, f32),
            pltpu.VMEM((slabs, slab_rows, ACTIVE), f32),
            pltpu.SemaphoreType.DMA((2,)),
        ],
        input_output_aliases={1: 1},
        compiler_params=pltpu.CompilerParams(vmem_limit_bytes=32 * 2**20),
        cost_estimate=pl.CostEstimate(
            flops=0, bytes_accessed=8 * got.size, transcendentals=0
        ),
        name="finish",
    )(got, sinogram)


def local(intensity, angles, volume, vol_list):
    n_slab = lax.axis_size("slab")
    n_ray = lax.axis_size("ray")
    devices = n_slab * n_ray
    height, band = intensity.shape[2:]
    slab_rows = height // n_slab
    slices = height // devices
    slots = volume.shape[1]
    count = angles.shape[0] * angles.shape[1]
    step_size = relax * ROI / count
    theta = angles.reshape(-1)
    rank = lax.axis_index("slab")

    spread = volume.reshape(n_ray, slices * slots, VOX)
    own_volume = lax.all_to_all(spread, "ray", split_axis=0, concat_axis=0, tiled=True)

    *parts, active = paganin(intensity.reshape(height, band), rank, n_slab)
    active, own_volume = lax.optimization_barrier((active, own_volume))
    own_rays = lax.all_to_all(
        active.reshape(devices, slices, ACTIVE),
        ("slab", "ray"),
        split_axis=0,
        concat_axis=0,
        tiled=True,
    )
    parts = [
        lax.ppermute(part, "slab", [(i, i ^ d) for i in range(n_slab)]) if d else part
        for d, part in enumerate(parts)
    ]

    padded = -(-slices // ROWS) * ROWS
    if padded != slices:
        widen = ((0, 0), (0, padded - slices), (0, 0))
        own_volume = jnp.pad(own_volume, ((0, 0), (0, (padded - slices) * slots), (0, 0)))
        own_rays = jnp.pad(own_rays, widen)
    result = sirt(own_volume, own_rays, theta, vol_list, step_size)
    if padded != slices:
        lower = result[:, padded * slots :].reshape(n_ray, n_slab, padded, ACTIVE)
        lower = lower[:, :, :slices].reshape(n_ray, n_slab * slices, ACTIVE)
        result = jnp.concatenate([result[:, : slices * slots], lower], axis=1)
    result, parts = lax.optimization_barrier((result, parts))
    result = lax.all_to_all(result, "ray", split_axis=0, concat_axis=0, tiled=True)
    sinogram = gather_parts(parts, rank)
    reconstruction, residual = finish(result, sinogram, volume.shape)
    return (reconstruction, residual[:, None])


def solution(mesh):
    placed = (P("slab", "ray", None, None), P(), P("slab", "ray", None), P())
    return jax.shard_map(
        local,
        mesh=mesh,
        in_specs=placed,
        out_specs=(P("slab", "ray", None), P(None, "ray", "slab", None)),
        check_vma=False,
    )
```

```python
import functools
import math

import jax
import jax.numpy as jnp
import ml_dtypes
import numpy as np
from jax import lax
from jax.experimental import pallas as pl
from jax.experimental.pallas import tpu as pltpu
from jax.sharding import PartitionSpec as P

BAND = 2048
PGRID = 8
ROI = 128
SIDE = 16
VOX = SIDE * SIDE
WIN = 24
ACTIVE = 256
LANES = 128
ROWS = 8
SPLIT = 64
GROUP = 8
PAIR_UNROLL = 2

paganin_strength = 10.0
relax = 1.8
row_floor = 0.25

bf16 = jnp.bfloat16
f32 = jnp.float32


def halves(values):
    high = values.astype(bf16)
    low = (values - high.astype(f32)).astype(bf16)
    return high, low


def thirds(values):
    high = values.astype(bf16)
    rest = values - high.astype(f32)
    middle = rest.astype(bf16)
    low = (rest - middle.astype(f32)).astype(bf16)
    return high, middle, low


def dot(left, right):
    return jnp.dot(left, right, preferred_element_type=f32)


def repeat(count, body, unroll):
    unroll = math.gcd(count, unroll)

    def several(index, carry):
        for step in range(unroll):
            body(index * unroll + step)
        return carry

    lax.fori_loop(0, count // unroll, several, 0)


def filter_tables(height):
    index = np.arange(height)
    phase = 2.0 * np.pi * (np.outer(index, index) % height) / height
    cas = (np.cos(phase) + np.sin(phase)) / math.sqrt(height)
    row_freq = 2.0 - 2.0 * np.cos(2.0 * np.pi * index / height)
    middle = (1.0 + paganin_strength * row_freq) / paganin_strength + 2.0
    rho = (middle - np.sqrt(middle * middle - 4.0)) / 2.0
    return np.concatenate([cas, np.repeat(rho[None, :], ROWS, axis=0)], axis=0).astype(np.float32)


def chunk_carry(ends, power, forward):
    shift = 1
    for _ in range(3):
        ends = ends + power * pltpu.roll(ends, shift if forward else ROWS - shift, 0)
        power = power * power
        shift *= 2
    return pltpu.roll(ends, 1 if forward else ROWS - 1, 0) / (1.0 - power)


def filter_kernel(rank_ref, image_ref, table_ref, *refs):
    *part_refs, active_ref, out_ref, spec_ref, up_ref, down_ref = refs
    height, width = image_ref.shape
    rank = rank_ref[0]
    share = height // len(part_refs)
    length = width // ROWS
    blocks = height // LANES
    unroll = 8
    cas_high, cas_low = halves(table_ref[0:height, :])
    rho_all = table_ref[height : height + ROWS, :]
    rhos = [rho_all[:, b * LANES : (b + 1) * LANES] for b in range(blocks)]
    zeros = [jnp.zeros((ROWS, LANES), f32)] * blocks

    def transform(values):
        high, low = halves(values)
        return dot(high, cas_high) + dot(low, cas_high) + dot(high, cas_low)

    for c in range(ROWS):
        image = 1.0 - image_ref[:, c * length : (c + 1) * length]
        spectrum = transform(jnp.transpose(image))
        for b in range(blocks):
            spec_ref[b, pl.ds(c, length, stride=ROWS), :] = spectrum[
                :, b * LANES : (b + 1) * LANES
            ]

    def rows(position):
        return pl.ds(pl.multiple_of(position * ROWS, ROWS), ROWS)

    def advance(position, ups, downs):
        ups = [spec_ref[b, rows(position), :] + rhos[b] * ups[b] for b in range(blocks)]
        back = length - 1 - position
        downs = [spec_ref[b, rows(back), :] + rhos[b] * downs[b] for b in range(blocks)]
        return ups, downs

    def sweep(index, carry):
        ups, downs = carry
        for step in range(unroll):
            ups, downs = advance(index * unroll + step, ups, downs)
        return ups, downs

    ups, downs = lax.fori_loop(0, length // unroll, sweep, (zeros, zeros))
    powers = list(rhos)
    for _ in range(int(math.log2(length))):
        powers = [power * power for power in powers]
    ups = [chunk_carry(ups[b], powers[b], True) for b in range(blocks)]
    downs = [chunk_carry(downs[b], powers[b], False) for b in range(blocks)]
    scales = [rho / (paganin_strength * (1.0 - rho * rho)) for rho in rhos]

    def outer(index, carry):
        ups, downs = carry
        for step in range(unroll):
            position = index * unroll + step
            ups, downs = advance(position, ups, downs)
            for b in range(blocks):
                up_ref[b, rows(position), :] = ups[b]
                down_ref[b, rows(position), :] = downs[b]
        return ups, downs

    def inner(index, carry):
        ups, downs = carry
        for step in range(unroll):
            position = index * unroll + step
            back = length - 1 - position
            ups, downs = advance(position, ups, downs)
            for b in range(blocks):
                here = ups[b] + down_ref[b, rows(back), :] - spec_ref[b, rows(position), :]
                there = downs[b] + up_ref[b, rows(back), :] - spec_ref[b, rows(back), :]
                up_ref[b, rows(position), :] = here * scales[b]
                up_ref[b, rows(back), :] = there * scales[b]
        return ups, downs

    half = length // 2 // unroll
    carry = lax.fori_loop(0, half, outer, (ups, downs))
    lax.fori_loop(half, 2 * half, inner, carry)

    offset = (width - ACTIVE) // 2
    for c in range(ROWS):
        spectrum = jnp.concatenate(
            [up_ref[b, pl.ds(c, length, stride=ROWS), :] for b in range(blocks)], axis=1
        )
        filtered = 1.0 - jnp.transpose(transform(spectrum))
        out_ref[:, c * length : (c + 1) * length] = -jnp.log(filtered)
    active_ref[...] = out_ref[:, offset : offset + ACTIVE]
    for d, part_ref in enumerate(part_refs):
        part_ref[...] = out_ref[pl.ds(pl.multiple_of((rank ^ d) * share, share), share), :]


def paganin(image, rank, parts):
    height, width = image.shape
    blocks = height // LANES
    return pl.pallas_call(
        filter_kernel,
        out_shape=[jax.ShapeDtypeStruct((height // parts, width), f32)] * parts
        + [jax.ShapeDtypeStruct((height, ACTIVE), f32)],
        in_specs=[pl.BlockSpec(memory_space=pltpu.SMEM)]
        + [pl.BlockSpec(memory_space=pltpu.VMEM)] * 2,
        out_specs=[pl.BlockSpec(memory_space=pltpu.VMEM)] * (parts + 1),
        scratch_shapes=[
            pltpu.VMEM((height, width), f32),
            pltpu.VMEM((blocks, width, LANES), f32),
            pltpu.VMEM((blocks, width, LANES), f32),
            pltpu.VMEM((blocks, width // 2, LANES), f32),
        ],
        compiler_params=pltpu.CompilerParams(vmem_limit_bytes=32 * 2**20),
        cost_estimate=pl.CostEstimate(
            flops=64 * height * height * width,
            bytes_accessed=8 * height * width,
            transcendentals=height * width,
        ),
        name="paganin",
    )(rank.reshape(1), image, jnp.asarray(filter_tables(height)))


def reversed_exact(values, flip):
    return sum(dot(part, flip) for part in thirds(values))


class Weights:
    def __init__(self, ref, along_ref, place_ref, angles, chunk, held):
        self.ref = ref
        self.along_ref = along_ref
        self.place_ref = place_ref
        self.angles = angles
        self.chunk = chunk
        self.held = held
        self.ray = lax.broadcasted_iota(jnp.int32, (ROWS, VOX), 0).astype(f32)

    def prepare(self, shift_x_ref, shift_y_ref, cos_ref, sin_ref):
        def along_angle(t):
            self.along_ref[t] = shift_x_ref[...] * cos_ref[t] + shift_y_ref[...] * sin_ref[t]

        repeat(self.angles, along_angle, 8)

    def make(self, q, c):
        place = q if self.held else 0
        for two in range(self.chunk // 2):
            pieces = []
            for t in (2 * two, 2 * two + 1):
                angle = c * self.chunk + t
                along = self.along_ref[angle] + self.place_ref[q * self.angles + angle]
                base = self.ray - along
                for group in range(WIN // ROWS):
                    distance = base + float(group * ROWS)
                    pieces.append(jnp.maximum(0.0, 1.0 - jnp.abs(distance)))
            high, low = halves(jnp.concatenate(pieces, axis=0))
            self.ref[place, 2 * two * WIN : (2 * two + 2) * WIN, 0:VOX] = high
            self.ref[place, 2 * two * WIN : (2 * two + 2) * WIN, VOX : 2 * VOX] = low

    def get(self, q):
        return self.ref[q if self.held else 0]


def project(weights, make, values_of, offset_ref, acc_ref, pairs, both):
    angles, chunk = weights.angles, weights.chunk
    acc_ref[...] = jnp.zeros(acc_ref.shape, f32)

    def pair(q):
        high, low = halves(values_of(q))
        operand = jnp.concatenate(
            [
                jnp.concatenate([high, high], axis=1),
                jnp.concatenate([low, jnp.zeros_like(low)], axis=1),
                jnp.ones((both, 2 * VOX), bf16),
                jnp.zeros((LANES - 3 * both, 2 * VOX), bf16),
            ],
            axis=0,
        )
        for c in range(angles // chunk):
            if make:
                weights.make(q, c)
            sums = lax.dot_general(
                weights.get(q),
                operand,
                (((1,), (1,)), ((), ())),
                preferred_element_type=f32,
            )
            for begin in range(0, chunk, GROUP):
                places = []
                for t in range(begin, min(begin + GROUP, chunk)):
                    angle = c * chunk + t
                    rows = pl.ds(offset_ref[q * angles + angle], WIN)
                    values = acc_ref[angle, rows, :] + sums[t * WIN : (t + 1) * WIN, :]
                    places.append((angle, rows, values))
                for angle, rows, values in places:
                    acc_ref[angle, rows, :] = values

    repeat(pairs, pair, PAIR_UNROLL)


def spread_rays(acc_ref, direct_ref, mirror_ref, total_ref, slices):
    both = 2 * slices

    def spread(t):
        rows = jnp.transpose(acc_ref[t]) * (1.0 / ROI)
        direct_ref[t] = rows[0:slices] + rows[both : both + slices]
        mirror_ref[t] = rows[slices:both] + rows[both + slices : 2 * both]
        if total_ref is not None:
            total_ref[t] = rows[2 * both : 2 * both + slices]

    repeat(acc_ref.shape[0], spread, 8)


def turn_rays(values, flip):
    shape = values.shape
    return reversed_exact(values.reshape(-1, shape[-1]), flip).reshape(shape)


def back_project(weights, weighted, flip, window_ref, tile_ref, turn_ref, store, pairs):
    angles, slices, _ = weighted.shape
    chunk = weights.chunk
    both = 2 * slices
    width = chunk * WIN
    high, low = halves(weighted.reshape(angles * slices, ACTIVE))
    mirrored = (dot(high, flip) + dot(low, flip)).reshape(weighted.shape)
    lane = lax.broadcasted_iota(jnp.int32, (angles, slices, LANES), 2)
    lane_rows = lax.broadcasted_iota(jnp.int32, (both, LANES), 1)
    for part, source in enumerate((weighted, mirrored)):
        rows = slice(part * slices, (part + 1) * slices)
        left = source[:, :, 0:LANES]
        right = source[:, :, LANES : 2 * LANES]
        window_ref[:, 0, rows, :] = left
        window_ref[:, 2, rows, :] = right
        mixed = jnp.where(lane >= SPLIT, left, right)
        window_ref[:, 1, rows, :] = pltpu.roll(mixed, SPLIT, 2)

    def pair(q):
        total = None
        for c in range(angles // chunk):
            if not weights.held:
                weights.make(q, c)
            tiles = [None] * (-(-width // LANES))
            for t in range(chunk):
                index = q * angles + c * chunk + t
                piece = pltpu.roll(
                    window_ref[c * chunk + t, tile_ref[index]], turn_ref[index], 1
                )
                begin = t * WIN
                for place in range(begin // LANES, (begin + WIN - 1) // LANES + 1):
                    if tiles[place] is None:
                        tiles[place] = piece
                    else:
                        tiles[place] = jnp.where(
                            lane_rows >= begin - place * LANES, piece, tiles[place]
                        )
            high, low = halves(jnp.concatenate(tiles, axis=1))
            sums = dot(jnp.concatenate([high, low], axis=0), weights.get(q))
            piece = sums[0:both, 0:VOX] + sums[both:, 0:VOX] + sums[0:both, VOX:]
            total = piece if total is None else total + piece
        store(q, total)

    repeat(pairs, pair, PAIR_UNROLL)


def first_kernel(
    sizes,
    offset_ref,
    place_ref,
    slot_ref,
    cos_ref,
    sin_ref,
    vol_ref,
    flip_ref,
    shift_x_ref,
    shift_y_ref,
    weight_ref,
    start_ref,
    predicted_ref,
    gain_ref,
    acc_ref,
    along_ref,
    half_ref,
    mirror_ref,
):
    angles, chunk, held, slots = sizes
    patches = slot_ref.shape[0]
    pairs, both, _ = start_ref.shape
    slices = both // 2
    flip = flip_ref[...]

    def slot_values(patch):
        slot = slot_ref[patch]
        rows = pl.ds(slot % slots, slices, stride=slots)
        return jnp.concatenate(
            [half_ref[part, slot // slots, rows, :] for part in range(2)], axis=1
        )

    weights = Weights(weight_ref, along_ref, place_ref, angles, chunk, held)
    weights.prepare(shift_x_ref, shift_y_ref, cos_ref, sin_ref)
    for part in range(2):
        half_ref[part] = vol_ref[:, :, part * LANES : (part + 1) * LANES]

    def order(q):
        start_ref[q, 0:slices, :] = slot_values(q)
        mirror_ref[q] = slot_values(patches - 1 - q)

    repeat(pairs, order, 8)
    start_ref[:, slices:both, :] = turn_rays(mirror_ref[0:pairs], flip)
    project(weights, True, lambda q: start_ref[q], offset_ref, acc_ref, pairs, both)
    spread_rays(acc_ref, predicted_ref, mirror_ref, gain_ref, slices)
    predicted_ref[...] = predicted_ref[...] + turn_rays(mirror_ref[0:angles], flip)
    direct = gain_ref[...]
    gain_ref[...] = 1.0 / jnp.maximum(direct + turn_rays(direct, flip), row_floor)


def second_kernel(
    sizes,
    step_size,
    offset_ref,
    place_ref,
    tile_ref,
    turn_ref,
    cos_ref,
    sin_ref,
    start_ref,
    predicted_ref,
    gain_ref,
    sino_ref,
    flip_ref,
    shift_x_ref,
    shift_y_ref,
    weight_ref,
    update_ref,
    res_ref,
    acc_ref,
    along_ref,
    direct_ref,
    mirror_ref,
    window_ref,
):
    angles, chunk, held, _ = sizes
    pairs, both, _ = start_ref.shape
    slices = both // 2
    rays = res_ref.shape[0]
    flip = flip_ref[...]
    weights = Weights(weight_ref, along_ref, place_ref, angles, chunk, held)
    if not held:
        weights.prepare(shift_x_ref, shift_y_ref, cos_ref, sin_ref)
    weighted = (sino_ref[...] - predicted_ref[...]) * gain_ref[...] * (1.0 / ROI)

    def store(q, total):
        update_ref[q] = total

    back_project(weights, weighted, flip, window_ref, tile_ref, turn_ref, store, pairs)

    def values_of(q):
        return start_ref[q] + step_size * update_ref[q]

    project(weights, not held, values_of, offset_ref, acc_ref, pairs, both)
    spread_rays(acc_ref, direct_ref, mirror_ref, None, slices)
    residual = sino_ref[...] - direct_ref[...] - turn_rays(mirror_ref[...], flip)
    for t in range(angles):
        begin = t // rays * slices
        res_ref[t % rays, begin : begin + slices, :] = residual[t]


def third_kernel(
    sizes,
    step_size,
    place_ref,
    tile_ref,
    turn_ref,
    slot_ref,
    cos_ref,
    sin_ref,
    update_ref,
    res_ref,
    gain_ref,
    vol_ref,
    flip_ref,
    shift_x_ref,
    shift_y_ref,
    weight_ref,
    out_ref,
    along_ref,
    total_ref,
    mirror_ref,
    window_ref,
    half_ref,
):
    angles, chunk, held, slots = sizes
    patches = slot_ref.shape[0]
    pairs, both, _ = update_ref.shape
    slices = both // 2
    rays = res_ref.shape[0]
    flip = flip_ref[...]
    weights = Weights(weight_ref, along_ref, place_ref, angles, chunk, held)
    if not held:
        weights.prepare(shift_x_ref, shift_y_ref, cos_ref, sin_ref)
    residual = [
        res_ref[t % rays, t // rays * slices : (t // rays + 1) * slices, :][None]
        for t in range(angles)
    ]
    weighted = jnp.concatenate(residual, axis=0) * gain_ref[...] * (1.0 / ROI)

    def store(q, total):
        total_ref[q] = (update_ref[q] + total) * step_size

    back_project(weights, weighted, flip, window_ref, tile_ref, turn_ref, store, pairs)
    mirror_ref[...] = turn_rays(total_ref[:, slices:both, :], flip)
    for part in range(2):
        half_ref[part] = vol_ref[:, :, part * LANES : (part + 1) * LANES]

    def finish(q):
        for patch, update in (
            (q, total_ref[q, 0:slices, :]),
            (patches - 1 - q, mirror_ref[q]),
        ):
            slot = slot_ref[patch]
            rows = pl.ds(slot % slots, slices, stride=slots)
            for part in range(2):
                half_ref[part, slot // slots, rows, :] = (
                    half_ref[part, slot // slots, rows, :]
                    + update[:, part * LANES : (part + 1) * LANES]
                )

    repeat(pairs, finish, 8)
    for part in range(2):
        out_ref[:, :, part * LANES : (part + 1) * LANES] = half_ref[part]


def call(kernel, name, inputs, outputs, scratch, micros, room):
    smem = pl.BlockSpec(memory_space=pltpu.SMEM)
    vmem = pl.BlockSpec(memory_space=pltpu.VMEM)
    return pl.pallas_call(
        kernel,
        out_shape=[jax.ShapeDtypeStruct(shape, dtype) for shape, dtype in outputs],
        in_specs=[smem if value.ndim == 1 else vmem for value in inputs],
        out_specs=[vmem] * len(outputs),
        scratch_shapes=[pltpu.VMEM(shape, dtype) for shape, dtype in scratch],
        compiler_params=pltpu.CompilerParams(vmem_limit_bytes=room * 2**20),
        cost_estimate=pl.CostEstimate(
            flops=int(micros * 1e9), bytes_accessed=4 * 2**20, transcendentals=0
        ),
        name=name,
    )(*inputs)


class Sirt:
    def __init__(self, theta, vol_list, slices, slots, rays, step_size):
        angles = theta.shape[0]
        patches = vol_list.shape[0]
        pairs = patches // 2
        both = 2 * slices
        chunk = math.gcd(angles, 32)
        self.held = angles == chunk
        self.room = 24 if self.held else 48
        self.sizes = (angles, chunk, self.held, slots)
        self.step_size = step_size
        self.rays = rays
        self.patches = patches
        centre = (ROI - 1) / 2.0
        ids = np.arange(pairs)
        centre_x = (ids // PGRID * float(SIDE) + (SIDE - 1) / 2.0 - centre).astype(np.float32)
        centre_y = (ids % PGRID * float(SIDE) + (SIDE - 1) / 2.0 - centre).astype(np.float32)
        self.cosine = jnp.cos(theta)
        self.sine = jnp.sin(theta)
        along = (
            centre_x[:, None] * self.cosine[None, :]
            + centre_y[:, None] * self.sine[None, :]
            + 0.5
        )
        whole = jnp.floor(along)
        lead = WIN // 2 - 1
        place = along - whole + float(lead)
        offset = whole.astype(jnp.int32) + (ACTIVE // 2 - 1 - lead)
        tile = jnp.minimum(offset // SPLIT, 2)
        local = jnp.arange(angles, dtype=jnp.int32) % chunk * WIN
        turn = (local[None, :] - offset + tile * SPLIT) % LANES
        self.offset = offset.reshape(-1)
        self.place = place.reshape(-1)
        self.tile = tile.reshape(-1)
        self.turn = turn.reshape(-1)
        ids = jnp.arange(patches, dtype=jnp.int32)
        self.slot = jnp.sum(
            jnp.where(vol_list[None, :] == ids[:, None], ids[None, :], 0), axis=1
        )
        voxel = np.arange(VOX)
        shift_x = np.repeat((voxel // SIDE - (SIDE - 1) / 2.0)[None, :], ROWS, axis=0)
        shift_y = np.repeat((voxel % SIDE - (SIDE - 1) / 2.0)[None, :], ROWS, axis=0)
        flip = np.eye(ACTIVE)[::-1].astype(ml_dtypes.bfloat16)
        self.fixed = [jnp.asarray(flip), jnp.asarray(shift_x, f32), jnp.asarray(shift_y, f32)]
        self.weight = ((pairs if self.held else 1, chunk * WIN, 2 * VOX), bf16)
        self.acc = ((angles, ACTIVE, LANES), f32)
        self.along = ((angles, ROWS, VOX), f32)
        self.by_ray = ((angles, slices, ACTIVE), f32)
        self.by_pair = ((pairs, both, VOX), f32)
        self.window = ((angles, 3, both, LANES), f32)
        self.half = ((2, rays, slices * slots, LANES), f32)
        self.mirror = ((max(pairs, angles), slices, ACTIVE), f32)
        self.sent = ((rays, angles // rays * slices, ACTIVE), f32)

    def first(self, volume):
        inputs = [self.offset, self.place, self.slot, self.cosine, self.sine, volume]
        outputs = [self.by_pair, self.by_ray, self.by_ray]
        scratch = [self.acc, self.along, self.half, self.mirror]
        held = [self.weight] if self.held else []
        spare = [] if self.held else [self.weight]

        def kernel(*refs):
            refs = list(refs)
            count = len(inputs) + len(self.fixed)
            if not self.held:
                refs.insert(count, refs.pop(count + len(outputs)))
            first_kernel(self.sizes, *refs)

        results = call(
            kernel, "first", inputs + self.fixed, held + outputs, spare + scratch, 16, self.room
        )
        return (results[:1], results[1:]) if self.held else ([], results)

    def second(self, weight, start, predicted, gain, sino):
        inputs = [self.offset, self.place, self.tile, self.turn, self.cosine, self.sine]
        inputs += [start, predicted, gain, sino] + self.fixed + list(weight)
        outputs = [self.by_pair, self.sent]
        scratch = [self.acc, self.along, self.by_ray, self.by_ray, self.window]
        spare = [] if self.held else [self.weight]

        def kernel(*refs):
            refs = list(refs)
            count = len(inputs)
            if not self.held:
                refs.insert(count, refs.pop(count + len(outputs)))
            second_kernel(self.sizes, self.step_size, *refs)

        return call(kernel, "second", inputs, outputs, spare + scratch, 20, self.room)

    def third(self, weight, update, residual, gain, volume):
        inputs = [self.place, self.tile, self.turn, self.slot, self.cosine, self.sine]
        inputs += [update, residual, gain, volume] + self.fixed + list(weight)
        outputs = [(volume.shape, f32)]
        pairs = self.patches // 2
        mirror = ((pairs,) + self.by_ray[0][1:], f32)
        scratch = [self.along, self.by_pair, mirror, self.window, self.half]
        spare = [] if self.held else [self.weight]

        def kernel(*refs):
            refs = list(refs)
            count = len(inputs)
            if not self.held:
                refs.insert(count, refs.pop(count + len(outputs)))
            third_kernel(self.sizes, self.step_size, *refs)

        return call(kernel, "third", inputs, outputs, spare + scratch, 10, self.room)[0]


def gather_kernel(rank_ref, *refs):
    *part_refs, out_ref, sems = refs
    rank = rank_ref[0]
    copies = [
        pltpu.make_async_copy(part_ref, out_ref.at[rank ^ d], sems.at[d])
        for d, part_ref in enumerate(part_refs)
    ]
    for copy in copies:
        copy.start()
    for copy in copies:
        copy.wait()


def gather_parts(parts, rank):
    count = len(parts)
    return pl.pallas_call(
        gather_kernel,
        out_shape=jax.ShapeDtypeStruct((count,) + parts[0].shape, f32),
        in_specs=[pl.BlockSpec(memory_space=pltpu.SMEM)]
        + [pl.BlockSpec(memory_space=pltpu.VMEM)] * count,
        out_specs=pl.BlockSpec(memory_space=pl.ANY),
        scratch_shapes=[pltpu.SemaphoreType.DMA((count,))],
        cost_estimate=pl.CostEstimate(
            flops=0, bytes_accessed=8 * count * parts[0].size, transcendentals=0
        ),
        name="gather_parts",
    )(rank.reshape(1), *parts)


def finish_kernel(got_ref, sino_ref, out_ref, active_ref, sem):
    rays, rows, _ = got_ref.shape
    slabs = active_ref.shape[0]
    slices = rows // slabs
    for ray in range(rays):
        for k in range(slabs):
            active_ref[k, ray * slices : (ray + 1) * slices, :] = got_ref[
                ray, k * slices : (k + 1) * slices, :
            ]
    offset = (out_ref.shape[2] - ACTIVE) // 2
    copy = pltpu.make_async_copy(
        active_ref, out_ref.at[:, :, offset : offset + ACTIVE], sem
    )
    copy.start()
    copy.wait()


def finish(got, sinogram):
    slabs, slab_rows, _ = sinogram.shape
    any_space = pl.BlockSpec(memory_space=pl.ANY)
    return pl.pallas_call(
        finish_kernel,
        out_shape=jax.ShapeDtypeStruct(sinogram.shape, f32),
        in_specs=[pl.BlockSpec(memory_space=pltpu.VMEM), any_space],
        out_specs=any_space,
        scratch_shapes=[
            pltpu.VMEM((slabs, slab_rows, ACTIVE), f32),
            pltpu.SemaphoreType.DMA,
        ],
        input_output_aliases={1: 0},
        cost_estimate=pl.CostEstimate(
            flops=0, bytes_accessed=8 * got.size, transcendentals=0
        ),
        name="finish",
    )(got, sinogram)


def local(intensity, angles, volume, vol_list):
    n_slab = lax.axis_size("slab")
    n_ray = lax.axis_size("ray")
    devices = n_slab * n_ray
    height, band = intensity.shape[2:]
    slices = height // devices
    slots = volume.shape[1]
    count = angles.shape[0] * angles.shape[1]
    step_size = relax * ROI / count
    rank = lax.axis_index("slab")
    padded = -(-slices // ROWS) * ROWS

    def to_all(values, axes):
        return lax.all_to_all(values, axes, split_axis=0, concat_axis=0, tiled=True)

    own_volume = to_all(volume.reshape(n_ray, slices * slots, VOX), "ray")
    *parts, active = paganin(intensity.reshape(height, band), rank, n_slab)
    active, own_volume = lax.optimization_barrier((active, own_volume))
    own_rays = to_all(active.reshape(devices, slices, ACTIVE), ("slab", "ray"))
    if padded != slices:
        widen = ((0, 0), (0, padded - slices), (0, 0))
        own_volume = jnp.pad(own_volume, ((0, 0), (0, (padded - slices) * slots), (0, 0)))
        own_rays = jnp.pad(own_rays, widen)

    sirt = Sirt(angles.reshape(-1), vol_list, padded, slots, n_ray, step_size)
    weight, (start, predicted, gain) = sirt.first(own_volume)
    own_rays, parts, start = lax.optimization_barrier((own_rays, parts, start))
    parts = [
        lax.ppermute(part, "slab", [(i, i ^ d) for i in range(n_slab)]) if d else part
        for d, part in enumerate(parts)
    ]
    update, residual = sirt.second(weight, start, predicted, gain, own_rays)
    sent = residual
    if padded != slices:
        sent = sent.reshape(n_ray, n_slab, padded, ACTIVE)[:, :, :slices]
        sent = sent.reshape(n_ray, n_slab * slices, ACTIVE)
    got = to_all(sent, "ray")
    result = sirt.third(weight, update, residual, gain, own_volume)
    result = result[:, : slices * slots]
    result, got, parts = lax.optimization_barrier((result, got, parts))
    reconstruction = to_all(result, "ray").reshape(volume.shape)
    sinogram = gather_parts(parts, rank)
    residual = finish(got, sinogram)
    return (reconstruction, residual[:, None])


def solution(mesh):
    placed = (P("slab", "ray", None, None), P(), P("slab", "ray", None), P())
    return jax.shard_map(
        local,
        mesh=mesh,
        in_specs=placed,
        out_specs=(P("slab", "ray", None), P(None, "ray", "slab", None)),
        check_vma=False,
    )
```

```python
import functools
import math

import jax
import jax.numpy as jnp
import ml_dtypes
import numpy as np
from jax import lax
from jax.experimental import pallas as pl
from jax.experimental.pallas import tpu as pltpu
from jax.sharding import PartitionSpec as P

BAND = 2048
PGRID = 8
ROI = 128
SIDE = 16
VOX = SIDE * SIDE
WIN = 24
ACTIVE = 256
LANES = 128
ROWS = 8
SPLIT = 64
GROUP = 8

paganin_strength = 10.0
relax = 1.8
row_floor = 0.25

bf16 = jnp.bfloat16
f32 = jnp.float32


def halves(values):
    high = values.astype(bf16)
    low = (values - high.astype(f32)).astype(bf16)
    return high, low


def thirds(values):
    high = values.astype(bf16)
    rest = values - high.astype(f32)
    middle = rest.astype(bf16)
    low = (rest - middle.astype(f32)).astype(bf16)
    return high, middle, low


def dot(left, right):
    return jnp.dot(left, right, preferred_element_type=f32)


def repeat(count, body, unroll):
    unroll = math.gcd(count, unroll)

    def several(index, carry):
        for step in range(unroll):
            body(index * unroll + step)
        return carry

    lax.fori_loop(0, count // unroll, several, 0)


def filter_tables(height):
    index = np.arange(height)
    phase = 2.0 * np.pi * (np.outer(index, index) % height) / height
    cas = (np.cos(phase) + np.sin(phase)) / math.sqrt(height)
    row_freq = 2.0 - 2.0 * np.cos(2.0 * np.pi * index / height)
    middle = (1.0 + paganin_strength * row_freq) / paganin_strength + 2.0
    rho = (middle - np.sqrt(middle * middle - 4.0)) / 2.0
    return np.concatenate([cas, np.repeat(rho[None, :], ROWS, axis=0)], axis=0).astype(np.float32)


def chunk_carry(ends, power, forward):
    shift = 1
    for _ in range(3):
        ends = ends + power * pltpu.roll(ends, shift if forward else ROWS - shift, 0)
        power = power * power
        shift *= 2
    return pltpu.roll(ends, 1 if forward else ROWS - 1, 0) / (1.0 - power)


def filter_kernel(rank_ref, source_ref, given_ref, *refs):
    *part_refs, active_ref, image_ref, table_ref, out_ref, spec_ref, up_ref, down_ref, sems = refs
    height, width = image_ref.shape
    rank = rank_ref[0]
    share = height // len(part_refs)
    length = width // ROWS
    blocks = height // LANES
    unroll = 8
    copies = []
    for c in range(ROWS):
        columns = slice(c * length, (c + 1) * length)
        copies.append(
            pltpu.make_async_copy(
                source_ref.at[:, columns], image_ref.at[:, columns], sems.at[c]
            )
        )
    given = pltpu.make_async_copy(given_ref, table_ref, sems.at[ROWS])
    given.start()
    for copy in copies:
        copy.start()
    given.wait()
    cas_high, cas_low = halves(table_ref[0:height, :])
    rho_all = table_ref[height : height + ROWS, :]
    rhos = [rho_all[:, b * LANES : (b + 1) * LANES] for b in range(blocks)]
    zeros = [jnp.zeros((ROWS, LANES), f32)] * blocks

    def transform(values):
        high, low = halves(values)
        return dot(high, cas_high) + dot(low, cas_high) + dot(high, cas_low)

    for c in range(ROWS):
        copies[c].wait()
        image = 1.0 - image_ref[:, c * length : (c + 1) * length]
        spectrum = transform(jnp.transpose(image))
        for b in range(blocks):
            spec_ref[b, pl.ds(c, length, stride=ROWS), :] = spectrum[
                :, b * LANES : (b + 1) * LANES
            ]

    def rows(position):
        return pl.ds(pl.multiple_of(position * ROWS, ROWS), ROWS)

    def advance(position, ups, downs):
        ups = [spec_ref[b, rows(position), :] + rhos[b] * ups[b] for b in range(blocks)]
        back = length - 1 - position
        downs = [spec_ref[b, rows(back), :] + rhos[b] * downs[b] for b in range(blocks)]
        return ups, downs

    def sweep(index, carry):
        ups, downs = carry
        for step in range(unroll):
            ups, downs = advance(index * unroll + step, ups, downs)
        return ups, downs

    ups, downs = lax.fori_loop(0, length // unroll, sweep, (zeros, zeros))
    powers = list(rhos)
    for _ in range(int(math.log2(length))):
        powers = [power * power for power in powers]
    ups = [chunk_carry(ups[b], powers[b], True) for b in range(blocks)]
    downs = [chunk_carry(downs[b], powers[b], False) for b in range(blocks)]
    scales = [rho / (paganin_strength * (1.0 - rho * rho)) for rho in rhos]

    def outer(index, carry):
        ups, downs = carry
        for step in range(unroll):
            position = index * unroll + step
            ups, downs = advance(position, ups, downs)
            for b in range(blocks):
                up_ref[b, rows(position), :] = ups[b]
                down_ref[b, rows(position), :] = downs[b]
        return ups, downs

    def inner(index, carry):
        ups, downs = carry
        for step in range(unroll):
            position = index * unroll + step
            back = length - 1 - position
            ups, downs = advance(position, ups, downs)
            for b in range(blocks):
                here = ups[b] + down_ref[b, rows(back), :] - spec_ref[b, rows(position), :]
                there = downs[b] + up_ref[b, rows(back), :] - spec_ref[b, rows(back), :]
                up_ref[b, rows(position), :] = here * scales[b]
                up_ref[b, rows(back), :] = there * scales[b]
        return ups, downs

    half = length // 2 // unroll
    carry = lax.fori_loop(0, half, outer, (ups, downs))
    lax.fori_loop(half, 2 * half, inner, carry)

    offset = (width - ACTIVE) // 2
    for c in range(ROWS):
        spectrum = jnp.concatenate(
            [up_ref[b, pl.ds(c, length, stride=ROWS), :] for b in range(blocks)], axis=1
        )
        filtered = 1.0 - jnp.transpose(transform(spectrum))
        out_ref[:, c * length : (c + 1) * length] = -jnp.log(filtered)
    active_ref[...] = out_ref[:, offset : offset + ACTIVE]
    for d, part_ref in enumerate(part_refs):
        part_ref[...] = out_ref[pl.ds(pl.multiple_of((rank ^ d) * share, share), share), :]


def paganin(image, rank, parts):
    height, width = image.shape
    blocks = height // LANES
    return pl.pallas_call(
        filter_kernel,
        out_shape=[jax.ShapeDtypeStruct((height // parts, width), f32)] * parts
        + [jax.ShapeDtypeStruct((height, ACTIVE), f32)],
        in_specs=[pl.BlockSpec(memory_space=pltpu.SMEM)]
        + [pl.BlockSpec(memory_space=pltpu.HBM)] * 2,
        out_specs=[pl.BlockSpec(memory_space=pltpu.VMEM)] * (parts + 1),
        scratch_shapes=[
            pltpu.VMEM((height, width), f32),
            pltpu.VMEM((height + ROWS, height), f32),
            pltpu.VMEM((height, width), f32),
            pltpu.VMEM((blocks, width, LANES), f32),
            pltpu.VMEM((blocks, width, LANES), f32),
            pltpu.VMEM((blocks, width // 2, LANES), f32),
            pltpu.SemaphoreType.DMA((ROWS + 1,)),
        ],
        compiler_params=pltpu.CompilerParams(vmem_limit_bytes=58 * 2**20),
        cost_estimate=pl.CostEstimate(
            flops=64 * height * height * width,
            bytes_accessed=8 * height * width,
            transcendentals=height * width,
        ),
        name="paganin",
    )(rank.reshape(1), image, jnp.asarray(filter_tables(height)))


def reversed_exact(values, flip):
    return sum(dot(part, flip) for part in thirds(values))


class Weights:
    def __init__(self, ref, along_ref, place_ref, angles, chunk, count):
        self.ref = ref
        self.along_ref = along_ref
        self.place_ref = place_ref
        self.angles = angles
        self.chunk = chunk
        self.count = count
        self.ray = lax.broadcasted_iota(jnp.int32, (ROWS, VOX), 0).astype(f32)

    def prepare(self, shift_x_ref, shift_y_ref, cos_ref, sin_ref):
        def along_angle(t):
            self.along_ref[t] = shift_x_ref[...] * cos_ref[t] + shift_y_ref[...] * sin_ref[t]

        repeat(self.angles, along_angle, 8)

    def make(self, q, c):
        place = q % self.count
        for two in range(self.chunk // 2):
            pieces = []
            for t in (2 * two, 2 * two + 1):
                angle = c * self.chunk + t
                along = self.along_ref[angle] + self.place_ref[q * self.angles + angle]
                base = self.ray - along
                for group in range(WIN // ROWS):
                    distance = base + float(group * ROWS)
                    pieces.append(jnp.maximum(0.0, 1.0 - jnp.abs(distance)))
            high, low = halves(jnp.concatenate(pieces, axis=0))
            self.ref[place, 2 * two * WIN : (2 * two + 2) * WIN, 0:VOX] = high
            self.ref[place, 2 * two * WIN : (2 * two + 2) * WIN, VOX : 2 * VOX] = low

    def get(self, q):
        return self.ref[q % self.count]


class Stream:
    def __init__(self, hbm_ref, vmem_ref, sems, outward):
        self.hbm_ref = hbm_ref
        self.vmem_ref = vmem_ref
        self.sems = sems
        self.outward = outward
        self.count = vmem_ref.shape[0]

    def copy(self, q):
        place = q % self.count
        here, there = self.vmem_ref.at[place], self.hbm_ref.at[q]
        if self.outward:
            return pltpu.make_async_copy(here, there, self.sems.at[place])
        return pltpu.make_async_copy(there, here, self.sems.at[place])


def project(weights, make, values_of, offset_ref, acc_ref, pairs, both, stream, unroll):
    angles, chunk = weights.angles, weights.chunk
    acc_ref[...] = jnp.zeros(acc_ref.shape, f32)

    def pair(q):
        high, low = halves(values_of(q))
        operand = jnp.concatenate(
            [
                jnp.concatenate([high, high], axis=1),
                jnp.concatenate([low, jnp.zeros_like(low)], axis=1),
                jnp.ones((both, 2 * VOX), bf16),
                jnp.zeros((LANES - 3 * both, 2 * VOX), bf16),
            ],
            axis=0,
        )
        if stream is not None:

            @pl.when(q >= stream.count)
            def _():
                stream.copy(q - stream.count).wait()

        for c in range(angles // chunk):
            if make:
                weights.make(q, c)
            if stream is not None:
                stream.copy(q).start()
            sums = lax.dot_general(
                weights.get(q),
                operand,
                (((1,), (1,)), ((), ())),
                preferred_element_type=f32,
            )
            for begin in range(0, chunk, GROUP):
                places = []
                for t in range(begin, min(begin + GROUP, chunk)):
                    angle = c * chunk + t
                    rows = pl.ds(offset_ref[q * angles + angle], WIN)
                    values = acc_ref[angle, rows, :] + sums[t * WIN : (t + 1) * WIN, :]
                    places.append((angle, rows, values))
                for angle, rows, values in places:
                    acc_ref[angle, rows, :] = values

    repeat(pairs, pair, unroll)
    if stream is not None:
        for q in range(pairs - stream.count, pairs):
            stream.copy(q).wait()


def spread_rays(acc_ref, direct_ref, mirror_ref, total_ref, slices):
    both = 2 * slices

    def spread(t):
        rows = jnp.transpose(acc_ref[t]) * (1.0 / ROI)
        direct_ref[t] = rows[0:slices] + rows[both : both + slices]
        mirror_ref[t] = rows[slices:both] + rows[both + slices : 2 * both]
        if total_ref is not None:
            total_ref[t] = rows[2 * both : 2 * both + slices]

    repeat(acc_ref.shape[0], spread, 8)


def turn_rays(values, flip):
    shape = values.shape
    return reversed_exact(values.reshape(-1, shape[-1]), flip).reshape(shape)


def back_project(
    weights, weighted, flip, window_ref, tile_ref, turn_ref, store, pairs, stream, unroll
):
    angles, slices, _ = weighted.shape
    chunk = weights.chunk
    both = 2 * slices
    width = chunk * WIN
    high, low = halves(weighted.reshape(angles * slices, ACTIVE))
    mirrored = (dot(high, flip) + dot(low, flip)).reshape(weighted.shape)
    lane = lax.broadcasted_iota(jnp.int32, (angles, slices, LANES), 2)
    lane_rows = lax.broadcasted_iota(jnp.int32, (both, LANES), 1)
    for part, source in enumerate((weighted, mirrored)):
        rows = slice(part * slices, (part + 1) * slices)
        left = source[:, :, 0:LANES]
        right = source[:, :, LANES : 2 * LANES]
        window_ref[:, 0, rows, :] = left
        window_ref[:, 2, rows, :] = right
        mixed = jnp.where(lane >= SPLIT, left, right)
        window_ref[:, 1, rows, :] = pltpu.roll(mixed, SPLIT, 2)

    def pair(q):
        total = None
        for c in range(angles // chunk):
            if stream is None:
                weights.make(q, c)
            else:
                stream.copy(q).wait()
            tiles = [None] * (-(-width // LANES))
            for t in range(chunk):
                index = q * angles + c * chunk + t
                piece = pltpu.roll(
                    window_ref[c * chunk + t, tile_ref[index]], turn_ref[index], 1
                )
                begin = t * WIN
                for place in range(begin // LANES, (begin + WIN - 1) // LANES + 1):
                    if tiles[place] is None:
                        tiles[place] = piece
                    else:
                        tiles[place] = jnp.where(
                            lane_rows >= begin - place * LANES, piece, tiles[place]
                        )
            high, low = halves(jnp.concatenate(tiles, axis=1))
            sums = dot(jnp.concatenate([high, low], axis=0), weights.get(q))
            piece = sums[0:both, 0:VOX] + sums[both:, 0:VOX] + sums[0:both, VOX:]
            total = piece if total is None else total + piece
        store(q, total)

    repeat(pairs, pair, unroll)


def first_kernel(
    sizes,
    offset_ref,
    place_ref,
    slot_ref,
    cos_ref,
    sin_ref,
    vol_ref,
    flip_ref,
    shift_x_ref,
    shift_y_ref,
    held_ref,
    start_ref,
    predicted_ref,
    gain_ref,
    weight_ref,
    sems,
    acc_ref,
    along_ref,
    half_ref,
    mirror_ref,
):
    angles, chunk, held, slots = sizes
    patches = slot_ref.shape[0]
    pairs, both, _ = start_ref.shape
    slices = both // 2
    flip = flip_ref[...]

    def slot_values(patch):
        slot = slot_ref[patch]
        rows = pl.ds(slot % slots, slices, stride=slots)
        return jnp.concatenate(
            [half_ref[part, slot // slots, rows, :] for part in range(2)], axis=1
        )

    weights = Weights(
        weight_ref, along_ref, place_ref, angles, chunk, weight_ref.shape[0]
    )
    stream = Stream(held_ref, weight_ref, sems, True) if held else None
    weights.prepare(shift_x_ref, shift_y_ref, cos_ref, sin_ref)
    for part in range(2):
        half_ref[part] = vol_ref[:, :, part * LANES : (part + 1) * LANES]

    def order(q):
        start_ref[q, 0:slices, :] = slot_values(q)
        mirror_ref[q] = slot_values(patches - 1 - q)

    repeat(pairs, order, 8)
    start_ref[:, slices:both, :] = turn_rays(mirror_ref[0:pairs], flip)
    project(
        weights, True, lambda q: start_ref[q], offset_ref, acc_ref, pairs, both, stream, 2
    )
    spread_rays(acc_ref, predicted_ref, mirror_ref, gain_ref, slices)
    predicted_ref[...] = predicted_ref[...] + turn_rays(mirror_ref[0:angles], flip)
    direct = gain_ref[...]
    gain_ref[...] = 1.0 / jnp.maximum(direct + turn_rays(direct, flip), row_floor)


def second_kernel(
    sizes,
    step_size,
    offset_ref,
    place_ref,
    tile_ref,
    turn_ref,
    cos_ref,
    sin_ref,
    start_ref,
    predicted_ref,
    gain_ref,
    sino_ref,
    flip_ref,
    shift_x_ref,
    shift_y_ref,
    held_ref,
    update_ref,
    res_ref,
    weight_ref,
    sems,
    acc_ref,
    along_ref,
    direct_ref,
    mirror_ref,
    window_ref,
):
    angles, chunk, held, _ = sizes
    pairs, both, _ = start_ref.shape
    slices = both // 2
    rays = res_ref.shape[0]
    flip = flip_ref[...]
    weights = Weights(
        weight_ref, along_ref, place_ref, angles, chunk, weight_ref.shape[0]
    )
    stream = Stream(held_ref, weight_ref, sems, False) if held else None
    if held:
        repeat(pairs, lambda q: stream.copy(q).start(), 8)
    else:
        weights.prepare(shift_x_ref, shift_y_ref, cos_ref, sin_ref)
    weighted = (sino_ref[...] - predicted_ref[...]) * gain_ref[...] * (1.0 / ROI)

    def store(q, total):
        update_ref[q] = total

    back_project(
        weights, weighted, flip, window_ref, tile_ref, turn_ref, store, pairs, stream, 4
    )

    def values_of(q):
        return start_ref[q] + step_size * update_ref[q]

    project(weights, not held, values_of, offset_ref, acc_ref, pairs, both, None, 4)
    spread_rays(acc_ref, direct_ref, mirror_ref, None, slices)
    residual = sino_ref[...] - direct_ref[...] - turn_rays(mirror_ref[...], flip)
    for t in range(angles):
        begin = t // rays * slices
        res_ref[t % rays, begin : begin + slices, :] = residual[t]


def third_kernel(
    sizes,
    step_size,
    place_ref,
    tile_ref,
    turn_ref,
    slot_ref,
    cos_ref,
    sin_ref,
    update_ref,
    res_ref,
    gain_ref,
    vol_ref,
    flip_ref,
    shift_x_ref,
    shift_y_ref,
    held_ref,
    out_ref,
    weight_ref,
    sems,
    along_ref,
    total_ref,
    mirror_ref,
    window_ref,
    half_ref,
):
    angles, chunk, held, slots = sizes
    patches = slot_ref.shape[0]
    pairs, both, _ = update_ref.shape
    slices = both // 2
    rays = res_ref.shape[0]
    flip = flip_ref[...]
    weights = Weights(
        weight_ref, along_ref, place_ref, angles, chunk, weight_ref.shape[0]
    )
    stream = Stream(held_ref, weight_ref, sems, False) if held else None
    if held:
        repeat(pairs, lambda q: stream.copy(q).start(), 8)
    else:
        weights.prepare(shift_x_ref, shift_y_ref, cos_ref, sin_ref)
    residual = [
        res_ref[t % rays, t // rays * slices : (t // rays + 1) * slices, :][None]
        for t in range(angles)
    ]
    weighted = jnp.concatenate(residual, axis=0) * gain_ref[...] * (1.0 / ROI)

    def store(q, total):
        total_ref[q] = (update_ref[q] + total) * step_size

    back_project(
        weights, weighted, flip, window_ref, tile_ref, turn_ref, store, pairs, stream, 4
    )
    mirror_ref[...] = turn_rays(total_ref[:, slices:both, :], flip)
    for part in range(2):
        half_ref[part] = vol_ref[:, :, part * LANES : (part + 1) * LANES]

    def finish(q):
        for patch, update in (
            (q, total_ref[q, 0:slices, :]),
            (patches - 1 - q, mirror_ref[q]),
        ):
            slot = slot_ref[patch]
            rows = pl.ds(slot % slots, slices, stride=slots)
            for part in range(2):
                half_ref[part, slot // slots, rows, :] = (
                    half_ref[part, slot // slots, rows, :]
                    + update[:, part * LANES : (part + 1) * LANES]
                )

    repeat(pairs, finish, 8)
    for part in range(2):
        out_ref[:, :, part * LANES : (part + 1) * LANES] = half_ref[part]


def call(kernel, name, inputs, held_in, outputs, held_out, scratch, micros, room):
    smem = pl.BlockSpec(memory_space=pltpu.SMEM)
    vmem = pl.BlockSpec(memory_space=pltpu.VMEM)
    hbm = [pl.BlockSpec(memory_space=pltpu.HBM)]
    before = len(inputs)

    def body(*refs):
        refs = list(refs)
        if not held_in and not held_out:
            refs.insert(before, None)
        kernel(*refs)

    return pl.pallas_call(
        body,
        out_shape=[jax.ShapeDtypeStruct(*value) for value in held_out + outputs],
        in_specs=[smem if value.ndim == 1 else vmem for value in inputs] + hbm * len(held_in),
        out_specs=hbm * len(held_out) + [vmem] * len(outputs),
        scratch_shapes=scratch,
        compiler_params=pltpu.CompilerParams(vmem_limit_bytes=room * 2**20),
        cost_estimate=pl.CostEstimate(
            flops=int(micros * 1e9), bytes_accessed=4 * 2**20, transcendentals=0
        ),
        name=name,
    )(*inputs, *held_in)


class Sirt:
    def __init__(self, theta, vol_list, slices, slots, rays, step_size):
        angles = theta.shape[0]
        patches = vol_list.shape[0]
        pairs = patches // 2
        both = 2 * slices
        chunk = math.gcd(angles, 32)
        self.held = angles == chunk
        self.room = 52
        self.sizes = (angles, chunk, self.held, slots)
        self.step_size = step_size
        self.rays = rays
        self.patches = patches
        centre = (ROI - 1) / 2.0
        ids = np.arange(pairs)
        centre_x = (ids // PGRID * float(SIDE) + (SIDE - 1) / 2.0 - centre).astype(np.float32)
        centre_y = (ids % PGRID * float(SIDE) + (SIDE - 1) / 2.0 - centre).astype(np.float32)
        self.cosine = jnp.cos(theta)
        self.sine = jnp.sin(theta)
        along = (
            centre_x[:, None] * self.cosine[None, :]
            + centre_y[:, None] * self.sine[None, :]
            + 0.5
        )
        whole = jnp.floor(along)
        lead = WIN // 2 - 1
        place = along - whole + float(lead)
        offset = whole.astype(jnp.int32) + (ACTIVE // 2 - 1 - lead)
        tile = jnp.minimum(offset // SPLIT, 2)
        local = jnp.arange(angles, dtype=jnp.int32) % chunk * WIN
        turn = (local[None, :] - offset + tile * SPLIT) % LANES
        self.offset = offset.reshape(-1)
        self.place = place.reshape(-1)
        self.tile = tile.reshape(-1)
        self.turn = turn.reshape(-1)
        ids = jnp.arange(patches, dtype=jnp.int32)
        self.slot = jnp.sum(
            jnp.where(vol_list[None, :] == ids[:, None], ids[None, :], 0), axis=1
        )
        voxel = np.arange(VOX)
        shift_x = np.repeat((voxel // SIDE - (SIDE - 1) / 2.0)[None, :], ROWS, axis=0)
        shift_y = np.repeat((voxel % SIDE - (SIDE - 1) / 2.0)[None, :], ROWS, axis=0)
        flip = np.eye(ACTIVE)[::-1].astype(ml_dtypes.bfloat16)
        self.fixed = [jnp.asarray(flip), jnp.asarray(shift_x, f32), jnp.asarray(shift_y, f32)]
        self.held_weight = ((pairs, chunk * WIN, 2 * VOX), bf16)
        self.acc = ((angles, ACTIVE, LANES), f32)
        self.along = ((angles, ROWS, VOX), f32)
        self.by_ray = ((angles, slices, ACTIVE), f32)
        self.by_pair = ((pairs, both, VOX), f32)
        self.window = ((angles, 3, both, LANES), f32)
        self.half = ((2, rays, slices * slots, LANES), f32)
        self.mirror = ((max(pairs, angles), slices, ACTIVE), f32)
        self.sent = ((rays, angles // rays * slices, ACTIVE), f32)

    def scratch(self, held, *shapes):
        count = held if self.held else 1
        shape, dtype = self.held_weight
        weight = pltpu.VMEM((count,) + shape[1:], dtype)
        rest = [pltpu.VMEM(*shape) for shape in shapes]
        return [weight, pltpu.SemaphoreType.DMA((count,))] + rest

    def first(self, volume):
        inputs = [self.offset, self.place, self.slot, self.cosine, self.sine, volume]
        results = call(
            functools.partial(first_kernel, self.sizes),
            "first",
            inputs + self.fixed,
            [],
            [self.by_pair, self.by_ray, self.by_ray],
            [self.held_weight] if self.held else [],
            self.scratch(4, self.acc, self.along, self.half, self.mirror),
            16,
            self.room,
        )
        return (results[:1], results[1:]) if self.held else ([], results)

    def second(self, weight, start, predicted, gain, sino):
        inputs = [self.offset, self.place, self.tile, self.turn, self.cosine, self.sine]
        inputs += [start, predicted, gain, sino]
        return call(
            functools.partial(second_kernel, self.sizes, self.step_size),
            "second",
            inputs + self.fixed,
            list(weight),
            [self.by_pair, self.sent],
            [],
            self.scratch(
                self.patches // 2, self.acc, self.along, self.by_ray, self.by_ray, self.window
            ),
            20,
            self.room,
        )

    def third(self, weight, update, residual, gain, volume):
        inputs = [self.place, self.tile, self.turn, self.slot, self.cosine, self.sine]
        inputs += [update, residual, gain, volume]
        pairs = self.patches // 2
        mirror = ((pairs,) + self.by_ray[0][1:], f32)
        return call(
            functools.partial(third_kernel, self.sizes, self.step_size),
            "third",
            inputs + self.fixed,
            list(weight),
            [(volume.shape, f32)],
            [],
            self.scratch(pairs, self.along, self.by_pair, mirror, self.window, self.half),
            10,
            self.room,
        )[0]


def gather_kernel(rank_ref, *refs):
    *part_refs, out_ref, sems = refs
    rank = rank_ref[0]
    copies = [
        pltpu.make_async_copy(part_ref, out_ref.at[rank ^ d], sems.at[d])
        for d, part_ref in enumerate(part_refs)
    ]
    for copy in copies:
        copy.start()
    for copy in copies:
        copy.wait()


def gather_parts(parts, rank):
    count = len(parts)
    return pl.pallas_call(
        gather_kernel,
        out_shape=jax.ShapeDtypeStruct((count,) + parts[0].shape, f32),
        in_specs=[pl.BlockSpec(memory_space=pltpu.SMEM)]
        + [pl.BlockSpec(memory_space=pltpu.VMEM)] * count,
        out_specs=pl.BlockSpec(memory_space=pl.ANY),
        scratch_shapes=[pltpu.SemaphoreType.DMA((count,))],
        cost_estimate=pl.CostEstimate(
            flops=0, bytes_accessed=8 * count * parts[0].size, transcendentals=0
        ),
        name="gather_parts",
    )(rank.reshape(1), *parts)


def finish_kernel(got_ref, sino_ref, out_ref, active_ref, sem):
    rays, rows, _ = got_ref.shape
    slabs = active_ref.shape[0]
    slices = rows // slabs
    for ray in range(rays):
        for k in range(slabs):
            active_ref[k, ray * slices : (ray + 1) * slices, :] = got_ref[
                ray, k * slices : (k + 1) * slices, :
            ]
    offset = (out_ref.shape[2] - ACTIVE) // 2
    copy = pltpu.make_async_copy(
        active_ref, out_ref.at[:, :, offset : offset + ACTIVE], sem
    )
    copy.start()
    copy.wait()


def finish(got, sinogram):
    slabs, slab_rows, _ = sinogram.shape
    any_space = pl.BlockSpec(memory_space=pl.ANY)
    return pl.pallas_call(
        finish_kernel,
        out_shape=jax.ShapeDtypeStruct(sinogram.shape, f32),
        in_specs=[pl.BlockSpec(memory_space=pltpu.VMEM), any_space],
        out_specs=any_space,
        scratch_shapes=[
            pltpu.VMEM((slabs, slab_rows, ACTIVE), f32),
            pltpu.SemaphoreType.DMA,
        ],
        input_output_aliases={1: 0},
        cost_estimate=pl.CostEstimate(
            flops=0, bytes_accessed=8 * got.size, transcendentals=0
        ),
        name="finish",
    )(got, sinogram)


def local(intensity, angles, volume, vol_list):
    n_slab = lax.axis_size("slab")
    n_ray = lax.axis_size("ray")
    devices = n_slab * n_ray
    height, band = intensity.shape[2:]
    slices = height // devices
    slots = volume.shape[1]
    count = angles.shape[0] * angles.shape[1]
    step_size = relax * ROI / count
    rank = lax.axis_index("slab")
    padded = -(-slices // ROWS) * ROWS

    def to_all(values, axes):
        return lax.all_to_all(values, axes, split_axis=0, concat_axis=0, tiled=True)

    own_volume = to_all(volume.reshape(n_ray, slices * slots, VOX), "ray")
    *parts, active = paganin(intensity.reshape(height, band), rank, n_slab)
    active, own_volume = lax.optimization_barrier((active, own_volume))
    own_rays = to_all(active.reshape(devices, slices, ACTIVE), ("slab", "ray"))
    if padded != slices:
        widen = ((0, 0), (0, padded - slices), (0, 0))
        own_volume = jnp.pad(own_volume, ((0, 0), (0, (padded - slices) * slots), (0, 0)))
        own_rays = jnp.pad(own_rays, widen)

    theta, vol_list, own_volume, parts = lax.optimization_barrier(
        (angles.reshape(-1), vol_list, own_volume, parts)
    )
    sirt = Sirt(theta, vol_list, padded, slots, n_ray, step_size)
    weight, (start, predicted, gain) = sirt.first(own_volume)
    own_rays, parts, start = lax.optimization_barrier((own_rays, parts, start))
    parts = [
        lax.ppermute(part, "slab", [(i, i ^ d) for i in range(n_slab)]) if d else part
        for d, part in enumerate(parts)
    ]
    update, residual = sirt.second(weight, start, predicted, gain, own_rays)
    sent = residual
    if padded != slices:
        sent = sent.reshape(n_ray, n_slab, padded, ACTIVE)[:, :, :slices]
        sent = sent.reshape(n_ray, n_slab * slices, ACTIVE)
    got = to_all(sent, "ray")
    ready = [d for d in range(n_slab) if d != n_slab // 2]
    update, *early = lax.optimization_barrier((update, *[parts[d] for d in ready]))
    for d, part in zip(ready, early):
        parts[d] = part
    result = sirt.third(weight, update, residual, gain, own_volume)
    result = result[:, : slices * slots]
    result, got, parts = lax.optimization_barrier((result, got, parts))
    reconstruction = to_all(result, "ray").reshape(volume.shape)
    sinogram = gather_parts(parts, rank)
    residual = finish(got, sinogram)
    return (reconstruction, residual[:, None])


def solution(mesh):
    placed = (P("slab", "ray", None, None), P(), P("slab", "ray", None), P())
    return jax.shard_map(
        local,
        mesh=mesh,
        in_specs=placed,
        out_specs=(P("slab", "ray", None), P(None, "ray", "slab", None)),
        check_vma=False,
    )
```

```python
import functools
import math

import jax
import jax.numpy as jnp
import ml_dtypes
import numpy as np
from jax import lax
from jax.experimental import pallas as pl
from jax.experimental.pallas import tpu as pltpu
from jax.sharding import PartitionSpec as P

BAND = 2048
PGRID = 8
ROI = 128
SIDE = 16
VOX = SIDE * SIDE
WIN = 24
ACTIVE = 256
LANES = 128
ROWS = 8
SPLIT = 64
GROUP = 8

paganin_strength = 10.0
relax = 1.8
row_floor = 0.25

bf16 = jnp.bfloat16
f32 = jnp.float32


def halves(values):
    high = values.astype(bf16)
    low = (values - high.astype(f32)).astype(bf16)
    return high, low


def thirds(values):
    high = values.astype(bf16)
    rest = values - high.astype(f32)
    middle = rest.astype(bf16)
    low = (rest - middle.astype(f32)).astype(bf16)
    return high, middle, low


def dot(left, right):
    return jnp.dot(left, right, preferred_element_type=f32)


def repeat(count, body, unroll):
    unroll = math.gcd(count, unroll)

    def several(index, carry):
        for step in range(unroll):
            body(index * unroll + step)
        return carry

    lax.fori_loop(0, count // unroll, several, 0)


def filter_tables(height):
    index = np.arange(height)
    phase = 2.0 * np.pi * (np.outer(index, index) % height) / height
    cas = (np.cos(phase) + np.sin(phase)) / math.sqrt(height)
    row_freq = 2.0 - 2.0 * np.cos(2.0 * np.pi * index / height)
    middle = (1.0 + paganin_strength * row_freq) / paganin_strength + 2.0
    rho = (middle - np.sqrt(middle * middle - 4.0)) / 2.0
    return np.concatenate([cas, np.repeat(rho[None, :], ROWS, axis=0)], axis=0).astype(np.float32)


def chunk_carry(ends, power, forward):
    shift = 1
    for _ in range(3):
        ends = ends + power * pltpu.roll(ends, shift if forward else ROWS - shift, 0)
        power = power * power
        shift *= 2
    return pltpu.roll(ends, 1 if forward else ROWS - 1, 0) / (1.0 - power)


def filter_kernel(rank_ref, source_ref, given_ref, *refs):
    *part_refs, active_ref, image_ref, table_ref, out_ref, spec_ref, up_ref, down_ref = refs[:-2]
    sems, out_sems = refs[-2:]
    height, width = image_ref.shape
    rank = rank_ref[0]
    share = height // len(part_refs)
    length = width // ROWS
    blocks = height // LANES
    unroll = 8
    copies = []
    for c in range(ROWS):
        columns = slice(c * length, (c + 1) * length)
        copies.append(
            pltpu.make_async_copy(
                source_ref.at[:, columns], image_ref.at[:, columns], sems.at[c]
            )
        )
    given = pltpu.make_async_copy(given_ref, table_ref, sems.at[ROWS])
    given.start()
    for copy in copies:
        copy.start()
    given.wait()
    cas_high, cas_low = halves(table_ref[0:height, :])
    rho_all = table_ref[height : height + ROWS, :]
    rhos = [rho_all[:, b * LANES : (b + 1) * LANES] for b in range(blocks)]
    zeros = [jnp.zeros((ROWS, LANES), f32)] * blocks

    def transform(values):
        high, low = halves(values)
        return dot(high, cas_high) + dot(low, cas_high) + dot(high, cas_low)

    for c in range(ROWS):
        copies[c].wait()
        image = 1.0 - image_ref[:, c * length : (c + 1) * length]
        spectrum = transform(jnp.transpose(image))
        for b in range(blocks):
            spec_ref[b, pl.ds(c, length, stride=ROWS), :] = spectrum[
                :, b * LANES : (b + 1) * LANES
            ]

    def rows(position):
        return pl.ds(pl.multiple_of(position * ROWS, ROWS), ROWS)

    def advance(position, ups, downs):
        ups = [spec_ref[b, rows(position), :] + rhos[b] * ups[b] for b in range(blocks)]
        back = length - 1 - position
        downs = [spec_ref[b, rows(back), :] + rhos[b] * downs[b] for b in range(blocks)]
        return ups, downs

    def sweep(index, carry):
        ups, downs = carry
        for step in range(unroll):
            ups, downs = advance(index * unroll + step, ups, downs)
        return ups, downs

    ups, downs = lax.fori_loop(0, length // unroll, sweep, (zeros, zeros))
    powers = list(rhos)
    for _ in range(int(math.log2(length))):
        powers = [power * power for power in powers]
    ups = [chunk_carry(ups[b], powers[b], True) for b in range(blocks)]
    downs = [chunk_carry(downs[b], powers[b], False) for b in range(blocks)]
    scales = [rho / (paganin_strength * (1.0 - rho * rho)) for rho in rhos]

    def outer(index, carry):
        ups, downs = carry
        for step in range(unroll):
            position = index * unroll + step
            ups, downs = advance(position, ups, downs)
            for b in range(blocks):
                up_ref[b, rows(position), :] = ups[b]
                down_ref[b, rows(position), :] = downs[b]
        return ups, downs

    def inner(index, carry):
        ups, downs = carry
        for step in range(unroll):
            position = index * unroll + step
            back = length - 1 - position
            ups, downs = advance(position, ups, downs)
            for b in range(blocks):
                here = ups[b] + down_ref[b, rows(back), :] - spec_ref[b, rows(position), :]
                there = downs[b] + up_ref[b, rows(back), :] - spec_ref[b, rows(back), :]
                up_ref[b, rows(position), :] = here * scales[b]
                up_ref[b, rows(back), :] = there * scales[b]
        return ups, downs

    half = length // 2 // unroll
    carry = lax.fori_loop(0, half, outer, (ups, downs))
    lax.fori_loop(half, 2 * half, inner, carry)

    offset = (width - ACTIVE) // 2
    sent = []
    for c in range(ROWS):
        spectrum = jnp.concatenate(
            [up_ref[b, pl.ds(c, length, stride=ROWS), :] for b in range(blocks)], axis=1
        )
        filtered = 1.0 - jnp.transpose(transform(spectrum))
        columns = slice(c * length, (c + 1) * length)
        out_ref[:, columns] = -jnp.log(filtered)
        for d, part_ref in enumerate(part_refs):
            rows = pl.ds(pl.multiple_of((rank ^ d) * share, share), share)
            sent.append(
                pltpu.make_async_copy(
                    out_ref.at[rows, columns], part_ref.at[:, columns], out_sems.at[c, d]
                )
            )
            sent[-1].start()
    active_ref[...] = out_ref[:, offset : offset + ACTIVE]
    for copy in sent:
        copy.wait()


def paganin(image, rank, parts):
    height, width = image.shape
    blocks = height // LANES
    return pl.pallas_call(
        filter_kernel,
        out_shape=[jax.ShapeDtypeStruct((height // parts, width), f32)] * parts
        + [jax.ShapeDtypeStruct((height, ACTIVE), f32)],
        in_specs=[pl.BlockSpec(memory_space=pltpu.SMEM)]
        + [pl.BlockSpec(memory_space=pltpu.HBM)] * 2,
        out_specs=[pl.BlockSpec(memory_space=pltpu.HBM)] * parts
        + [pl.BlockSpec(memory_space=pltpu.VMEM)],
        scratch_shapes=[
            pltpu.VMEM((height, width), f32),
            pltpu.VMEM((height + ROWS, height), f32),
            pltpu.VMEM((height, width), f32),
            pltpu.VMEM((blocks, width, LANES), f32),
            pltpu.VMEM((blocks, width, LANES), f32),
            pltpu.VMEM((blocks, width // 2, LANES), f32),
            pltpu.SemaphoreType.DMA((ROWS + 1,)),
            pltpu.SemaphoreType.DMA((ROWS, parts)),
        ],
        compiler_params=pltpu.CompilerParams(vmem_limit_bytes=58 * 2**20),
        cost_estimate=pl.CostEstimate(
            flops=64 * height * height * width,
            bytes_accessed=8 * height * width,
            transcendentals=height * width,
        ),
        name="paganin",
    )(rank.reshape(1), image, jnp.asarray(filter_tables(height)))


def reversed_exact(values, flip):
    return sum(dot(part, flip) for part in thirds(values))


class Weights:
    def __init__(self, ref, along_ref, place_ref, angles, chunk):
        self.ref = ref
        self.along_ref = along_ref
        self.place_ref = place_ref
        self.angles = angles
        self.chunk = chunk
        self.ray = lax.broadcasted_iota(jnp.int32, (ROWS, VOX), 0).astype(f32)

    def prepare(self, shift_x_ref, shift_y_ref, cos_ref, sin_ref):
        def along_angle(t):
            self.along_ref[t] = shift_x_ref[...] * cos_ref[t] + shift_y_ref[...] * sin_ref[t]

        repeat(self.angles, along_angle, 8)

    def make(self, q, c, place):
        ref = self.ref.at[place]
        for two in range(self.chunk // 2):
            pieces = []
            for t in (2 * two, 2 * two + 1):
                angle = c * self.chunk + t
                along = self.along_ref[angle] + self.place_ref[q * self.angles + angle]
                base = self.ray - along
                for group in range(WIN // ROWS):
                    distance = base + float(group * ROWS)
                    pieces.append(jnp.maximum(0.0, 1.0 - jnp.abs(distance)))
            high, low = halves(jnp.concatenate(pieces, axis=0))
            ref[2 * two * WIN : (2 * two + 2) * WIN, 0:VOX] = high
            ref[2 * two * WIN : (2 * two + 2) * WIN, VOX : 2 * VOX] = low


def project(weights, values_of, weights_of, offset_ref, acc_ref, pairs, both, unroll):
    angles, chunk = weights.angles, weights.chunk
    acc_ref[...] = jnp.zeros(acc_ref.shape, f32)

    def pair(q, step):
        high, low = halves(values_of(q))
        operand = jnp.concatenate(
            [
                jnp.concatenate([high, high], axis=1),
                jnp.concatenate([low, jnp.zeros_like(low)], axis=1),
                jnp.ones((both, 2 * VOX), bf16),
                jnp.zeros((LANES - 3 * both, 2 * VOX), bf16),
            ],
            axis=0,
        )
        for c in range(angles // chunk):
            sums = lax.dot_general(
                weights_of(q, c, step),
                operand,
                (((1,), (1,)), ((), ())),
                preferred_element_type=f32,
            )
            for begin in range(0, chunk, GROUP):
                places = []
                for t in range(begin, min(begin + GROUP, chunk)):
                    angle = c * chunk + t
                    rows = pl.ds(offset_ref[q * angles + angle], WIN)
                    values = acc_ref[angle, rows, :] + sums[t * WIN : (t + 1) * WIN, :]
                    places.append((angle, rows, values))
                for angle, rows, values in places:
                    acc_ref[angle, rows, :] = values

    def several(index, carry):
        for step in range(unroll):
            pair(index * unroll + step, step)
        return carry

    lax.fori_loop(0, pairs // unroll, several, 0)


def spread_rays(acc_ref, direct_ref, mirror_ref, total_ref, slices):
    both = 2 * slices

    def spread(t):
        rows = jnp.transpose(acc_ref[t]) * (1.0 / ROI)
        direct_ref[t] = rows[0:slices] + rows[both : both + slices]
        mirror_ref[t] = rows[slices:both] + rows[both + slices : 2 * both]
        if total_ref is not None:
            total_ref[t] = rows[2 * both : 2 * both + slices]

    repeat(acc_ref.shape[0], spread, 8)


def turn_rays(values, flip):
    shape = values.shape
    return reversed_exact(values.reshape(-1, shape[-1]), flip).reshape(shape)


def back_project(
    weights, weights_of, weighted, flip, window_ref, tile_ref, turn_ref, store, pairs, unroll
):
    angles, slices, _ = weighted.shape
    chunk = weights.chunk
    both = 2 * slices
    width = chunk * WIN
    high, low = halves(weighted.reshape(angles * slices, ACTIVE))
    mirrored = (dot(high, flip) + dot(low, flip)).reshape(weighted.shape)
    lane = lax.broadcasted_iota(jnp.int32, (angles, slices, LANES), 2)
    lane_rows = lax.broadcasted_iota(jnp.int32, (both, LANES), 1)
    for part, source in enumerate((weighted, mirrored)):
        rows = slice(part * slices, (part + 1) * slices)
        left = source[:, :, 0:LANES]
        right = source[:, :, LANES : 2 * LANES]
        window_ref[:, 0, rows, :] = left
        window_ref[:, 2, rows, :] = right
        mixed = jnp.where(lane >= SPLIT, left, right)
        window_ref[:, 1, rows, :] = pltpu.roll(mixed, SPLIT, 2)

    def pair(q):
        total = None
        for c in range(angles // chunk):
            held = weights_of(q, c)
            tiles = [None] * (-(-width // LANES))
            for t in range(chunk):
                index = q * angles + c * chunk + t
                piece = pltpu.roll(
                    window_ref[c * chunk + t, tile_ref[index]], turn_ref[index], 1
                )
                begin = t * WIN
                for place in range(begin // LANES, (begin + WIN - 1) // LANES + 1):
                    if tiles[place] is None:
                        tiles[place] = piece
                    else:
                        tiles[place] = jnp.where(
                            lane_rows >= begin - place * LANES, piece, tiles[place]
                        )
            high, low = halves(jnp.concatenate(tiles, axis=1))
            sums = dot(jnp.concatenate([high, low], axis=0), held)
            piece = sums[0:both, 0:VOX] + sums[both:, 0:VOX] + sums[0:both, VOX:]
            total = piece if total is None else total + piece
        store(q, total)

    repeat(pairs, pair, unroll)


def first_kernel(
    sizes,
    rank_ref,
    offset_ref,
    place_ref,
    slot_ref,
    cos_ref,
    sin_ref,
    flip_ref,
    shift_x_ref,
    shift_y_ref,
    *refs,
):
    angles, chunk, held, slots, rays = sizes
    vol_refs, refs = refs[:rays], list(refs[rays:])
    held_ref = refs.pop(0) if held else None
    half_ref, start_ref, predicted_ref, gain_ref = refs[:4]
    weight_a_ref, weight_b_ref, sems, acc_ref, along_ref, mirror_ref = refs[4:]
    patches = slot_ref.shape[0]
    pairs, both, _ = start_ref.shape
    slices = both // 2
    rank = rank_ref[0]
    flip = flip_ref[...]

    def slot_values(patch):
        slot = slot_ref[patch]
        rows = pl.ds(slot % slots, slices, stride=slots)
        return jnp.concatenate(
            [half_ref[part, slot // slots, rows, :] for part in range(2)], axis=1
        )

    for d, vol_ref in enumerate(vol_refs):
        for part in range(2):
            half_ref[part, rank ^ d] = vol_ref[:, part * LANES : (part + 1) * LANES]

    def order(q):
        start_ref[q, 0:slices, :] = slot_values(q)
        mirror_ref[q] = slot_values(patches - 1 - q)

    repeat(pairs, order, 8)
    start_ref[:, slices:both, :] = turn_rays(mirror_ref[0:pairs], flip)
    both_weights = [
        Weights(ref, along_ref, place_ref, angles, chunk) for ref in (weight_a_ref, weight_b_ref)
    ]
    both_weights[0].prepare(shift_x_ref, shift_y_ref, cos_ref, sin_ref)

    def outward(q, step):
        place = q // 2 % 2
        return pltpu.make_async_copy(
            both_weights[step].ref.at[place], held_ref.at[q], sems.at[step, place]
        )

    def weights_of(q, c, step):
        if held:

            @pl.when(q >= 4)
            def _():
                outward(q - 4, step).wait()

        place = q // 2 % 2
        both_weights[step].make(q, c, place)
        if held:
            outward(q, step).start()
        return both_weights[step].ref[place]

    project(
        both_weights[0], lambda q: start_ref[q], weights_of, offset_ref, acc_ref, pairs, both, 2
    )
    if held:
        for q in range(pairs - 4, pairs):
            outward(q, q % 2).wait()
    spread_rays(acc_ref, predicted_ref, mirror_ref, gain_ref, slices)
    predicted_ref[...] = predicted_ref[...] + turn_rays(mirror_ref[0:angles], flip)
    direct = gain_ref[...]
    gain_ref[...] = 1.0 / jnp.maximum(direct + turn_rays(direct, flip), row_floor)


def second_kernel(
    sizes,
    step_size,
    rank_ref,
    offset_ref,
    place_ref,
    tile_ref,
    turn_ref,
    slot_ref,
    cos_ref,
    sin_ref,
    flip_ref,
    shift_x_ref,
    shift_y_ref,
    half_in_ref,
    start_ref,
    predicted_ref,
    gain_ref,
    sino_ref,
    *refs,
):
    angles, chunk, held, slots, rays = sizes
    refs = list(refs)
    held_ref = refs.pop(0) if held else None
    out_refs, refs = refs[:rays], refs[rays:]
    weight_ref, sems, acc_ref, along_ref, direct_ref, mirror_ref, window_ref = refs[:7]
    update_ref, half_ref = refs[7:]
    patches = slot_ref.shape[0]
    pairs, both, _ = start_ref.shape
    slices = both // 2
    rank = rank_ref[0]
    flip = flip_ref[...]
    weights = Weights(weight_ref, along_ref, place_ref, angles, chunk)
    ahead = 4

    def inward(q):
        return pltpu.make_async_copy(held_ref.at[q], weight_ref.at[q], sems.at[q])

    if held:
        for q in range(ahead):
            inward(q).start()
    else:
        weights.prepare(shift_x_ref, shift_y_ref, cos_ref, sin_ref)

    def arriving(q, c):
        if not held:
            weights.make(q, c, 0)
            return weight_ref[0]

        @pl.when(q + ahead < pairs)
        def _():
            inward(q + ahead).start()

        inward(q).wait()
        return weight_ref[q]

    def ready(q, c, step=0):
        if not held:
            weights.make(q, c, 0)
            return weight_ref[0]
        return weight_ref[q]

    def first_update(q, total):
        update_ref[q] = total

    def second_update(q, total):
        update_ref[q] = (update_ref[q] + total) * step_size

    rest = (flip, window_ref, tile_ref, turn_ref)
    weighted = (sino_ref[...] - predicted_ref[...]) * gain_ref[...] * (1.0 / ROI)
    back_project(weights, arriving, weighted, *rest, first_update, pairs, 2)

    def values_of(q):
        return start_ref[q] + step_size * update_ref[q]

    project(weights, values_of, ready, offset_ref, acc_ref, pairs, both, 2)
    spread_rays(acc_ref, direct_ref, mirror_ref, None, slices)
    turned = turn_rays(mirror_ref[0:angles], flip)
    direct_ref[...] = sino_ref[...] - direct_ref[...] - turned
    weighted = direct_ref[...] * gain_ref[...] * (1.0 / ROI)
    back_project(weights, ready, weighted, *rest, second_update, pairs, 2)

    mirror_ref[0:pairs] = turn_rays(update_ref[:, slices:both, :], flip)
    half_ref[...] = half_in_ref[...]

    def finish(q):
        for patch, update in (
            (q, update_ref[q, 0:slices, :]),
            (patches - 1 - q, mirror_ref[q]),
        ):
            slot = slot_ref[patch]
            rows = pl.ds(slot % slots, slices, stride=slots)
            for part in range(2):
                half_ref[part, slot // slots, rows, :] = (
                    half_ref[part, slot // slots, rows, :]
                    + update[:, part * LANES : (part + 1) * LANES]
                )

    repeat(pairs, finish, 8)
    lead = slices * slots
    for d, out_ref in enumerate(out_refs):
        ray = rank ^ d
        for part in range(2):
            out_ref[0:lead, part * LANES : (part + 1) * LANES] = half_ref[part, ray]
        for k in range(angles // rays):
            begin = lead + k * slices
            out_ref[begin : begin + slices, :] = direct_ref[k * rays + ray]


def call(kernel, name, inputs, held_in, held_out, outputs, scratch, micros):
    smem = pl.BlockSpec(memory_space=pltpu.SMEM)
    vmem = pl.BlockSpec(memory_space=pltpu.VMEM)
    hbm = [pl.BlockSpec(memory_space=pltpu.HBM)]
    return pl.pallas_call(
        kernel,
        out_shape=[jax.ShapeDtypeStruct(*value) for value in held_out + outputs],
        in_specs=[smem if value.ndim == 1 else vmem for value in inputs] + hbm * len(held_in),
        out_specs=hbm * len(held_out) + [vmem] * len(outputs),
        scratch_shapes=scratch,
        compiler_params=pltpu.CompilerParams(vmem_limit_bytes=52 * 2**20),
        cost_estimate=pl.CostEstimate(
            flops=int(micros * 1e9), bytes_accessed=4 * 2**20, transcendentals=0
        ),
        name=name,
    )(*inputs, *held_in)


class Sirt:
    def __init__(self, rank, theta, vol_list, slices, slots, rays, step_size):
        angles = theta.shape[0]
        patches = vol_list.shape[0]
        pairs = patches // 2
        both = 2 * slices
        chunk = math.gcd(angles, 32)
        self.held = angles == chunk
        self.sizes = (angles, chunk, self.held, slots, rays)
        self.rank = rank.reshape(1)
        self.step_size = step_size
        self.rays = rays
        self.patches = patches
        centre = (ROI - 1) / 2.0
        ids = np.arange(pairs)
        centre_x = (ids // PGRID * float(SIDE) + (SIDE - 1) / 2.0 - centre).astype(np.float32)
        centre_y = (ids % PGRID * float(SIDE) + (SIDE - 1) / 2.0 - centre).astype(np.float32)
        self.cosine = jnp.cos(theta)
        self.sine = jnp.sin(theta)
        along = (
            centre_x[:, None] * self.cosine[None, :]
            + centre_y[:, None] * self.sine[None, :]
            + 0.5
        )
        whole = jnp.floor(along)
        lead = WIN // 2 - 1
        place = along - whole + float(lead)
        offset = whole.astype(jnp.int32) + (ACTIVE // 2 - 1 - lead)
        tile = jnp.minimum(offset // SPLIT, 2)
        local = jnp.arange(angles, dtype=jnp.int32) % chunk * WIN
        turn = (local[None, :] - offset + tile * SPLIT) % LANES
        self.offset = offset.reshape(-1)
        self.place = place.reshape(-1)
        self.tile = tile.reshape(-1)
        self.turn = turn.reshape(-1)
        ids = jnp.arange(patches, dtype=jnp.int32)
        self.slot = jnp.sum(
            jnp.where(vol_list[None, :] == ids[:, None], ids[None, :], 0), axis=1
        )
        voxel = np.arange(VOX)
        shift_x = np.repeat((voxel // SIDE - (SIDE - 1) / 2.0)[None, :], ROWS, axis=0)
        shift_y = np.repeat((voxel % SIDE - (SIDE - 1) / 2.0)[None, :], ROWS, axis=0)
        flip = np.eye(ACTIVE)[::-1].astype(ml_dtypes.bfloat16)
        self.fixed = [jnp.asarray(flip), jnp.asarray(shift_x, f32), jnp.asarray(shift_y, f32)]
        self.held_weight = ((pairs, chunk * WIN, 2 * VOX), bf16)
        self.acc = ((angles, ACTIVE, LANES), f32)
        self.along = ((angles, ROWS, VOX), f32)
        self.by_ray = ((angles, slices, ACTIVE), f32)
        self.by_pair = ((pairs, both, VOX), f32)
        self.window = ((angles, 3, both, LANES), f32)
        self.half = ((2, rays, slices * slots, LANES), f32)
        self.mirror = ((max(pairs, angles), slices, ACTIVE), f32)
        self.sent = ((slices * (slots + angles // rays), ACTIVE), f32)

    def weight(self, count):
        shape, dtype = self.held_weight
        return pltpu.VMEM((count,) + shape[1:], dtype)

    def first(self, volumes):
        inputs = [self.rank, self.offset, self.place, self.slot, self.cosine, self.sine]
        shapes = (self.acc, self.along, self.mirror)
        results = call(
            functools.partial(first_kernel, self.sizes),
            "first",
            inputs + self.fixed + volumes,
            [],
            [self.held_weight] if self.held else [],
            [self.half, self.by_pair, self.by_ray, self.by_ray],
            [self.weight(2), self.weight(2), pltpu.SemaphoreType.DMA((2, 2))]
            + [pltpu.VMEM(*shape) for shape in shapes],
            16,
        )
        return (results[:1], results[1:]) if self.held else ([], results)

    def second(self, weight, half, start, predicted, gain, sino):
        inputs = [self.rank, self.offset, self.place, self.tile, self.turn, self.slot]
        inputs += [self.cosine, self.sine] + self.fixed
        inputs += [half, start, predicted, gain, sino]
        count = self.patches // 2 if self.held else 1
        shapes = (self.acc, self.along, self.by_ray, self.mirror, self.window)
        shapes += (self.by_pair, self.half)
        return call(
            functools.partial(second_kernel, self.sizes, self.step_size),
            "second",
            inputs,
            list(weight),
            [],
            [self.sent] * self.rays,
            [self.weight(count), pltpu.SemaphoreType.DMA((count,))]
            + [pltpu.VMEM(*shape) for shape in shapes],
            30,
        )


def gather_kernel(rank_ref, *refs):
    *part_refs, out_ref, sems = refs
    rank = rank_ref[0]
    copies = [
        pltpu.make_async_copy(part_ref, out_ref.at[rank ^ d], sems.at[d])
        for d, part_ref in enumerate(part_refs)
    ]
    for copy in copies:
        copy.start()
    for copy in copies:
        copy.wait()


def gather_parts(parts, rank):
    count = len(parts)
    return pl.pallas_call(
        gather_kernel,
        out_shape=jax.ShapeDtypeStruct((count,) + parts[0].shape, f32),
        in_specs=[pl.BlockSpec(memory_space=pltpu.SMEM)]
        + [pl.BlockSpec(memory_space=pltpu.VMEM)] * count,
        out_specs=pl.BlockSpec(memory_space=pl.ANY),
        scratch_shapes=[pltpu.SemaphoreType.DMA((count,))],
        cost_estimate=pl.CostEstimate(
            flops=0, bytes_accessed=8 * count * parts[0].size, transcendentals=0
        ),
        name="gather_parts",
    )(rank.reshape(1), *parts)


def finish_kernel(rank_ref, *refs):
    *got_refs, _, rec_ref, out_ref, values_ref, active_ref, sems = refs
    rank = rank_ref[0]
    rays = len(got_refs)
    slots = values_ref.shape[1]
    slabs = active_ref.shape[0]
    slices = values_ref.shape[0] // rays
    lead = slices * slots
    for d, got_ref in enumerate(got_refs):
        rows = pl.ds(pl.multiple_of((rank ^ d) * slices, slices), slices)
        values_ref[rows] = got_ref[0:lead, :].reshape(slices, slots, VOX)
        for k in range(slabs):
            begin = lead + k * slices
            active_ref[k, rows, :] = got_ref[begin : begin + slices, :]
    offset = (out_ref.shape[2] - ACTIVE) // 2
    copies = [
        pltpu.make_async_copy(values_ref, rec_ref, sems.at[0]),
        pltpu.make_async_copy(
            active_ref, out_ref.at[:, :, offset : offset + ACTIVE], sems.at[1]
        ),
    ]
    for copy in copies:
        copy.start()
    for copy in copies:
        copy.wait()


def finish(pieces, sinogram, rank, shape):
    slabs, slab_rows, _ = sinogram.shape
    any_space = pl.BlockSpec(memory_space=pl.ANY)
    return pl.pallas_call(
        finish_kernel,
        out_shape=(
            jax.ShapeDtypeStruct(shape, f32),
            jax.ShapeDtypeStruct(sinogram.shape, f32),
        ),
        in_specs=[pl.BlockSpec(memory_space=pltpu.SMEM)]
        + [pl.BlockSpec(memory_space=pltpu.VMEM)] * len(pieces)
        + [any_space],
        out_specs=[any_space, any_space],
        scratch_shapes=[
            pltpu.VMEM(shape, f32),
            pltpu.VMEM((slabs, slab_rows, ACTIVE), f32),
            pltpu.SemaphoreType.DMA((2,)),
        ],
        input_output_aliases={len(pieces) + 1: 1},
        cost_estimate=pl.CostEstimate(
            flops=0, bytes_accessed=8 * len(pieces) * pieces[0].size, transcendentals=0
        ),
        name="finish",
    )(rank.reshape(1), *pieces, sinogram)


def split_kernel(rank_ref, source_ref, *piece_refs):
    for d, piece_ref in enumerate(piece_refs):
        piece_ref[...] = source_ref[rank_ref[0] ^ d]


def split(values, rank):
    vmem = pl.BlockSpec(memory_space=pltpu.VMEM)
    count = values.shape[0]
    return pl.pallas_call(
        split_kernel,
        out_shape=[jax.ShapeDtypeStruct(values.shape[1:], f32)] * count,
        in_specs=[pl.BlockSpec(memory_space=pltpu.SMEM), vmem],
        out_specs=[vmem] * count,
        cost_estimate=pl.CostEstimate(
            flops=0, bytes_accessed=8 * values.size, transcendentals=0
        ),
        name="split",
    )(rank.reshape(1), values)


def exchange(pieces, axis):
    count = len(pieces)
    return [
        lax.ppermute(piece, axis, [(i, i ^ d) for i in range(count)]) if d else piece
        for d, piece in enumerate(pieces)
    ]


def local(intensity, angles, volume, vol_list):
    n_slab = lax.axis_size("slab")
    n_ray = lax.axis_size("ray")
    devices = n_slab * n_ray
    height, band = intensity.shape[2:]
    slices = height // devices
    slots = volume.shape[1]
    count = angles.shape[0] * angles.shape[1]
    step_size = relax * ROI / count
    rank = lax.axis_index("slab")
    ray_rank = lax.axis_index("ray")
    padded = -(-slices // ROWS) * ROWS

    volumes = exchange(split(volume.reshape(n_ray, slices * slots, VOX), ray_rank), "ray")
    *parts, active = paganin(intensity.reshape(height, band), rank, n_slab)
    active, volumes = lax.optimization_barrier((active, volumes))
    own_rays = lax.all_to_all(
        active.reshape(devices, slices, ACTIVE),
        ("slab", "ray"),
        split_axis=0,
        concat_axis=0,
        tiled=True,
    )
    if padded != slices:
        more = padded - slices
        volumes = [jnp.pad(value, ((0, more * slots), (0, 0))) for value in volumes]
        own_rays = jnp.pad(own_rays, ((0, 0), (0, more), (0, 0)))

    theta, vol_list, volumes, parts = lax.optimization_barrier(
        (angles.reshape(-1), vol_list, volumes, parts)
    )
    sirt = Sirt(ray_rank, theta, vol_list, padded, slots, n_ray, step_size)
    weight, (half, start, predicted, gain) = sirt.first(volumes)
    own_rays, parts, start = lax.optimization_barrier((own_rays, parts, start))
    parts = exchange(parts, "slab")
    pieces = sirt.second(weight, half, start, predicted, gain, own_rays)
    pieces, parts = lax.optimization_barrier((pieces, parts))
    if padded != slices:
        narrow = []
        for piece in pieces:
            lower = piece[padded * slots :].reshape(n_slab, padded, ACTIVE)[:, :slices]
            lower = lower.reshape(n_slab * slices, ACTIVE)
            narrow.append(jnp.concatenate([piece[: slices * slots], lower], axis=0))
        pieces = narrow
    pieces = exchange(pieces, "ray")
    sinogram = gather_parts(parts, rank)
    if padded == slices:
        reconstruction, residual = finish(pieces, sinogram, ray_rank, volume.shape)
    else:
        order = ray_rank ^ jnp.arange(n_ray, dtype=jnp.int32)
        pieces = jnp.take(jnp.stack(pieces), order, axis=0)
        reconstruction = pieces[:, : slices * slots].reshape(volume.shape)
        lower = pieces[:, slices * slots :].reshape(n_ray, n_slab, slices, ACTIVE)
        lower = jnp.transpose(lower, (1, 0, 2, 3)).reshape(n_slab, n_ray * slices, ACTIVE)
        begin = (band - ACTIVE) // 2
        residual = lax.dynamic_update_slice(sinogram, lower, (0, 0, begin))
    return (reconstruction, residual[:, None])


def solution(mesh):
    placed = (P("slab", "ray", None, None), P(), P("slab", "ray", None), P())
    return jax.shard_map(
        local,
        mesh=mesh,
        in_specs=placed,
        out_specs=(P("slab", "ray", None), P(None, "ray", "slab", None)),
        check_vma=False,
    )
```

```python
import functools
import math

import jax
import jax.numpy as jnp
import ml_dtypes
import numpy as np
from jax import lax
from jax.experimental import pallas as pl
from jax.experimental.pallas import tpu as pltpu
from jax.sharding import PartitionSpec as P

BAND = 2048
PGRID = 8
ROI = 128
SIDE = 16
VOX = SIDE * SIDE
WIN = 24
ACTIVE = 256
LANES = 128
ROWS = 8
SPLIT = 64
GROUP = 8
CYCLE = 4

paganin_strength = 10.0
relax = 1.8
row_floor = 0.25

bf16 = jnp.bfloat16
f32 = jnp.float32


def halves(values):
    high = values.astype(bf16)
    low = (values - high.astype(f32)).astype(bf16)
    return high, low


def thirds(values):
    high = values.astype(bf16)
    rest = values - high.astype(f32)
    middle = rest.astype(bf16)
    low = (rest - middle.astype(f32)).astype(bf16)
    return high, middle, low


def dot(left, right):
    return jnp.dot(left, right, preferred_element_type=f32)


def repeat(count, body, unroll):
    unroll = math.gcd(count, unroll)

    def several(index, carry):
        for step in range(unroll):
            body(index * unroll + step)
        return carry

    lax.fori_loop(0, count // unroll, several, 0)


def filter_tables(height):
    index = np.arange(height)
    phase = 2.0 * np.pi * (np.outer(index, index) % height) / height
    cas = (np.cos(phase) + np.sin(phase)) / math.sqrt(height)
    row_freq = 2.0 - 2.0 * np.cos(2.0 * np.pi * index / height)
    middle = (1.0 + paganin_strength * row_freq) / paganin_strength + 2.0
    rho = (middle - np.sqrt(middle * middle - 4.0)) / 2.0
    return np.concatenate([cas, np.repeat(rho[None, :], ROWS, axis=0)], axis=0).astype(np.float32)


def chunk_carry(ends, power, forward):
    shift = 1
    for _ in range(3):
        ends = ends + power * pltpu.roll(ends, shift if forward else ROWS - shift, 0)
        power = power * power
        shift *= 2
    return pltpu.roll(ends, 1 if forward else ROWS - 1, 0) / (1.0 - power)


def filter_kernel(rank_ref, source_ref, given_ref, *refs):
    *part_refs, active_ref, image_ref, table_ref, out_ref, spec_ref, up_ref, down_ref = refs[:-2]
    sems, out_sems = refs[-2:]
    height, width = image_ref.shape
    rank = rank_ref[0]
    share = height // len(part_refs)
    length = width // ROWS
    blocks = height // LANES
    unroll = 8
    copies = []
    for c in range(ROWS):
        columns = slice(c * length, (c + 1) * length)
        copies.append(
            pltpu.make_async_copy(
                source_ref.at[:, columns], image_ref.at[:, columns], sems.at[c]
            )
        )
    given = pltpu.make_async_copy(given_ref, table_ref, sems.at[ROWS])
    given.start()
    for copy in copies:
        copy.start()
    given.wait()
    cas_high, cas_low = halves(table_ref[0:height, :])
    rho_all = table_ref[height : height + ROWS, :]
    rhos = [rho_all[:, b * LANES : (b + 1) * LANES] for b in range(blocks)]
    zeros = [jnp.zeros((ROWS, LANES), f32)] * blocks

    def transform(values):
        high, low = halves(values)
        return dot(high, cas_high) + dot(low, cas_high) + dot(high, cas_low)

    for c in range(ROWS):
        copies[c].wait()
        image = 1.0 - image_ref[:, c * length : (c + 1) * length]
        spectrum = transform(jnp.transpose(image))
        for b in range(blocks):
            spec_ref[b, pl.ds(c, length, stride=ROWS), :] = spectrum[
                :, b * LANES : (b + 1) * LANES
            ]

    def rows(position):
        return pl.ds(pl.multiple_of(position * ROWS, ROWS), ROWS)

    def advance(position, ups, downs):
        ups = [spec_ref[b, rows(position), :] + rhos[b] * ups[b] for b in range(blocks)]
        back = length - 1 - position
        downs = [spec_ref[b, rows(back), :] + rhos[b] * downs[b] for b in range(blocks)]
        return ups, downs

    def sweep(index, carry):
        ups, downs = carry
        for step in range(unroll):
            ups, downs = advance(index * unroll + step, ups, downs)
        return ups, downs

    ups, downs = lax.fori_loop(0, length // unroll, sweep, (zeros, zeros))
    powers = list(rhos)
    for _ in range(int(math.log2(length))):
        powers = [power * power for power in powers]
    ups = [chunk_carry(ups[b], powers[b], True) for b in range(blocks)]
    downs = [chunk_carry(downs[b], powers[b], False) for b in range(blocks)]
    scales = [rho / (paganin_strength * (1.0 - rho * rho)) for rho in rhos]

    def outer(index, carry):
        ups, downs = carry
        for step in range(unroll):
            position = index * unroll + step
            ups, downs = advance(position, ups, downs)
            for b in range(blocks):
                up_ref[b, rows(position), :] = ups[b]
                down_ref[b, rows(position), :] = downs[b]
        return ups, downs

    def inner(index, carry):
        ups, downs = carry
        for step in range(unroll):
            position = index * unroll + step
            back = length - 1 - position
            ups, downs = advance(position, ups, downs)
            for b in range(blocks):
                here = ups[b] + down_ref[b, rows(back), :] - spec_ref[b, rows(position), :]
                there = downs[b] + up_ref[b, rows(back), :] - spec_ref[b, rows(back), :]
                up_ref[b, rows(position), :] = here * scales[b]
                up_ref[b, rows(back), :] = there * scales[b]
        return ups, downs

    half = length // 2 // unroll
    carry = lax.fori_loop(0, half, outer, (ups, downs))
    lax.fori_loop(half, 2 * half, inner, carry)

    offset = (width - ACTIVE) // 2
    sent = []
    for c in range(ROWS):
        spectrum = jnp.concatenate(
            [up_ref[b, pl.ds(c, length, stride=ROWS), :] for b in range(blocks)], axis=1
        )
        filtered = 1.0 - jnp.transpose(transform(spectrum))
        columns = slice(c * length, (c + 1) * length)
        out_ref[:, columns] = -jnp.log(filtered)
        for d, part_ref in enumerate(part_refs):
            rows = pl.ds(pl.multiple_of((rank ^ d) * share, share), share)
            sent.append(
                pltpu.make_async_copy(
                    out_ref.at[rows, columns], part_ref.at[:, columns], out_sems.at[c, d]
                )
            )
            sent[-1].start()
    active_ref[...] = out_ref[:, offset : offset + ACTIVE]
    for copy in sent:
        copy.wait()


def paganin(image, rank, parts):
    height, width = image.shape
    blocks = height // LANES
    return pl.pallas_call(
        filter_kernel,
        out_shape=[jax.ShapeDtypeStruct((height // parts, width), f32)] * parts
        + [jax.ShapeDtypeStruct((height, ACTIVE), f32)],
        in_specs=[pl.BlockSpec(memory_space=pltpu.SMEM)]
        + [pl.BlockSpec(memory_space=pltpu.HBM)] * 2,
        out_specs=[pl.BlockSpec(memory_space=pltpu.HBM)] * parts
        + [pl.BlockSpec(memory_space=pltpu.VMEM)],
        scratch_shapes=[
            pltpu.VMEM((height, width), f32),
            pltpu.VMEM((height + ROWS, height), f32),
            pltpu.VMEM((height, width), f32),
            pltpu.VMEM((blocks, width, LANES), f32),
            pltpu.VMEM((blocks, width, LANES), f32),
            pltpu.VMEM((blocks, width // 2, LANES), f32),
            pltpu.SemaphoreType.DMA((ROWS + 1,)),
            pltpu.SemaphoreType.DMA((ROWS, parts)),
        ],
        compiler_params=pltpu.CompilerParams(vmem_limit_bytes=58 * 2**20),
        cost_estimate=pl.CostEstimate(
            flops=64 * height * height * width,
            bytes_accessed=8 * height * width,
            transcendentals=height * width,
        ),
        name="paganin",
    )(rank.reshape(1), image, jnp.asarray(filter_tables(height)))


def reversed_exact(values, flip):
    return sum(dot(part, flip) for part in thirds(values))


class Weights:
    def __init__(self, along_ref, place_ref, angles, chunk):
        self.along_ref = along_ref
        self.place_ref = place_ref
        self.angles = angles
        self.chunk = chunk
        self.ray = lax.broadcasted_iota(jnp.int32, (ROWS, VOX), 0).astype(f32)

    def prepare(self, shift_x_ref, shift_y_ref, cos_ref, sin_ref):
        def along_angle(t):
            self.along_ref[t] = shift_x_ref[...] * cos_ref[t] + shift_y_ref[...] * sin_ref[t]

        repeat(self.angles, along_angle, 8)

    def make(self, q, c, ref):
        for two in range(self.chunk // 2):
            pieces = []
            for t in (2 * two, 2 * two + 1):
                angle = c * self.chunk + t
                along = self.along_ref[angle] + self.place_ref[q * self.angles + angle]
                base = self.ray - along
                for group in range(WIN // ROWS):
                    distance = base + float(group * ROWS)
                    pieces.append(jnp.maximum(0.0, 1.0 - jnp.abs(distance)))
            high, low = halves(jnp.concatenate(pieces, axis=0))
            ref[2 * two * WIN : (2 * two + 2) * WIN, 0:VOX] = high
            ref[2 * two * WIN : (2 * two + 2) * WIN, VOX : 2 * VOX] = low


def ray_operand(values, sums_too):
    high, low = halves(values)
    both = values.shape[0]
    rows = [
        jnp.concatenate([high, high], axis=1),
        jnp.concatenate([low, jnp.zeros_like(low)], axis=1),
    ]
    if sums_too:
        rows.append(jnp.ones((both, 2 * VOX), bf16))
    rows.append(jnp.zeros((LANES - len(rows) * both, 2 * VOX), bf16))
    return jnp.concatenate(rows, axis=0)


def project_pair(held, operand, q, c, sizes, offset_ref, acc_ref):
    angles, chunk = sizes[:2]
    sums = lax.dot_general(
        held, operand, (((1,), (1,)), ((), ())), preferred_element_type=f32
    )
    for begin in range(0, chunk, GROUP):
        places = []
        for t in range(begin, min(begin + GROUP, chunk)):
            angle = c * chunk + t
            rows = pl.ds(offset_ref[q * angles + angle], WIN)
            values = acc_ref[angle, rows, :] + sums[t * WIN : (t + 1) * WIN, :]
            places.append((angle, rows, values))
        for angle, rows, values in places:
            acc_ref[angle, rows, :] = values


def spread_rays(acc_ref, direct_ref, mirror_ref, total_ref, slices):
    both = 2 * slices

    def spread(t):
        rows = jnp.transpose(acc_ref[t]) * (1.0 / ROI)
        direct_ref[t] = rows[0:slices] + rows[both : both + slices]
        mirror_ref[t] = rows[slices:both] + rows[both + slices : 2 * both]
        if total_ref is not None:
            total_ref[t] = rows[2 * both : 2 * both + slices]

    repeat(acc_ref.shape[0], spread, 8)


def turn_rays(values, flip):
    shape = values.shape
    return reversed_exact(values.reshape(-1, shape[-1]), flip).reshape(shape)


def fill_windows(weighted, flip, window_ref):
    angles, slices, _ = weighted.shape
    high, low = halves(weighted.reshape(angles * slices, ACTIVE))
    mirrored = (dot(high, flip) + dot(low, flip)).reshape(weighted.shape)
    lane = lax.broadcasted_iota(jnp.int32, (angles, slices, LANES), 2)
    for part, source in enumerate((weighted, mirrored)):
        rows = slice(part * slices, (part + 1) * slices)
        left = source[:, :, 0:LANES]
        right = source[:, :, LANES : 2 * LANES]
        window_ref[:, 0, rows, :] = left
        window_ref[:, 2, rows, :] = right
        mixed = jnp.where(lane >= SPLIT, left, right)
        window_ref[:, 1, rows, :] = pltpu.roll(mixed, SPLIT, 2)


def update_pair(held, q, c, sizes, window_ref, tile_ref, turn_ref):
    angles, chunk = sizes[:2]
    both = window_ref.shape[2]
    lane_rows = lax.broadcasted_iota(jnp.int32, (both, LANES), 1)
    tiles = [None] * (-(-chunk * WIN // LANES))
    for t in range(chunk):
        index = q * angles + c * chunk + t
        piece = pltpu.roll(window_ref[c * chunk + t, tile_ref[index]], turn_ref[index], 1)
        begin = t * WIN
        for place in range(begin // LANES, (begin + WIN - 1) // LANES + 1):
            if tiles[place] is None:
                tiles[place] = piece
            else:
                tiles[place] = jnp.where(
                    lane_rows >= begin - place * LANES, piece, tiles[place]
                )
    high, low = halves(jnp.concatenate(tiles, axis=1))
    sums = dot(jnp.concatenate([high, low], axis=0), held)
    return sums[0:both, 0:VOX] + sums[both:, 0:VOX] + sums[0:both, VOX:]


def first_kernel(
    sizes,
    offset_ref,
    place_ref,
    slot_ref,
    cos_ref,
    sin_ref,
    vol_ref,
    flip_ref,
    shift_x_ref,
    shift_y_ref,
    start_ref,
    predicted_ref,
    gain_ref,
    even_ref,
    odd_ref,
    acc_ref,
    along_ref,
    half_ref,
    mirror_ref,
):
    angles, chunk, slots = sizes
    patches = slot_ref.shape[0]
    pairs, both, _ = start_ref.shape
    slices = both // 2
    flip = flip_ref[...]

    def slot_values(patch):
        slot = slot_ref[patch]
        rows = pl.ds(slot % slots, slices, stride=slots)
        return jnp.concatenate(
            [half_ref[part, slot // slots, rows, :] for part in range(2)], axis=1
        )

    for part in range(2):
        half_ref[part] = vol_ref[:, :, part * LANES : (part + 1) * LANES]

    def order(q):
        start_ref[q, 0:slices, :] = slot_values(q)
        mirror_ref[q] = slot_values(patches - 1 - q)

    repeat(pairs, order, 8)
    start_ref[:, slices:both, :] = turn_rays(mirror_ref[0:pairs], flip)
    weights = Weights(along_ref, place_ref, angles, chunk)
    weights.prepare(shift_x_ref, shift_y_ref, cos_ref, sin_ref)
    acc_ref[...] = jnp.zeros(acc_ref.shape, f32)

    def two(index, carry):
        q = 2 * index
        for c in range(angles // chunk):
            weights.make(q, c, even_ref)
            operand = ray_operand(start_ref[q], True)
            project_pair(even_ref[...], operand, q, c, sizes, offset_ref, acc_ref)
            weights.make(q + 1, c, odd_ref)
            operand = ray_operand(start_ref[q + 1], True)
            project_pair(odd_ref[...], operand, q + 1, c, sizes, offset_ref, acc_ref)
        return carry

    lax.fori_loop(0, pairs // 2, two, 0)
    spread_rays(acc_ref, predicted_ref, mirror_ref, gain_ref, slices)
    predicted_ref[...] = predicted_ref[...] + turn_rays(mirror_ref[0:angles], flip)
    direct = gain_ref[...]
    gain_ref[...] = 1.0 / jnp.maximum(direct + turn_rays(direct, flip), row_floor)


def second_kernel(
    sizes,
    step_size,
    offset_ref,
    place_ref,
    tile_ref,
    turn_ref,
    slot_ref,
    cos_ref,
    sin_ref,
    vol_ref,
    start_ref,
    predicted_ref,
    gain_ref,
    sino_ref,
    flip_ref,
    shift_x_ref,
    shift_y_ref,
    out_ref,
    *refs,
):
    angles, chunk, slots = sizes
    held_refs = refs[:CYCLE]
    acc_ref, along_ref, direct_ref, mirror_ref, window_ref, update_ref, half_ref = refs[CYCLE:]
    patches = slot_ref.shape[0]
    pairs, both, _ = start_ref.shape
    slices = both // 2
    rays = out_ref.shape[0]
    flip = flip_ref[...]
    weights = Weights(along_ref, place_ref, angles, chunk)
    weights.prepare(shift_x_ref, shift_y_ref, cos_ref, sin_ref)
    chunks = angles // chunk
    windows = (sizes, window_ref, tile_ref, turn_ref)
    fill_windows(
        (sino_ref[...] - predicted_ref[...]) * gain_ref[...] * (1.0 / ROI), flip, window_ref
    )
    acc_ref[...] = jnp.zeros(acc_ref.shape, f32)

    def advance(q, held):
        total = update_pair(held, q, 0, *windows)
        update_ref[q] = total
        return start_ref[q] + step_size * total

    def forward(values, q, held):
        project_pair(held, ray_operand(values, False), q, 0, sizes, offset_ref, acc_ref)

    def cycle(index, values):
        for step in range(CYCLE):
            q = index * CYCLE + step
            after = (step + 1) % CYCLE
            before = (step - 1) % CYCLE
            later = index + (step + 1) // CYCLE
            earlier = index if step else jnp.maximum(index - 1, 0)
            weights.make(jnp.minimum(q + 1, pairs - 1), 0, held_refs[after].at[later])
            new_values = advance(q, held_refs[step][index])
            forward(values, jnp.maximum(q - 1, 0), held_refs[before][earlier])
            values = new_values
        return values

    def all_chunks(q, body):
        for c in range(chunks):
            weights.make(q, c, held_refs[0].at[0])
            body(c, held_refs[0][0])

    def plain_update(q, carry):
        update_ref[q] = jnp.zeros(update_ref.shape[1:], f32)

        def add(c, held):
            update_ref[q] = update_ref[q] + update_pair(held, q, c, *windows)

        all_chunks(q, add)
        return carry

    def plain_forward(q, carry):
        operand = ray_operand(start_ref[q] + step_size * update_ref[q], False)
        all_chunks(
            q,
            lambda c, held: project_pair(held, operand, q, c, sizes, offset_ref, acc_ref),
        )
        return carry

    if chunks == 1:
        held_refs[CYCLE - 1][0] = jnp.zeros(held_refs[CYCLE - 1].shape[1:], bf16)
        weights.make(0, 0, held_refs[0].at[0])
        values = lax.fori_loop(0, pairs // CYCLE, cycle, jnp.zeros((both, VOX), f32))
        forward(values, pairs - 1, held_refs[CYCLE - 1][pairs // CYCLE - 1])
    else:
        lax.fori_loop(0, pairs, plain_update, 0)
        lax.fori_loop(0, pairs, plain_forward, 0)

    spread_rays(acc_ref, direct_ref, mirror_ref, None, slices)
    turned = turn_rays(mirror_ref[0:angles], flip)
    direct_ref[...] = sino_ref[...] - direct_ref[...] - turned
    fill_windows(direct_ref[...] * gain_ref[...] * (1.0 / ROI), flip, window_ref)

    def last_cycle(index, carry):
        for step in range(CYCLE):
            q = index * CYCLE + step
            total = update_pair(held_refs[step][index], q, 0, *windows)
            update_ref[q] = (update_ref[q] + total) * step_size
        return carry

    def plain_last(q, carry):
        def add(c, held):
            update_ref[q] = update_ref[q] + update_pair(held, q, c, *windows)

        all_chunks(q, add)
        update_ref[q] = update_ref[q] * step_size
        return carry

    if chunks == 1:
        lax.fori_loop(0, pairs // CYCLE, last_cycle, 0)
    else:
        lax.fori_loop(0, pairs, plain_last, 0)

    mirror_ref[0:pairs] = turn_rays(update_ref[:, slices:both, :], flip)
    for part in range(2):
        half_ref[part] = vol_ref[:, :, part * LANES : (part + 1) * LANES]

    def finish(q):
        for patch, update in (
            (q, update_ref[q, 0:slices, :]),
            (patches - 1 - q, mirror_ref[q]),
        ):
            slot = slot_ref[patch]
            rows = pl.ds(slot % slots, slices, stride=slots)
            for part in range(2):
                half_ref[part, slot // slots, rows, :] = (
                    half_ref[part, slot // slots, rows, :]
                    + update[:, part * LANES : (part + 1) * LANES]
                )

    repeat(pairs, finish, 8)
    lead = slices * slots
    for part in range(2):
        out_ref[:, 0:lead, part * LANES : (part + 1) * LANES] = half_ref[part]
    for t in range(angles):
        begin = lead + t // rays * slices
        out_ref[t % rays, begin : begin + slices, :] = direct_ref[t]


def call(kernel, name, inputs, outputs, scratch, micros):
    smem = pl.BlockSpec(memory_space=pltpu.SMEM)
    vmem = pl.BlockSpec(memory_space=pltpu.VMEM)
    return pl.pallas_call(
        kernel,
        out_shape=[jax.ShapeDtypeStruct(*value) for value in outputs],
        in_specs=[smem if value.ndim == 1 else vmem for value in inputs],
        out_specs=[vmem] * len(outputs),
        scratch_shapes=[pltpu.VMEM(*value) for value in scratch],
        compiler_params=pltpu.CompilerParams(vmem_limit_bytes=52 * 2**20),
        cost_estimate=pl.CostEstimate(
            flops=int(micros * 1e9), bytes_accessed=4 * 2**20, transcendentals=0
        ),
        name=name,
    )(*inputs)


class Sirt:
    def __init__(self, theta, vol_list, slices, slots, rays, step_size):
        angles = theta.shape[0]
        patches = vol_list.shape[0]
        pairs = patches // 2
        both = 2 * slices
        chunk = math.gcd(angles, 32)
        self.sizes = (angles, chunk, slots)
        self.step_size = step_size
        self.rays = rays
        self.patches = patches
        centre = (ROI - 1) / 2.0
        ids = np.arange(pairs)
        centre_x = (ids // PGRID * float(SIDE) + (SIDE - 1) / 2.0 - centre).astype(np.float32)
        centre_y = (ids % PGRID * float(SIDE) + (SIDE - 1) / 2.0 - centre).astype(np.float32)
        self.cosine = jnp.cos(theta)
        self.sine = jnp.sin(theta)
        along = (
            centre_x[:, None] * self.cosine[None, :]
            + centre_y[:, None] * self.sine[None, :]
            + 0.5
        )
        whole = jnp.floor(along)
        lead = WIN // 2 - 1
        place = along - whole + float(lead)
        offset = whole.astype(jnp.int32) + (ACTIVE // 2 - 1 - lead)
        tile = jnp.minimum(offset // SPLIT, 2)
        local = jnp.arange(angles, dtype=jnp.int32) % chunk * WIN
        turn = (local[None, :] - offset + tile * SPLIT) % LANES
        self.offset = offset.reshape(-1)
        self.place = place.reshape(-1)
        self.tile = tile.reshape(-1)
        self.turn = turn.reshape(-1)
        ids = jnp.arange(patches, dtype=jnp.int32)
        self.slot = jnp.sum(
            jnp.where(vol_list[None, :] == ids[:, None], ids[None, :], 0), axis=1
        )
        voxel = np.arange(VOX)
        shift_x = np.repeat((voxel // SIDE - (SIDE - 1) / 2.0)[None, :], ROWS, axis=0)
        shift_y = np.repeat((voxel % SIDE - (SIDE - 1) / 2.0)[None, :], ROWS, axis=0)
        flip = np.eye(ACTIVE)[::-1].astype(ml_dtypes.bfloat16)
        self.fixed = [jnp.asarray(flip), jnp.asarray(shift_x, f32), jnp.asarray(shift_y, f32)]
        self.weight = ((chunk * WIN, 2 * VOX), bf16)
        self.held = (pairs // CYCLE + 1 if angles == chunk else 1,) + self.weight[0]
        self.acc = ((angles, ACTIVE, LANES), f32)
        self.along = ((angles, ROWS, VOX), f32)
        self.by_ray = ((angles, slices, ACTIVE), f32)
        self.by_pair = ((pairs, both, VOX), f32)
        self.window = ((angles, 3, both, LANES), f32)
        self.half = ((2, rays, slices * slots, LANES), f32)
        self.mirror = ((max(pairs, angles), slices, ACTIVE), f32)
        self.sent = ((rays, slices * (slots + angles // rays), ACTIVE), f32)

    def first(self, volume):
        inputs = [self.offset, self.place, self.slot, self.cosine, self.sine, volume]
        return call(
            functools.partial(first_kernel, self.sizes),
            "first",
            inputs + self.fixed,
            [self.by_pair, self.by_ray, self.by_ray],
            [self.weight, self.weight, self.acc, self.along, self.half, self.mirror],
            14,
        )

    def second(self, volume, start, predicted, gain, sino):
        inputs = [self.offset, self.place, self.tile, self.turn, self.slot]
        inputs += [self.cosine, self.sine, volume, start, predicted, gain, sino]
        scratch = [(self.held, bf16)] * CYCLE
        scratch += [self.acc, self.along, self.by_ray, self.mirror, self.window]
        return call(
            functools.partial(second_kernel, self.sizes, self.step_size),
            "second",
            inputs + self.fixed,
            [self.sent],
            scratch + [self.by_pair, self.half],
            26,
        )[0]


def gather_kernel(rank_ref, *refs):
    *part_refs, out_ref, sems = refs
    rank = rank_ref[0]
    copies = [
        pltpu.make_async_copy(part_ref, out_ref.at[rank ^ d], sems.at[d])
        for d, part_ref in enumerate(part_refs)
    ]
    for copy in copies:
        copy.start()
    for copy in copies:
        copy.wait()


def gather_parts(parts, rank):
    count = len(parts)
    return pl.pallas_call(
        gather_kernel,
        out_shape=jax.ShapeDtypeStruct((count,) + parts[0].shape, f32),
        in_specs=[pl.BlockSpec(memory_space=pltpu.SMEM)]
        + [pl.BlockSpec(memory_space=pltpu.VMEM)] * count,
        out_specs=pl.BlockSpec(memory_space=pl.ANY),
        scratch_shapes=[pltpu.SemaphoreType.DMA((count,))],
        cost_estimate=pl.CostEstimate(
            flops=0, bytes_accessed=8 * count * parts[0].size, transcendentals=0
        ),
        name="gather_parts",
    )(rank.reshape(1), *parts)


def finish_kernel(got_ref, _, rec_ref, out_ref, values_ref, active_ref, sems):
    rays = got_ref.shape[0]
    slots = values_ref.shape[1]
    slabs = active_ref.shape[0]
    slices = values_ref.shape[0] // rays
    lead = slices * slots
    for ray in range(rays):
        rows = slice(ray * slices, (ray + 1) * slices)
        values_ref[rows] = got_ref[ray, 0:lead, :].reshape(slices, slots, VOX)
        for k in range(slabs):
            begin = lead + k * slices
            active_ref[k, rows, :] = got_ref[ray, begin : begin + slices, :]
    offset = (out_ref.shape[2] - ACTIVE) // 2
    copies = [
        pltpu.make_async_copy(values_ref, rec_ref, sems.at[0]),
        pltpu.make_async_copy(
            active_ref, out_ref.at[:, :, offset : offset + ACTIVE], sems.at[1]
        ),
    ]
    for copy in copies:
        copy.start()
    for copy in copies:
        copy.wait()


def finish(got, sinogram, shape):
    slabs, slab_rows, _ = sinogram.shape
    any_space = pl.BlockSpec(memory_space=pl.ANY)
    return pl.pallas_call(
        finish_kernel,
        out_shape=(
            jax.ShapeDtypeStruct(shape, f32),
            jax.ShapeDtypeStruct(sinogram.shape, f32),
        ),
        in_specs=[pl.BlockSpec(memory_space=pltpu.VMEM), any_space],
        out_specs=[any_space, any_space],
        scratch_shapes=[
            pltpu.VMEM(shape, f32),
            pltpu.VMEM((slabs, slab_rows, ACTIVE), f32),
            pltpu.SemaphoreType.DMA((2,)),
        ],
        input_output_aliases={1: 1},
        cost_estimate=pl.CostEstimate(
            flops=0, bytes_accessed=8 * got.size, transcendentals=0
        ),
        name="finish",
    )(got, sinogram)


def local(intensity, angles, volume, vol_list):
    n_slab = lax.axis_size("slab")
    n_ray = lax.axis_size("ray")
    devices = n_slab * n_ray
    height, band = intensity.shape[2:]
    slices = height // devices
    slots = volume.shape[1]
    count = angles.shape[0] * angles.shape[1]
    step_size = relax * ROI / count
    rank = lax.axis_index("slab")
    padded = -(-slices // ROWS) * ROWS

    def to_all(values, axes):
        return lax.all_to_all(values, axes, split_axis=0, concat_axis=0, tiled=True)

    own_volume = to_all(volume.reshape(n_ray, slices * slots, VOX), "ray")
    *parts, active = paganin(intensity.reshape(height, band), rank, n_slab)
    active, own_volume = lax.optimization_barrier((active, own_volume))
    own_rays = to_all(active.reshape(devices, slices, ACTIVE), ("slab", "ray"))
    if padded != slices:
        more = padded - slices
        own_volume = jnp.pad(own_volume, ((0, 0), (0, more * slots), (0, 0)))
        own_rays = jnp.pad(own_rays, ((0, 0), (0, more), (0, 0)))

    theta, vol_list, own_volume, parts = lax.optimization_barrier(
        (angles.reshape(-1), vol_list, own_volume, parts)
    )
    sirt = Sirt(theta, vol_list, padded, slots, n_ray, step_size)
    start, predicted, gain = sirt.first(own_volume)
    own_rays, parts, start = lax.optimization_barrier((own_rays, parts, start))
    parts = [
        lax.ppermute(part, "slab", [(i, i ^ d) for i in range(n_slab)]) if d else part
        for d, part in enumerate(parts)
    ]
    result = sirt.second(own_volume, start, predicted, gain, own_rays)
    result, parts = lax.optimization_barrier((result, parts))
    if padded != slices:
        lower = result[:, padded * slots :].reshape(n_ray, n_slab, padded, ACTIVE)
        lower = lower[:, :, :slices].reshape(n_ray, n_slab * slices, ACTIVE)
        result = jnp.concatenate([result[:, : slices * slots], lower], axis=1)
    got = to_all(result, "ray")
    sinogram = gather_parts(parts, rank)
    reconstruction, residual = finish(got, sinogram, volume.shape)
    return (reconstruction, residual[:, None])


def solution(mesh):
    placed = (P("slab", "ray", None, None), P(), P("slab", "ray", None), P())
    return jax.shard_map(
        local,
        mesh=mesh,
        in_specs=placed,
        out_specs=(P("slab", "ray", None), P(None, "ray", "slab", None)),
        check_vma=False,
    )
```

```python
import functools
import math

import jax
import jax.numpy as jnp
import ml_dtypes
import numpy as np
from jax import lax
from jax.experimental import pallas as pl
from jax.experimental.pallas import tpu as pltpu
from jax.sharding import PartitionSpec as P

BAND = 2048
PGRID = 8
ROI = 128
SIDE = 16
VOX = SIDE * SIDE
WIN = 24
ACTIVE = 256
LANES = 128
ROWS = 8
SPLIT = 64
GROUP = 8
CYCLE = 4

paganin_strength = 10.0
relax = 1.8
row_floor = 0.25

bf16 = jnp.bfloat16
f32 = jnp.float32


def halves(values):
    high = values.astype(bf16)
    low = (values - high.astype(f32)).astype(bf16)
    return high, low


def thirds(values):
    high = values.astype(bf16)
    rest = values - high.astype(f32)
    middle = rest.astype(bf16)
    low = (rest - middle.astype(f32)).astype(bf16)
    return high, middle, low


def dot(left, right):
    return jnp.dot(left, right, preferred_element_type=f32)


def repeat(count, body, unroll):
    unroll = math.gcd(count, unroll)

    def several(index, carry):
        for step in range(unroll):
            body(index * unroll + step)
        return carry

    lax.fori_loop(0, count // unroll, several, 0)


def filter_tables(height):
    index = np.arange(height)
    phase = 2.0 * np.pi * (np.outer(index, index) % height) / height
    cas = (np.cos(phase) + np.sin(phase)) / math.sqrt(height)
    row_freq = 2.0 - 2.0 * np.cos(2.0 * np.pi * index / height)
    middle = (1.0 + paganin_strength * row_freq) / paganin_strength + 2.0
    rho = (middle - np.sqrt(middle * middle - 4.0)) / 2.0
    return np.concatenate([cas, np.repeat(rho[None, :], ROWS, axis=0)], axis=0).astype(np.float32)


def chunk_carry(ends, power, forward):
    shift = 1
    for _ in range(3):
        ends = ends + power * pltpu.roll(ends, shift if forward else ROWS - shift, 0)
        power = power * power
        shift *= 2
    return pltpu.roll(ends, 1 if forward else ROWS - 1, 0) / (1.0 - power)


def filter_kernel(rank_ref, source_ref, given_ref, *refs):
    *part_refs, active_ref, image_ref, table_ref, out_ref, spec_ref, up_ref, down_ref = refs[:-2]
    sems, out_sems = refs[-2:]
    height, width = image_ref.shape
    rank = rank_ref[0]
    share = height // len(part_refs)
    length = width // ROWS
    blocks = height // LANES
    unroll = 8
    copies = []
    for c in range(ROWS):
        columns = slice(c * length, (c + 1) * length)
        copies.append(
            pltpu.make_async_copy(
                source_ref.at[:, columns], image_ref.at[:, columns], sems.at[c]
            )
        )
    given = pltpu.make_async_copy(given_ref, table_ref, sems.at[ROWS])
    given.start()
    for copy in copies:
        copy.start()
    given.wait()
    cas_high, cas_low = halves(table_ref[0:height, :])
    rho_all = table_ref[height : height + ROWS, :]
    rhos = [rho_all[:, b * LANES : (b + 1) * LANES] for b in range(blocks)]
    zeros = [jnp.zeros((ROWS, LANES), f32)] * blocks

    def transform(values):
        high, low = halves(values)
        return dot(high, cas_high) + dot(low, cas_high) + dot(high, cas_low)

    for c in range(ROWS):
        copies[c].wait()
        image = 1.0 - image_ref[:, c * length : (c + 1) * length]
        spectrum = transform(jnp.transpose(image))
        for b in range(blocks):
            spec_ref[b, pl.ds(c, length, stride=ROWS), :] = spectrum[
                :, b * LANES : (b + 1) * LANES
            ]

    def rows(position):
        return pl.ds(pl.multiple_of(position * ROWS, ROWS), ROWS)

    def advance(position, ups, downs):
        ups = [spec_ref[b, rows(position), :] + rhos[b] * ups[b] for b in range(blocks)]
        back = length - 1 - position
        downs = [spec_ref[b, rows(back), :] + rhos[b] * downs[b] for b in range(blocks)]
        return ups, downs

    def sweep(index, carry):
        ups, downs = carry
        for step in range(unroll):
            ups, downs = advance(index * unroll + step, ups, downs)
        return ups, downs

    ups, downs = lax.fori_loop(0, length // unroll, sweep, (zeros, zeros))
    powers = list(rhos)
    for _ in range(int(math.log2(length))):
        powers = [power * power for power in powers]
    ups = [chunk_carry(ups[b], powers[b], True) for b in range(blocks)]
    downs = [chunk_carry(downs[b], powers[b], False) for b in range(blocks)]
    scales = [rho / (paganin_strength * (1.0 - rho * rho)) for rho in rhos]

    def outer(index, carry):
        ups, downs = carry
        for step in range(unroll):
            position = index * unroll + step
            ups, downs = advance(position, ups, downs)
            for b in range(blocks):
                up_ref[b, rows(position), :] = ups[b]
                down_ref[b, rows(position), :] = downs[b]
        return ups, downs

    def inner(index, carry):
        ups, downs = carry
        for step in range(unroll):
            position = index * unroll + step
            back = length - 1 - position
            ups, downs = advance(position, ups, downs)
            for b in range(blocks):
                here = ups[b] + down_ref[b, rows(back), :] - spec_ref[b, rows(position), :]
                there = downs[b] + up_ref[b, rows(back), :] - spec_ref[b, rows(back), :]
                up_ref[b, rows(position), :] = here * scales[b]
                up_ref[b, rows(back), :] = there * scales[b]
        return ups, downs

    half = length // 2 // unroll
    carry = lax.fori_loop(0, half, outer, (ups, downs))
    lax.fori_loop(half, 2 * half, inner, carry)

    offset = (width - ACTIVE) // 2
    sent = []
    for c in range(ROWS):
        spectrum = jnp.concatenate(
            [up_ref[b, pl.ds(c, length, stride=ROWS), :] for b in range(blocks)], axis=1
        )
        filtered = 1.0 - jnp.transpose(transform(spectrum))
        columns = slice(c * length, (c + 1) * length)
        out_ref[:, columns] = -jnp.log(filtered)
        for d, part_ref in enumerate(part_refs):
            rows = pl.ds(pl.multiple_of((rank ^ d) * share, share), share)
            sent.append(
                pltpu.make_async_copy(
                    out_ref.at[rows, columns], part_ref.at[:, columns], out_sems.at[c, d]
                )
            )
            sent[-1].start()
    active_ref[...] = out_ref[:, offset : offset + ACTIVE]
    for copy in sent:
        copy.wait()


def paganin(image, rank, parts):
    height, width = image.shape
    blocks = height // LANES
    return pl.pallas_call(
        filter_kernel,
        out_shape=[jax.ShapeDtypeStruct((height // parts, width), f32)] * parts
        + [jax.ShapeDtypeStruct((height, ACTIVE), f32)],
        in_specs=[pl.BlockSpec(memory_space=pltpu.SMEM)]
        + [pl.BlockSpec(memory_space=pltpu.HBM)] * 2,
        out_specs=[pl.BlockSpec(memory_space=pltpu.HBM)] * parts
        + [pl.BlockSpec(memory_space=pltpu.VMEM)],
        scratch_shapes=[
            pltpu.VMEM((height, width), f32),
            pltpu.VMEM((height + ROWS, height), f32),
            pltpu.VMEM((height, width), f32),
            pltpu.VMEM((blocks, width, LANES), f32),
            pltpu.VMEM((blocks, width, LANES), f32),
            pltpu.VMEM((blocks, width // 2, LANES), f32),
            pltpu.SemaphoreType.DMA((ROWS + 1,)),
            pltpu.SemaphoreType.DMA((ROWS, parts)),
        ],
        compiler_params=pltpu.CompilerParams(vmem_limit_bytes=58 * 2**20),
        cost_estimate=pl.CostEstimate(
            flops=64 * height * height * width,
            bytes_accessed=8 * height * width,
            transcendentals=height * width,
        ),
        name="paganin",
    )(rank.reshape(1), image, jnp.asarray(filter_tables(height)))


def reversed_exact(values, flip):
    return sum(dot(part, flip) for part in thirds(values))


class Weights:
    def __init__(self, along_ref, place_ref, angles, chunk):
        self.along_ref = along_ref
        self.place_ref = place_ref
        self.angles = angles
        self.chunk = chunk
        self.ray = lax.broadcasted_iota(jnp.int32, (ROWS, VOX), 0).astype(f32)

    def prepare(self, shift_x_ref, shift_y_ref, cos_ref, sin_ref):
        def along_angle(t):
            self.along_ref[t] = shift_x_ref[...] * cos_ref[t] + shift_y_ref[...] * sin_ref[t]

        repeat(self.angles, along_angle, 8)

    def make(self, q, c, ref):
        for two in range(self.chunk // 2):
            pieces = []
            for t in (2 * two, 2 * two + 1):
                angle = c * self.chunk + t
                along = self.along_ref[angle] + self.place_ref[q * self.angles + angle]
                base = self.ray - along
                for group in range(WIN // ROWS):
                    distance = base + float(group * ROWS)
                    pieces.append(jnp.maximum(0.0, 1.0 - jnp.abs(distance)))
            high, low = halves(jnp.concatenate(pieces, axis=0))
            ref[2 * two * WIN : (2 * two + 2) * WIN, 0:VOX] = high
            ref[2 * two * WIN : (2 * two + 2) * WIN, VOX : 2 * VOX] = low


def ray_operand(values, sums_too):
    high, low = halves(values)
    both = values.shape[0]
    rows = [
        jnp.concatenate([high, high], axis=1),
        jnp.concatenate([low, jnp.zeros_like(low)], axis=1),
    ]
    if sums_too:
        rows.append(jnp.ones((both, 2 * VOX), bf16))
    rows.append(jnp.zeros((LANES - len(rows) * both, 2 * VOX), bf16))
    return jnp.concatenate(rows, axis=0)


def project_pair(held, operand, q, c, sizes, offset_ref, acc_ref):
    angles, chunk = sizes[:2]
    sums = lax.dot_general(
        held, operand, (((1,), (1,)), ((), ())), preferred_element_type=f32
    )
    for begin in range(0, chunk, GROUP):
        places = []
        for t in range(begin, min(begin + GROUP, chunk)):
            angle = c * chunk + t
            rows = pl.ds(offset_ref[q * angles + angle], WIN)
            values = acc_ref[angle, rows, :] + sums[t * WIN : (t + 1) * WIN, :]
            places.append((angle, rows, values))
        for angle, rows, values in places:
            acc_ref[angle, rows, :] = values


def spread_rays(acc_ref, direct_ref, mirror_ref, total_ref, slices):
    both = 2 * slices

    def spread(t):
        rows = jnp.transpose(acc_ref[t]) * (1.0 / ROI)
        direct_ref[t] = rows[0:slices] + rows[both : both + slices]
        mirror_ref[t] = rows[slices:both] + rows[both + slices : 2 * both]
        if total_ref is not None:
            total_ref[t] = rows[2 * both : 2 * both + slices]

    repeat(acc_ref.shape[0], spread, 8)


def turn_rays(values, flip):
    shape = values.shape
    return reversed_exact(values.reshape(-1, shape[-1]), flip).reshape(shape)


def fill_windows(weighted, flip, window_ref):
    angles, slices, _ = weighted.shape
    high, low = halves(weighted.reshape(angles * slices, ACTIVE))
    mirrored = (dot(high, flip) + dot(low, flip)).reshape(weighted.shape)
    lane = lax.broadcasted_iota(jnp.int32, (angles, slices, LANES), 2)
    for part, source in enumerate((weighted, mirrored)):
        rows = slice(part * slices, (part + 1) * slices)
        left = source[:, :, 0:LANES]
        right = source[:, :, LANES : 2 * LANES]
        window_ref[:, 0, rows, :] = left
        window_ref[:, 2, rows, :] = right
        mixed = jnp.where(lane >= SPLIT, left, right)
        window_ref[:, 1, rows, :] = pltpu.roll(mixed, SPLIT, 2)


def update_pair(held, q, c, sizes, window_ref, tile_ref, turn_ref):
    angles, chunk = sizes[:2]
    both = window_ref.shape[2]
    lane_rows = lax.broadcasted_iota(jnp.int32, (both, LANES), 1)
    tiles = [None] * (-(-chunk * WIN // LANES))
    for t in range(chunk):
        index = q * angles + c * chunk + t
        piece = pltpu.roll(window_ref[c * chunk + t, tile_ref[index]], turn_ref[index], 1)
        begin = t * WIN
        for place in range(begin // LANES, (begin + WIN - 1) // LANES + 1):
            if tiles[place] is None:
                tiles[place] = piece
            else:
                tiles[place] = jnp.where(
                    lane_rows >= begin - place * LANES, piece, tiles[place]
                )
    high, low = halves(jnp.concatenate(tiles, axis=1))
    sums = dot(jnp.concatenate([high, low], axis=0), held)
    return sums[0:both, 0:VOX] + sums[both:, 0:VOX] + sums[0:both, VOX:]


def first_kernel(
    sizes,
    offset_ref,
    place_ref,
    slot_ref,
    cos_ref,
    sin_ref,
    vol_ref,
    flip_ref,
    shift_x_ref,
    shift_y_ref,
    start_ref,
    predicted_ref,
    gain_ref,
    even_ref,
    odd_ref,
    acc_ref,
    along_ref,
    half_ref,
    mirror_ref,
):
    angles, chunk, slots = sizes
    patches = slot_ref.shape[0]
    pairs, both, _ = start_ref.shape
    slices = both // 2
    flip = flip_ref[...]

    def slot_values(patch):
        slot = slot_ref[patch]
        rows = pl.ds(slot % slots, slices, stride=slots)
        return jnp.concatenate(
            [half_ref[part, slot // slots, rows, :] for part in range(2)], axis=1
        )

    for part in range(2):
        half_ref[part] = vol_ref[:, :, part * LANES : (part + 1) * LANES]

    def order(q):
        start_ref[q, 0:slices, :] = slot_values(q)
        mirror_ref[q] = slot_values(patches - 1 - q)

    repeat(pairs, order, 8)
    start_ref[:, slices:both, :] = turn_rays(mirror_ref[0:pairs], flip)
    weights = Weights(along_ref, place_ref, angles, chunk)
    weights.prepare(shift_x_ref, shift_y_ref, cos_ref, sin_ref)
    acc_ref[...] = jnp.zeros(acc_ref.shape, f32)

    def two(index, carry):
        q = 2 * index
        for c in range(angles // chunk):
            weights.make(q, c, even_ref)
            operand = ray_operand(start_ref[q], True)
            project_pair(even_ref[...], operand, q, c, sizes, offset_ref, acc_ref)
            weights.make(q + 1, c, odd_ref)
            operand = ray_operand(start_ref[q + 1], True)
            project_pair(odd_ref[...], operand, q + 1, c, sizes, offset_ref, acc_ref)
        return carry

    lax.fori_loop(0, pairs // 2, two, 0)
    spread_rays(acc_ref, predicted_ref, mirror_ref, gain_ref, slices)
    predicted_ref[...] = predicted_ref[...] + turn_rays(mirror_ref[0:angles], flip)
    direct = gain_ref[...]
    gain_ref[...] = 1.0 / jnp.maximum(direct + turn_rays(direct, flip), row_floor)


def second_kernel(
    sizes,
    step_size,
    rank_ref,
    offset_ref,
    place_ref,
    tile_ref,
    turn_ref,
    slot_ref,
    cos_ref,
    sin_ref,
    vol_ref,
    start_ref,
    predicted_ref,
    gain_ref,
    sino_ref,
    flip_ref,
    shift_x_ref,
    shift_y_ref,
    *refs,
):
    angles, chunk, slots = sizes
    rays = vol_ref.shape[0]
    out_refs, refs = refs[:rays], refs[rays:]
    held_refs = refs[:CYCLE]
    acc_ref, along_ref, direct_ref, mirror_ref, window_ref, update_ref, half_ref = refs[CYCLE:]
    patches = slot_ref.shape[0]
    pairs, both, _ = start_ref.shape
    slices = both // 2
    flip = flip_ref[...]
    weights = Weights(along_ref, place_ref, angles, chunk)
    weights.prepare(shift_x_ref, shift_y_ref, cos_ref, sin_ref)
    chunks = angles // chunk
    windows = (sizes, window_ref, tile_ref, turn_ref)
    fill_windows(
        (sino_ref[...] - predicted_ref[...]) * gain_ref[...] * (1.0 / ROI), flip, window_ref
    )
    acc_ref[...] = jnp.zeros(acc_ref.shape, f32)

    def advance(q, held):
        total = update_pair(held, q, 0, *windows)
        update_ref[q] = total
        return start_ref[q] + step_size * total

    def forward(values, q, held):
        project_pair(held, ray_operand(values, False), q, 0, sizes, offset_ref, acc_ref)

    def cycle(index, values):
        for step in range(CYCLE):
            q = index * CYCLE + step
            after = (step + 1) % CYCLE
            before = (step - 1) % CYCLE
            later = index + (step + 1) // CYCLE
            earlier = index if step else jnp.maximum(index - 1, 0)
            weights.make(jnp.minimum(q + 1, pairs - 1), 0, held_refs[after].at[later])
            new_values = advance(q, held_refs[step][index])
            forward(values, jnp.maximum(q - 1, 0), held_refs[before][earlier])
            values = new_values
        return values

    def all_chunks(q, body):
        for c in range(chunks):
            weights.make(q, c, held_refs[0].at[0])
            body(c, held_refs[0][0])

    def plain_update(q, carry):
        update_ref[q] = jnp.zeros(update_ref.shape[1:], f32)

        def add(c, held):
            update_ref[q] = update_ref[q] + update_pair(held, q, c, *windows)

        all_chunks(q, add)
        return carry

    def plain_forward(q, carry):
        operand = ray_operand(start_ref[q] + step_size * update_ref[q], False)
        all_chunks(
            q,
            lambda c, held: project_pair(held, operand, q, c, sizes, offset_ref, acc_ref),
        )
        return carry

    if chunks == 1:
        held_refs[CYCLE - 1][0] = jnp.zeros(held_refs[CYCLE - 1].shape[1:], bf16)
        weights.make(0, 0, held_refs[0].at[0])
        values = lax.fori_loop(0, pairs // CYCLE, cycle, jnp.zeros((both, VOX), f32))
        forward(values, pairs - 1, held_refs[CYCLE - 1][pairs // CYCLE - 1])
    else:
        lax.fori_loop(0, pairs, plain_update, 0)
        lax.fori_loop(0, pairs, plain_forward, 0)

    spread_rays(acc_ref, direct_ref, mirror_ref, None, slices)
    turned = turn_rays(mirror_ref[0:angles], flip)
    direct_ref[...] = sino_ref[...] - direct_ref[...] - turned
    fill_windows(direct_ref[...] * gain_ref[...] * (1.0 / ROI), flip, window_ref)

    def last_cycle(index, carry):
        for step in range(CYCLE):
            q = index * CYCLE + step
            total = update_pair(held_refs[step][index], q, 0, *windows)
            update_ref[q] = (update_ref[q] + total) * step_size
        return carry

    def plain_last(q, carry):
        def add(c, held):
            update_ref[q] = update_ref[q] + update_pair(held, q, c, *windows)

        all_chunks(q, add)
        update_ref[q] = update_ref[q] * step_size
        return carry

    if chunks == 1:
        lax.fori_loop(0, pairs // CYCLE, last_cycle, 0)
    else:
        lax.fori_loop(0, pairs, plain_last, 0)

    mirror_ref[0:pairs] = turn_rays(update_ref[:, slices:both, :], flip)
    for part in range(2):
        half_ref[part] = vol_ref[:, :, part * LANES : (part + 1) * LANES]

    def finish(q):
        for patch, update in (
            (q, update_ref[q, 0:slices, :]),
            (patches - 1 - q, mirror_ref[q]),
        ):
            slot = slot_ref[patch]
            rows = pl.ds(slot % slots, slices, stride=slots)
            for part in range(2):
                half_ref[part, slot // slots, rows, :] = (
                    half_ref[part, slot // slots, rows, :]
                    + update[:, part * LANES : (part + 1) * LANES]
                )

    repeat(pairs, finish, 8)
    lead = slices * slots
    for d, out_ref in enumerate(out_refs):
        ray = rank_ref[0] ^ d
        for part in range(2):
            out_ref[0:lead, part * LANES : (part + 1) * LANES] = half_ref[part, ray]
        for k in range(angles // rays):
            begin = lead + k * slices
            out_ref[begin : begin + slices, :] = direct_ref[k * rays + ray]


def call(kernel, name, inputs, outputs, scratch, micros):
    smem = pl.BlockSpec(memory_space=pltpu.SMEM)
    vmem = pl.BlockSpec(memory_space=pltpu.VMEM)
    return pl.pallas_call(
        kernel,
        out_shape=[jax.ShapeDtypeStruct(*value) for value in outputs],
        in_specs=[smem if value.ndim == 1 else vmem for value in inputs],
        out_specs=[vmem] * len(outputs),
        scratch_shapes=[pltpu.VMEM(*value) for value in scratch],
        compiler_params=pltpu.CompilerParams(vmem_limit_bytes=52 * 2**20),
        cost_estimate=pl.CostEstimate(
            flops=int(micros * 1e9), bytes_accessed=4 * 2**20, transcendentals=0
        ),
        name=name,
    )(*inputs)


class Sirt:
    def __init__(self, theta, vol_list, slices, slots, rays, step_size):
        angles = theta.shape[0]
        patches = vol_list.shape[0]
        pairs = patches // 2
        both = 2 * slices
        chunk = math.gcd(angles, 32)
        self.sizes = (angles, chunk, slots)
        self.step_size = step_size
        self.rays = rays
        self.patches = patches
        centre = (ROI - 1) / 2.0
        ids = np.arange(pairs)
        centre_x = (ids // PGRID * float(SIDE) + (SIDE - 1) / 2.0 - centre).astype(np.float32)
        centre_y = (ids % PGRID * float(SIDE) + (SIDE - 1) / 2.0 - centre).astype(np.float32)
        self.cosine = jnp.cos(theta)
        self.sine = jnp.sin(theta)
        along = (
            centre_x[:, None] * self.cosine[None, :]
            + centre_y[:, None] * self.sine[None, :]
            + 0.5
        )
        whole = jnp.floor(along)
        lead = WIN // 2 - 1
        place = along - whole + float(lead)
        offset = whole.astype(jnp.int32) + (ACTIVE // 2 - 1 - lead)
        tile = jnp.minimum(offset // SPLIT, 2)
        local = jnp.arange(angles, dtype=jnp.int32) % chunk * WIN
        turn = (local[None, :] - offset + tile * SPLIT) % LANES
        self.offset = offset.reshape(-1)
        self.place = place.reshape(-1)
        self.tile = tile.reshape(-1)
        self.turn = turn.reshape(-1)
        ids = jnp.arange(patches, dtype=jnp.int32)
        self.slot = jnp.sum(
            jnp.where(vol_list[None, :] == ids[:, None], ids[None, :], 0), axis=1
        )
        voxel = np.arange(VOX)
        shift_x = np.repeat((voxel // SIDE - (SIDE - 1) / 2.0)[None, :], ROWS, axis=0)
        shift_y = np.repeat((voxel % SIDE - (SIDE - 1) / 2.0)[None, :], ROWS, axis=0)
        flip = np.eye(ACTIVE)[::-1].astype(ml_dtypes.bfloat16)
        self.fixed = [jnp.asarray(flip), jnp.asarray(shift_x, f32), jnp.asarray(shift_y, f32)]
        self.weight = ((chunk * WIN, 2 * VOX), bf16)
        self.held = (pairs // CYCLE + 1 if angles == chunk else 1,) + self.weight[0]
        self.acc = ((angles, ACTIVE, LANES), f32)
        self.along = ((angles, ROWS, VOX), f32)
        self.by_ray = ((angles, slices, ACTIVE), f32)
        self.by_pair = ((pairs, both, VOX), f32)
        self.window = ((angles, 3, both, LANES), f32)
        self.half = ((2, rays, slices * slots, LANES), f32)
        self.mirror = ((max(pairs, angles), slices, ACTIVE), f32)
        self.sent = [((slices * (slots + angles // rays), ACTIVE), f32)] * rays

    def first(self, volume):
        inputs = [self.offset, self.place, self.slot, self.cosine, self.sine, volume]
        return call(
            functools.partial(first_kernel, self.sizes),
            "first",
            inputs + self.fixed,
            [self.by_pair, self.by_ray, self.by_ray],
            [self.weight, self.weight, self.acc, self.along, self.half, self.mirror],
            14,
        )

    def second(self, rank, volume, start, predicted, gain, sino):
        inputs = [rank.reshape(1), self.offset, self.place, self.tile, self.turn, self.slot]
        inputs += [self.cosine, self.sine, volume, start, predicted, gain, sino]
        scratch = [(self.held, bf16)] * CYCLE
        scratch += [self.acc, self.along, self.by_ray, self.mirror, self.window]
        return call(
            functools.partial(second_kernel, self.sizes, self.step_size),
            "second",
            inputs + self.fixed,
            self.sent,
            scratch + [self.by_pair, self.half],
            26,
        )


def gather_kernel(rank_ref, *refs):
    *part_refs, out_ref, sems = refs
    rank = rank_ref[0]
    copies = [
        pltpu.make_async_copy(part_ref, out_ref.at[rank ^ d], sems.at[d])
        for d, part_ref in enumerate(part_refs)
    ]
    for copy in copies:
        copy.start()
    for copy in copies:
        copy.wait()


def gather_parts(parts, rank):
    count = len(parts)
    return pl.pallas_call(
        gather_kernel,
        out_shape=jax.ShapeDtypeStruct((count,) + parts[0].shape, f32),
        in_specs=[pl.BlockSpec(memory_space=pltpu.SMEM)]
        + [pl.BlockSpec(memory_space=pltpu.VMEM)] * count,
        out_specs=pl.BlockSpec(memory_space=pl.ANY),
        scratch_shapes=[pltpu.SemaphoreType.DMA((count,))],
        compiler_params=pltpu.CompilerParams(vmem_limit_bytes=8 * 2**20),
        cost_estimate=pl.CostEstimate(
            flops=0, bytes_accessed=8 * count * parts[0].size, transcendentals=0
        ),
        name="gather_parts",
    )(rank.reshape(1), *parts)


def finish_kernel(rank_ref, *refs):
    *got_refs, _, rec_ref, out_ref, values_ref, active_ref, sems = refs
    rays = len(got_refs)
    slots = values_ref.shape[1]
    slabs = active_ref.shape[0]
    slices = values_ref.shape[0] // rays
    lead = slices * slots
    for d, got_ref in enumerate(reversed(got_refs)):
        rows = pl.ds(pl.multiple_of((rank_ref[0] ^ d) * slices, slices), slices)
        values_ref[rows] = got_ref[0:lead, :].reshape(slices, slots, VOX)
        for k in range(slabs):
            begin = lead + k * slices
            active_ref[k, rows, :] = got_ref[begin : begin + slices, :]
    offset = (out_ref.shape[2] - ACTIVE) // 2
    copies = [
        pltpu.make_async_copy(values_ref, rec_ref, sems.at[0]),
        pltpu.make_async_copy(
            active_ref, out_ref.at[:, :, offset : offset + ACTIVE], sems.at[1]
        ),
    ]
    for copy in copies:
        copy.start()
    for copy in copies:
        copy.wait()


def finish(pieces, sinogram, rank, shape):
    slabs, slab_rows, _ = sinogram.shape
    hbm = pl.BlockSpec(memory_space=pltpu.HBM)
    return pl.pallas_call(
        finish_kernel,
        out_shape=(
            jax.ShapeDtypeStruct(shape, f32),
            jax.ShapeDtypeStruct(sinogram.shape, f32),
        ),
        in_specs=[pl.BlockSpec(memory_space=pltpu.SMEM)]
        + [pl.BlockSpec(memory_space=pltpu.VMEM)] * len(pieces)
        + [hbm],
        out_specs=[hbm, hbm],
        scratch_shapes=[
            pltpu.VMEM(shape, f32),
            pltpu.VMEM((slabs, slab_rows, ACTIVE), f32),
            pltpu.SemaphoreType.DMA((2,)),
        ],
        input_output_aliases={len(pieces) + 1: 1},
        compiler_params=pltpu.CompilerParams(vmem_limit_bytes=8 * 2**20),
        cost_estimate=pl.CostEstimate(
            flops=0, bytes_accessed=8 * len(pieces) * pieces[0].size, transcendentals=0
        ),
        name="finish",
    )(rank.reshape(1), *reversed(pieces), sinogram)


def exchange(pieces, axis):
    count = len(pieces)
    results = list(pieces)
    for d in range(count - 1, 0, -1):
        results[d] = lax.ppermute(pieces[d], axis, [(i, i ^ d) for i in range(count)])
    return results


def local(intensity, angles, volume, vol_list):
    n_slab = lax.axis_size("slab")
    n_ray = lax.axis_size("ray")
    devices = n_slab * n_ray
    height, band = intensity.shape[2:]
    slices = height // devices
    slots = volume.shape[1]
    count = angles.shape[0] * angles.shape[1]
    step_size = relax * ROI / count
    rank = lax.axis_index("slab")
    ray_rank = lax.axis_index("ray")
    padded = -(-slices // ROWS) * ROWS

    def to_all(values, axes):
        return lax.all_to_all(values, axes, split_axis=0, concat_axis=0, tiled=True)

    own_volume = to_all(volume.reshape(n_ray, slices * slots, VOX), "ray")
    *parts, active = paganin(intensity.reshape(height, band), rank, n_slab)
    active, own_volume = lax.optimization_barrier((active, own_volume))
    own_rays = to_all(active.reshape(devices, slices, ACTIVE), ("slab", "ray"))
    if padded != slices:
        more = padded - slices
        own_volume = jnp.pad(own_volume, ((0, 0), (0, more * slots), (0, 0)))
        own_rays = jnp.pad(own_rays, ((0, 0), (0, more), (0, 0)))

    theta, vol_list, own_volume, parts = lax.optimization_barrier(
        (angles.reshape(-1), vol_list, own_volume, parts)
    )
    sirt = Sirt(theta, vol_list, padded, slots, n_ray, step_size)
    start, predicted, gain = sirt.first(own_volume)
    own_rays, parts, start = lax.optimization_barrier((own_rays, parts, start))
    parts = exchange(parts, "slab")
    pieces = sirt.second(ray_rank, own_volume, start, predicted, gain, own_rays)
    pieces, parts = lax.optimization_barrier((pieces, parts))
    if padded != slices:
        narrow = []
        for piece in pieces:
            lower = piece[padded * slots :].reshape(n_slab, padded, ACTIVE)[:, :slices]
            lower = lower.reshape(n_slab * slices, ACTIVE)
            narrow.append(jnp.concatenate([piece[: slices * slots], lower], axis=0))
        pieces = narrow
    pieces = exchange(pieces, "ray")
    sinogram = gather_parts(parts, rank)
    if padded == slices:
        reconstruction, residual = finish(pieces, sinogram, ray_rank, volume.shape)
    else:
        order = ray_rank ^ jnp.arange(n_ray, dtype=jnp.int32)
        pieces = jnp.take(jnp.stack(pieces), order, axis=0)
        reconstruction = pieces[:, : slices * slots].reshape(volume.shape)
        lower = pieces[:, slices * slots :].reshape(n_ray, n_slab, slices, ACTIVE)
        lower = jnp.transpose(lower, (1, 0, 2, 3)).reshape(n_slab, n_ray * slices, ACTIVE)
        begin = (band - ACTIVE) // 2
        residual = lax.dynamic_update_slice(sinogram, lower, (0, 0, begin))
    return (reconstruction, residual[:, None])


def solution(mesh):
    placed = (P("slab", "ray", None, None), P(), P("slab", "ray", None), P())
    return jax.shard_map(
        local,
        mesh=mesh,
        in_specs=placed,
        out_specs=(P("slab", "ray", None), P(None, "ray", "slab", None)),
        check_vma=False,
    )
```

```python
import functools
import math

import jax
import jax.numpy as jnp
import ml_dtypes
import numpy as np
from jax import lax
from jax.experimental import pallas as pl
from jax.experimental.pallas import tpu as pltpu
from jax.sharding import PartitionSpec as P

BAND = 2048
PGRID = 8
ROI = 128
SIDE = 16
VOX = SIDE * SIDE
WIN = 24
ACTIVE = 256
LANES = 128
ROWS = 8
SPLIT = 64
GROUP = 8
CYCLE = 4

paganin_strength = 10.0
relax = 1.8
row_floor = 0.25

bf16 = jnp.bfloat16
f32 = jnp.float32


def halves(values):
    high = values.astype(bf16)
    low = (values - high.astype(f32)).astype(bf16)
    return high, low


def thirds(values):
    high = values.astype(bf16)
    rest = values - high.astype(f32)
    middle = rest.astype(bf16)
    low = (rest - middle.astype(f32)).astype(bf16)
    return high, middle, low


def dot(left, right):
    return jnp.dot(left, right, preferred_element_type=f32)


def repeat(count, body, unroll):
    unroll = math.gcd(count, unroll)

    def several(index, carry):
        for step in range(unroll):
            body(index * unroll + step)
        return carry

    lax.fori_loop(0, count // unroll, several, 0)


def filter_tables(height):
    index = np.arange(height)
    phase = 2.0 * np.pi * (np.outer(index, index) % height) / height
    cas = (np.cos(phase) + np.sin(phase)) / math.sqrt(height)
    row_freq = 2.0 - 2.0 * np.cos(2.0 * np.pi * index / height)
    middle = (1.0 + paganin_strength * row_freq) / paganin_strength + 2.0
    rho = (middle - np.sqrt(middle * middle - 4.0)) / 2.0
    return np.concatenate([cas, np.repeat(rho[None, :], ROWS, axis=0)], axis=0).astype(np.float32)


def chunk_carry(ends, power, forward):
    shift = 1
    for _ in range(3):
        ends = ends + power * pltpu.roll(ends, shift if forward else ROWS - shift, 0)
        power = power * power
        shift *= 2
    return pltpu.roll(ends, 1 if forward else ROWS - 1, 0) / (1.0 - power)


def filter_kernel(rank_ref, source_ref, given_ref, *refs):
    *part_refs, active_ref, image_ref, table_ref, out_ref, spec_ref, up_ref, down_ref = refs[:-2]
    sems, out_sems = refs[-2:]
    height, width = image_ref.shape
    rank = rank_ref[0]
    share = height // len(part_refs)
    length = width // ROWS
    blocks = height // LANES
    unroll = 8
    copies = []
    for c in range(ROWS):
        columns = slice(c * length, (c + 1) * length)
        copies.append(
            pltpu.make_async_copy(
                source_ref.at[:, columns], image_ref.at[:, columns], sems.at[c]
            )
        )
    given = pltpu.make_async_copy(given_ref, table_ref, sems.at[ROWS])
    given.start()
    for copy in copies:
        copy.start()
    given.wait()
    cas_high, cas_low = halves(table_ref[0:height, :])
    rho_all = table_ref[height : height + ROWS, :]
    rhos = [rho_all[:, b * LANES : (b + 1) * LANES] for b in range(blocks)]
    zeros = [jnp.zeros((ROWS, LANES), f32)] * blocks

    def transform(values):
        high, low = halves(values)
        return dot(high, cas_high) + dot(low, cas_high) + dot(high, cas_low)

    for c in range(ROWS):
        copies[c].wait()
        image = 1.0 - image_ref[:, c * length : (c + 1) * length]
        spectrum = transform(jnp.transpose(image))
        for b in range(blocks):
            spec_ref[b, pl.ds(c, length, stride=ROWS), :] = spectrum[
                :, b * LANES : (b + 1) * LANES
            ]

    def rows(position):
        return pl.ds(pl.multiple_of(position * ROWS, ROWS), ROWS)

    def advance(position, ups, downs):
        ups = [spec_ref[b, rows(position), :] + rhos[b] * ups[b] for b in range(blocks)]
        back = length - 1 - position
        downs = [spec_ref[b, rows(back), :] + rhos[b] * downs[b] for b in range(blocks)]
        return ups, downs

    def sweep(index, carry):
        ups, downs = carry
        for step in range(unroll):
            ups, downs = advance(index * unroll + step, ups, downs)
        return ups, downs

    ups, downs = lax.fori_loop(0, length // unroll, sweep, (zeros, zeros))
    powers = list(rhos)
    for _ in range(int(math.log2(length))):
        powers = [power * power for power in powers]
    ups = [chunk_carry(ups[b], powers[b], True) for b in range(blocks)]
    downs = [chunk_carry(downs[b], powers[b], False) for b in range(blocks)]
    scales = [rho / (paganin_strength * (1.0 - rho * rho)) for rho in rhos]

    def outer(index, carry):
        ups, downs = carry
        for step in range(unroll):
            position = index * unroll + step
            ups, downs = advance(position, ups, downs)
            for b in range(blocks):
                up_ref[b, rows(position), :] = ups[b]
                down_ref[b, rows(position), :] = downs[b]
        return ups, downs

    def inner(index, carry):
        ups, downs = carry
        for step in range(unroll):
            position = index * unroll + step
            back = length - 1 - position
            ups, downs = advance(position, ups, downs)
            for b in range(blocks):
                here = ups[b] + down_ref[b, rows(back), :] - spec_ref[b, rows(position), :]
                there = downs[b] + up_ref[b, rows(back), :] - spec_ref[b, rows(back), :]
                up_ref[b, rows(position), :] = here * scales[b]
                up_ref[b, rows(back), :] = there * scales[b]
        return ups, downs

    half = length // 2 // unroll
    carry = lax.fori_loop(0, half, outer, (ups, downs))
    lax.fori_loop(half, 2 * half, inner, carry)

    offset = (width - ACTIVE) // 2
    sent = []
    for c in range(ROWS):
        spectrum = jnp.concatenate(
            [up_ref[b, pl.ds(c, length, stride=ROWS), :] for b in range(blocks)], axis=1
        )
        filtered = 1.0 - jnp.transpose(transform(spectrum))
        columns = slice(c * length, (c + 1) * length)
        out_ref[:, columns] = -jnp.log(filtered)
        for d, part_ref in enumerate(part_refs):
            rows = pl.ds(pl.multiple_of((rank ^ d) * share, share), share)
            sent.append(
                pltpu.make_async_copy(
                    out_ref.at[rows, columns], part_ref.at[:, columns], out_sems.at[c, d]
                )
            )
            sent[-1].start()
    active_ref[...] = out_ref[:, offset : offset + ACTIVE]
    for copy in sent:
        copy.wait()


def paganin(image, rank, parts):
    height, width = image.shape
    blocks = height // LANES
    return pl.pallas_call(
        filter_kernel,
        out_shape=[jax.ShapeDtypeStruct((height // parts, width), f32)] * parts
        + [jax.ShapeDtypeStruct((height, ACTIVE), f32)],
        in_specs=[pl.BlockSpec(memory_space=pltpu.SMEM)]
        + [pl.BlockSpec(memory_space=pltpu.HBM)] * 2,
        out_specs=[pl.BlockSpec(memory_space=pltpu.HBM)] * parts
        + [pl.BlockSpec(memory_space=pltpu.VMEM)],
        scratch_shapes=[
            pltpu.VMEM((height, width), f32),
            pltpu.VMEM((height + ROWS, height), f32),
            pltpu.VMEM((height, width), f32),
            pltpu.VMEM((blocks, width, LANES), f32),
            pltpu.VMEM((blocks, width, LANES), f32),
            pltpu.VMEM((blocks, width // 2, LANES), f32),
            pltpu.SemaphoreType.DMA((ROWS + 1,)),
            pltpu.SemaphoreType.DMA((ROWS, parts)),
        ],
        compiler_params=pltpu.CompilerParams(vmem_limit_bytes=58 * 2**20),
        cost_estimate=pl.CostEstimate(
            flops=64 * height * height * width,
            bytes_accessed=8 * height * width,
            transcendentals=height * width,
        ),
        name="paganin",
    )(rank.reshape(1), image, jnp.asarray(filter_tables(height)))


def reversed_exact(values, flip):
    return sum(dot(part, flip) for part in thirds(values))


class Weights:
    def __init__(self, along_ref, place_ref, angles, chunk):
        self.along_ref = along_ref
        self.place_ref = place_ref
        self.angles = angles
        self.chunk = chunk
        self.ray = lax.broadcasted_iota(jnp.int32, (ROWS, VOX), 0).astype(f32)

    def prepare(self, shift_x_ref, shift_y_ref, cos_ref, sin_ref):
        def along_angle(t):
            self.along_ref[t] = shift_x_ref[...] * cos_ref[t] + shift_y_ref[...] * sin_ref[t]

        repeat(self.angles, along_angle, 8)

    def make(self, q, c, ref):
        for two in range(self.chunk // 2):
            pieces = []
            for t in (2 * two, 2 * two + 1):
                angle = c * self.chunk + t
                along = self.along_ref[angle] + self.place_ref[q * self.angles + angle]
                base = self.ray - along
                for group in range(WIN // ROWS):
                    distance = base + float(group * ROWS)
                    pieces.append(jnp.maximum(0.0, 1.0 - jnp.abs(distance)))
            high, low = halves(jnp.concatenate(pieces, axis=0))
            ref[2 * two * WIN : (2 * two + 2) * WIN, 0:VOX] = high
            ref[2 * two * WIN : (2 * two + 2) * WIN, VOX : 2 * VOX] = low


def ray_operand(values, sums_too):
    high, low = halves(values)
    rows = [
        jnp.concatenate([high, high], axis=1),
        jnp.concatenate([low, jnp.zeros_like(low)], axis=1),
    ]
    if sums_too:
        rows.append(jnp.ones((values.shape[0], 2 * VOX), bf16))
    return jnp.concatenate(rows, axis=0)


def project_pair(held, operand, q, c, both, sizes, tile_ref, turn_ref, acc_ref):
    angles, chunk = sizes[:2]
    rows = acc_ref.shape[2]
    sums = lax.dot_general(
        operand, held, (((1,), (1,)), ((), ())), preferred_element_type=f32
    )
    total = sums[0:both] + sums[both : 2 * both]
    if rows != both:
        total = jnp.concatenate([total, sums[2 * both : 2 * both + ROWS]], axis=0)
    lane = lax.broadcasted_iota(jnp.int32, (rows, LANES), 1)
    for begin in range(0, chunk, GROUP):
        places = []
        for t in range(begin, min(begin + GROUP, chunk)):
            index = q * angles + c * chunk + t
            first = t * WIN // LANES
            last = (t * WIN + WIN - 1) // LANES
            low = t * WIN - first * LANES
            high = low + WIN
            piece = total[:, first * LANES : (first + 1) * LANES]
            if first == last:
                piece = jnp.where((lane >= low) & (lane < high), piece, 0.0)
            else:
                other = total[:, last * LANES : (last + 1) * LANES]
                piece = jnp.where(
                    lane >= low, piece, jnp.where(lane < high - LANES, other, 0.0)
                )
            tile = tile_ref[index]
            angle = c * chunk + t
            piece = pltpu.roll(piece, (LANES - turn_ref[index]) % LANES, 1)
            places.append((angle, tile, acc_ref[angle, tile] + piece))
        for angle, tile, values in places:
            acc_ref[angle, tile] = values


def join_tiles(acc_ref, rows):
    lane = lax.broadcasted_iota(jnp.int32, (acc_ref.shape[0], ROWS, LANES), 2)
    middle = pltpu.roll(acc_ref[:, 1, rows, :], SPLIT, 2)
    left = acc_ref[:, 0, rows, :] + jnp.where(lane >= SPLIT, middle, 0.0)
    right = acc_ref[:, 2, rows, :] + jnp.where(lane < SPLIT, middle, 0.0)
    return jnp.concatenate([left, right], axis=2) * (1.0 / ROI)


def turn_rays(values, flip):
    shape = values.shape
    return reversed_exact(values.reshape(-1, shape[-1]), flip).reshape(shape)


def fill_windows(weighted, flip, window_ref):
    angles, slices, _ = weighted.shape
    high, low = halves(weighted.reshape(angles * slices, ACTIVE))
    mirrored = (dot(high, flip) + dot(low, flip)).reshape(weighted.shape)
    lane = lax.broadcasted_iota(jnp.int32, (angles, slices, LANES), 2)
    for part, source in enumerate((weighted, mirrored)):
        rows = slice(part * slices, (part + 1) * slices)
        left = source[:, :, 0:LANES]
        right = source[:, :, LANES : 2 * LANES]
        window_ref[:, 0, rows, :] = left
        window_ref[:, 2, rows, :] = right
        mixed = jnp.where(lane >= SPLIT, left, right)
        window_ref[:, 1, rows, :] = pltpu.roll(mixed, SPLIT, 2)


def update_pair(held, q, c, sizes, window_ref, tile_ref, turn_ref):
    angles, chunk = sizes[:2]
    both = window_ref.shape[2]
    lane_rows = lax.broadcasted_iota(jnp.int32, (both, LANES), 1)
    tiles = [None] * (-(-chunk * WIN // LANES))
    for t in range(chunk):
        index = q * angles + c * chunk + t
        piece = pltpu.roll(window_ref[c * chunk + t, tile_ref[index]], turn_ref[index], 1)
        begin = t * WIN
        for place in range(begin // LANES, (begin + WIN - 1) // LANES + 1):
            if tiles[place] is None:
                tiles[place] = piece
            else:
                tiles[place] = jnp.where(
                    lane_rows >= begin - place * LANES, piece, tiles[place]
                )
    high, low = halves(jnp.concatenate(tiles, axis=1))
    sums = dot(jnp.concatenate([high, low], axis=0), held)
    return sums[0:both, 0:VOX] + sums[both:, 0:VOX] + sums[0:both, VOX:]


def first_kernel(
    sizes,
    place_ref,
    tile_ref,
    turn_ref,
    slot_ref,
    cos_ref,
    sin_ref,
    vol_ref,
    flip_ref,
    shift_x_ref,
    shift_y_ref,
    start_ref,
    predicted_ref,
    gain_ref,
    even_ref,
    odd_ref,
    acc_ref,
    along_ref,
    half_ref,
    mirror_ref,
):
    angles, chunk, slots = sizes
    patches = slot_ref.shape[0]
    pairs, both, _ = start_ref.shape
    slices = both // 2
    flip = flip_ref[...]

    def slot_values(patch):
        slot = slot_ref[patch]
        rows = pl.ds(slot % slots, slices, stride=slots)
        return jnp.concatenate(
            [half_ref[part, slot // slots, rows, :] for part in range(2)], axis=1
        )

    for part in range(2):
        half_ref[part] = vol_ref[:, :, part * LANES : (part + 1) * LANES]

    def order(q):
        start_ref[q, 0:slices, :] = slot_values(q)
        mirror_ref[q] = slot_values(patches - 1 - q)

    repeat(pairs, order, 8)
    start_ref[:, slices:both, :] = turn_rays(mirror_ref[0:pairs], flip)
    weights = Weights(along_ref, place_ref, angles, chunk)
    weights.prepare(shift_x_ref, shift_y_ref, cos_ref, sin_ref)
    acc_ref[...] = jnp.zeros(acc_ref.shape, f32)

    rest = (both, sizes, tile_ref, turn_ref, acc_ref)

    def two(index, carry):
        q = 2 * index
        for c in range(angles // chunk):
            weights.make(q, c, even_ref)
            operand = ray_operand(start_ref[q], True)
            project_pair(even_ref[...], operand, q, c, *rest)
            weights.make(q + 1, c, odd_ref)
            operand = ray_operand(start_ref[q + 1], True)
            project_pair(odd_ref[...], operand, q + 1, c, *rest)
        return carry

    lax.fori_loop(0, pairs // 2, two, 0)
    direct, mirror, weight_sums = (
        join_tiles(acc_ref, slice(part * ROWS, (part + 1) * ROWS)) for part in range(3)
    )
    predicted_ref[...] = direct + turn_rays(mirror, flip)
    direct = weight_sums
    gain_ref[...] = 1.0 / jnp.maximum(direct + turn_rays(direct, flip), row_floor)


def second_kernel(
    sizes,
    step_size,
    rank_ref,
    place_ref,
    tile_ref,
    turn_ref,
    slot_ref,
    cos_ref,
    sin_ref,
    vol_ref,
    start_ref,
    predicted_ref,
    gain_ref,
    sino_ref,
    flip_ref,
    shift_x_ref,
    shift_y_ref,
    *refs,
):
    angles, chunk, slots = sizes
    rays = vol_ref.shape[0]
    out_refs, refs = refs[:rays], refs[rays:]
    held_refs = refs[:CYCLE]
    acc_ref, along_ref, direct_ref, mirror_ref, window_ref, update_ref, half_ref = refs[CYCLE:]
    patches = slot_ref.shape[0]
    pairs, both, _ = start_ref.shape
    slices = both // 2
    flip = flip_ref[...]
    weights = Weights(along_ref, place_ref, angles, chunk)
    weights.prepare(shift_x_ref, shift_y_ref, cos_ref, sin_ref)
    chunks = angles // chunk
    windows = (sizes, window_ref, tile_ref, turn_ref)
    windows_out = (both, sizes, tile_ref, turn_ref, acc_ref)
    fill_windows(
        (sino_ref[...] - predicted_ref[...]) * gain_ref[...] * (1.0 / ROI), flip, window_ref
    )
    acc_ref[...] = jnp.zeros(acc_ref.shape, f32)

    def advance(q, held):
        total = update_pair(held, q, 0, *windows)
        update_ref[q] = total
        return start_ref[q] + step_size * total

    def forward(values, q, held):
        project_pair(held, ray_operand(values, False), q, 0, *windows_out)

    def cycle(index, values):
        for step in range(CYCLE):
            q = index * CYCLE + step
            after = (step + 1) % CYCLE
            before = (step - 1) % CYCLE
            later = index + (step + 1) // CYCLE
            earlier = index if step else jnp.maximum(index - 1, 0)
            weights.make(jnp.minimum(q + 1, pairs - 1), 0, held_refs[after].at[later])
            new_values = advance(q, held_refs[step][index])
            forward(values, jnp.maximum(q - 1, 0), held_refs[before][earlier])
            values = new_values
        return values

    def all_chunks(q, body):
        for c in range(chunks):
            weights.make(q, c, held_refs[0].at[0])
            body(c, held_refs[0][0])

    def plain_update(q, carry):
        update_ref[q] = jnp.zeros(update_ref.shape[1:], f32)

        def add(c, held):
            update_ref[q] = update_ref[q] + update_pair(held, q, c, *windows)

        all_chunks(q, add)
        return carry

    def plain_forward(q, carry):
        operand = ray_operand(start_ref[q] + step_size * update_ref[q], False)
        all_chunks(
            q,
            lambda c, held: project_pair(held, operand, q, c, *windows_out),
        )
        return carry

    if chunks == 1:
        held_refs[CYCLE - 1][0] = jnp.zeros(held_refs[CYCLE - 1].shape[1:], bf16)
        weights.make(0, 0, held_refs[0].at[0])
        values = lax.fori_loop(0, pairs // CYCLE, cycle, jnp.zeros((both, VOX), f32))
        forward(values, pairs - 1, held_refs[CYCLE - 1][pairs // CYCLE - 1])
    else:
        lax.fori_loop(0, pairs, plain_update, 0)
        lax.fori_loop(0, pairs, plain_forward, 0)

    direct, mirror = (
        join_tiles(acc_ref, slice(part * ROWS, (part + 1) * ROWS)) for part in range(2)
    )
    direct_ref[...] = sino_ref[...] - direct - turn_rays(mirror, flip)
    fill_windows(direct_ref[...] * gain_ref[...] * (1.0 / ROI), flip, window_ref)

    def last_cycle(index, carry):
        for step in range(CYCLE):
            q = index * CYCLE + step
            total = update_pair(held_refs[step][index], q, 0, *windows)
            update_ref[q] = (update_ref[q] + total) * step_size
        return carry

    def plain_last(q, carry):
        def add(c, held):
            update_ref[q] = update_ref[q] + update_pair(held, q, c, *windows)

        all_chunks(q, add)
        update_ref[q] = update_ref[q] * step_size
        return carry

    if chunks == 1:
        lax.fori_loop(0, pairs // CYCLE, last_cycle, 0)
    else:
        lax.fori_loop(0, pairs, plain_last, 0)

    mirror_ref[0:pairs] = turn_rays(update_ref[:, slices:both, :], flip)
    for part in range(2):
        half_ref[part] = vol_ref[:, :, part * LANES : (part + 1) * LANES]

    def finish(q):
        for patch, update in (
            (q, update_ref[q, 0:slices, :]),
            (patches - 1 - q, mirror_ref[q]),
        ):
            slot = slot_ref[patch]
            rows = pl.ds(slot % slots, slices, stride=slots)
            for part in range(2):
                half_ref[part, slot // slots, rows, :] = (
                    half_ref[part, slot // slots, rows, :]
                    + update[:, part * LANES : (part + 1) * LANES]
                )

    repeat(pairs, finish, 8)
    lead = slices * slots
    for d, out_ref in enumerate(out_refs):
        ray = rank_ref[0] ^ d
        for part in range(2):
            out_ref[0:lead, part * LANES : (part + 1) * LANES] = half_ref[part, ray]
        for k in range(angles // rays):
            begin = lead + k * slices
            out_ref[begin : begin + slices, :] = direct_ref[k * rays + ray]


def call(kernel, name, inputs, outputs, scratch, micros):
    smem = pl.BlockSpec(memory_space=pltpu.SMEM)
    vmem = pl.BlockSpec(memory_space=pltpu.VMEM)
    return pl.pallas_call(
        kernel,
        out_shape=[jax.ShapeDtypeStruct(*value) for value in outputs],
        in_specs=[smem if value.ndim == 1 else vmem for value in inputs],
        out_specs=[vmem] * len(outputs),
        scratch_shapes=[pltpu.VMEM(*value) for value in scratch],
        compiler_params=pltpu.CompilerParams(vmem_limit_bytes=52 * 2**20),
        cost_estimate=pl.CostEstimate(
            flops=int(micros * 1e9), bytes_accessed=4 * 2**20, transcendentals=0
        ),
        name=name,
    )(*inputs)


class Sirt:
    def __init__(self, theta, vol_list, slices, slots, rays, step_size):
        angles = theta.shape[0]
        patches = vol_list.shape[0]
        pairs = patches // 2
        both = 2 * slices
        chunk = math.gcd(angles, 32)
        self.sizes = (angles, chunk, slots)
        self.step_size = step_size
        self.rays = rays
        self.patches = patches
        centre = (ROI - 1) / 2.0
        ids = np.arange(pairs)
        centre_x = (ids // PGRID * float(SIDE) + (SIDE - 1) / 2.0 - centre).astype(np.float32)
        centre_y = (ids % PGRID * float(SIDE) + (SIDE - 1) / 2.0 - centre).astype(np.float32)
        self.cosine = jnp.cos(theta)
        self.sine = jnp.sin(theta)
        along = (
            centre_x[:, None] * self.cosine[None, :]
            + centre_y[:, None] * self.sine[None, :]
            + 0.5
        )
        whole = jnp.floor(along)
        lead = WIN // 2 - 1
        place = along - whole + float(lead)
        offset = whole.astype(jnp.int32) + (ACTIVE // 2 - 1 - lead)
        tile = jnp.minimum(offset // SPLIT, 2)
        local = jnp.arange(angles, dtype=jnp.int32) % chunk * WIN
        turn = (local[None, :] - offset + tile * SPLIT) % LANES
        self.place = place.reshape(-1)
        self.tile = tile.reshape(-1)
        self.turn = turn.reshape(-1)
        ids = jnp.arange(patches, dtype=jnp.int32)
        self.slot = jnp.sum(
            jnp.where(vol_list[None, :] == ids[:, None], ids[None, :], 0), axis=1
        )
        voxel = np.arange(VOX)
        shift_x = np.repeat((voxel // SIDE - (SIDE - 1) / 2.0)[None, :], ROWS, axis=0)
        shift_y = np.repeat((voxel % SIDE - (SIDE - 1) / 2.0)[None, :], ROWS, axis=0)
        flip = np.eye(ACTIVE)[::-1].astype(ml_dtypes.bfloat16)
        self.fixed = [jnp.asarray(flip), jnp.asarray(shift_x, f32), jnp.asarray(shift_y, f32)]
        self.weight = ((chunk * WIN, 2 * VOX), bf16)
        self.held = (pairs // CYCLE + 1 if angles == chunk else 1,) + self.weight[0]
        self.acc = ((angles, 3, both, LANES), f32)
        self.acc_sums = ((angles, 3, both + ROWS, LANES), f32)
        self.along = ((angles, ROWS, VOX), f32)
        self.by_ray = ((angles, slices, ACTIVE), f32)
        self.by_pair = ((pairs, both, VOX), f32)
        self.window = ((angles, 3, both, LANES), f32)
        self.half = ((2, rays, slices * slots, LANES), f32)
        self.mirror = ((max(pairs, angles), slices, ACTIVE), f32)
        self.sent = [((slices * (slots + angles // rays), ACTIVE), f32)] * rays

    def first(self, volume):
        inputs = [self.place, self.tile, self.turn, self.slot, self.cosine, self.sine, volume]
        return call(
            functools.partial(first_kernel, self.sizes),
            "first",
            inputs + self.fixed,
            [self.by_pair, self.by_ray, self.by_ray],
            [self.weight, self.weight, self.acc_sums, self.along, self.half, self.mirror],
            14,
        )

    def second(self, rank, volume, start, predicted, gain, sino):
        inputs = [rank.reshape(1), self.place, self.tile, self.turn, self.slot]
        inputs += [self.cosine, self.sine, volume, start, predicted, gain, sino]
        scratch = [(self.held, bf16)] * CYCLE
        scratch += [self.acc, self.along, self.by_ray, self.mirror, self.window]
        return call(
            functools.partial(second_kernel, self.sizes, self.step_size),
            "second",
            inputs + self.fixed,
            self.sent,
            scratch + [self.by_pair, self.half],
            26,
        )


def gather_kernel(rank_ref, *refs):
    *part_refs, out_ref, sems = refs
    rank = rank_ref[0]
    copies = [
        pltpu.make_async_copy(part_ref, out_ref.at[rank ^ d], sems.at[d])
        for d, part_ref in enumerate(part_refs)
    ]
    for copy in copies:
        copy.start()
    for copy in copies:
        copy.wait()


def gather_parts(parts, rank):
    count = len(parts)
    return pl.pallas_call(
        gather_kernel,
        out_shape=jax.ShapeDtypeStruct((count,) + parts[0].shape, f32),
        in_specs=[pl.BlockSpec(memory_space=pltpu.SMEM)]
        + [pl.BlockSpec(memory_space=pltpu.VMEM)] * count,
        out_specs=pl.BlockSpec(memory_space=pl.ANY),
        scratch_shapes=[pltpu.SemaphoreType.DMA((count,))],
        compiler_params=pltpu.CompilerParams(vmem_limit_bytes=8 * 2**20),
        cost_estimate=pl.CostEstimate(
            flops=0, bytes_accessed=8 * count * parts[0].size, transcendentals=0
        ),
        name="gather_parts",
    )(rank.reshape(1), *parts)


def finish_kernel(rank_ref, *refs):
    *got_refs, _, rec_ref, out_ref, values_ref, active_ref, sems = refs
    rays = len(got_refs)
    slots = values_ref.shape[1]
    slabs = active_ref.shape[0]
    slices = values_ref.shape[0] // rays
    lead = slices * slots
    for d, got_ref in enumerate(reversed(got_refs)):
        rows = pl.ds(pl.multiple_of((rank_ref[0] ^ d) * slices, slices), slices)
        values_ref[rows] = got_ref[0:lead, :].reshape(slices, slots, VOX)
        for k in range(slabs):
            begin = lead + k * slices
            active_ref[k, rows, :] = got_ref[begin : begin + slices, :]
    offset = (out_ref.shape[2] - ACTIVE) // 2
    copies = [
        pltpu.make_async_copy(values_ref, rec_ref, sems.at[0]),
        pltpu.make_async_copy(
            active_ref, out_ref.at[:, :, offset : offset + ACTIVE], sems.at[1]
        ),
    ]
    for copy in copies:
        copy.start()
    for copy in copies:
        copy.wait()


def finish(pieces, sinogram, rank, shape):
    slabs, slab_rows, _ = sinogram.shape
    hbm = pl.BlockSpec(memory_space=pltpu.HBM)
    return pl.pallas_call(
        finish_kernel,
        out_shape=(
            jax.ShapeDtypeStruct(shape, f32),
            jax.ShapeDtypeStruct(sinogram.shape, f32),
        ),
        in_specs=[pl.BlockSpec(memory_space=pltpu.SMEM)]
        + [pl.BlockSpec(memory_space=pltpu.VMEM)] * len(pieces)
        + [hbm],
        out_specs=[hbm, hbm],
        scratch_shapes=[
            pltpu.VMEM(shape, f32),
            pltpu.VMEM((slabs, slab_rows, ACTIVE), f32),
            pltpu.SemaphoreType.DMA((2,)),
        ],
        input_output_aliases={len(pieces) + 1: 1},
        compiler_params=pltpu.CompilerParams(vmem_limit_bytes=8 * 2**20),
        cost_estimate=pl.CostEstimate(
            flops=0, bytes_accessed=8 * len(pieces) * pieces[0].size, transcendentals=0
        ),
        name="finish",
    )(rank.reshape(1), *reversed(pieces), sinogram)


def exchange(pieces, axis):
    count = len(pieces)
    results = list(pieces)
    for d in range(count - 1, 0, -1):
        results[d] = lax.ppermute(pieces[d], axis, [(i, i ^ d) for i in range(count)])
    return results


def local(intensity, angles, volume, vol_list):
    n_slab = lax.axis_size("slab")
    n_ray = lax.axis_size("ray")
    devices = n_slab * n_ray
    height, band = intensity.shape[2:]
    slices = height // devices
    slots = volume.shape[1]
    count = angles.shape[0] * angles.shape[1]
    step_size = relax * ROI / count
    rank = lax.axis_index("slab")
    ray_rank = lax.axis_index("ray")
    padded = -(-slices // ROWS) * ROWS

    def to_all(values, axes):
        return lax.all_to_all(values, axes, split_axis=0, concat_axis=0, tiled=True)

    own_volume = to_all(volume.reshape(n_ray, slices * slots, VOX), "ray")
    *parts, active = paganin(intensity.reshape(height, band), rank, n_slab)
    active, own_volume = lax.optimization_barrier((active, own_volume))
    own_rays = to_all(active.reshape(devices, slices, ACTIVE), ("slab", "ray"))
    if padded != slices:
        more = padded - slices
        own_volume = jnp.pad(own_volume, ((0, 0), (0, more * slots), (0, 0)))
        own_rays = jnp.pad(own_rays, ((0, 0), (0, more), (0, 0)))

    angles, vol_list, own_volume, parts = lax.optimization_barrier(
        (angles, vol_list, own_volume, parts)
    )
    sirt = Sirt(angles.reshape(-1), vol_list, padded, slots, n_ray, step_size)
    start, predicted, gain = sirt.first(own_volume)
    own_rays, parts, start = lax.optimization_barrier((own_rays, parts, start))
    parts = exchange(parts, "slab")
    pieces = sirt.second(ray_rank, own_volume, start, predicted, gain, own_rays)
    pieces, parts = lax.optimization_barrier((pieces, parts))
    if padded != slices:
        narrow = []
        for piece in pieces:
            lower = piece[padded * slots :].reshape(n_slab, padded, ACTIVE)[:, :slices]
            lower = lower.reshape(n_slab * slices, ACTIVE)
            narrow.append(jnp.concatenate([piece[: slices * slots], lower], axis=0))
        pieces = narrow
    pieces = exchange(pieces, "ray")
    sinogram = gather_parts(parts, rank)
    if padded == slices:
        reconstruction, residual = finish(pieces, sinogram, ray_rank, volume.shape)
    else:
        order = ray_rank ^ jnp.arange(n_ray, dtype=jnp.int32)
        pieces = jnp.take(jnp.stack(pieces), order, axis=0)
        reconstruction = pieces[:, : slices * slots].reshape(volume.shape)
        lower = pieces[:, slices * slots :].reshape(n_ray, n_slab, slices, ACTIVE)
        lower = jnp.transpose(lower, (1, 0, 2, 3)).reshape(n_slab, n_ray * slices, ACTIVE)
        begin = (band - ACTIVE) // 2
        residual = lax.dynamic_update_slice(sinogram, lower, (0, 0, begin))
    return (reconstruction, residual[:, None])


def solution(mesh):
    placed = (P("slab", "ray", None, None), P(), P("slab", "ray", None), P())
    return jax.shard_map(
        local,
        mesh=mesh,
        in_specs=placed,
        out_specs=(P("slab", "ray", None), P(None, "ray", "slab", None)),
        check_vma=False,
    )
```

```python
import functools
import math

import jax
import jax.numpy as jnp
import ml_dtypes
import numpy as np
from jax import lax
from jax.experimental import pallas as pl
from jax.experimental.pallas import tpu as pltpu
from jax.sharding import PartitionSpec as P

BAND = 2048
PGRID = 8
ROI = 128
SIDE = 16
VOX = SIDE * SIDE
WIN = 24
ACTIVE = 256
LANES = 128
ROWS = 8
SPLIT = 64
GROUP = 8
CYCLE = 4

paganin_strength = 10.0
relax = 1.8
row_floor = 0.25

bf16 = jnp.bfloat16
f32 = jnp.float32


def halves(values):
    high = values.astype(bf16)
    low = (values - high.astype(f32)).astype(bf16)
    return high, low


def thirds(values):
    high = values.astype(bf16)
    rest = values - high.astype(f32)
    middle = rest.astype(bf16)
    low = (rest - middle.astype(f32)).astype(bf16)
    return high, middle, low


def dot(left, right):
    return jnp.dot(left, right, preferred_element_type=f32)


def repeat(count, body, unroll):
    unroll = math.gcd(count, unroll)

    def several(index, carry):
        for step in range(unroll):
            body(index * unroll + step)
        return carry

    lax.fori_loop(0, count // unroll, several, 0)


def filter_tables(height):
    index = np.arange(height)
    phase = 2.0 * np.pi * (np.outer(index, index) % height) / height
    cas = (np.cos(phase) + np.sin(phase)) / math.sqrt(height)
    row_freq = 2.0 - 2.0 * np.cos(2.0 * np.pi * index / height)
    middle = (1.0 + paganin_strength * row_freq) / paganin_strength + 2.0
    rho = (middle - np.sqrt(middle * middle - 4.0)) / 2.0
    return np.concatenate([cas, np.repeat(rho[None, :], ROWS, axis=0)], axis=0).astype(np.float32)


def chunk_carry(ends, power, forward):
    shift = 1
    for _ in range(3):
        ends = ends + power * pltpu.roll(ends, shift if forward else ROWS - shift, 0)
        power = power * power
        shift *= 2
    return pltpu.roll(ends, 1 if forward else ROWS - 1, 0) / (1.0 - power)


def filter_kernel(rank_ref, source_ref, given_ref, *refs):
    *part_refs, active_ref, image_ref, table_ref, out_ref, spec_ref, up_ref, down_ref = refs[:-2]
    sems, out_sems = refs[-2:]
    height, width = image_ref.shape
    rank = rank_ref[0]
    share = height // len(part_refs)
    length = width // ROWS
    blocks = height // LANES
    unroll = 8
    copies = []
    for c in range(ROWS):
        columns = slice(c * length, (c + 1) * length)
        copies.append(
            pltpu.make_async_copy(
                source_ref.at[:, columns], image_ref.at[:, columns], sems.at[c]
            )
        )
    given = pltpu.make_async_copy(given_ref, table_ref, sems.at[ROWS])
    copies[0].start()
    given.start()
    copies[1].start()
    given.wait()
    cas_high, cas_low = halves(table_ref[0:height, :])
    rho_all = table_ref[height : height + ROWS, :]
    rhos = [rho_all[:, b * LANES : (b + 1) * LANES] for b in range(blocks)]
    zeros = [jnp.zeros((ROWS, LANES), f32)] * blocks

    def transform(values):
        high, low = halves(values)
        return dot(high, cas_high) + dot(low, cas_high) + dot(high, cas_low)

    for c in range(ROWS):
        copies[c].wait()
        if c + 2 < ROWS:
            copies[c + 2].start()
        image = 1.0 - image_ref[:, c * length : (c + 1) * length]
        spectrum = transform(jnp.transpose(image))
        for b in range(blocks):
            spec_ref[b, pl.ds(c, length, stride=ROWS), :] = spectrum[
                :, b * LANES : (b + 1) * LANES
            ]

    def rows(position):
        return pl.ds(pl.multiple_of(position * ROWS, ROWS), ROWS)

    def advance(position, ups, downs):
        ups = [spec_ref[b, rows(position), :] + rhos[b] * ups[b] for b in range(blocks)]
        back = length - 1 - position
        downs = [spec_ref[b, rows(back), :] + rhos[b] * downs[b] for b in range(blocks)]
        return ups, downs

    def sweep(index, carry):
        ups, downs = carry
        for step in range(unroll):
            ups, downs = advance(index * unroll + step, ups, downs)
        return ups, downs

    ups, downs = lax.fori_loop(0, length // unroll, sweep, (zeros, zeros))
    powers = list(rhos)
    for _ in range(int(math.log2(length))):
        powers = [power * power for power in powers]
    ups = [chunk_carry(ups[b], powers[b], True) for b in range(blocks)]
    downs = [chunk_carry(downs[b], powers[b], False) for b in range(blocks)]
    scales = [rho / (paganin_strength * (1.0 - rho * rho)) for rho in rhos]

    def outer(index, carry):
        ups, downs = carry
        for step in range(unroll):
            position = index * unroll + step
            ups, downs = advance(position, ups, downs)
            for b in range(blocks):
                up_ref[b, rows(position), :] = ups[b]
                down_ref[b, rows(position), :] = downs[b]
        return ups, downs

    def inner(index, carry):
        ups, downs = carry
        for step in range(unroll):
            position = index * unroll + step
            back = length - 1 - position
            ups, downs = advance(position, ups, downs)
            for b in range(blocks):
                here = ups[b] + down_ref[b, rows(back), :] - spec_ref[b, rows(position), :]
                there = downs[b] + up_ref[b, rows(back), :] - spec_ref[b, rows(back), :]
                up_ref[b, rows(position), :] = here * scales[b]
                up_ref[b, rows(back), :] = there * scales[b]
        return ups, downs

    half = length // 2 // unroll
    carry = lax.fori_loop(0, half, outer, (ups, downs))
    lax.fori_loop(half, 2 * half, inner, carry)

    offset = (width - ACTIVE) // 2
    sent = []
    for c in range(ROWS):
        spectrum = jnp.concatenate(
            [up_ref[b, pl.ds(c, length, stride=ROWS), :] for b in range(blocks)], axis=1
        )
        filtered = 1.0 - jnp.transpose(transform(spectrum))
        columns = slice(c * length, (c + 1) * length)
        out_ref[:, columns] = -jnp.log(filtered)
        for d, part_ref in enumerate(part_refs):
            rows = pl.ds(pl.multiple_of((rank ^ d) * share, share), share)
            sent.append(
                pltpu.make_async_copy(
                    out_ref.at[rows, columns], part_ref.at[:, columns], out_sems.at[c, d]
                )
            )
            sent[-1].start()
    active_ref[...] = out_ref[:, offset : offset + ACTIVE]
    for copy in sent:
        copy.wait()


def paganin(image, rank, parts):
    height, width = image.shape
    blocks = height // LANES
    return pl.pallas_call(
        filter_kernel,
        out_shape=[jax.ShapeDtypeStruct((height // parts, width), f32)] * parts
        + [jax.ShapeDtypeStruct((height, ACTIVE), f32)],
        in_specs=[pl.BlockSpec(memory_space=pltpu.SMEM)]
        + [pl.BlockSpec(memory_space=pltpu.HBM)] * 2,
        out_specs=[pl.BlockSpec(memory_space=pltpu.HBM)] * parts
        + [pl.BlockSpec(memory_space=pltpu.VMEM)],
        scratch_shapes=[
            pltpu.VMEM((height, width), f32),
            pltpu.VMEM((height + ROWS, height), f32),
            pltpu.VMEM((height, width), f32),
            pltpu.VMEM((blocks, width, LANES), f32),
            pltpu.VMEM((blocks, width, LANES), f32),
            pltpu.VMEM((blocks, width // 2, LANES), f32),
            pltpu.SemaphoreType.DMA((ROWS + 1,)),
            pltpu.SemaphoreType.DMA((ROWS, parts)),
        ],
        compiler_params=pltpu.CompilerParams(vmem_limit_bytes=58 * 2**20),
        cost_estimate=pl.CostEstimate(
            flops=64 * height * height * width,
            bytes_accessed=8 * height * width,
            transcendentals=height * width,
        ),
        name="paganin",
    )(rank.reshape(1), image, jnp.asarray(filter_tables(height)))


def reversed_exact(values, flip):
    return sum(dot(part, flip) for part in thirds(values))


class Weights:
    def __init__(self, along_ref, place_ref, angles, chunk):
        self.along_ref = along_ref
        self.place_ref = place_ref
        self.angles = angles
        self.chunk = chunk
        self.ray = lax.broadcasted_iota(jnp.int32, (ROWS, VOX), 0).astype(f32)

    def prepare(self, shift_x_ref, shift_y_ref, cos_ref, sin_ref):
        def along_angle(t):
            self.along_ref[t] = shift_x_ref[...] * cos_ref[t] + shift_y_ref[...] * sin_ref[t]

        repeat(self.angles, along_angle, 8)

    def make(self, q, c, ref):
        for two in range(self.chunk // 2):
            pieces = []
            for t in (2 * two, 2 * two + 1):
                angle = c * self.chunk + t
                along = self.along_ref[angle] + self.place_ref[q * self.angles + angle]
                base = self.ray - along
                for group in range(WIN // ROWS):
                    distance = base + float(group * ROWS)
                    pieces.append(jnp.maximum(0.0, 1.0 - jnp.abs(distance)))
            high, low = halves(jnp.concatenate(pieces, axis=0))
            ref[2 * two * WIN : (2 * two + 2) * WIN, 0:VOX] = high
            ref[2 * two * WIN : (2 * two + 2) * WIN, VOX : 2 * VOX] = low


def ray_operand(values, sums_too):
    high, low = halves(values)
    rows = [
        jnp.concatenate([high, high], axis=1),
        jnp.concatenate([low, jnp.zeros_like(low)], axis=1),
    ]
    if sums_too:
        rows.append(jnp.ones((values.shape[0], 2 * VOX), bf16))
    return jnp.concatenate(rows, axis=0)


def project_pair(held, operand, q, c, both, sizes, tile_ref, turn_ref, acc_ref):
    angles, chunk = sizes[:2]
    rows = acc_ref.shape[2]
    sums = lax.dot_general(
        operand, held, (((1,), (1,)), ((), ())), preferred_element_type=f32
    )
    total = sums[0:both] + sums[both : 2 * both]
    if rows != both:
        total = jnp.concatenate([total, sums[2 * both : 2 * both + ROWS]], axis=0)
    lane = lax.broadcasted_iota(jnp.int32, (rows, LANES), 1)
    for begin in range(0, chunk, GROUP):
        places = []
        for t in range(begin, min(begin + GROUP, chunk)):
            index = q * angles + c * chunk + t
            first = t * WIN // LANES
            last = (t * WIN + WIN - 1) // LANES
            low = t * WIN - first * LANES
            high = low + WIN
            piece = total[:, first * LANES : (first + 1) * LANES]
            if first == last:
                piece = jnp.where((lane >= low) & (lane < high), piece, 0.0)
            else:
                other = total[:, last * LANES : (last + 1) * LANES]
                piece = jnp.where(
                    lane >= low, piece, jnp.where(lane < high - LANES, other, 0.0)
                )
            tile = tile_ref[index]
            angle = c * chunk + t
            piece = pltpu.roll(piece, (LANES - turn_ref[index]) % LANES, 1)
            places.append((angle, tile, acc_ref[angle, tile] + piece))
        for angle, tile, values in places:
            acc_ref[angle, tile] = values


def project_rows(held, operand, q, c, sizes, offset_ref, acc_ref):
    angles, chunk = sizes[:2]
    spare = jnp.zeros((LANES - operand.shape[0], operand.shape[1]), bf16)
    operand = jnp.concatenate([operand, spare], axis=0)
    sums = lax.dot_general(
        held, operand, (((1,), (1,)), ((), ())), preferred_element_type=f32
    )
    for begin in range(0, chunk, GROUP):
        places = []
        for t in range(begin, min(begin + GROUP, chunk)):
            angle = c * chunk + t
            rows = pl.ds(offset_ref[q * angles + angle], WIN)
            values = acc_ref[angle, rows, :] + sums[t * WIN : (t + 1) * WIN, :]
            places.append((angle, rows, values))
        for angle, rows, values in places:
            acc_ref[angle, rows, :] = values


def spread_rays(acc_ref, direct_ref, mirror_ref, total_ref, slices):
    both = 2 * slices

    def spread(t):
        rows = jnp.transpose(acc_ref[t]) * (1.0 / ROI)
        direct_ref[t] = rows[0:slices] + rows[both : both + slices]
        mirror_ref[t] = rows[slices:both] + rows[both + slices : 2 * both]
        if total_ref is not None:
            total_ref[t] = rows[2 * both : 2 * both + slices]

    repeat(acc_ref.shape[0], spread, 8)


def join_tiles(acc_ref, rows):
    lane = lax.broadcasted_iota(jnp.int32, (acc_ref.shape[0], ROWS, LANES), 2)
    middle = pltpu.roll(acc_ref[:, 1, rows, :], SPLIT, 2)
    left = acc_ref[:, 0, rows, :] + jnp.where(lane >= SPLIT, middle, 0.0)
    right = acc_ref[:, 2, rows, :] + jnp.where(lane < SPLIT, middle, 0.0)
    return jnp.concatenate([left, right], axis=2) * (1.0 / ROI)


def turn_rays(values, flip):
    shape = values.shape
    return reversed_exact(values.reshape(-1, shape[-1]), flip).reshape(shape)


def fill_windows(weighted, flip, window_ref):
    angles, slices, _ = weighted.shape
    high, low = halves(weighted.reshape(angles * slices, ACTIVE))
    mirrored = (dot(high, flip) + dot(low, flip)).reshape(weighted.shape)
    lane = lax.broadcasted_iota(jnp.int32, (angles, slices, LANES), 2)
    for part, source in enumerate((weighted, mirrored)):
        rows = slice(part * slices, (part + 1) * slices)
        left = source[:, :, 0:LANES]
        right = source[:, :, LANES : 2 * LANES]
        window_ref[:, 0, rows, :] = left
        window_ref[:, 2, rows, :] = right
        mixed = jnp.where(lane >= SPLIT, left, right)
        window_ref[:, 1, rows, :] = pltpu.roll(mixed, SPLIT, 2)


def update_pair(held, q, c, sizes, window_ref, tile_ref, turn_ref):
    angles, chunk = sizes[:2]
    both = window_ref.shape[2]
    lane_rows = lax.broadcasted_iota(jnp.int32, (both, LANES), 1)
    tiles = [None] * (-(-chunk * WIN // LANES))
    for t in range(chunk):
        index = q * angles + c * chunk + t
        piece = pltpu.roll(window_ref[c * chunk + t, tile_ref[index]], turn_ref[index], 1)
        begin = t * WIN
        for place in range(begin // LANES, (begin + WIN - 1) // LANES + 1):
            if tiles[place] is None:
                tiles[place] = piece
            else:
                tiles[place] = jnp.where(
                    lane_rows >= begin - place * LANES, piece, tiles[place]
                )
    high, low = halves(jnp.concatenate(tiles, axis=1))
    sums = dot(jnp.concatenate([high, low], axis=0), held)
    return sums[0:both, 0:VOX] + sums[both:, 0:VOX] + sums[0:both, VOX:]


def first_kernel(
    sizes,
    place_ref,
    offset_ref,
    slot_ref,
    cos_ref,
    sin_ref,
    vol_ref,
    flip_ref,
    shift_x_ref,
    shift_y_ref,
    kept_ref,
    predicted_ref,
    gain_ref,
    *refs,
):
    held_refs = refs[:CYCLE]
    acc_ref, along_ref, half_ref, mirror_ref, start_ref, sem = refs[CYCLE:]
    angles, chunk, slots = sizes
    patches = slot_ref.shape[0]
    pairs, both, _ = start_ref.shape
    slices = both // 2
    flip = flip_ref[...]

    def slot_values(patch):
        slot = slot_ref[patch]
        rows = pl.ds(slot % slots, slices, stride=slots)
        return jnp.concatenate(
            [half_ref[part, slot // slots, rows, :] for part in range(2)], axis=1
        )

    for part in range(2):
        half_ref[part] = vol_ref[:, :, part * LANES : (part + 1) * LANES]

    def order(q):
        start_ref[q, 0:slices, :] = slot_values(q)
        mirror_ref[q] = slot_values(patches - 1 - q)

    repeat(pairs, order, 8)
    start_ref[:, slices:both, :] = turn_rays(mirror_ref[0:pairs], flip)
    weights = Weights(along_ref, place_ref, angles, chunk)
    weights.prepare(shift_x_ref, shift_y_ref, cos_ref, sin_ref)
    acc_ref[...] = jnp.zeros(acc_ref.shape, f32)

    kept = pltpu.make_async_copy(start_ref, kept_ref, sem)
    kept.start()
    chunks = angles // chunk

    def cycle(index, carry):
        for step in range(CYCLE):
            q = index * CYCLE + step
            operand = ray_operand(start_ref[q], True)
            for c in range(chunks):
                more = jnp.minimum(q + (c + 1) // chunks, pairs - 1)
                after = (step * chunks + c + 1) % CYCLE
                weights.make(more, (c + 1) % chunks, held_refs[after])
                here = held_refs[(step * chunks + c) % CYCLE][...]
                project_rows(here, operand, q, c, sizes, offset_ref, acc_ref)
        return carry

    weights.make(0, 0, held_refs[0])
    lax.fori_loop(0, pairs // CYCLE, cycle, 0)
    spread_rays(acc_ref, predicted_ref, mirror_ref, gain_ref, slices)
    direct, mirror, weight_sums = predicted_ref[...], mirror_ref[0:angles], gain_ref[...]
    predicted_ref[...] = direct + turn_rays(mirror, flip)
    direct = weight_sums
    gain_ref[...] = 1.0 / jnp.maximum(direct + turn_rays(direct, flip), row_floor)
    kept.wait()


def second_kernel(
    sizes,
    step_size,
    rank_ref,
    place_ref,
    tile_ref,
    turn_ref,
    slot_ref,
    cos_ref,
    sin_ref,
    vol_ref,
    predicted_ref,
    gain_ref,
    sino_ref,
    flip_ref,
    shift_x_ref,
    shift_y_ref,
    kept_ref,
    *refs,
):
    angles, chunk, slots = sizes
    rays = vol_ref.shape[0]
    out_refs, refs = refs[:rays], refs[rays:]
    held_refs = refs[:CYCLE]
    acc_ref, along_ref, direct_ref, mirror_ref, window_ref, update_ref, half_ref = refs[
        CYCLE:-2
    ]
    start_ref, sem = refs[-2:]
    kept = pltpu.make_async_copy(kept_ref, start_ref, sem)
    kept.start()
    patches = slot_ref.shape[0]
    pairs, both, _ = start_ref.shape
    slices = both // 2
    flip = flip_ref[...]
    weights = Weights(along_ref, place_ref, angles, chunk)
    weights.prepare(shift_x_ref, shift_y_ref, cos_ref, sin_ref)
    chunks = angles // chunk
    windows = (sizes, window_ref, tile_ref, turn_ref)
    windows_out = (both, sizes, tile_ref, turn_ref, acc_ref)
    fill_windows(
        (sino_ref[...] - predicted_ref[...]) * gain_ref[...] * (1.0 / ROI), flip, window_ref
    )
    acc_ref[...] = jnp.zeros(acc_ref.shape, f32)
    kept.wait()

    def advance(q, held):
        total = update_pair(held, q, 0, *windows)
        update_ref[q] = total
        return start_ref[q] + step_size * total

    def forward(values, q, held):
        project_pair(held, ray_operand(values, False), q, 0, *windows_out)

    def cycle(index, values):
        for step in range(CYCLE):
            q = index * CYCLE + step
            after = (step + 1) % CYCLE
            before = (step - 1) % CYCLE
            later = index + (step + 1) // CYCLE
            earlier = index if step else jnp.maximum(index - 1, 0)
            weights.make(jnp.minimum(q + 1, pairs - 1), 0, held_refs[after].at[later])
            new_values = advance(q, held_refs[step][index])
            forward(values, jnp.maximum(q - 1, 0), held_refs[before][earlier])
            values = new_values
        return values

    def all_chunks(q, body):
        for c in range(chunks):
            weights.make(q, c, held_refs[0].at[0])
            body(c, held_refs[0][0])

    def plain_update(q, carry):
        update_ref[q] = jnp.zeros(update_ref.shape[1:], f32)

        def add(c, held):
            update_ref[q] = update_ref[q] + update_pair(held, q, c, *windows)

        all_chunks(q, add)
        return carry

    def plain_forward(q, carry):
        operand = ray_operand(start_ref[q] + step_size * update_ref[q], False)
        all_chunks(
            q,
            lambda c, held: project_pair(held, operand, q, c, *windows_out),
        )
        return carry

    if chunks == 1:
        held_refs[CYCLE - 1][0] = jnp.zeros(held_refs[CYCLE - 1].shape[1:], bf16)
        weights.make(0, 0, held_refs[0].at[0])
        values = lax.fori_loop(0, pairs // CYCLE, cycle, jnp.zeros((both, VOX), f32))
        forward(values, pairs - 1, held_refs[CYCLE - 1][pairs // CYCLE - 1])
    else:
        lax.fori_loop(0, pairs, plain_update, 0)
        lax.fori_loop(0, pairs, plain_forward, 0)

    direct, mirror = (
        join_tiles(acc_ref, slice(part * ROWS, (part + 1) * ROWS)) for part in range(2)
    )
    direct_ref[...] = sino_ref[...] - direct - turn_rays(mirror, flip)
    fill_windows(direct_ref[...] * gain_ref[...] * (1.0 / ROI), flip, window_ref)

    def last_cycle(index, carry):
        for step in range(CYCLE):
            q = index * CYCLE + step
            total = update_pair(held_refs[step][index], q, 0, *windows)
            update_ref[q] = (update_ref[q] + total) * step_size
        return carry

    def plain_last(q, carry):
        def add(c, held):
            update_ref[q] = update_ref[q] + update_pair(held, q, c, *windows)

        all_chunks(q, add)
        update_ref[q] = update_ref[q] * step_size
        return carry

    if chunks == 1:
        lax.fori_loop(0, pairs // CYCLE, last_cycle, 0)
    else:
        lax.fori_loop(0, pairs, plain_last, 0)

    mirror_ref[0:pairs] = turn_rays(update_ref[:, slices:both, :], flip)
    for part in range(2):
        half_ref[part] = vol_ref[:, :, part * LANES : (part + 1) * LANES]

    def finish(q):
        for patch, update in (
            (q, update_ref[q, 0:slices, :]),
            (patches - 1 - q, mirror_ref[q]),
        ):
            slot = slot_ref[patch]
            rows = pl.ds(slot % slots, slices, stride=slots)
            for part in range(2):
                half_ref[part, slot // slots, rows, :] = (
                    half_ref[part, slot // slots, rows, :]
                    + update[:, part * LANES : (part + 1) * LANES]
                )

    repeat(pairs, finish, 8)
    lead = slices * slots
    for d, out_ref in enumerate(out_refs):
        ray = rank_ref[0] ^ d
        for part in range(2):
            out_ref[0:lead, part * LANES : (part + 1) * LANES] = half_ref[part, ray]
        for k in range(angles // rays):
            begin = lead + k * slices
            out_ref[begin : begin + slices, :] = direct_ref[k * rays + ray]


def call(kernel, name, inputs, held_in, held_out, outputs, scratch, micros):
    smem = pl.BlockSpec(memory_space=pltpu.SMEM)
    vmem = pl.BlockSpec(memory_space=pltpu.VMEM)
    hbm = pl.BlockSpec(memory_space=pltpu.HBM)
    return pl.pallas_call(
        kernel,
        out_shape=[jax.ShapeDtypeStruct(*value) for value in held_out + outputs],
        in_specs=[smem if value.ndim == 1 else vmem for value in inputs] + [hbm] * len(held_in),
        out_specs=[hbm] * len(held_out) + [vmem] * len(outputs),
        scratch_shapes=[pltpu.VMEM(*value) for value in scratch]
        + [pltpu.SemaphoreType.DMA],
        compiler_params=pltpu.CompilerParams(vmem_limit_bytes=52 * 2**20),
        cost_estimate=pl.CostEstimate(
            flops=int(micros * 1e9), bytes_accessed=4 * 2**20, transcendentals=0
        ),
        name=name,
    )(*inputs, *held_in)


class Sirt:
    def __init__(self, theta, vol_list, slices, slots, rays, step_size):
        angles = theta.shape[0]
        patches = vol_list.shape[0]
        pairs = patches // 2
        both = 2 * slices
        chunk = math.gcd(angles, 32)
        self.sizes = (angles, chunk, slots)
        self.step_size = step_size
        self.rays = rays
        self.patches = patches
        centre = (ROI - 1) / 2.0
        ids = np.arange(pairs)
        centre_x = (ids // PGRID * float(SIDE) + (SIDE - 1) / 2.0 - centre).astype(np.float32)
        centre_y = (ids % PGRID * float(SIDE) + (SIDE - 1) / 2.0 - centre).astype(np.float32)
        self.cosine = jnp.cos(theta)
        self.sine = jnp.sin(theta)
        along = (
            centre_x[:, None] * self.cosine[None, :]
            + centre_y[:, None] * self.sine[None, :]
            + 0.5
        )
        whole = jnp.floor(along)
        lead = WIN // 2 - 1
        place = along - whole + float(lead)
        offset = whole.astype(jnp.int32) + (ACTIVE // 2 - 1 - lead)
        tile = jnp.minimum(offset // SPLIT, 2)
        local = jnp.arange(angles, dtype=jnp.int32) % chunk * WIN
        turn = (local[None, :] - offset + tile * SPLIT) % LANES
        self.offset = offset.reshape(-1)
        self.place = place.reshape(-1)
        self.tile = tile.reshape(-1)
        self.turn = turn.reshape(-1)
        ids = jnp.arange(patches, dtype=jnp.int32)
        self.slot = jnp.sum(
            jnp.where(vol_list[None, :] == ids[:, None], ids[None, :], 0), axis=1
        )
        voxel = np.arange(VOX)
        shift_x = np.repeat((voxel // SIDE - (SIDE - 1) / 2.0)[None, :], ROWS, axis=0)
        shift_y = np.repeat((voxel % SIDE - (SIDE - 1) / 2.0)[None, :], ROWS, axis=0)
        flip = np.eye(ACTIVE)[::-1].astype(ml_dtypes.bfloat16)
        self.fixed = [jnp.asarray(flip), jnp.asarray(shift_x, f32), jnp.asarray(shift_y, f32)]
        self.weight = ((chunk * WIN, 2 * VOX), bf16)
        self.held = (pairs // CYCLE + 1 if angles == chunk else 1,) + self.weight[0]
        self.acc = ((angles, 3, both, LANES), f32)
        self.acc_rows = ((angles, ACTIVE, LANES), f32)
        self.along = ((angles, ROWS, VOX), f32)
        self.by_ray = ((angles, slices, ACTIVE), f32)
        self.by_pair = ((pairs, both, VOX), f32)
        self.window = ((angles, 3, both, LANES), f32)
        self.half = ((2, rays, slices * slots, LANES), f32)
        self.mirror = ((max(pairs, angles), slices, ACTIVE), f32)
        self.sent = [((slices * (slots + angles // rays), ACTIVE), f32)] * rays

    def first(self, volume):
        inputs = [self.place, self.offset, self.slot, self.cosine, self.sine, volume]
        return call(
            functools.partial(first_kernel, self.sizes),
            "first",
            inputs + self.fixed,
            [],
            [self.by_pair],
            [self.by_ray, self.by_ray],
            [self.weight] * CYCLE
            + [self.acc_rows, self.along, self.half, self.mirror, self.by_pair],
            14,
        )

    def second(self, rank, volume, start, predicted, gain, sino):
        inputs = [rank.reshape(1), self.place, self.tile, self.turn, self.slot]
        inputs += [self.cosine, self.sine, volume, predicted, gain, sino]
        scratch = [(self.held, bf16)] * CYCLE
        scratch += [self.acc, self.along, self.by_ray, self.mirror, self.window]
        return call(
            functools.partial(second_kernel, self.sizes, self.step_size),
            "second",
            inputs + self.fixed,
            [start],
            [],
            self.sent,
            scratch + [self.by_pair, self.half, self.by_pair],
            26,
        )


def gather_kernel(rank_ref, *refs):
    *part_refs, out_ref, sems = refs
    rank = rank_ref[0]
    copies = [
        pltpu.make_async_copy(part_ref, out_ref.at[rank ^ d], sems.at[d])
        for d, part_ref in enumerate(part_refs)
    ]
    for copy in copies:
        copy.start()
    for copy in copies:
        copy.wait()


def gather_parts(parts, rank):
    count = len(parts)
    return pl.pallas_call(
        gather_kernel,
        out_shape=jax.ShapeDtypeStruct((count,) + parts[0].shape, f32),
        in_specs=[pl.BlockSpec(memory_space=pltpu.SMEM)]
        + [pl.BlockSpec(memory_space=pltpu.VMEM)] * count,
        out_specs=pl.BlockSpec(memory_space=pl.ANY),
        scratch_shapes=[pltpu.SemaphoreType.DMA((count,))],
        compiler_params=pltpu.CompilerParams(vmem_limit_bytes=8 * 2**20),
        cost_estimate=pl.CostEstimate(
            flops=0, bytes_accessed=8 * count * parts[0].size, transcendentals=0
        ),
        name="gather_parts",
    )(rank.reshape(1), *parts)


def finish_kernel(rank_ref, *refs):
    *got_refs, _, rec_ref, out_ref, values_ref, active_ref, sems = refs
    rays = len(got_refs)
    slots = values_ref.shape[1]
    slabs = active_ref.shape[0]
    slices = values_ref.shape[0] // rays
    lead = slices * slots
    for d, got_ref in enumerate(reversed(got_refs)):
        rows = pl.ds(pl.multiple_of((rank_ref[0] ^ d) * slices, slices), slices)
        values_ref[rows] = got_ref[0:lead, :].reshape(slices, slots, VOX)
        for k in range(slabs):
            begin = lead + k * slices
            active_ref[k, rows, :] = got_ref[begin : begin + slices, :]
    offset = (out_ref.shape[2] - ACTIVE) // 2
    copies = [
        pltpu.make_async_copy(values_ref, rec_ref, sems.at[0]),
        pltpu.make_async_copy(
            active_ref, out_ref.at[:, :, offset : offset + ACTIVE], sems.at[1]
        ),
    ]
    for copy in copies:
        copy.start()
    for copy in copies:
        copy.wait()


def finish(pieces, sinogram, rank, shape):
    slabs, slab_rows, _ = sinogram.shape
    hbm = pl.BlockSpec(memory_space=pltpu.HBM)
    return pl.pallas_call(
        finish_kernel,
        out_shape=(
            jax.ShapeDtypeStruct(shape, f32),
            jax.ShapeDtypeStruct(sinogram.shape, f32),
        ),
        in_specs=[pl.BlockSpec(memory_space=pltpu.SMEM)]
        + [pl.BlockSpec(memory_space=pltpu.VMEM)] * len(pieces)
        + [hbm],
        out_specs=[hbm, hbm],
        scratch_shapes=[
            pltpu.VMEM(shape, f32),
            pltpu.VMEM((slabs, slab_rows, ACTIVE), f32),
            pltpu.SemaphoreType.DMA((2,)),
        ],
        input_output_aliases={len(pieces) + 1: 1},
        compiler_params=pltpu.CompilerParams(vmem_limit_bytes=8 * 2**20),
        cost_estimate=pl.CostEstimate(
            flops=0, bytes_accessed=8 * len(pieces) * pieces[0].size, transcendentals=0
        ),
        name="finish",
    )(rank.reshape(1), *reversed(pieces), sinogram)


def exchange(pieces, axis):
    count = len(pieces)
    results = list(pieces)
    for d in range(count - 1, 0, -1):
        results[d] = lax.ppermute(pieces[d], axis, [(i, i ^ d) for i in range(count)])
    return results


def local(intensity, angles, volume, vol_list):
    n_slab = lax.axis_size("slab")
    n_ray = lax.axis_size("ray")
    devices = n_slab * n_ray
    height, band = intensity.shape[2:]
    slices = height // devices
    slots = volume.shape[1]
    count = angles.shape[0] * angles.shape[1]
    step_size = relax * ROI / count
    rank = lax.axis_index("slab")
    ray_rank = lax.axis_index("ray")
    padded = -(-slices // ROWS) * ROWS

    def to_all(values, axes):
        return lax.all_to_all(values, axes, split_axis=0, concat_axis=0, tiled=True)

    own_volume = to_all(volume.reshape(n_ray, slices * slots, VOX), "ray")
    *parts, active = paganin(intensity.reshape(height, band), rank, n_slab)
    active, own_volume = lax.optimization_barrier((active, own_volume))
    own_rays = to_all(active.reshape(devices, slices, ACTIVE), ("slab", "ray"))
    if padded != slices:
        more = padded - slices
        own_volume = jnp.pad(own_volume, ((0, 0), (0, more * slots), (0, 0)))
        own_rays = jnp.pad(own_rays, ((0, 0), (0, more), (0, 0)))

    angles, vol_list, own_volume, parts = lax.optimization_barrier(
        (angles, vol_list, own_volume, parts)
    )
    sirt = Sirt(angles.reshape(-1), vol_list, padded, slots, n_ray, step_size)
    start, predicted, gain = sirt.first(own_volume)
    own_rays, parts, start = lax.optimization_barrier((own_rays, parts, start))
    parts = exchange(parts, "slab")
    pieces = sirt.second(ray_rank, own_volume, start, predicted, gain, own_rays)
    pieces, parts = lax.optimization_barrier((pieces, parts))
    if padded != slices:
        narrow = []
        for piece in pieces:
            lower = piece[padded * slots :].reshape(n_slab, padded, ACTIVE)[:, :slices]
            lower = lower.reshape(n_slab * slices, ACTIVE)
            narrow.append(jnp.concatenate([piece[: slices * slots], lower], axis=0))
        pieces = narrow
    pieces = exchange(pieces, "ray")
    sinogram = gather_parts(parts, rank)
    if padded == slices:
        reconstruction, residual = finish(pieces, sinogram, ray_rank, volume.shape)
    else:
        order = ray_rank ^ jnp.arange(n_ray, dtype=jnp.int32)
        pieces = jnp.take(jnp.stack(pieces), order, axis=0)
        reconstruction = pieces[:, : slices * slots].reshape(volume.shape)
        lower = pieces[:, slices * slots :].reshape(n_ray, n_slab, slices, ACTIVE)
        lower = jnp.transpose(lower, (1, 0, 2, 3)).reshape(n_slab, n_ray * slices, ACTIVE)
        begin = (band - ACTIVE) // 2
        residual = lax.dynamic_update_slice(sinogram, lower, (0, 0, begin))
    return (reconstruction, residual[:, None])


def solution(mesh):
    placed = (P("slab", "ray", None, None), P(), P("slab", "ray", None), P())
    return jax.shard_map(
        local,
        mesh=mesh,
        in_specs=placed,
        out_specs=(P("slab", "ray", None), P(None, "ray", "slab", None)),
        check_vma=False,
    )
```

```python
import functools
import math

import jax
import jax.numpy as jnp
import ml_dtypes
import numpy as np
from jax import lax
from jax.experimental import pallas as pl
from jax.experimental.pallas import tpu as pltpu
from jax.sharding import PartitionSpec as P

BAND = 2048
PGRID = 8
ROI = 128
SIDE = 16
VOX = SIDE * SIDE
WIN = 24
ACTIVE = 256
LANES = 128
ROWS = 8
SPLIT = 64
EDGE = 32
GROUP = 8
CYCLE = 4

paganin_strength = 10.0
relax = 1.8
row_floor = 0.25

bf16 = jnp.bfloat16
f32 = jnp.float32


def halves(values):
    high = values.astype(bf16)
    low = (values - high.astype(f32)).astype(bf16)
    return high, low


def thirds(values):
    high = values.astype(bf16)
    rest = values - high.astype(f32)
    middle = rest.astype(bf16)
    low = (rest - middle.astype(f32)).astype(bf16)
    return high, middle, low


def dot(left, right):
    return jnp.dot(left, right, preferred_element_type=f32)


def repeat(count, body, unroll):
    unroll = math.gcd(count, unroll)

    def several(index, carry):
        for step in range(unroll):
            body(index * unroll + step)
        return carry

    lax.fori_loop(0, count // unroll, several, 0)


def filter_tables(height):
    index = np.arange(height)
    phase = 2.0 * np.pi * (np.outer(index, index) % height) / height
    cas = (np.cos(phase) + np.sin(phase)) / math.sqrt(height)
    row_freq = 2.0 - 2.0 * np.cos(2.0 * np.pi * index / height)
    middle = (1.0 + paganin_strength * row_freq) / paganin_strength + 2.0
    rho = (middle - np.sqrt(middle * middle - 4.0)) / 2.0
    return np.concatenate([cas, np.repeat(rho[None, :], ROWS, axis=0)], axis=0).astype(np.float32)


def chunk_carry(ends, power, forward):
    shift = 1
    for _ in range(3):
        ends = ends + power * pltpu.roll(ends, shift if forward else ROWS - shift, 0)
        power = power * power
        shift *= 2
    return pltpu.roll(ends, 1 if forward else ROWS - 1, 0) / (1.0 - power)


def filter_kernel(rank_ref, source_ref, given_ref, *refs):
    *part_refs, active_ref, image_ref, table_ref, out_ref, spec_ref, up_ref, down_ref = refs[:-2]
    sems, out_sems = refs[-2:]
    height, width = image_ref.shape
    rank = rank_ref[0]
    share = height // len(part_refs)
    length = width // ROWS
    blocks = height // LANES
    unroll = 8
    copies = []
    for c in range(ROWS):
        columns = slice(c * length, (c + 1) * length)
        copies.append(
            pltpu.make_async_copy(
                source_ref.at[:, columns], image_ref.at[:, columns], sems.at[c]
            )
        )
    given = pltpu.make_async_copy(given_ref, table_ref, sems.at[ROWS])
    given.start()
    for copy in copies:
        copy.start()
    given.wait()
    cas_high, cas_low = halves(table_ref[0:height, :])
    rho_all = table_ref[height : height + ROWS, :]
    rhos = [rho_all[:, b * LANES : (b + 1) * LANES] for b in range(blocks)]
    zeros = [jnp.zeros((ROWS, LANES), f32)] * blocks

    def transform(values):
        high, low = halves(values)
        return dot(high, cas_high) + dot(low, cas_high) + dot(high, cas_low)

    for c in range(ROWS):
        copies[c].wait()
        image = 1.0 - image_ref[:, c * length : (c + 1) * length]
        spectrum = transform(jnp.transpose(image))
        for b in range(blocks):
            spec_ref[b, pl.ds(c, length, stride=ROWS), :] = spectrum[
                :, b * LANES : (b + 1) * LANES
            ]

    def rows(position):
        return pl.ds(pl.multiple_of(position * ROWS, ROWS), ROWS)

    def advance(position, ups, downs):
        ups = [spec_ref[b, rows(position), :] + rhos[b] * ups[b] for b in range(blocks)]
        back = length - 1 - position
        downs = [spec_ref[b, rows(back), :] + rhos[b] * downs[b] for b in range(blocks)]
        return ups, downs

    def sweep(index, carry):
        ups, downs = carry
        for step in range(unroll):
            ups, downs = advance(index * unroll + step, ups, downs)
        return ups, downs

    ups, downs = lax.fori_loop(0, length // unroll, sweep, (zeros, zeros))
    powers = list(rhos)
    for _ in range(int(math.log2(length))):
        powers = [power * power for power in powers]
    ups = [chunk_carry(ups[b], powers[b], True) for b in range(blocks)]
    downs = [chunk_carry(downs[b], powers[b], False) for b in range(blocks)]
    scales = [rho / (paganin_strength * (1.0 - rho * rho)) for rho in rhos]

    def outer(index, carry):
        ups, downs = carry
        for step in range(unroll):
            position = index * unroll + step
            ups, downs = advance(position, ups, downs)
            for b in range(blocks):
                up_ref[b, rows(position), :] = ups[b]
                down_ref[b, rows(position), :] = downs[b]
        return ups, downs

    def inner(index, carry):
        ups, downs = carry
        for step in range(unroll):
            position = index * unroll + step
            back = length - 1 - position
            ups, downs = advance(position, ups, downs)
            for b in range(blocks):
                here = ups[b] + down_ref[b, rows(back), :] - spec_ref[b, rows(position), :]
                there = downs[b] + up_ref[b, rows(back), :] - spec_ref[b, rows(back), :]
                up_ref[b, rows(position), :] = here * scales[b]
                up_ref[b, rows(back), :] = there * scales[b]
        return ups, downs

    half = length // 2 // unroll
    carry = lax.fori_loop(0, half, outer, (ups, downs))
    lax.fori_loop(half, 2 * half, inner, carry)

    offset = (width - ACTIVE) // 2
    sent = []
    for c in range(ROWS):
        spectrum = jnp.concatenate(
            [up_ref[b, pl.ds(c, length, stride=ROWS), :] for b in range(blocks)], axis=1
        )
        filtered = 1.0 - jnp.transpose(transform(spectrum))
        columns = slice(c * length, (c + 1) * length)
        out_ref[:, columns] = -jnp.log(filtered)
        for d, part_ref in enumerate(part_refs):
            rows = pl.ds(pl.multiple_of((rank ^ d) * share, share), share)
            sent.append(
                pltpu.make_async_copy(
                    out_ref.at[rows, columns], part_ref.at[:, columns], out_sems.at[c, d]
                )
            )
            sent[-1].start()
        if c == (offset + ACTIVE - 1) // length:
            columns = slice(offset, offset + ACTIVE)
            sent.append(
                pltpu.make_async_copy(out_ref.at[:, columns], active_ref, sems.at[0])
            )
            sent[-1].start()
    for copy in sent:
        copy.wait()


def paganin(image, rank, parts):
    height, width = image.shape
    blocks = height // LANES
    return pl.pallas_call(
        filter_kernel,
        out_shape=[jax.ShapeDtypeStruct((height // parts, width), f32)] * parts
        + [jax.ShapeDtypeStruct((height, ACTIVE), f32)],
        in_specs=[pl.BlockSpec(memory_space=pltpu.SMEM)]
        + [pl.BlockSpec(memory_space=pltpu.HBM)] * 2,
        out_specs=[pl.BlockSpec(memory_space=pltpu.HBM)] * (parts + 1),
        scratch_shapes=[
            pltpu.VMEM((height, width), f32),
            pltpu.VMEM((height + ROWS, height), f32),
            pltpu.VMEM((height, width), f32),
            pltpu.VMEM((blocks, width, LANES), f32),
            pltpu.VMEM((blocks, width, LANES), f32),
            pltpu.VMEM((blocks, width // 2, LANES), f32),
            pltpu.SemaphoreType.DMA((ROWS + 1,)),
            pltpu.SemaphoreType.DMA((ROWS, parts)),
        ],
        compiler_params=pltpu.CompilerParams(vmem_limit_bytes=58 * 2**20),
        cost_estimate=pl.CostEstimate(
            flops=64 * height * height * width,
            bytes_accessed=8 * height * width,
            transcendentals=height * width,
        ),
        name="paganin",
    )(rank.reshape(1), image, jnp.asarray(filter_tables(height)))


def reversed_exact(values, flip):
    return sum(dot(part, flip) for part in thirds(values))


class Weights:
    def __init__(self, along_ref, place_ref, angles, chunk):
        self.along_ref = along_ref
        self.place_ref = place_ref
        self.angles = angles
        self.chunk = chunk
        self.ray = lax.broadcasted_iota(jnp.int32, (ROWS, VOX), 0).astype(f32)

    def prepare(self, shift_x_ref, shift_y_ref, cos_ref, sin_ref):
        def along_angle(t):
            self.along_ref[t] = shift_x_ref[...] * cos_ref[t] + shift_y_ref[...] * sin_ref[t]

        repeat(self.angles, along_angle, 8)

    def make(self, q, c, ref):
        for two in range(self.chunk // 2):
            pieces = []
            for t in (2 * two, 2 * two + 1):
                angle = c * self.chunk + t
                along = self.along_ref[angle] + self.place_ref[q * self.angles + angle]
                base = self.ray - along
                for group in range(WIN // ROWS):
                    distance = base + float(group * ROWS)
                    pieces.append(jnp.maximum(0.0, 1.0 - jnp.abs(distance)))
            high, low = halves(jnp.concatenate(pieces, axis=0))
            ref[2 * two * WIN : (2 * two + 2) * WIN, 0:VOX] = high
            ref[2 * two * WIN : (2 * two + 2) * WIN, VOX : 2 * VOX] = low


def ray_operand(values, sums_too):
    high, low = halves(values)
    rows = [
        jnp.concatenate([high, high], axis=1),
        jnp.concatenate([low, jnp.zeros_like(low)], axis=1),
    ]
    if sums_too:
        rows.append(jnp.ones((values.shape[0], 2 * VOX), bf16))
    return jnp.concatenate(rows, axis=0)


def project_pair(held, operand, q, c, both, sizes, tile_ref, turn_ref, acc_ref):
    angles, chunk = sizes[:2]
    rows = acc_ref.shape[2]
    sums = lax.dot_general(
        operand, held, (((1,), (1,)), ((), ())), preferred_element_type=f32
    )
    total = sums[0:both] + sums[both : 2 * both]
    if rows != both:
        total = jnp.concatenate([total, sums[2 * both : 2 * both + ROWS]], axis=0)
    lane = lax.broadcasted_iota(jnp.int32, (rows, LANES), 1)
    for begin in range(0, chunk, GROUP):
        places = []
        for t in range(begin, min(begin + GROUP, chunk)):
            index = q * angles + c * chunk + t
            first = t * WIN // LANES
            last = (t * WIN + WIN - 1) // LANES
            low = t * WIN - first * LANES
            high = low + WIN
            piece = total[:, first * LANES : (first + 1) * LANES]
            if first == last:
                piece = jnp.where((lane >= low) & (lane < high), piece, 0.0)
            else:
                other = total[:, last * LANES : (last + 1) * LANES]
                piece = jnp.where(
                    lane >= low, piece, jnp.where(lane < high - LANES, other, 0.0)
                )
            tile = tile_ref[index]
            angle = c * chunk + t
            piece = pltpu.roll(piece, (LANES - turn_ref[index]) % LANES, 1)
            places.append((angle, tile, acc_ref[angle, tile] + piece))
        for angle, tile, values in places:
            acc_ref[angle, tile] = values


def row_operands(values):
    rows = ray_operand(values, True)
    count, width = rows.shape
    spare = jnp.zeros((SPLIT - count, width), bf16)
    empty = jnp.zeros((SPLIT, width), bf16)
    return (
        jnp.concatenate([rows, spare, empty], axis=0),
        jnp.concatenate([empty, rows, spare], axis=0),
    )


def project_rows(held_ref, operands, q, c, sizes, offset_ref, acc_ref):
    angles, chunk = sizes[:2]
    half = chunk // 2
    for begin in range(0, chunk, GROUP):
        sums = lax.dot_general(
            held_ref[begin * WIN : (begin + GROUP) * WIN, :],
            operands[begin // half],
            (((1,), (1,)), ((), ())),
            preferred_element_type=f32,
        )
        places = []
        for t in range(begin, begin + GROUP):
            rows = pl.ds(offset_ref[q * angles + c * chunk + t], WIN)
            piece = sums[(t - begin) * WIN : (t - begin + 1) * WIN, :]
            index = c * half + t % half
            places.append((index, rows, acc_ref[index, rows, :] + piece))
        for index, rows, values in places:
            acc_ref[index, rows, :] = values


def spread_rays(acc_ref, direct_ref, mirror_ref, total_ref, slices, chunk):
    both = 2 * slices
    half = chunk // 2

    def spread(index):
        turned = jnp.transpose(acc_ref[index]) * (1.0 / ROI)
        for part in range(2):
            rows = turned[part * SPLIT : (part + 1) * SPLIT]
            t = index // half * chunk + part * half + index % half
            direct_ref[t] = rows[0:slices] + rows[both : both + slices]
            mirror_ref[t] = rows[slices:both] + rows[both + slices : 2 * both]
            total_ref[t] = rows[2 * both : 2 * both + slices]

    repeat(acc_ref.shape[0], spread, 8)


def join_tiles(acc_ref, rows):
    lane = lax.broadcasted_iota(jnp.int32, (acc_ref.shape[0], ROWS, LANES), 2)
    middle = pltpu.roll(acc_ref[:, 1, rows, :], SPLIT, 2)
    left = acc_ref[:, 0, rows, :] + jnp.where(lane >= SPLIT, middle, 0.0)
    right = acc_ref[:, 2, rows, :] + jnp.where(lane < SPLIT, middle, 0.0)
    return jnp.concatenate([left, right], axis=2) * (1.0 / ROI)


def turn_rays(values, flip):
    shape = values.shape
    return reversed_exact(values.reshape(-1, shape[-1]), flip).reshape(shape)


def fill_windows(weighted, flip, window_ref):
    angles, slices, _ = weighted.shape
    high, low = halves(weighted.reshape(angles * slices, ACTIVE))
    mirrored = (dot(high, flip) + dot(low, flip)).reshape(weighted.shape)
    lane = lax.broadcasted_iota(jnp.int32, (angles, slices, LANES), 2)
    for part, source in enumerate((weighted, mirrored)):
        rows = slice(part * slices, (part + 1) * slices)
        left = source[:, :, 0:LANES]
        right = source[:, :, LANES : 2 * LANES]
        window_ref[:, 0, rows, :] = left
        window_ref[:, 2, rows, :] = right
        mixed = jnp.where(lane >= SPLIT, left, right)
        window_ref[:, 1, rows, :] = pltpu.roll(mixed, SPLIT, 2)


def update_pair(held, q, c, sizes, window_ref, tile_ref, turn_ref):
    angles, chunk = sizes[:2]
    both = window_ref.shape[2]
    lane_rows = lax.broadcasted_iota(jnp.int32, (both, LANES), 1)
    tiles = [None] * (-(-chunk * WIN // LANES))
    for t in range(chunk):
        index = q * angles + c * chunk + t
        piece = pltpu.roll(window_ref[c * chunk + t, tile_ref[index]], turn_ref[index], 1)
        begin = t * WIN
        for place in range(begin // LANES, (begin + WIN - 1) // LANES + 1):
            if tiles[place] is None:
                tiles[place] = piece
            else:
                tiles[place] = jnp.where(
                    lane_rows >= begin - place * LANES, piece, tiles[place]
                )
    high, low = halves(jnp.concatenate(tiles, axis=1))
    sums = dot(jnp.concatenate([high, low], axis=0), held)
    return sums[0:both, 0:VOX] + sums[both:, 0:VOX] + sums[0:both, VOX:]


def first_kernel(
    sizes,
    place_ref,
    offset_ref,
    slot_ref,
    cos_ref,
    sin_ref,
    vol_ref,
    flip_ref,
    shift_x_ref,
    shift_y_ref,
    kept_ref,
    predicted_ref,
    gain_ref,
    *refs,
):
    held_refs = refs[:CYCLE]
    acc_ref, along_ref, half_ref, mirror_ref, start_ref, sem = refs[CYCLE:]
    angles, chunk, slots = sizes
    patches = slot_ref.shape[0]
    pairs, both, _ = start_ref.shape
    slices = both // 2
    flip = flip_ref[...]

    def slot_values(patch):
        slot = slot_ref[patch]
        rows = pl.ds(slot % slots, slices, stride=slots)
        return jnp.concatenate(
            [half_ref[part, slot // slots, rows, :] for part in range(2)], axis=1
        )

    for part in range(2):
        half_ref[part] = vol_ref[:, :, part * LANES : (part + 1) * LANES]

    def order(q):
        start_ref[q, 0:slices, :] = slot_values(q)
        mirror_ref[q] = slot_values(patches - 1 - q)

    repeat(pairs, order, 8)
    start_ref[:, slices:both, :] = turn_rays(mirror_ref[0:pairs], flip)
    weights = Weights(along_ref, place_ref, angles, chunk)
    weights.prepare(shift_x_ref, shift_y_ref, cos_ref, sin_ref)
    acc_ref[...] = jnp.zeros(acc_ref.shape, f32)

    kept = pltpu.make_async_copy(start_ref, kept_ref, sem)
    kept.start()
    chunks = angles // chunk

    def cycle(index, carry):
        for step in range(CYCLE):
            q = index * CYCLE + step
            operands = row_operands(start_ref[q])
            for c in range(chunks):
                more = jnp.minimum(q + (c + 1) // chunks, pairs - 1)
                after = (step * chunks + c + 1) % CYCLE
                weights.make(more, (c + 1) % chunks, held_refs[after])
                here = held_refs[(step * chunks + c) % CYCLE]
                project_rows(here, operands, q, c, sizes, offset_ref, acc_ref)
        return carry

    weights.make(0, 0, held_refs[0])
    lax.fori_loop(0, pairs // CYCLE, cycle, 0)
    spread_rays(acc_ref, predicted_ref, mirror_ref, gain_ref, slices, chunk)
    direct, mirror, weight_sums = predicted_ref[...], mirror_ref[0:angles], gain_ref[...]
    predicted_ref[...] = direct + turn_rays(mirror, flip)
    direct = weight_sums
    gain_ref[...] = 1.0 / jnp.maximum(direct + turn_rays(direct, flip), row_floor)
    kept.wait()


def second_kernel(
    sizes,
    step_size,
    rank_ref,
    place_ref,
    tile_ref,
    turn_ref,
    slot_ref,
    cos_ref,
    sin_ref,
    vol_ref,
    predicted_ref,
    gain_ref,
    sino_ref,
    flip_ref,
    shift_x_ref,
    shift_y_ref,
    kept_ref,
    *refs,
):
    angles, chunk, slots = sizes
    rays = vol_ref.shape[0]
    out_refs, refs = refs[:rays], refs[rays:]
    held_refs = refs[:CYCLE]
    acc_ref, along_ref, direct_ref, mirror_ref, window_ref, update_ref, half_ref = refs[
        CYCLE:-2
    ]
    start_ref, sem = refs[-2:]
    kept = pltpu.make_async_copy(kept_ref, start_ref, sem)
    kept.start()
    patches = slot_ref.shape[0]
    pairs, both, _ = start_ref.shape
    slices = both // 2
    flip = flip_ref[...]
    weights = Weights(along_ref, place_ref, angles, chunk)
    weights.prepare(shift_x_ref, shift_y_ref, cos_ref, sin_ref)
    chunks = angles // chunk
    windows = (sizes, window_ref, tile_ref, turn_ref)
    windows_out = (both, sizes, tile_ref, turn_ref, acc_ref)
    fill_windows(
        (sino_ref[...] - predicted_ref[...]) * gain_ref[...] * (1.0 / ROI), flip, window_ref
    )
    acc_ref[...] = jnp.zeros(acc_ref.shape, f32)
    kept.wait()

    def advance(q, held):
        total = update_pair(held, q, 0, *windows)
        update_ref[q] = total
        return start_ref[q] + step_size * total

    def forward(values, q, held):
        project_pair(held, ray_operand(values, False), q, 0, *windows_out)

    def cycle(index, values):
        for step in range(CYCLE):
            q = index * CYCLE + step
            after = (step + 1) % CYCLE
            before = (step - 1) % CYCLE
            later = index + (step + 1) // CYCLE
            earlier = index if step else jnp.maximum(index - 1, 0)
            weights.make(jnp.minimum(q + 1, pairs - 1), 0, held_refs[after].at[later])
            new_values = advance(q, held_refs[step][index])
            forward(values, jnp.maximum(q - 1, 0), held_refs[before][earlier])
            values = new_values
        return values

    def all_chunks(q, body):
        for c in range(chunks):
            weights.make(q, c, held_refs[0].at[0])
            body(c, held_refs[0][0])

    def plain_update(q, carry):
        update_ref[q] = jnp.zeros(update_ref.shape[1:], f32)

        def add(c, held):
            update_ref[q] = update_ref[q] + update_pair(held, q, c, *windows)

        all_chunks(q, add)
        return carry

    def plain_forward(q, carry):
        operand = ray_operand(start_ref[q] + step_size * update_ref[q], False)
        all_chunks(
            q,
            lambda c, held: project_pair(held, operand, q, c, *windows_out),
        )
        return carry

    if chunks == 1:
        held_refs[CYCLE - 1][0] = jnp.zeros(held_refs[CYCLE - 1].shape[1:], bf16)
        weights.make(0, 0, held_refs[0].at[0])
        values = lax.fori_loop(0, pairs // CYCLE, cycle, jnp.zeros((both, VOX), f32))
        forward(values, pairs - 1, held_refs[CYCLE - 1][pairs // CYCLE - 1])
    else:
        lax.fori_loop(0, pairs, plain_update, 0)
        lax.fori_loop(0, pairs, plain_forward, 0)

    direct, mirror = (
        join_tiles(acc_ref, slice(part * ROWS, (part + 1) * ROWS)) for part in range(2)
    )
    direct_ref[...] = sino_ref[...] - direct - turn_rays(mirror, flip)
    fill_windows(direct_ref[...] * gain_ref[...] * (1.0 / ROI), flip, window_ref)

    def last_cycle(index, carry):
        for step in range(CYCLE):
            q = index * CYCLE + step
            total = update_pair(held_refs[step][index], q, 0, *windows)
            update_ref[q] = (update_ref[q] + total) * step_size
        return carry

    def plain_last(q, carry):
        def add(c, held):
            update_ref[q] = update_ref[q] + update_pair(held, q, c, *windows)

        all_chunks(q, add)
        update_ref[q] = update_ref[q] * step_size
        return carry

    if chunks == 1:
        lax.fori_loop(0, pairs // CYCLE, last_cycle, 0)
    else:
        lax.fori_loop(0, pairs, plain_last, 0)

    mirror_ref[0:pairs] = turn_rays(update_ref[:, slices:both, :], flip)
    for part in range(2):
        half_ref[part] = vol_ref[:, :, part * LANES : (part + 1) * LANES]

    def finish(q):
        for patch, update in (
            (q, update_ref[q, 0:slices, :]),
            (patches - 1 - q, mirror_ref[q]),
        ):
            slot = slot_ref[patch]
            rows = pl.ds(slot % slots, slices, stride=slots)
            for part in range(2):
                half_ref[part, slot // slots, rows, :] = (
                    half_ref[part, slot // slots, rows, :]
                    + update[:, part * LANES : (part + 1) * LANES]
                )

    repeat(pairs, finish, 8)
    lead = slices * slots
    lane = lax.broadcasted_iota(jnp.int32, (slices, LANES), 1)
    for d, out_ref in enumerate(out_refs):
        ray = rank_ref[0] ^ d
        for part in range(2):
            out_ref[0:lead, part * LANES : (part + 1) * LANES] = half_ref[part, ray]
        for k in range(0, angles // rays, 4):
            begin = lead + k // 4 * 3 * slices
            live = [
                pltpu.roll(direct_ref[(k + i) * rays + ray], ACTIVE - EDGE, 1)
                for i in range(4)
            ]
            rest = [part[:, LANES:] for part in live]
            for i in range(2):
                here = begin + i * slices
                out_ref[here : here + slices, 0:LANES] = live[2 * i][:, 0:LANES]
                out_ref[here : here + slices, LANES:] = live[2 * i + 1][:, 0:LANES]
                here = begin + 2 * slices
                out_ref[here : here + slices, i * LANES : (i + 1) * LANES] = jnp.where(
                    lane < SPLIT, rest[2 * i], pltpu.roll(rest[2 * i + 1], SPLIT, 1)
                )


def call(kernel, name, inputs, held_in, held_out, outputs, scratch, micros):
    smem = pl.BlockSpec(memory_space=pltpu.SMEM)
    vmem = pl.BlockSpec(memory_space=pltpu.VMEM)
    hbm = pl.BlockSpec(memory_space=pltpu.HBM)
    return pl.pallas_call(
        kernel,
        out_shape=[jax.ShapeDtypeStruct(*value) for value in held_out + outputs],
        in_specs=[smem if value.ndim == 1 else vmem for value in inputs] + [hbm] * len(held_in),
        out_specs=[hbm] * len(held_out) + [vmem] * len(outputs),
        scratch_shapes=[pltpu.VMEM(*value) for value in scratch]
        + [pltpu.SemaphoreType.DMA],
        compiler_params=pltpu.CompilerParams(vmem_limit_bytes=52 * 2**20),
        cost_estimate=pl.CostEstimate(
            flops=int(micros * 1e9), bytes_accessed=4 * 2**20, transcendentals=0
        ),
        name=name,
    )(*inputs, *held_in)


class Sirt:
    def __init__(self, theta, vol_list, slices, slots, rays, step_size):
        angles = theta.shape[0]
        patches = vol_list.shape[0]
        pairs = patches // 2
        both = 2 * slices
        chunk = math.gcd(angles, 32)
        self.sizes = (angles, chunk, slots)
        self.step_size = step_size
        self.rays = rays
        self.patches = patches
        centre = (ROI - 1) / 2.0
        ids = np.arange(pairs)
        centre_x = (ids // PGRID * float(SIDE) + (SIDE - 1) / 2.0 - centre).astype(np.float32)
        centre_y = (ids % PGRID * float(SIDE) + (SIDE - 1) / 2.0 - centre).astype(np.float32)
        self.cosine = jnp.cos(theta)
        self.sine = jnp.sin(theta)
        along = (
            centre_x[:, None] * self.cosine[None, :]
            + centre_y[:, None] * self.sine[None, :]
            + 0.5
        )
        whole = jnp.floor(along)
        lead = WIN // 2 - 1
        place = along - whole + float(lead)
        offset = whole.astype(jnp.int32) + (ACTIVE // 2 - 1 - lead)
        tile = jnp.minimum(offset // SPLIT, 2)
        local = jnp.arange(angles, dtype=jnp.int32) % chunk * WIN
        turn = (local[None, :] - offset + tile * SPLIT) % LANES
        self.offset = offset.reshape(-1)
        self.place = place.reshape(-1)
        self.tile = tile.reshape(-1)
        self.turn = turn.reshape(-1)
        ids = jnp.arange(patches, dtype=jnp.int32)
        self.slot = jnp.sum(
            jnp.where(vol_list[None, :] == ids[:, None], ids[None, :], 0), axis=1
        )
        voxel = np.arange(VOX)
        shift_x = np.repeat((voxel // SIDE - (SIDE - 1) / 2.0)[None, :], ROWS, axis=0)
        shift_y = np.repeat((voxel % SIDE - (SIDE - 1) / 2.0)[None, :], ROWS, axis=0)
        flip = np.eye(ACTIVE)[::-1].astype(ml_dtypes.bfloat16)
        self.fixed = [jnp.asarray(flip), jnp.asarray(shift_x, f32), jnp.asarray(shift_y, f32)]
        self.weight = ((chunk * WIN, 2 * VOX), bf16)
        self.held = (pairs // CYCLE + 1 if angles == chunk else 1,) + self.weight[0]
        self.acc = ((angles, 3, both, LANES), f32)
        self.acc_rows = ((angles // 2, ACTIVE, LANES), f32)
        self.along = ((angles, ROWS, VOX), f32)
        self.by_ray = ((angles, slices, ACTIVE), f32)
        self.by_pair = ((pairs, both, VOX), f32)
        self.window = ((angles, 3, both, LANES), f32)
        self.half = ((2, rays, slices * slots, LANES), f32)
        self.mirror = ((max(pairs, angles), slices, ACTIVE), f32)
        self.sent = [((slices * (slots + angles // rays * 3 // 4), ACTIVE), f32)] * rays

    def first(self, volume):
        inputs = [self.place, self.offset, self.slot, self.cosine, self.sine, volume]
        return call(
            functools.partial(first_kernel, self.sizes),
            "first",
            inputs + self.fixed,
            [],
            [self.by_pair],
            [self.by_ray, self.by_ray],
            [self.weight] * CYCLE
            + [self.acc_rows, self.along, self.half, self.mirror, self.by_pair],
            14,
        )

    def second(self, rank, volume, start, predicted, gain, sino):
        inputs = [rank.reshape(1), self.place, self.tile, self.turn, self.slot]
        inputs += [self.cosine, self.sine, volume, predicted, gain, sino]
        scratch = [(self.held, bf16)] * CYCLE
        scratch += [self.acc, self.along, self.by_ray, self.mirror, self.window]
        return call(
            functools.partial(second_kernel, self.sizes, self.step_size),
            "second",
            inputs + self.fixed,
            [start],
            [],
            self.sent,
            scratch + [self.by_pair, self.half, self.by_pair],
            26,
        )


def gather_kernel(rank_ref, *refs):
    *part_refs, out_ref, active_ref, sems = refs
    rank = rank_ref[0]
    copies = [
        pltpu.make_async_copy(part_ref, out_ref.at[rank ^ d], sems.at[d])
        for d, part_ref in enumerate(part_refs)
    ]
    for copy in copies:
        copy.start()
    offset = (out_ref.shape[2] - ACTIVE) // 2
    for d, part_ref in enumerate(part_refs):
        active_ref[rank ^ d] = part_ref[:, offset : offset + ACTIVE]
    for copy in copies:
        copy.wait()


def gather_parts(parts, rank):
    count = len(parts)
    rows = parts[0].shape[0]
    vmem = pl.BlockSpec(memory_space=pltpu.VMEM)
    return pl.pallas_call(
        gather_kernel,
        out_shape=(
            jax.ShapeDtypeStruct((count,) + parts[0].shape, f32),
            jax.ShapeDtypeStruct((count, rows, ACTIVE), f32),
        ),
        in_specs=[pl.BlockSpec(memory_space=pltpu.SMEM)] + [vmem] * count,
        out_specs=(pl.BlockSpec(memory_space=pltpu.HBM), vmem),
        scratch_shapes=[pltpu.SemaphoreType.DMA((count,))],
        compiler_params=pltpu.CompilerParams(vmem_limit_bytes=8 * 2**20),
        cost_estimate=pl.CostEstimate(
            flops=0, bytes_accessed=8 * count * parts[0].size, transcendentals=0
        ),
        name="gather_parts",
    )(rank.reshape(1), *parts)


def finish_kernel(rank_ref, *refs):
    *got_refs, given_ref, _, rec_ref, out_ref, values_ref, active_ref, sems = refs
    rays = len(got_refs)
    slots = values_ref.shape[1]
    slabs = active_ref.shape[0]
    slices = values_ref.shape[0] // rays
    lead = slices * slots
    lane = lax.broadcasted_iota(jnp.int32, (slices, ACTIVE), 1)
    live = (lane >= EDGE) & (lane < ACTIVE - EDGE)
    for d, got_ref in enumerate(reversed(got_refs)):
        rows = pl.ds(pl.multiple_of((rank_ref[0] ^ d) * slices, slices), slices)
        values_ref[rows] = got_ref[0:lead, :].reshape(slices, slots, VOX)
        for k in range(slabs):
            begin = lead + k // 4 * 3 * slices
            pair, side = k % 4 // 2, k % 2
            here = begin + pair * slices
            left = got_ref[here : here + slices, side * LANES : (side + 1) * LANES]
            here = begin + 2 * slices
            rest = got_ref[here : here + slices, pair * LANES : (pair + 1) * LANES]
            if side:
                rest = pltpu.roll(rest, SPLIT, 1)
            whole = pltpu.roll(jnp.concatenate([left, rest], axis=1), EDGE, 1)
            active_ref[k, rows, :] = jnp.where(live, whole, given_ref[k, rows, :])
    offset = (out_ref.shape[2] - ACTIVE) // 2
    copies = [
        pltpu.make_async_copy(values_ref, rec_ref, sems.at[0]),
        pltpu.make_async_copy(
            active_ref, out_ref.at[:, :, offset : offset + ACTIVE], sems.at[1]
        ),
    ]
    for copy in copies:
        copy.start()
    for copy in copies:
        copy.wait()


def finish(pieces, given, sinogram, rank, shape):
    slabs, slab_rows, _ = sinogram.shape
    hbm = pl.BlockSpec(memory_space=pltpu.HBM)
    vmem = pl.BlockSpec(memory_space=pltpu.VMEM)
    return pl.pallas_call(
        finish_kernel,
        out_shape=(
            jax.ShapeDtypeStruct(shape, f32),
            jax.ShapeDtypeStruct(sinogram.shape, f32),
        ),
        in_specs=[pl.BlockSpec(memory_space=pltpu.SMEM)]
        + [vmem] * (len(pieces) + 1)
        + [hbm],
        out_specs=[hbm, hbm],
        scratch_shapes=[
            pltpu.VMEM(shape, f32),
            pltpu.VMEM((slabs, slab_rows, ACTIVE), f32),
            pltpu.SemaphoreType.DMA((2,)),
        ],
        input_output_aliases={len(pieces) + 2: 1},
        compiler_params=pltpu.CompilerParams(vmem_limit_bytes=8 * 2**20),
        cost_estimate=pl.CostEstimate(
            flops=0, bytes_accessed=8 * len(pieces) * pieces[0].size, transcendentals=0
        ),
        name="finish",
    )(rank.reshape(1), *reversed(pieces), given, sinogram)


def exchange(pieces, axis):
    count = len(pieces)
    results = list(pieces)
    for d in range(count - 1, 0, -1):
        results[d] = lax.ppermute(pieces[d], axis, [(i, i ^ d) for i in range(count)])
    return results


def local(intensity, angles, volume, vol_list):
    n_slab = lax.axis_size("slab")
    n_ray = lax.axis_size("ray")
    devices = n_slab * n_ray
    height, band = intensity.shape[2:]
    slices = height // devices
    slots = volume.shape[1]
    count = angles.shape[0] * angles.shape[1]
    step_size = relax * ROI / count
    rank = lax.axis_index("slab")
    ray_rank = lax.axis_index("ray")
    padded = -(-slices // ROWS) * ROWS

    def to_all(values, axes):
        return lax.all_to_all(values, axes, split_axis=0, concat_axis=0, tiled=True)

    own_volume = to_all(volume.reshape(n_ray, slices * slots, VOX), "ray")
    *parts, active = paganin(intensity.reshape(height, band), rank, n_slab)
    active, own_volume = lax.optimization_barrier((active, own_volume))
    own_rays = to_all(active.reshape(devices, slices, ACTIVE), ("slab", "ray"))
    if padded != slices:
        more = padded - slices
        own_volume = jnp.pad(own_volume, ((0, 0), (0, more * slots), (0, 0)))
        own_rays = jnp.pad(own_rays, ((0, 0), (0, more), (0, 0)))

    angles, vol_list, own_volume, parts = lax.optimization_barrier(
        (angles, vol_list, own_volume, parts)
    )
    sirt = Sirt(angles.reshape(-1), vol_list, padded, slots, n_ray, step_size)
    start, predicted, gain = sirt.first(own_volume)
    own_rays, parts, start = lax.optimization_barrier((own_rays, parts, start))
    parts = exchange(parts, "slab")
    pieces = sirt.second(ray_rank, own_volume, start, predicted, gain, own_rays)
    pieces, parts = lax.optimization_barrier((pieces, parts))
    if padded != slices:
        narrow = []
        for piece in pieces:
            lower = piece[padded * slots :].reshape(-1, padded, ACTIVE)[:, :slices]
            lower = lower.reshape(-1, ACTIVE)
            narrow.append(jnp.concatenate([piece[: slices * slots], lower], axis=0))
        pieces = narrow
    pieces = exchange(pieces, "ray")
    sinogram, given = gather_parts(parts, rank)
    if padded == slices:
        reconstruction, residual = finish(pieces, given, sinogram, ray_rank, volume.shape)
    else:
        order = ray_rank ^ jnp.arange(n_ray, dtype=jnp.int32)
        pieces = jnp.take(jnp.stack(pieces), order, axis=0)
        reconstruction = pieces[:, : slices * slots].reshape(volume.shape)
        lower = pieces[:, slices * slots :].reshape(n_ray, -1, 3, slices, ACTIVE)
        left = lower[:, :, :2].reshape(n_ray, -1, 2, slices, 2, LANES)
        left = jnp.transpose(left, (1, 2, 4, 0, 3, 5)).reshape(n_slab, n_ray * slices, LANES)
        rest = lower[:, :, 2].reshape(n_ray, -1, slices, 4, SPLIT)
        rest = jnp.transpose(rest, (1, 3, 0, 2, 4)).reshape(n_slab, n_ray * slices, SPLIT)
        begin = (band - ACTIVE) // 2 + EDGE
        live = jnp.concatenate([left, rest], axis=2)
        residual = lax.dynamic_update_slice(sinogram, live, (0, 0, begin))
    return (reconstruction, residual[:, None])


def solution(mesh):
    placed = (P("slab", "ray", None, None), P(), P("slab", "ray", None), P())
    return jax.shard_map(
        local,
        mesh=mesh,
        in_specs=placed,
        out_specs=(P("slab", "ray", None), P(None, "ray", "slab", None)),
        check_vma=False,
    )
```

```python
import functools
import math

import jax
import jax.numpy as jnp
import ml_dtypes
import numpy as np
from jax import lax
from jax.experimental import pallas as pl
from jax.experimental.pallas import tpu as pltpu
from jax.sharding import PartitionSpec as P

BAND = 2048
PGRID = 8
ROI = 128
SIDE = 16
VOX = SIDE * SIDE
WIN = 24
ACTIVE = 256
LANES = 128
ROWS = 8
SPLIT = 64
EDGE = 32
GROUP = 8
CYCLE = 4

paganin_strength = 10.0
relax = 1.8
row_floor = 0.25

bf16 = jnp.bfloat16
f32 = jnp.float32


def halves(values):
    high = values.astype(bf16)
    low = (values - high.astype(f32)).astype(bf16)
    return high, low


def thirds(values):
    high = values.astype(bf16)
    rest = values - high.astype(f32)
    middle = rest.astype(bf16)
    low = (rest - middle.astype(f32)).astype(bf16)
    return high, middle, low


def dot(left, right):
    return jnp.dot(left, right, preferred_element_type=f32)


def repeat(count, body, unroll):
    unroll = math.gcd(count, unroll)

    def several(index, carry):
        for step in range(unroll):
            body(index * unroll + step)
        return carry

    lax.fori_loop(0, count // unroll, several, 0)


def filter_tables(height):
    index = np.arange(height)
    phase = 2.0 * np.pi * (np.outer(index, index) % height) / height
    cas = (np.cos(phase) + np.sin(phase)) / math.sqrt(height)
    row_freq = 2.0 - 2.0 * np.cos(2.0 * np.pi * index / height)
    middle = (1.0 + paganin_strength * row_freq) / paganin_strength + 2.0
    rho = (middle - np.sqrt(middle * middle - 4.0)) / 2.0
    return np.concatenate([cas, np.repeat(rho[None, :], ROWS, axis=0)], axis=0).astype(np.float32)


def chunk_carry(ends, power, forward):
    shift = 1
    for _ in range(3):
        ends = ends + power * pltpu.roll(ends, shift if forward else ROWS - shift, 0)
        power = power * power
        shift *= 2
    return pltpu.roll(ends, 1 if forward else ROWS - 1, 0) / (1.0 - power)


def filter_kernel(rank_ref, source_ref, given_ref, *refs):
    *part_refs, active_ref, image_ref, table_ref, out_ref, spec_ref, up_ref, down_ref = refs[:-2]
    sems, out_sems = refs[-2:]
    height, width = image_ref.shape
    rank = rank_ref[0]
    share = height // len(part_refs)
    length = width // ROWS
    blocks = height // LANES
    unroll = 8
    copies = []
    for c in range(ROWS):
        columns = slice(c * length, (c + 1) * length)
        copies.append(
            pltpu.make_async_copy(
                source_ref.at[:, columns], image_ref.at[:, columns], sems.at[c]
            )
        )
    given = pltpu.make_async_copy(given_ref, table_ref, sems.at[ROWS])
    given.start()
    for copy in copies:
        copy.start()
    given.wait()
    cas_high, cas_low = halves(table_ref[0:height, :])
    rho_all = table_ref[height : height + ROWS, :]
    rhos = [rho_all[:, b * LANES : (b + 1) * LANES] for b in range(blocks)]
    zeros = [jnp.zeros((ROWS, LANES), f32)] * blocks

    def transform(values):
        high, low = halves(values)
        return dot(high, cas_high) + dot(low, cas_high) + dot(high, cas_low)

    for c in range(ROWS):
        copies[c].wait()
        image = 1.0 - image_ref[:, c * length : (c + 1) * length]
        spectrum = transform(jnp.transpose(image))
        for b in range(blocks):
            spec_ref[b, pl.ds(c, length, stride=ROWS), :] = spectrum[
                :, b * LANES : (b + 1) * LANES
            ]

    def rows(position):
        return pl.ds(pl.multiple_of(position * ROWS, ROWS), ROWS)

    def advance(position, ups, downs):
        ups = [spec_ref[b, rows(position), :] + rhos[b] * ups[b] for b in range(blocks)]
        back = length - 1 - position
        downs = [spec_ref[b, rows(back), :] + rhos[b] * downs[b] for b in range(blocks)]
        return ups, downs

    def sweep(index, carry):
        ups, downs = carry
        for step in range(unroll):
            ups, downs = advance(index * unroll + step, ups, downs)
        return ups, downs

    ups, downs = lax.fori_loop(0, length // unroll, sweep, (zeros, zeros))
    powers = list(rhos)
    for _ in range(int(math.log2(length))):
        powers = [power * power for power in powers]
    ups = [chunk_carry(ups[b], powers[b], True) for b in range(blocks)]
    downs = [chunk_carry(downs[b], powers[b], False) for b in range(blocks)]
    scales = [rho / (paganin_strength * (1.0 - rho * rho)) for rho in rhos]

    def outer(index, carry):
        ups, downs = carry
        for step in range(unroll):
            position = index * unroll + step
            ups, downs = advance(position, ups, downs)
            for b in range(blocks):
                up_ref[b, rows(position), :] = ups[b]
                down_ref[b, rows(position), :] = downs[b]
        return ups, downs

    def inner(index, carry):
        ups, downs = carry
        for step in range(unroll):
            position = index * unroll + step
            back = length - 1 - position
            ups, downs = advance(position, ups, downs)
            for b in range(blocks):
                here = ups[b] + down_ref[b, rows(back), :] - spec_ref[b, rows(position), :]
                there = downs[b] + up_ref[b, rows(back), :] - spec_ref[b, rows(back), :]
                up_ref[b, rows(position), :] = here * scales[b]
                up_ref[b, rows(back), :] = there * scales[b]
        return ups, downs

    half = length // 2 // unroll
    carry = lax.fori_loop(0, half, outer, (ups, downs))
    lax.fori_loop(half, 2 * half, inner, carry)

    offset = (width - ACTIVE) // 2
    sent = []
    for c in range(ROWS):
        spectrum = jnp.concatenate(
            [up_ref[b, pl.ds(c, length, stride=ROWS), :] for b in range(blocks)], axis=1
        )
        filtered = 1.0 - jnp.transpose(transform(spectrum))
        columns = slice(c * length, (c + 1) * length)
        out_ref[:, columns] = -jnp.log(filtered)
        for d, part_ref in enumerate(part_refs):
            rows = pl.ds(pl.multiple_of((rank ^ d) * share, share), share)
            sent.append(
                pltpu.make_async_copy(
                    out_ref.at[rows, columns], part_ref.at[:, columns], out_sems.at[c, d]
                )
            )
            sent[-1].start()
        if c == (offset + ACTIVE - 1) // length:
            columns = slice(offset, offset + ACTIVE)
            sent.append(
                pltpu.make_async_copy(out_ref.at[:, columns], active_ref, sems.at[0])
            )
            sent[-1].start()
    for copy in sent:
        copy.wait()


def paganin(image, rank, parts):
    height, width = image.shape
    blocks = height // LANES
    return pl.pallas_call(
        filter_kernel,
        out_shape=[jax.ShapeDtypeStruct((height // parts, width), f32)] * parts
        + [jax.ShapeDtypeStruct((height, ACTIVE), f32)],
        in_specs=[pl.BlockSpec(memory_space=pltpu.SMEM)]
        + [pl.BlockSpec(memory_space=pltpu.HBM)] * 2,
        out_specs=[pl.BlockSpec(memory_space=pltpu.HBM)] * (parts + 1),
        scratch_shapes=[
            pltpu.VMEM((height, width), f32),
            pltpu.VMEM((height + ROWS, height), f32),
            pltpu.VMEM((height, width), f32),
            pltpu.VMEM((blocks, width, LANES), f32),
            pltpu.VMEM((blocks, width, LANES), f32),
            pltpu.VMEM((blocks, width // 2, LANES), f32),
            pltpu.SemaphoreType.DMA((ROWS + 1,)),
            pltpu.SemaphoreType.DMA((ROWS, parts)),
        ],
        compiler_params=pltpu.CompilerParams(vmem_limit_bytes=58 * 2**20),
        cost_estimate=pl.CostEstimate(
            flops=64 * height * height * width,
            bytes_accessed=8 * height * width,
            transcendentals=height * width,
        ),
        name="paganin",
    )(rank.reshape(1), image, jnp.asarray(filter_tables(height)))


def reversed_exact(values, flip):
    return sum(dot(part, flip) for part in thirds(values))


class Weights:
    def __init__(self, along_ref, place_ref, angles, chunk):
        self.along_ref = along_ref
        self.place_ref = place_ref
        self.angles = angles
        self.chunk = chunk
        self.ray = lax.broadcasted_iota(jnp.int32, (ROWS, VOX), 0).astype(f32)

    def prepare(self, shift_x_ref, shift_y_ref, cos_ref, sin_ref):
        def along_angle(t):
            self.along_ref[t] = shift_x_ref[...] * cos_ref[t] + shift_y_ref[...] * sin_ref[t]

        repeat(self.angles, along_angle, 8)

    def make(self, q, c, ref):
        for two in range(self.chunk // 2):
            pieces = []
            for t in (2 * two, 2 * two + 1):
                angle = c * self.chunk + t
                along = self.along_ref[angle] + self.place_ref[q * self.angles + angle]
                base = self.ray - along
                for group in range(WIN // ROWS):
                    distance = base + float(group * ROWS)
                    pieces.append(jnp.maximum(0.0, 1.0 - jnp.abs(distance)))
            high, low = halves(jnp.concatenate(pieces, axis=0))
            ref[2 * two * WIN : (2 * two + 2) * WIN, 0:VOX] = high
            ref[2 * two * WIN : (2 * two + 2) * WIN, VOX : 2 * VOX] = low


def ray_operand(values, sums_too):
    high, low = halves(values)
    rows = [
        jnp.concatenate([high, high], axis=1),
        jnp.concatenate([low, jnp.zeros_like(low)], axis=1),
    ]
    if sums_too:
        rows.append(jnp.ones((values.shape[0], 2 * VOX), bf16))
    return jnp.concatenate(rows, axis=0)


def row_operands(values, sums_too):
    rows = ray_operand(values, sums_too)
    count, width = rows.shape
    spare = jnp.zeros((SPLIT - count, width), bf16)
    empty = jnp.zeros((SPLIT, width), bf16)
    return (
        jnp.concatenate([rows, spare, empty], axis=0),
        jnp.concatenate([empty, rows, spare], axis=0),
    )


def project_rows(held_ref, operands, q, c, sizes, offset_ref, acc_ref):
    angles, chunk = sizes[:2]
    half = chunk // 2
    for begin in range(0, chunk, GROUP):
        sums = lax.dot_general(
            held_ref[begin * WIN : (begin + GROUP) * WIN, :],
            operands[begin // half],
            (((1,), (1,)), ((), ())),
            preferred_element_type=f32,
        )
        places = []
        for t in range(begin, begin + GROUP):
            rows = pl.ds(offset_ref[q * angles + c * chunk + t], WIN)
            piece = sums[(t - begin) * WIN : (t - begin + 1) * WIN, :]
            index = c * half + t % half
            places.append((index, rows, acc_ref[index, rows, :] + piece))
        for index, rows, values in places:
            acc_ref[index, rows, :] = values


def spread_rays(acc_ref, direct_ref, mirror_ref, total_ref, slices, chunk):
    both = 2 * slices
    half = chunk // 2

    def spread(index):
        turned = jnp.transpose(acc_ref[index]) * (1.0 / ROI)
        for part in range(2):
            rows = turned[part * SPLIT : (part + 1) * SPLIT]
            t = index // half * chunk + part * half + index % half
            direct_ref[t] = rows[0:slices] + rows[both : both + slices]
            mirror_ref[t] = rows[slices:both] + rows[both + slices : 2 * both]
            if total_ref is not None:
                total_ref[t] = rows[2 * both : 2 * both + slices]

    repeat(acc_ref.shape[0], spread, 8)


def turn_rays(values, flip):
    shape = values.shape
    return reversed_exact(values.reshape(-1, shape[-1]), flip).reshape(shape)


def fill_windows(weighted, flip, window_ref):
    angles, slices, _ = weighted.shape
    high, low = halves(weighted.reshape(angles * slices, ACTIVE))
    mirrored = (dot(high, flip) + dot(low, flip)).reshape(weighted.shape)
    lane = lax.broadcasted_iota(jnp.int32, (angles, slices, LANES), 2)
    for part, source in enumerate((weighted, mirrored)):
        rows = slice(part * slices, (part + 1) * slices)
        left = source[:, :, 0:LANES]
        right = source[:, :, LANES : 2 * LANES]
        window_ref[:, 0, rows, :] = left
        window_ref[:, 2, rows, :] = right
        mixed = jnp.where(lane >= SPLIT, left, right)
        window_ref[:, 1, rows, :] = pltpu.roll(mixed, SPLIT, 2)


def window_operand(q, c, sizes, window_ref, tile_ref, turn_ref):
    angles, chunk = sizes[:2]
    both = window_ref.shape[2]
    lane_rows = lax.broadcasted_iota(jnp.int32, (both, LANES), 1)
    tiles = [None] * (-(-chunk * WIN // LANES))
    for t in range(chunk):
        index = q * angles + c * chunk + t
        piece = pltpu.roll(window_ref[c * chunk + t, tile_ref[index]], turn_ref[index], 1)
        begin = t * WIN
        for place in range(begin // LANES, (begin + WIN - 1) // LANES + 1):
            if tiles[place] is None:
                tiles[place] = piece
            else:
                tiles[place] = jnp.where(
                    lane_rows >= begin - place * LANES, piece, tiles[place]
                )
    high, low = halves(jnp.concatenate(tiles, axis=1))
    return jnp.concatenate([high, low], axis=0)


def update_pair(operand, held):
    both = operand.shape[0] // 2
    sums = dot(operand, held)
    return sums[0:both, 0:VOX] + sums[both:, 0:VOX] + sums[0:both, VOX:]


def first_kernel(
    sizes,
    place_ref,
    offset_ref,
    slot_ref,
    cos_ref,
    sin_ref,
    vol_ref,
    flip_ref,
    shift_x_ref,
    shift_y_ref,
    kept_ref,
    predicted_ref,
    gain_ref,
    *refs,
):
    held_refs = refs[:CYCLE]
    acc_ref, along_ref, half_ref, mirror_ref, start_ref, sem = refs[CYCLE:]
    angles, chunk, slots = sizes
    patches = slot_ref.shape[0]
    pairs, both, _ = start_ref.shape
    slices = both // 2
    flip = flip_ref[...]

    def slot_values(patch):
        slot = slot_ref[patch]
        rows = pl.ds(slot % slots, slices, stride=slots)
        return jnp.concatenate(
            [half_ref[part, slot // slots, rows, :] for part in range(2)], axis=1
        )

    for part in range(2):
        half_ref[part] = vol_ref[:, :, part * LANES : (part + 1) * LANES]

    def order(q):
        start_ref[q, 0:slices, :] = slot_values(q)
        mirror_ref[q] = slot_values(patches - 1 - q)

    repeat(pairs, order, 8)
    start_ref[:, slices:both, :] = turn_rays(mirror_ref[0:pairs], flip)
    weights = Weights(along_ref, place_ref, angles, chunk)
    weights.prepare(shift_x_ref, shift_y_ref, cos_ref, sin_ref)
    acc_ref[...] = jnp.zeros(acc_ref.shape, f32)

    kept = pltpu.make_async_copy(start_ref, kept_ref, sem)
    kept.start()
    chunks = angles // chunk

    def cycle(index, carry):
        for step in range(CYCLE):
            q = index * CYCLE + step
            operands = row_operands(start_ref[q], True)
            for c in range(chunks):
                more = jnp.minimum(q + (c + 1) // chunks, pairs - 1)
                after = (step * chunks + c + 1) % CYCLE
                weights.make(more, (c + 1) % chunks, held_refs[after])
                here = held_refs[(step * chunks + c) % CYCLE]
                project_rows(here, operands, q, c, sizes, offset_ref, acc_ref)
        return carry

    weights.make(0, 0, held_refs[0])
    lax.fori_loop(0, pairs // CYCLE, cycle, 0)
    spread_rays(acc_ref, predicted_ref, mirror_ref, gain_ref, slices, chunk)
    direct, mirror, weight_sums = predicted_ref[...], mirror_ref[0:angles], gain_ref[...]
    predicted_ref[...] = direct + turn_rays(mirror, flip)
    direct = weight_sums
    gain_ref[...] = 1.0 / jnp.maximum(direct + turn_rays(direct, flip), row_floor)
    kept.wait()


def second_kernel(
    sizes,
    step_size,
    rank_ref,
    offset_ref,
    place_ref,
    tile_ref,
    turn_ref,
    slot_ref,
    cos_ref,
    sin_ref,
    vol_ref,
    predicted_ref,
    gain_ref,
    sino_ref,
    flip_ref,
    shift_x_ref,
    shift_y_ref,
    kept_ref,
    *refs,
):
    angles, chunk, slots = sizes
    rays = vol_ref.shape[0]
    out_refs, refs = refs[:rays], refs[rays:]
    held_refs = refs[:CYCLE]
    acc_ref, along_ref, direct_ref, mirror_ref, window_ref, update_ref, half_ref = refs[
        CYCLE:-2
    ]
    start_ref, sem = refs[-2:]
    kept = pltpu.make_async_copy(kept_ref, start_ref, sem)
    kept.start()
    patches = slot_ref.shape[0]
    pairs, both, _ = start_ref.shape
    slices = both // 2
    flip = flip_ref[...]
    weights = Weights(along_ref, place_ref, angles, chunk)
    weights.prepare(shift_x_ref, shift_y_ref, cos_ref, sin_ref)
    chunks = angles // chunk
    windows = (sizes, window_ref, tile_ref, turn_ref)
    rest = (sizes, offset_ref, acc_ref)
    fill_windows(
        (sino_ref[...] - predicted_ref[...]) * gain_ref[...] * (1.0 / ROI), flip, window_ref
    )
    acc_ref[...] = jnp.zeros(acc_ref.shape, f32)
    kept.wait()

    def advance(q, operand, held):
        total = update_pair(operand, held)
        update_ref[q] = total
        return start_ref[q] + step_size * total

    def forward(values, q, held):
        project_rows(held, row_operands(values, False), q, 0, *rest)

    def cycle(index, carry):
        values, operand = carry
        for step in range(CYCLE):
            q = index * CYCLE + step
            after = (step + 1) % CYCLE
            before = (step - 1) % CYCLE
            later = index + (step + 1) // CYCLE
            earlier = index if step else jnp.maximum(index - 1, 0)
            following = jnp.minimum(q + 1, pairs - 1)
            next_operand = window_operand(following, 0, *windows)
            weights.make(following, 0, held_refs[after].at[later])
            new_values = advance(q, operand, held_refs[step][index])
            forward(values, jnp.maximum(q - 1, 0), held_refs[before].at[earlier])
            values, operand = new_values, next_operand
        return values, operand

    def all_chunks(q, body):
        for c in range(chunks):
            weights.make(q, c, held_refs[0].at[0])
            body(c, held_refs[0].at[0])

    def plain_update(q, carry):
        update_ref[q] = jnp.zeros(update_ref.shape[1:], f32)

        def add(c, held):
            operand = window_operand(q, c, *windows)
            update_ref[q] = update_ref[q] + update_pair(operand, held[...])

        all_chunks(q, add)
        return carry

    def plain_forward(q, carry):
        operands = row_operands(start_ref[q] + step_size * update_ref[q], False)
        all_chunks(q, lambda c, held: project_rows(held, operands, q, c, *rest))
        return carry

    if chunks == 1:
        held_refs[CYCLE - 1][0] = jnp.zeros(held_refs[CYCLE - 1].shape[1:], bf16)
        weights.make(0, 0, held_refs[0].at[0])
        begin = (jnp.zeros((both, VOX), f32), window_operand(0, 0, *windows))
        values, _ = lax.fori_loop(0, pairs // CYCLE, cycle, begin)
        forward(values, pairs - 1, held_refs[CYCLE - 1].at[pairs // CYCLE - 1])
    else:
        lax.fori_loop(0, pairs, plain_update, 0)
        lax.fori_loop(0, pairs, plain_forward, 0)

    spread_rays(acc_ref, direct_ref, mirror_ref, None, slices, chunk)
    turned = turn_rays(mirror_ref[0:angles], flip)
    direct_ref[...] = sino_ref[...] - direct_ref[...] - turned
    fill_windows(direct_ref[...] * gain_ref[...] * (1.0 / ROI), flip, window_ref)

    def last_cycle(index, operand):
        for step in range(CYCLE):
            q = index * CYCLE + step
            next_operand = window_operand(jnp.minimum(q + 1, pairs - 1), 0, *windows)
            total = update_pair(operand, held_refs[step][index])
            update_ref[q] = (update_ref[q] + total) * step_size
            operand = next_operand
        return operand

    def plain_last(q, carry):
        def add(c, held):
            operand = window_operand(q, c, *windows)
            update_ref[q] = update_ref[q] + update_pair(operand, held[...])

        all_chunks(q, add)
        update_ref[q] = update_ref[q] * step_size
        return carry

    if chunks == 1:
        lax.fori_loop(0, pairs // CYCLE, last_cycle, window_operand(0, 0, *windows))
    else:
        lax.fori_loop(0, pairs, plain_last, 0)

    mirror_ref[0:pairs] = turn_rays(update_ref[:, slices:both, :], flip)
    for part in range(2):
        half_ref[part] = vol_ref[:, :, part * LANES : (part + 1) * LANES]

    def finish(q):
        for patch, update in (
            (q, update_ref[q, 0:slices, :]),
            (patches - 1 - q, mirror_ref[q]),
        ):
            slot = slot_ref[patch]
            rows = pl.ds(slot % slots, slices, stride=slots)
            for part in range(2):
                half_ref[part, slot // slots, rows, :] = (
                    half_ref[part, slot // slots, rows, :]
                    + update[:, part * LANES : (part + 1) * LANES]
                )

    repeat(pairs, finish, 8)
    lead = slices * slots
    lane = lax.broadcasted_iota(jnp.int32, (slices, LANES), 1)
    for d, out_ref in enumerate(out_refs):
        ray = rank_ref[0] ^ d
        for part in range(2):
            out_ref[0:lead, part * LANES : (part + 1) * LANES] = half_ref[part, ray]
        for k in range(0, angles // rays, 4):
            begin = lead + k // 4 * 3 * slices
            live = [
                pltpu.roll(direct_ref[(k + i) * rays + ray], ACTIVE - EDGE, 1)
                for i in range(4)
            ]
            rest = [part[:, LANES:] for part in live]
            for i in range(2):
                here = begin + i * slices
                out_ref[here : here + slices, 0:LANES] = live[2 * i][:, 0:LANES]
                out_ref[here : here + slices, LANES:] = live[2 * i + 1][:, 0:LANES]
                here = begin + 2 * slices
                out_ref[here : here + slices, i * LANES : (i + 1) * LANES] = jnp.where(
                    lane < SPLIT, rest[2 * i], pltpu.roll(rest[2 * i + 1], SPLIT, 1)
                )


def call(kernel, name, inputs, held_in, held_out, outputs, scratch, micros):
    smem = pl.BlockSpec(memory_space=pltpu.SMEM)
    vmem = pl.BlockSpec(memory_space=pltpu.VMEM)
    hbm = pl.BlockSpec(memory_space=pltpu.HBM)
    return pl.pallas_call(
        kernel,
        out_shape=[jax.ShapeDtypeStruct(*value) for value in held_out + outputs],
        in_specs=[smem if value.ndim == 1 else vmem for value in inputs] + [hbm] * len(held_in),
        out_specs=[hbm] * len(held_out) + [vmem] * len(outputs),
        scratch_shapes=[pltpu.VMEM(*value) for value in scratch]
        + [pltpu.SemaphoreType.DMA],
        compiler_params=pltpu.CompilerParams(vmem_limit_bytes=52 * 2**20),
        cost_estimate=pl.CostEstimate(
            flops=int(micros * 1e9), bytes_accessed=4 * 2**20, transcendentals=0
        ),
        name=name,
    )(*inputs, *held_in)


class Sirt:
    def __init__(self, theta, vol_list, slices, slots, rays, step_size):
        angles = theta.shape[0]
        patches = vol_list.shape[0]
        pairs = patches // 2
        both = 2 * slices
        chunk = math.gcd(angles, 32)
        self.sizes = (angles, chunk, slots)
        self.step_size = step_size
        self.rays = rays
        self.patches = patches
        centre = (ROI - 1) / 2.0
        ids = np.arange(pairs)
        centre_x = (ids // PGRID * float(SIDE) + (SIDE - 1) / 2.0 - centre).astype(np.float32)
        centre_y = (ids % PGRID * float(SIDE) + (SIDE - 1) / 2.0 - centre).astype(np.float32)
        self.cosine = jnp.cos(theta)
        self.sine = jnp.sin(theta)
        along = (
            centre_x[:, None] * self.cosine[None, :]
            + centre_y[:, None] * self.sine[None, :]
            + 0.5
        )
        whole = jnp.floor(along)
        lead = WIN // 2 - 1
        place = along - whole + float(lead)
        offset = whole.astype(jnp.int32) + (ACTIVE // 2 - 1 - lead)
        tile = jnp.minimum(offset // SPLIT, 2)
        local = jnp.arange(angles, dtype=jnp.int32) % chunk * WIN
        turn = (local[None, :] - offset + tile * SPLIT) % LANES
        self.offset = offset.reshape(-1)
        self.place = place.reshape(-1)
        self.tile = tile.reshape(-1)
        self.turn = turn.reshape(-1)
        ids = jnp.arange(patches, dtype=jnp.int32)
        self.slot = jnp.sum(
            jnp.where(vol_list[None, :] == ids[:, None], ids[None, :], 0), axis=1
        )
        voxel = np.arange(VOX)
        shift_x = np.repeat((voxel // SIDE - (SIDE - 1) / 2.0)[None, :], ROWS, axis=0)
        shift_y = np.repeat((voxel % SIDE - (SIDE - 1) / 2.0)[None, :], ROWS, axis=0)
        flip = np.eye(ACTIVE)[::-1].astype(ml_dtypes.bfloat16)
        self.fixed = [jnp.asarray(flip), jnp.asarray(shift_x, f32), jnp.asarray(shift_y, f32)]
        self.weight = ((chunk * WIN, 2 * VOX), bf16)
        self.held = (pairs // CYCLE + 1 if angles == chunk else 1,) + self.weight[0]
        self.acc_rows = ((angles // 2, ACTIVE, LANES), f32)
        self.along = ((angles, ROWS, VOX), f32)
        self.by_ray = ((angles, slices, ACTIVE), f32)
        self.by_pair = ((pairs, both, VOX), f32)
        self.window = ((angles, 3, both, LANES), f32)
        self.half = ((2, rays, slices * slots, LANES), f32)
        self.mirror = ((max(pairs, angles), slices, ACTIVE), f32)
        self.sent = [((slices * (slots + angles // rays * 3 // 4), ACTIVE), f32)] * rays

    def first(self, volume):
        inputs = [self.place, self.offset, self.slot, self.cosine, self.sine, volume]
        return call(
            functools.partial(first_kernel, self.sizes),
            "first",
            inputs + self.fixed,
            [],
            [self.by_pair],
            [self.by_ray, self.by_ray],
            [self.weight] * CYCLE
            + [self.acc_rows, self.along, self.half, self.mirror, self.by_pair],
            14,
        )

    def second(self, rank, volume, start, predicted, gain, sino):
        inputs = [rank.reshape(1), self.offset, self.place, self.tile, self.turn, self.slot]
        inputs += [self.cosine, self.sine, volume, predicted, gain, sino]
        scratch = [(self.held, bf16)] * CYCLE
        scratch += [self.acc_rows, self.along, self.by_ray, self.mirror, self.window]
        return call(
            functools.partial(second_kernel, self.sizes, self.step_size),
            "second",
            inputs + self.fixed,
            [start],
            [],
            self.sent,
            scratch + [self.by_pair, self.half, self.by_pair],
            26,
        )


def gather_kernel(rank_ref, *refs):
    *part_refs, out_ref, active_ref, sems = refs
    rank = rank_ref[0]
    copies = [
        pltpu.make_async_copy(part_ref, out_ref.at[rank ^ d], sems.at[d])
        for d, part_ref in enumerate(part_refs)
    ]
    for copy in copies:
        copy.start()
    offset = (out_ref.shape[2] - ACTIVE) // 2
    for d, part_ref in enumerate(part_refs):
        active_ref[rank ^ d] = part_ref[:, offset : offset + ACTIVE]
    for copy in copies:
        copy.wait()


def gather_parts(parts, rank):
    count = len(parts)
    rows = parts[0].shape[0]
    vmem = pl.BlockSpec(memory_space=pltpu.VMEM)
    return pl.pallas_call(
        gather_kernel,
        out_shape=(
            jax.ShapeDtypeStruct((count,) + parts[0].shape, f32),
            jax.ShapeDtypeStruct((count, rows, ACTIVE), f32),
        ),
        in_specs=[pl.BlockSpec(memory_space=pltpu.SMEM)] + [vmem] * count,
        out_specs=(pl.BlockSpec(memory_space=pltpu.HBM), vmem),
        scratch_shapes=[pltpu.SemaphoreType.DMA((count,))],
        compiler_params=pltpu.CompilerParams(vmem_limit_bytes=8 * 2**20),
        cost_estimate=pl.CostEstimate(
            flops=0, bytes_accessed=8 * count * parts[0].size, transcendentals=0
        ),
        name="gather_parts",
    )(rank.reshape(1), *parts)


def finish_kernel(rank_ref, *refs):
    *got_refs, given_ref, _, rec_ref, out_ref, values_ref, active_ref, sems = refs
    rays = len(got_refs)
    slots = values_ref.shape[1]
    slabs = active_ref.shape[0]
    slices = values_ref.shape[0] // rays
    lead = slices * slots
    lane = lax.broadcasted_iota(jnp.int32, (slices, ACTIVE), 1)
    live = (lane >= EDGE) & (lane < ACTIVE - EDGE)
    for d, got_ref in enumerate(reversed(got_refs)):
        rows = pl.ds(pl.multiple_of((rank_ref[0] ^ d) * slices, slices), slices)
        values_ref[rows] = got_ref[0:lead, :].reshape(slices, slots, VOX)
        for k in range(slabs):
            begin = lead + k // 4 * 3 * slices
            pair, side = k % 4 // 2, k % 2
            here = begin + pair * slices
            left = got_ref[here : here + slices, side * LANES : (side + 1) * LANES]
            here = begin + 2 * slices
            rest = got_ref[here : here + slices, pair * LANES : (pair + 1) * LANES]
            if side:
                rest = pltpu.roll(rest, SPLIT, 1)
            whole = pltpu.roll(jnp.concatenate([left, rest], axis=1), EDGE, 1)
            active_ref[k, rows, :] = jnp.where(live, whole, given_ref[k, rows, :])
    offset = (out_ref.shape[2] - ACTIVE) // 2
    copies = [
        pltpu.make_async_copy(values_ref, rec_ref, sems.at[0]),
        pltpu.make_async_copy(
            active_ref, out_ref.at[:, :, offset : offset + ACTIVE], sems.at[1]
        ),
    ]
    for copy in copies:
        copy.start()
    for copy in copies:
        copy.wait()


def finish(pieces, given, sinogram, rank, shape):
    slabs, slab_rows, _ = sinogram.shape
    hbm = pl.BlockSpec(memory_space=pltpu.HBM)
    vmem = pl.BlockSpec(memory_space=pltpu.VMEM)
    return pl.pallas_call(
        finish_kernel,
        out_shape=(
            jax.ShapeDtypeStruct(shape, f32),
            jax.ShapeDtypeStruct(sinogram.shape, f32),
        ),
        in_specs=[pl.BlockSpec(memory_space=pltpu.SMEM)]
        + [vmem] * (len(pieces) + 1)
        + [hbm],
        out_specs=[hbm, hbm],
        scratch_shapes=[
            pltpu.VMEM(shape, f32),
            pltpu.VMEM((slabs, slab_rows, ACTIVE), f32),
            pltpu.SemaphoreType.DMA((2,)),
        ],
        input_output_aliases={len(pieces) + 2: 1},
        compiler_params=pltpu.CompilerParams(vmem_limit_bytes=8 * 2**20),
        cost_estimate=pl.CostEstimate(
            flops=0, bytes_accessed=8 * len(pieces) * pieces[0].size, transcendentals=0
        ),
        name="finish",
    )(rank.reshape(1), *reversed(pieces), given, sinogram)


def exchange(pieces, axis):
    count = len(pieces)
    results = list(pieces)
    for d in range(count - 1, 0, -1):
        results[d] = lax.ppermute(pieces[d], axis, [(i, i ^ d) for i in range(count)])
    return results


def local(intensity, angles, volume, vol_list):
    n_slab = lax.axis_size("slab")
    n_ray = lax.axis_size("ray")
    devices = n_slab * n_ray
    height, band = intensity.shape[2:]
    slices = height // devices
    slots = volume.shape[1]
    count = angles.shape[0] * angles.shape[1]
    step_size = relax * ROI / count
    rank = lax.axis_index("slab")
    ray_rank = lax.axis_index("ray")
    padded = -(-slices // ROWS) * ROWS

    def to_all(values, axes):
        return lax.all_to_all(values, axes, split_axis=0, concat_axis=0, tiled=True)

    own_volume = to_all(volume.reshape(n_ray, slices * slots, VOX), "ray")
    *parts, active = paganin(intensity.reshape(height, band), rank, n_slab)
    active, own_volume = lax.optimization_barrier((active, own_volume))
    own_rays = to_all(active.reshape(devices, slices, ACTIVE), ("slab", "ray"))
    if padded != slices:
        more = padded - slices
        own_volume = jnp.pad(own_volume, ((0, 0), (0, more * slots), (0, 0)))
        own_rays = jnp.pad(own_rays, ((0, 0), (0, more), (0, 0)))

    angles, vol_list, own_volume, parts = lax.optimization_barrier(
        (angles, vol_list, own_volume, parts)
    )
    sirt = Sirt(angles.reshape(-1), vol_list, padded, slots, n_ray, step_size)
    start, predicted, gain = sirt.first(own_volume)
    own_rays, parts, start = lax.optimization_barrier((own_rays, parts, start))
    parts = exchange(parts, "slab")
    pieces = sirt.second(ray_rank, own_volume, start, predicted, gain, own_rays)
    pieces, parts = lax.optimization_barrier((pieces, parts))
    if padded != slices:
        narrow = []
        for piece in pieces:
            lower = piece[padded * slots :].reshape(-1, padded, ACTIVE)[:, :slices]
            lower = lower.reshape(-1, ACTIVE)
            narrow.append(jnp.concatenate([piece[: slices * slots], lower], axis=0))
        pieces = narrow
    pieces = exchange(pieces, "ray")
    sinogram, given = gather_parts(parts, rank)
    if padded == slices:
        reconstruction, residual = finish(pieces, given, sinogram, ray_rank, volume.shape)
    else:
        order = ray_rank ^ jnp.arange(n_ray, dtype=jnp.int32)
        pieces = jnp.take(jnp.stack(pieces), order, axis=0)
        reconstruction = pieces[:, : slices * slots].reshape(volume.shape)
        lower = pieces[:, slices * slots :].reshape(n_ray, -1, 3, slices, ACTIVE)
        left = lower[:, :, :2].reshape(n_ray, -1, 2, slices, 2, LANES)
        left = jnp.transpose(left, (1, 2, 4, 0, 3, 5)).reshape(n_slab, n_ray * slices, LANES)
        rest = lower[:, :, 2].reshape(n_ray, -1, slices, 4, SPLIT)
        rest = jnp.transpose(rest, (1, 3, 0, 2, 4)).reshape(n_slab, n_ray * slices, SPLIT)
        begin = (band - ACTIVE) // 2 + EDGE
        live = jnp.concatenate([left, rest], axis=2)
        residual = lax.dynamic_update_slice(sinogram, live, (0, 0, begin))
    return (reconstruction, residual[:, None])


def solution(mesh):
    placed = (P("slab", "ray", None, None), P(), P("slab", "ray", None), P())
    return jax.shard_map(
        local,
        mesh=mesh,
        in_specs=placed,
        out_specs=(P("slab", "ray", None), P(None, "ray", "slab", None)),
        check_vma=False,
    )
```

```python
import functools
import math

import jax
import jax.numpy as jnp
import ml_dtypes
import numpy as np
from jax import lax
from jax.experimental import pallas as pl
from jax.experimental.pallas import tpu as pltpu
from jax.sharding import PartitionSpec as P

BAND = 2048
PGRID = 8
ROI = 128
SIDE = 16
VOX = SIDE * SIDE
WIN = 24
ACTIVE = 256
LANES = 128
ROWS = 8
SPLIT = 64
EDGE = 32
GROUP = 8
CYCLE = 4

paganin_strength = 10.0
relax = 1.8
row_floor = 0.25

bf16 = jnp.bfloat16
f32 = jnp.float32


def halves(values):
    high = values.astype(bf16)
    low = (values - high.astype(f32)).astype(bf16)
    return high, low


def thirds(values):
    high = values.astype(bf16)
    rest = values - high.astype(f32)
    middle = rest.astype(bf16)
    low = (rest - middle.astype(f32)).astype(bf16)
    return high, middle, low


def dot(left, right):
    return jnp.dot(left, right, preferred_element_type=f32)


def repeat(count, body, unroll):
    unroll = math.gcd(count, unroll)

    def several(index, carry):
        for step in range(unroll):
            body(index * unroll + step)
        return carry

    lax.fori_loop(0, count // unroll, several, 0)


def filter_tables(height):
    index = np.arange(height)
    phase = 2.0 * np.pi * (np.outer(index, index) % height) / height
    cas = (np.cos(phase) + np.sin(phase)) / math.sqrt(height)
    row_freq = 2.0 - 2.0 * np.cos(2.0 * np.pi * index / height)
    middle = (1.0 + paganin_strength * row_freq) / paganin_strength + 2.0
    rho = (middle - np.sqrt(middle * middle - 4.0)) / 2.0
    return np.concatenate([cas, np.repeat(rho[None, :], ROWS, axis=0)], axis=0).astype(np.float32)


def chunk_carry(ends, power, forward):
    shift = 1
    for _ in range(3):
        ends = ends + power * pltpu.roll(ends, shift if forward else ROWS - shift, 0)
        power = power * power
        shift *= 2
    return pltpu.roll(ends, 1 if forward else ROWS - 1, 0) / (1.0 - power)


def filter_kernel(rank_ref, source_ref, given_ref, *refs):
    *part_refs, active_ref, image_ref, table_ref, out_ref, spec_ref, up_ref, down_ref = refs[:-2]
    sems, out_sems = refs[-2:]
    height, width = image_ref.shape
    rank = rank_ref[0]
    share = height // len(part_refs)
    length = width // ROWS
    blocks = height // LANES
    unroll = 8
    copies = []
    for c in range(ROWS):
        columns = slice(c * length, (c + 1) * length)
        copies.append(
            pltpu.make_async_copy(
                source_ref.at[:, columns], image_ref.at[:, columns], sems.at[c]
            )
        )
    given = pltpu.make_async_copy(given_ref, table_ref, sems.at[ROWS])
    given.start()
    for copy in copies:
        copy.start()
    given.wait()
    cas_high, cas_low = halves(table_ref[0:height, :])
    rho_all = table_ref[height : height + ROWS, :]
    rhos = [rho_all[:, b * LANES : (b + 1) * LANES] for b in range(blocks)]
    zeros = [jnp.zeros((ROWS, LANES), f32)] * blocks

    def transform(values):
        high, low = halves(values)
        return dot(high, cas_high) + dot(low, cas_high) + dot(high, cas_low)

    for c in range(ROWS):
        copies[c].wait()
        image = 1.0 - image_ref[:, c * length : (c + 1) * length]
        spectrum = transform(jnp.transpose(image))
        for b in range(blocks):
            spec_ref[b, pl.ds(c, length, stride=ROWS), :] = spectrum[
                :, b * LANES : (b + 1) * LANES
            ]

    def rows(position):
        return pl.ds(pl.multiple_of(position * ROWS, ROWS), ROWS)

    def advance(position, ups, downs):
        ups = [spec_ref[b, rows(position), :] + rhos[b] * ups[b] for b in range(blocks)]
        back = length - 1 - position
        downs = [spec_ref[b, rows(back), :] + rhos[b] * downs[b] for b in range(blocks)]
        return ups, downs

    def sweep(index, carry):
        ups, downs = carry
        for step in range(unroll):
            ups, downs = advance(index * unroll + step, ups, downs)
        return ups, downs

    ups, downs = lax.fori_loop(0, length // unroll, sweep, (zeros, zeros))
    powers = list(rhos)
    for _ in range(int(math.log2(length))):
        powers = [power * power for power in powers]
    ups = [chunk_carry(ups[b], powers[b], True) for b in range(blocks)]
    downs = [chunk_carry(downs[b], powers[b], False) for b in range(blocks)]
    scales = [rho / (paganin_strength * (1.0 - rho * rho)) for rho in rhos]

    def outer(index, carry):
        ups, downs = carry
        for step in range(unroll):
            position = index * unroll + step
            ups, downs = advance(position, ups, downs)
            for b in range(blocks):
                up_ref[b, rows(position), :] = ups[b]
                down_ref[b, rows(position), :] = downs[b]
        return ups, downs

    def inner(index, carry):
        ups, downs = carry
        for step in range(unroll):
            position = index * unroll + step
            back = length - 1 - position
            ups, downs = advance(position, ups, downs)
            for b in range(blocks):
                here = ups[b] + down_ref[b, rows(back), :] - spec_ref[b, rows(position), :]
                there = downs[b] + up_ref[b, rows(back), :] - spec_ref[b, rows(back), :]
                up_ref[b, rows(position), :] = here * scales[b]
                up_ref[b, rows(back), :] = there * scales[b]
        return ups, downs

    half = length // 2 // unroll
    carry = lax.fori_loop(0, half, outer, (ups, downs))
    lax.fori_loop(half, 2 * half, inner, carry)

    offset = (width - ACTIVE) // 2
    sent = []
    for c in range(ROWS):
        spectrum = jnp.concatenate(
            [up_ref[b, pl.ds(c, length, stride=ROWS), :] for b in range(blocks)], axis=1
        )
        filtered = 1.0 - jnp.transpose(transform(spectrum))
        columns = slice(c * length, (c + 1) * length)
        out_ref[:, columns] = -jnp.log(filtered)
        for d, part_ref in enumerate(part_refs):
            rows = pl.ds(pl.multiple_of((rank ^ d) * share, share), share)
            sent.append(
                pltpu.make_async_copy(
                    out_ref.at[rows, columns], part_ref.at[:, columns], out_sems.at[c, d]
                )
            )
            sent[-1].start()
        if c == (offset + ACTIVE - 1) // length:
            columns = slice(offset, offset + ACTIVE)
            sent.append(
                pltpu.make_async_copy(out_ref.at[:, columns], active_ref, sems.at[0])
            )
            sent[-1].start()
    for copy in sent:
        copy.wait()


def paganin(image, rank, parts):
    height, width = image.shape
    blocks = height // LANES
    return pl.pallas_call(
        filter_kernel,
        out_shape=[jax.ShapeDtypeStruct((height // parts, width), f32)] * parts
        + [jax.ShapeDtypeStruct((height, ACTIVE), f32)],
        in_specs=[pl.BlockSpec(memory_space=pltpu.SMEM)]
        + [pl.BlockSpec(memory_space=pltpu.HBM)] * 2,
        out_specs=[pl.BlockSpec(memory_space=pltpu.HBM)] * (parts + 1),
        scratch_shapes=[
            pltpu.VMEM((height, width), f32),
            pltpu.VMEM((height + ROWS, height), f32),
            pltpu.VMEM((height, width), f32),
            pltpu.VMEM((blocks, width, LANES), f32),
            pltpu.VMEM((blocks, width, LANES), f32),
            pltpu.VMEM((blocks, width // 2, LANES), f32),
            pltpu.SemaphoreType.DMA((ROWS + 1,)),
            pltpu.SemaphoreType.DMA((ROWS, parts)),
        ],
        compiler_params=pltpu.CompilerParams(vmem_limit_bytes=58 * 2**20),
        cost_estimate=pl.CostEstimate(
            flops=64 * height * height * width,
            bytes_accessed=8 * height * width,
            transcendentals=height * width,
        ),
        name="paganin",
    )(rank.reshape(1), image, jnp.asarray(filter_tables(height)))


def reversed_exact(values, flip):
    return sum(dot(part, flip) for part in thirds(values))


class Weights:
    def __init__(self, along_ref, place_ref, angles, chunk):
        self.along_ref = along_ref
        self.place_ref = place_ref
        self.angles = angles
        self.chunk = chunk
        self.ray = lax.broadcasted_iota(jnp.int32, (ROWS, VOX), 0).astype(f32)

    def prepare(self, shift_x_ref, shift_y_ref, cos_ref, sin_ref):
        def along_angle(t):
            along = shift_x_ref[...] * cos_ref[t] + shift_y_ref[...] * sin_ref[t]
            self.along_ref[t] = self.ray - along

        repeat(self.angles, along_angle, 8)

    def make(self, q, c, ref):
        for two in range(self.chunk // 2):
            pieces = []
            for t in (2 * two, 2 * two + 1):
                angle = c * self.chunk + t
                base = self.along_ref[angle] - self.place_ref[q * self.angles + angle]
                for group in range(WIN // ROWS):
                    distance = base + float(group * ROWS)
                    pieces.append(jnp.maximum(0.0, 1.0 - jnp.abs(distance)))
            high, low = halves(jnp.concatenate(pieces, axis=0))
            ref[2 * two * WIN : (2 * two + 2) * WIN, 0:VOX] = high
            ref[2 * two * WIN : (2 * two + 2) * WIN, VOX : 2 * VOX] = low


def ray_operand(values, sums_too):
    high, low = halves(values)
    rows = [
        jnp.concatenate([high, high], axis=1),
        jnp.concatenate([low, jnp.zeros_like(low)], axis=1),
    ]
    if sums_too:
        rows.append(jnp.ones((values.shape[0], 2 * VOX), bf16))
    return jnp.concatenate(rows, axis=0)


def row_operands(values, sums_too):
    rows = ray_operand(values, sums_too)
    count, width = rows.shape
    spare = jnp.zeros((SPLIT - count, width), bf16)
    empty = jnp.zeros((SPLIT, width), bf16)
    return (
        jnp.concatenate([rows, spare, empty], axis=0),
        jnp.concatenate([empty, rows, spare], axis=0),
    )


def project_rows(held_ref, operands, q, c, sizes, offset_ref, acc_ref):
    angles, chunk = sizes[:2]
    half = chunk // 2
    for begin in range(0, chunk, GROUP):
        sums = lax.dot_general(
            held_ref[begin * WIN : (begin + GROUP) * WIN, :],
            operands[begin // half],
            (((1,), (1,)), ((), ())),
            preferred_element_type=f32,
        )
        places = []
        for t in range(begin, begin + GROUP):
            rows = pl.ds(offset_ref[q * angles + c * chunk + t], WIN)
            piece = sums[(t - begin) * WIN : (t - begin + 1) * WIN, :]
            index = c * half + t % half
            places.append((index, rows, acc_ref[index, rows, :] + piece))
        for index, rows, values in places:
            acc_ref[index, rows, :] = values


def spread_rays(acc_ref, direct_ref, mirror_ref, total_ref, slices, chunk):
    both = 2 * slices
    half = chunk // 2

    def spread(index):
        turned = jnp.transpose(acc_ref[index]) * (1.0 / ROI)
        for part in range(2):
            rows = turned[part * SPLIT : (part + 1) * SPLIT]
            t = index // half * chunk + part * half + index % half
            direct_ref[t] = rows[0:slices] + rows[both : both + slices]
            mirror_ref[t] = rows[slices:both] + rows[both + slices : 2 * both]
            if total_ref is not None:
                total_ref[t] = rows[2 * both : 2 * both + slices]

    repeat(acc_ref.shape[0], spread, 8)


def turn_rays(values, flip):
    shape = values.shape
    return reversed_exact(values.reshape(-1, shape[-1]), flip).reshape(shape)


def fill_windows(weighted, flip, window_ref):
    angles, slices, _ = weighted.shape
    high, low = halves(weighted.reshape(angles * slices, ACTIVE))
    mirrored = (dot(high, flip) + dot(low, flip)).reshape(weighted.shape)
    lane = lax.broadcasted_iota(jnp.int32, (angles, slices, LANES), 2)
    for part, source in enumerate((weighted, mirrored)):
        rows = slice(part * slices, (part + 1) * slices)
        left = source[:, :, 0:LANES]
        right = source[:, :, LANES : 2 * LANES]
        window_ref[:, 0, rows, :] = left
        window_ref[:, 2, rows, :] = right
        mixed = jnp.where(lane >= SPLIT, left, right)
        window_ref[:, 1, rows, :] = pltpu.roll(mixed, SPLIT, 2)


def window_operand(q, c, sizes, window_ref, tile_ref, turn_ref):
    angles, chunk = sizes[:2]
    both = window_ref.shape[2]
    lane_rows = lax.broadcasted_iota(jnp.int32, (both, LANES), 1)
    tiles = [None] * (-(-chunk * WIN // LANES))
    for t in range(chunk):
        index = q * angles + c * chunk + t
        piece = pltpu.roll(window_ref[c * chunk + t, tile_ref[index]], turn_ref[index], 1)
        begin = t * WIN
        for place in range(begin // LANES, (begin + WIN - 1) // LANES + 1):
            if tiles[place] is None:
                tiles[place] = piece
            else:
                tiles[place] = jnp.where(
                    lane_rows >= begin - place * LANES, piece, tiles[place]
                )
    high, low = halves(jnp.concatenate(tiles, axis=1))
    return jnp.concatenate([high, low], axis=0)


def update_pair(operand, held):
    both = operand.shape[0] // 2
    sums = dot(operand, held)
    return sums[0:both, 0:VOX] + sums[both:, 0:VOX] + sums[0:both, VOX:]


def first_kernel(
    sizes,
    place_ref,
    offset_ref,
    slot_ref,
    cos_ref,
    sin_ref,
    vol_ref,
    flip_ref,
    shift_x_ref,
    shift_y_ref,
    kept_ref,
    predicted_ref,
    gain_ref,
    *refs,
):
    held_refs = refs[:CYCLE]
    acc_ref, along_ref, half_ref, mirror_ref, start_ref, sem = refs[CYCLE:]
    angles, chunk, slots = sizes
    patches = slot_ref.shape[0]
    pairs, both, _ = start_ref.shape
    slices = both // 2
    flip = flip_ref[...]

    def slot_values(patch):
        slot = slot_ref[patch]
        rows = pl.ds(slot % slots, slices, stride=slots)
        return jnp.concatenate(
            [half_ref[part, slot // slots, rows, :] for part in range(2)], axis=1
        )

    for part in range(2):
        half_ref[part] = vol_ref[:, :, part * LANES : (part + 1) * LANES]

    def order(q):
        start_ref[q, 0:slices, :] = slot_values(q)
        mirror_ref[q] = slot_values(patches - 1 - q)

    repeat(pairs, order, 8)
    start_ref[:, slices:both, :] = turn_rays(mirror_ref[0:pairs], flip)
    weights = Weights(along_ref, place_ref, angles, chunk)
    weights.prepare(shift_x_ref, shift_y_ref, cos_ref, sin_ref)
    acc_ref[...] = jnp.zeros(acc_ref.shape, f32)

    kept = pltpu.make_async_copy(start_ref, kept_ref, sem)
    kept.start()
    chunks = angles // chunk

    def cycle(index, carry):
        for step in range(CYCLE):
            q = index * CYCLE + step
            operands = row_operands(start_ref[q], True)
            for c in range(chunks):
                more = jnp.minimum(q + (c + 1) // chunks, pairs - 1)
                after = (step * chunks + c + 1) % CYCLE
                weights.make(more, (c + 1) % chunks, held_refs[after])
                here = held_refs[(step * chunks + c) % CYCLE]
                project_rows(here, operands, q, c, sizes, offset_ref, acc_ref)
        return carry

    weights.make(0, 0, held_refs[0])
    lax.fori_loop(0, pairs // CYCLE, cycle, 0)
    spread_rays(acc_ref, predicted_ref, mirror_ref, gain_ref, slices, chunk)
    direct, mirror, weight_sums = predicted_ref[...], mirror_ref[0:angles], gain_ref[...]
    predicted_ref[...] = direct + turn_rays(mirror, flip)
    turned = turn_rays(weight_sums[:, 0, :], flip)
    total = weight_sums + turned[:, None, :]
    gain_ref[...] = 1.0 / jnp.maximum(total, row_floor)
    kept.wait()


def second_kernel(
    sizes,
    step_size,
    rank_ref,
    offset_ref,
    place_ref,
    tile_ref,
    turn_ref,
    slot_ref,
    cos_ref,
    sin_ref,
    vol_ref,
    predicted_ref,
    gain_ref,
    sino_ref,
    flip_ref,
    shift_x_ref,
    shift_y_ref,
    kept_ref,
    *refs,
):
    angles, chunk, slots = sizes
    rays = vol_ref.shape[0]
    out_refs, refs = refs[:rays], refs[rays:]
    held_refs = refs[:CYCLE]
    acc_ref, along_ref, direct_ref, mirror_ref, window_ref, update_ref, half_ref = refs[
        CYCLE:-2
    ]
    start_ref, sem = refs[-2:]
    kept = pltpu.make_async_copy(kept_ref, start_ref, sem)
    kept.start()
    patches = slot_ref.shape[0]
    pairs, both, _ = start_ref.shape
    slices = both // 2
    flip = flip_ref[...]
    weights = Weights(along_ref, place_ref, angles, chunk)
    weights.prepare(shift_x_ref, shift_y_ref, cos_ref, sin_ref)
    chunks = angles // chunk
    windows = (sizes, window_ref, tile_ref, turn_ref)
    rest = (sizes, offset_ref, acc_ref)
    fill_windows(
        (sino_ref[...] - predicted_ref[...]) * gain_ref[...] * (1.0 / ROI), flip, window_ref
    )
    acc_ref[...] = jnp.zeros(acc_ref.shape, f32)
    kept.wait()

    def advance(q, operand, held):
        total = update_pair(operand, held)
        update_ref[q] = total
        return start_ref[q] + step_size * total

    def forward(values, q, held):
        project_rows(held, row_operands(values, False), q, 0, *rest)

    def cycle(index, carry):
        values, operand = carry
        for step in range(CYCLE):
            q = index * CYCLE + step
            after = (step + 1) % CYCLE
            before = (step - 1) % CYCLE
            later = index + (step + 1) // CYCLE
            earlier = index if step else jnp.maximum(index - 1, 0)
            following = jnp.minimum(q + 1, pairs - 1)
            next_operand = window_operand(following, 0, *windows)
            weights.make(following, 0, held_refs[after].at[later])
            new_values = advance(q, operand, held_refs[step][index])
            forward(values, jnp.maximum(q - 1, 0), held_refs[before].at[earlier])
            values, operand = new_values, next_operand
        return values, operand

    def all_chunks(q, body):
        for c in range(chunks):
            weights.make(q, c, held_refs[0].at[0])
            body(c, held_refs[0].at[0])

    def plain_update(q, carry):
        update_ref[q] = jnp.zeros(update_ref.shape[1:], f32)

        def add(c, held):
            operand = window_operand(q, c, *windows)
            update_ref[q] = update_ref[q] + update_pair(operand, held[...])

        all_chunks(q, add)
        return carry

    def plain_forward(q, carry):
        operands = row_operands(start_ref[q] + step_size * update_ref[q], False)
        all_chunks(q, lambda c, held: project_rows(held, operands, q, c, *rest))
        return carry

    if chunks == 1:
        held_refs[CYCLE - 1][0] = jnp.zeros(held_refs[CYCLE - 1].shape[1:], bf16)
        weights.make(0, 0, held_refs[0].at[0])
        begin = (jnp.zeros((both, VOX), f32), window_operand(0, 0, *windows))
        values, _ = lax.fori_loop(0, pairs // CYCLE, cycle, begin)
        forward(values, pairs - 1, held_refs[CYCLE - 1].at[pairs // CYCLE - 1])
    else:
        lax.fori_loop(0, pairs, plain_update, 0)
        lax.fori_loop(0, pairs, plain_forward, 0)

    spread_rays(acc_ref, direct_ref, mirror_ref, None, slices, chunk)
    turned = turn_rays(mirror_ref[0:angles], flip)
    direct_ref[...] = sino_ref[...] - direct_ref[...] - turned
    fill_windows(direct_ref[...] * gain_ref[...] * (1.0 / ROI), flip, window_ref)

    def last_cycle(index, operand):
        for step in range(CYCLE):
            q = index * CYCLE + step
            next_operand = window_operand(jnp.minimum(q + 1, pairs - 1), 0, *windows)
            total = update_pair(operand, held_refs[step][index])
            update_ref[q] = (update_ref[q] + total) * step_size
            operand = next_operand
        return operand

    def plain_last(q, carry):
        def add(c, held):
            operand = window_operand(q, c, *windows)
            update_ref[q] = update_ref[q] + update_pair(operand, held[...])

        all_chunks(q, add)
        update_ref[q] = update_ref[q] * step_size
        return carry

    if chunks == 1:
        lax.fori_loop(0, pairs // CYCLE, last_cycle, window_operand(0, 0, *windows))
    else:
        lax.fori_loop(0, pairs, plain_last, 0)

    mirror_ref[0:pairs] = turn_rays(update_ref[:, slices:both, :], flip)
    for part in range(2):
        half_ref[part] = vol_ref[:, :, part * LANES : (part + 1) * LANES]

    def finish(q):
        for patch, update in (
            (q, update_ref[q, 0:slices, :]),
            (patches - 1 - q, mirror_ref[q]),
        ):
            slot = slot_ref[patch]
            rows = pl.ds(slot % slots, slices, stride=slots)
            for part in range(2):
                half_ref[part, slot // slots, rows, :] = (
                    half_ref[part, slot // slots, rows, :]
                    + update[:, part * LANES : (part + 1) * LANES]
                )

    repeat(pairs, finish, 8)
    lead = slices * slots
    lane = lax.broadcasted_iota(jnp.int32, (slices, LANES), 1)
    for d, out_ref in enumerate(out_refs):
        ray = rank_ref[0] ^ d
        for part in range(2):
            out_ref[0:lead, part * LANES : (part + 1) * LANES] = half_ref[part, ray]
        for k in range(0, angles // rays, 4):
            begin = lead + k // 4 * 3 * slices
            live = [
                pltpu.roll(direct_ref[(k + i) * rays + ray], ACTIVE - EDGE, 1)
                for i in range(4)
            ]
            rest = [part[:, LANES:] for part in live]
            for i in range(2):
                here = begin + i * slices
                out_ref[here : here + slices, 0:LANES] = live[2 * i][:, 0:LANES]
                out_ref[here : here + slices, LANES:] = live[2 * i + 1][:, 0:LANES]
                here = begin + 2 * slices
                out_ref[here : here + slices, i * LANES : (i + 1) * LANES] = jnp.where(
                    lane < SPLIT, rest[2 * i], pltpu.roll(rest[2 * i + 1], SPLIT, 1)
                )


def call(kernel, name, inputs, held_in, held_out, outputs, scratch, micros):
    smem = pl.BlockSpec(memory_space=pltpu.SMEM)
    vmem = pl.BlockSpec(memory_space=pltpu.VMEM)
    hbm = pl.BlockSpec(memory_space=pltpu.HBM)
    return pl.pallas_call(
        kernel,
        out_shape=[jax.ShapeDtypeStruct(*value) for value in held_out + outputs],
        in_specs=[smem if value.ndim == 1 else vmem for value in inputs] + [hbm] * len(held_in),
        out_specs=[hbm] * len(held_out) + [vmem] * len(outputs),
        scratch_shapes=[pltpu.VMEM(*value) for value in scratch]
        + [pltpu.SemaphoreType.DMA],
        compiler_params=pltpu.CompilerParams(vmem_limit_bytes=52 * 2**20),
        cost_estimate=pl.CostEstimate(
            flops=int(micros * 1e9), bytes_accessed=4 * 2**20, transcendentals=0
        ),
        name=name,
    )(*inputs, *held_in)


class Sirt:
    def __init__(self, theta, vol_list, slices, slots, rays, step_size):
        angles = theta.shape[0]
        patches = vol_list.shape[0]
        pairs = patches // 2
        both = 2 * slices
        chunk = math.gcd(angles, 32)
        self.sizes = (angles, chunk, slots)
        self.step_size = step_size
        self.rays = rays
        self.patches = patches
        centre = (ROI - 1) / 2.0
        ids = np.arange(pairs)
        centre_x = (ids // PGRID * float(SIDE) + (SIDE - 1) / 2.0 - centre).astype(np.float32)
        centre_y = (ids % PGRID * float(SIDE) + (SIDE - 1) / 2.0 - centre).astype(np.float32)
        self.cosine = jnp.cos(theta)
        self.sine = jnp.sin(theta)
        along = (
            centre_x[:, None] * self.cosine[None, :]
            + centre_y[:, None] * self.sine[None, :]
            + 0.5
        )
        whole = jnp.floor(along)
        lead = WIN // 2 - 1
        place = along - whole + float(lead)
        offset = whole.astype(jnp.int32) + (ACTIVE // 2 - 1 - lead)
        tile = jnp.minimum(offset // SPLIT, 2)
        local = jnp.arange(angles, dtype=jnp.int32) % chunk * WIN
        turn = (local[None, :] - offset + tile * SPLIT) % LANES
        self.offset = offset.reshape(-1)
        self.place = place.reshape(-1)
        self.tile = tile.reshape(-1)
        self.turn = turn.reshape(-1)
        ids = jnp.arange(patches, dtype=jnp.int32)
        self.slot = jnp.sum(
            jnp.where(vol_list[None, :] == ids[:, None], ids[None, :], 0), axis=1
        )
        voxel = np.arange(VOX)
        shift_x = np.repeat((voxel // SIDE - (SIDE - 1) / 2.0)[None, :], ROWS, axis=0)
        shift_y = np.repeat((voxel % SIDE - (SIDE - 1) / 2.0)[None, :], ROWS, axis=0)
        flip = np.eye(ACTIVE)[::-1].astype(ml_dtypes.bfloat16)
        self.fixed = [jnp.asarray(flip), jnp.asarray(shift_x, f32), jnp.asarray(shift_y, f32)]
        self.weight = ((chunk * WIN, 2 * VOX), bf16)
        self.held = (pairs // CYCLE + 1 if angles == chunk else 1,) + self.weight[0]
        self.acc_rows = ((angles // 2, ACTIVE, LANES), f32)
        self.along = ((angles, ROWS, VOX), f32)
        self.by_ray = ((angles, slices, ACTIVE), f32)
        self.by_pair = ((pairs, both, VOX), f32)
        self.window = ((angles, 3, both, LANES), f32)
        self.half = ((2, rays, slices * slots, LANES), f32)
        self.mirror = ((max(pairs, angles), slices, ACTIVE), f32)
        self.sent = [((slices * (slots + angles // rays * 3 // 4), ACTIVE), f32)] * rays

    def first(self, volume):
        inputs = [self.place, self.offset, self.slot, self.cosine, self.sine, volume]
        return call(
            functools.partial(first_kernel, self.sizes),
            "first",
            inputs + self.fixed,
            [],
            [self.by_pair],
            [self.by_ray, self.by_ray],
            [self.weight] * CYCLE
            + [self.acc_rows, self.along, self.half, self.mirror, self.by_pair],
            14,
        )

    def second(self, rank, volume, start, predicted, gain, sino):
        inputs = [rank.reshape(1), self.offset, self.place, self.tile, self.turn, self.slot]
        inputs += [self.cosine, self.sine, volume, predicted, gain, sino]
        scratch = [(self.held, bf16)] * CYCLE
        scratch += [self.acc_rows, self.along, self.by_ray, self.mirror, self.window]
        return call(
            functools.partial(second_kernel, self.sizes, self.step_size),
            "second",
            inputs + self.fixed,
            [start],
            [],
            self.sent,
            scratch + [self.by_pair, self.half, self.by_pair],
            26,
        )


def gather_kernel(rank_ref, *refs):
    *part_refs, out_ref, active_ref, sems = refs
    rank = rank_ref[0]
    copies = [
        pltpu.make_async_copy(part_ref, out_ref.at[rank ^ d], sems.at[d])
        for d, part_ref in enumerate(part_refs)
    ]
    for copy in copies:
        copy.start()
    offset = (out_ref.shape[2] - ACTIVE) // 2
    for d, part_ref in enumerate(part_refs):
        active_ref[rank ^ d] = part_ref[:, offset : offset + ACTIVE]
    for copy in copies:
        copy.wait()


def gather_parts(parts, rank):
    count = len(parts)
    rows = parts[0].shape[0]
    vmem = pl.BlockSpec(memory_space=pltpu.VMEM)
    return pl.pallas_call(
        gather_kernel,
        out_shape=(
            jax.ShapeDtypeStruct((count,) + parts[0].shape, f32),
            jax.ShapeDtypeStruct((count, rows, ACTIVE), f32),
        ),
        in_specs=[pl.BlockSpec(memory_space=pltpu.SMEM)] + [vmem] * count,
        out_specs=(pl.BlockSpec(memory_space=pltpu.HBM), vmem),
        scratch_shapes=[pltpu.SemaphoreType.DMA((count,))],
        compiler_params=pltpu.CompilerParams(vmem_limit_bytes=8 * 2**20),
        cost_estimate=pl.CostEstimate(
            flops=0, bytes_accessed=8 * count * parts[0].size, transcendentals=0
        ),
        name="gather_parts",
    )(rank.reshape(1), *parts)


def message_order(count):
    near = [d for d in (1, 2) if d < count // 2]
    far = list(range(count - 1, count // 2 - 1, -1))
    return near + far + [d for d in range(count // 2 - 1, -1, -1) if d not in near]


def finish_kernel(rank_ref, *refs):
    *got_refs, given_ref, _, rec_ref, out_ref, values_ref, active_ref, sems = refs
    rays = len(got_refs)
    slots = values_ref.shape[1]
    slabs = active_ref.shape[0]
    slices = values_ref.shape[0] // rays
    lead = slices * slots
    lane = lax.broadcasted_iota(jnp.int32, (slices, ACTIVE), 1)
    live = (lane >= EDGE) & (lane < ACTIVE - EDGE)
    for d, got_ref in zip(message_order(rays), got_refs):
        rows = pl.ds(pl.multiple_of((rank_ref[0] ^ d) * slices, slices), slices)
        values_ref[rows] = got_ref[0:lead, :].reshape(slices, slots, VOX)
        for k in range(slabs):
            begin = lead + k // 4 * 3 * slices
            pair, side = k % 4 // 2, k % 2
            here = begin + pair * slices
            left = got_ref[here : here + slices, side * LANES : (side + 1) * LANES]
            here = begin + 2 * slices
            rest = got_ref[here : here + slices, pair * LANES : (pair + 1) * LANES]
            if side:
                rest = pltpu.roll(rest, SPLIT, 1)
            whole = pltpu.roll(jnp.concatenate([left, rest], axis=1), EDGE, 1)
            active_ref[k, rows, :] = jnp.where(live, whole, given_ref[k, rows, :])
    offset = (out_ref.shape[2] - ACTIVE) // 2
    copies = [
        pltpu.make_async_copy(values_ref, rec_ref, sems.at[0]),
        pltpu.make_async_copy(
            active_ref, out_ref.at[:, :, offset : offset + ACTIVE], sems.at[1]
        ),
    ]
    for copy in copies:
        copy.start()
    for copy in copies:
        copy.wait()


def finish(pieces, given, sinogram, rank, shape):
    slabs, slab_rows, _ = sinogram.shape
    hbm = pl.BlockSpec(memory_space=pltpu.HBM)
    vmem = pl.BlockSpec(memory_space=pltpu.VMEM)
    return pl.pallas_call(
        finish_kernel,
        out_shape=(
            jax.ShapeDtypeStruct(shape, f32),
            jax.ShapeDtypeStruct(sinogram.shape, f32),
        ),
        in_specs=[pl.BlockSpec(memory_space=pltpu.SMEM)]
        + [vmem] * (len(pieces) + 1)
        + [hbm],
        out_specs=[hbm, hbm],
        scratch_shapes=[
            pltpu.VMEM(shape, f32),
            pltpu.VMEM((slabs, slab_rows, ACTIVE), f32),
            pltpu.SemaphoreType.DMA((2,)),
        ],
        input_output_aliases={len(pieces) + 2: 1},
        compiler_params=pltpu.CompilerParams(vmem_limit_bytes=8 * 2**20),
        cost_estimate=pl.CostEstimate(
            flops=0, bytes_accessed=8 * len(pieces) * pieces[0].size, transcendentals=0
        ),
        name="finish",
    )(rank.reshape(1), *[pieces[d] for d in message_order(len(pieces))], given, sinogram)


def exchange(pieces, axis):
    count = len(pieces)
    results = list(pieces)
    for d in range(count - 1, 0, -1):
        results[d] = lax.ppermute(pieces[d], axis, [(i, i ^ d) for i in range(count)])
    return results


def local(intensity, angles, volume, vol_list):
    n_slab = lax.axis_size("slab")
    n_ray = lax.axis_size("ray")
    devices = n_slab * n_ray
    height, band = intensity.shape[2:]
    slices = height // devices
    slots = volume.shape[1]
    count = angles.shape[0] * angles.shape[1]
    step_size = relax * ROI / count
    rank = lax.axis_index("slab")
    ray_rank = lax.axis_index("ray")
    padded = -(-slices // ROWS) * ROWS

    def to_all(values, axes):
        return lax.all_to_all(values, axes, split_axis=0, concat_axis=0, tiled=True)

    own_volume = to_all(volume.reshape(n_ray, slices * slots, VOX), "ray")
    *parts, active = paganin(intensity.reshape(height, band), rank, n_slab)
    active, own_volume = lax.optimization_barrier((active, own_volume))
    own_rays = to_all(active.reshape(devices, slices, ACTIVE), ("slab", "ray"))
    if padded != slices:
        more = padded - slices
        own_volume = jnp.pad(own_volume, ((0, 0), (0, more * slots), (0, 0)))
        own_rays = jnp.pad(own_rays, ((0, 0), (0, more), (0, 0)))

    angles, vol_list, own_volume, parts = lax.optimization_barrier(
        (angles, vol_list, own_volume, parts)
    )
    sirt = Sirt(angles.reshape(-1), vol_list, padded, slots, n_ray, step_size)
    start, predicted, gain = sirt.first(own_volume)
    own_rays, parts, start = lax.optimization_barrier((own_rays, parts, start))
    parts = exchange(parts, "slab")
    pieces = sirt.second(ray_rank, own_volume, start, predicted, gain, own_rays)
    pieces, parts = lax.optimization_barrier((pieces, parts))
    if padded != slices:
        narrow = []
        for piece in pieces:
            lower = piece[padded * slots :].reshape(-1, padded, ACTIVE)[:, :slices]
            lower = lower.reshape(-1, ACTIVE)
            narrow.append(jnp.concatenate([piece[: slices * slots], lower], axis=0))
        pieces = narrow
    pieces = exchange(pieces, "ray")
    sinogram, given = gather_parts(parts, rank)
    if padded == slices:
        reconstruction, residual = finish(pieces, given, sinogram, ray_rank, volume.shape)
    else:
        order = ray_rank ^ jnp.arange(n_ray, dtype=jnp.int32)
        pieces = jnp.take(jnp.stack(pieces), order, axis=0)
        reconstruction = pieces[:, : slices * slots].reshape(volume.shape)
        lower = pieces[:, slices * slots :].reshape(n_ray, -1, 3, slices, ACTIVE)
        left = lower[:, :, :2].reshape(n_ray, -1, 2, slices, 2, LANES)
        left = jnp.transpose(left, (1, 2, 4, 0, 3, 5)).reshape(n_slab, n_ray * slices, LANES)
        rest = lower[:, :, 2].reshape(n_ray, -1, slices, 4, SPLIT)
        rest = jnp.transpose(rest, (1, 3, 0, 2, 4)).reshape(n_slab, n_ray * slices, SPLIT)
        begin = (band - ACTIVE) // 2 + EDGE
        live = jnp.concatenate([left, rest], axis=2)
        residual = lax.dynamic_update_slice(sinogram, live, (0, 0, begin))
    return (reconstruction, residual[:, None])


def solution(mesh):
    placed = (P("slab", "ray", None, None), P(), P("slab", "ray", None), P())
    return jax.shard_map(
        local,
        mesh=mesh,
        in_specs=placed,
        out_specs=(P("slab", "ray", None), P(None, "ray", "slab", None)),
        check_vma=False,
    )
```

```python
import functools
import math

import jax
import jax.numpy as jnp
import ml_dtypes
import numpy as np
from jax import lax
from jax.experimental import pallas as pl
from jax.experimental.pallas import tpu as pltpu
from jax.sharding import PartitionSpec as P

BAND = 2048
PGRID = 8
ROI = 128
SIDE = 16
VOX = SIDE * SIDE
WIN = 24
ACTIVE = 256
LANES = 128
ROWS = 8
SPLIT = 64
EDGE = 32
GROUP = 8
CYCLE = 8

paganin_strength = 10.0
relax = 1.8
row_floor = 0.25

bf16 = jnp.bfloat16
f32 = jnp.float32


def halves(values):
    high = values.astype(bf16)
    low = (values - high.astype(f32)).astype(bf16)
    return high, low


def thirds(values):
    high = values.astype(bf16)
    rest = values - high.astype(f32)
    middle = rest.astype(bf16)
    low = (rest - middle.astype(f32)).astype(bf16)
    return high, middle, low


def dot(left, right):
    return jnp.dot(left, right, preferred_element_type=f32)


def repeat(count, body, unroll):
    unroll = math.gcd(count, unroll)

    def several(index, carry):
        for step in range(unroll):
            body(index * unroll + step)
        return carry

    lax.fori_loop(0, count // unroll, several, 0)


def filter_tables(height):
    index = np.arange(height)
    phase = 2.0 * np.pi * (np.outer(index, index) % height) / height
    cas = (np.cos(phase) + np.sin(phase)) / math.sqrt(height)
    row_freq = 2.0 - 2.0 * np.cos(2.0 * np.pi * index / height)
    middle = (1.0 + paganin_strength * row_freq) / paganin_strength + 2.0
    rho = (middle - np.sqrt(middle * middle - 4.0)) / 2.0
    return np.concatenate([cas, np.repeat(rho[None, :], ROWS, axis=0)], axis=0).astype(np.float32)


def chunk_carry(ends, power, forward):
    shift = 1
    for _ in range(3):
        ends = ends + power * pltpu.roll(ends, shift if forward else ROWS - shift, 0)
        power = power * power
        shift *= 2
    return pltpu.roll(ends, 1 if forward else ROWS - 1, 0) / (1.0 - power)


def filter_kernel(rank_ref, source_ref, given_ref, *refs):
    *part_refs, active_ref, image_ref, table_ref, out_ref, spec_ref, up_ref, down_ref = refs[:-2]
    sems, out_sems = refs[-2:]
    height, width = image_ref.shape
    rank = rank_ref[0]
    share = height // len(part_refs)
    length = width // ROWS
    blocks = height // LANES
    unroll = 8
    copies = []
    for c in range(ROWS):
        columns = slice(c * length, (c + 1) * length)
        copies.append(
            pltpu.make_async_copy(
                source_ref.at[:, columns], image_ref.at[:, columns], sems.at[c]
            )
        )
    given = pltpu.make_async_copy(given_ref, table_ref, sems.at[ROWS])
    given.start()
    for copy in copies:
        copy.start()
    given.wait()
    cas_high, cas_low = halves(table_ref[0:height, :])
    rho_all = table_ref[height : height + ROWS, :]
    rhos = [rho_all[:, b * LANES : (b + 1) * LANES] for b in range(blocks)]
    zeros = [jnp.zeros((ROWS, LANES), f32)] * blocks

    def transform(values):
        high, low = halves(values)
        return dot(high, cas_high) + dot(low, cas_high) + dot(high, cas_low)

    for c in range(ROWS):
        copies[c].wait()
        image = 1.0 - image_ref[:, c * length : (c + 1) * length]
        spectrum = transform(jnp.transpose(image))
        for b in range(blocks):
            spec_ref[b, pl.ds(c, length, stride=ROWS), :] = spectrum[
                :, b * LANES : (b + 1) * LANES
            ]

    def rows(position):
        return pl.ds(pl.multiple_of(position * ROWS, ROWS), ROWS)

    def advance(position, ups, downs):
        ups = [spec_ref[b, rows(position), :] + rhos[b] * ups[b] for b in range(blocks)]
        back = length - 1 - position
        downs = [spec_ref[b, rows(back), :] + rhos[b] * downs[b] for b in range(blocks)]
        return ups, downs

    def sweep(index, carry):
        ups, downs = carry
        for step in range(unroll):
            ups, downs = advance(index * unroll + step, ups, downs)
        return ups, downs

    ups, downs = lax.fori_loop(0, length // unroll, sweep, (zeros, zeros))
    powers = list(rhos)
    for _ in range(int(math.log2(length))):
        powers = [power * power for power in powers]
    ups = [chunk_carry(ups[b], powers[b], True) for b in range(blocks)]
    downs = [chunk_carry(downs[b], powers[b], False) for b in range(blocks)]
    scales = [rho / (paganin_strength * (1.0 - rho * rho)) for rho in rhos]

    def outer(index, carry):
        ups, downs = carry
        for step in range(unroll):
            position = index * unroll + step
            ups, downs = advance(position, ups, downs)
            for b in range(blocks):
                up_ref[b, rows(position), :] = ups[b]
                down_ref[b, rows(position), :] = downs[b]
        return ups, downs

    def inner(index, carry):
        ups, downs = carry
        for step in range(unroll):
            position = index * unroll + step
            back = length - 1 - position
            ups, downs = advance(position, ups, downs)
            for b in range(blocks):
                here = ups[b] + down_ref[b, rows(back), :] - spec_ref[b, rows(position), :]
                there = downs[b] + up_ref[b, rows(back), :] - spec_ref[b, rows(back), :]
                up_ref[b, rows(position), :] = here * scales[b]
                up_ref[b, rows(back), :] = there * scales[b]
        return ups, downs

    half = length // 2 // unroll
    carry = lax.fori_loop(0, half, outer, (ups, downs))
    lax.fori_loop(half, 2 * half, inner, carry)

    offset = (width - ACTIVE) // 2
    sent = []
    for c in range(ROWS):
        spectrum = jnp.concatenate(
            [up_ref[b, pl.ds(c, length, stride=ROWS), :] for b in range(blocks)], axis=1
        )
        filtered = 1.0 - jnp.transpose(transform(spectrum))
        columns = slice(c * length, (c + 1) * length)
        out_ref[:, columns] = -jnp.log(filtered)
        for d, part_ref in enumerate(part_refs):
            rows = pl.ds(pl.multiple_of((rank ^ d) * share, share), share)
            sent.append(
                pltpu.make_async_copy(
                    out_ref.at[rows, columns], part_ref.at[:, columns], out_sems.at[c, d]
                )
            )
            sent[-1].start()
        if c == (offset + ACTIVE - 1) // length:
            columns = slice(offset, offset + ACTIVE)
            sent.append(
                pltpu.make_async_copy(out_ref.at[:, columns], active_ref, sems.at[0])
            )
            sent[-1].start()
    for copy in sent:
        copy.wait()


def paganin(image, rank, parts):
    height, width = image.shape
    blocks = height // LANES
    return pl.pallas_call(
        filter_kernel,
        out_shape=[jax.ShapeDtypeStruct((height // parts, width), f32)] * parts
        + [jax.ShapeDtypeStruct((height, ACTIVE), f32)],
        in_specs=[pl.BlockSpec(memory_space=pltpu.SMEM)]
        + [pl.BlockSpec(memory_space=pltpu.HBM)] * 2,
        out_specs=[pl.BlockSpec(memory_space=pltpu.HBM)] * (parts + 1),
        scratch_shapes=[
            pltpu.VMEM((height, width), f32),
            pltpu.VMEM((height + ROWS, height), f32),
            pltpu.VMEM((height, width), f32),
            pltpu.VMEM((blocks, width, LANES), f32),
            pltpu.VMEM((blocks, width, LANES), f32),
            pltpu.VMEM((blocks, width // 2, LANES), f32),
            pltpu.SemaphoreType.DMA((ROWS + 1,)),
            pltpu.SemaphoreType.DMA((ROWS, parts)),
        ],
        compiler_params=pltpu.CompilerParams(vmem_limit_bytes=58 * 2**20),
        cost_estimate=pl.CostEstimate(
            flops=64 * height * height * width,
            bytes_accessed=8 * height * width,
            transcendentals=height * width,
        ),
        name="paganin",
    )(rank.reshape(1), image, jnp.asarray(filter_tables(height)))


def reversed_exact(values, flip):
    return sum(dot(part, flip) for part in thirds(values))


class Weights:
    def __init__(self, along_ref, place_ref, angles, chunk):
        self.along_ref = along_ref
        self.place_ref = place_ref
        self.angles = angles
        self.chunk = chunk
        self.ray = lax.broadcasted_iota(jnp.int32, (ROWS, VOX), 0).astype(f32)

    def prepare(self, shift_x_ref, shift_y_ref, cos_ref, sin_ref):
        def along_angle(t):
            along = shift_x_ref[...] * cos_ref[t] + shift_y_ref[...] * sin_ref[t]
            self.along_ref[t] = self.ray - along

        repeat(self.angles, along_angle, 8)

    def make(self, q, c, ref):
        for two in range(self.chunk // 2):
            pieces = []
            for t in (2 * two, 2 * two + 1):
                angle = c * self.chunk + t
                base = self.along_ref[angle] - self.place_ref[q * self.angles + angle]
                for group in range(WIN // ROWS):
                    distance = base + float(group * ROWS)
                    pieces.append(jnp.maximum(0.0, 1.0 - jnp.abs(distance)))
            high, low = halves(jnp.concatenate(pieces, axis=0))
            ref[2 * two * WIN : (2 * two + 2) * WIN, 0:VOX] = high
            ref[2 * two * WIN : (2 * two + 2) * WIN, VOX : 2 * VOX] = low


def ray_operand(values, sums_too):
    high, low = halves(values)
    rows = [
        jnp.concatenate([high, high], axis=1),
        jnp.concatenate([low, jnp.zeros_like(low)], axis=1),
    ]
    if sums_too:
        rows.append(jnp.ones((values.shape[0], 2 * VOX), bf16))
    return jnp.concatenate(rows, axis=0)


def row_operands(values, sums_too):
    rows = ray_operand(values, sums_too)
    count, width = rows.shape
    spare = jnp.zeros((SPLIT - count, width), bf16)
    empty = jnp.zeros((SPLIT, width), bf16)
    return (
        jnp.concatenate([rows, spare, empty], axis=0),
        jnp.concatenate([empty, rows, spare], axis=0),
    )


def project_rows(held_ref, operands, q, c, sizes, offset_ref, acc_ref):
    angles, chunk = sizes[:2]
    half = chunk // 2
    for begin in range(0, chunk, GROUP):
        sums = lax.dot_general(
            held_ref[begin * WIN : (begin + GROUP) * WIN, :],
            operands[begin // half],
            (((1,), (1,)), ((), ())),
            preferred_element_type=f32,
        )
        places = []
        for t in range(begin, begin + GROUP):
            rows = pl.ds(offset_ref[q * angles + c * chunk + t], WIN)
            piece = sums[(t - begin) * WIN : (t - begin + 1) * WIN, :]
            index = c * half + t % half
            places.append((index, rows, acc_ref[index, rows, :] + piece))
        for index, rows, values in places:
            acc_ref[index, rows, :] = values


def spread_rays(acc_ref, direct_ref, mirror_ref, total_ref, slices, chunk):
    both = 2 * slices
    half = chunk // 2

    def spread(index):
        turned = jnp.transpose(acc_ref[index]) * (1.0 / ROI)
        for part in range(2):
            rows = turned[part * SPLIT : (part + 1) * SPLIT]
            t = index // half * chunk + part * half + index % half
            direct_ref[t] = rows[0:slices] + rows[both : both + slices]
            mirror_ref[t] = rows[slices:both] + rows[both + slices : 2 * both]
            if total_ref is not None:
                total_ref[t] = rows[2 * both : 2 * both + slices]

    repeat(acc_ref.shape[0], spread, 8)


def turn_rays(values, flip):
    shape = values.shape
    return reversed_exact(values.reshape(-1, shape[-1]), flip).reshape(shape)


def fill_windows(weighted, flip, window_ref):
    angles, slices, _ = weighted.shape
    high, low = halves(weighted.reshape(angles * slices, ACTIVE))
    mirrored = (dot(high, flip) + dot(low, flip)).reshape(weighted.shape)
    lane = lax.broadcasted_iota(jnp.int32, (angles, slices, LANES), 2)
    for part, source in enumerate((weighted, mirrored)):
        rows = slice(part * slices, (part + 1) * slices)
        left = source[:, :, 0:LANES]
        right = source[:, :, LANES : 2 * LANES]
        window_ref[:, 0, rows, :] = left
        window_ref[:, 2, rows, :] = right
        mixed = jnp.where(lane >= SPLIT, left, right)
        window_ref[:, 1, rows, :] = pltpu.roll(mixed, SPLIT, 2)


def window_operand(q, c, sizes, window_ref, tile_ref, turn_ref):
    angles, chunk = sizes[:2]
    both = window_ref.shape[2]
    lane_rows = lax.broadcasted_iota(jnp.int32, (both, LANES), 1)
    tiles = [None] * (-(-chunk * WIN // LANES))
    for t in range(chunk):
        index = q * angles + c * chunk + t
        piece = pltpu.roll(window_ref[c * chunk + t, tile_ref[index]], turn_ref[index], 1)
        begin = t * WIN
        for place in range(begin // LANES, (begin + WIN - 1) // LANES + 1):
            if tiles[place] is None:
                tiles[place] = piece
            else:
                tiles[place] = jnp.where(
                    lane_rows >= begin - place * LANES, piece, tiles[place]
                )
    high, low = halves(jnp.concatenate(tiles, axis=1))
    return jnp.concatenate([high, low], axis=0)


def update_pair(operand, held):
    both = operand.shape[0] // 2
    sums = dot(operand, held)
    return sums[0:both, 0:VOX] + sums[both:, 0:VOX] + sums[0:both, VOX:]


def first_kernel(
    sizes,
    place_ref,
    offset_ref,
    slot_ref,
    cos_ref,
    sin_ref,
    vol_ref,
    flip_ref,
    shift_x_ref,
    shift_y_ref,
    kept_ref,
    predicted_ref,
    gain_ref,
    *refs,
):
    held_refs = refs[:CYCLE]
    acc_ref, along_ref, half_ref, mirror_ref, start_ref, sem = refs[CYCLE:]
    angles, chunk, slots = sizes
    patches = slot_ref.shape[0]
    pairs, both, _ = start_ref.shape
    slices = both // 2
    flip = flip_ref[...]

    def slot_values(patch):
        slot = slot_ref[patch]
        rows = pl.ds(slot % slots, slices, stride=slots)
        return jnp.concatenate(
            [half_ref[part, slot // slots, rows, :] for part in range(2)], axis=1
        )

    for part in range(2):
        half_ref[part] = vol_ref[:, :, part * LANES : (part + 1) * LANES]

    def order(q):
        start_ref[q, 0:slices, :] = slot_values(q)
        mirror_ref[q] = slot_values(patches - 1 - q)

    repeat(pairs, order, 8)
    start_ref[:, slices:both, :] = turn_rays(mirror_ref[0:pairs], flip)
    weights = Weights(along_ref, place_ref, angles, chunk)
    weights.prepare(shift_x_ref, shift_y_ref, cos_ref, sin_ref)
    acc_ref[...] = jnp.zeros(acc_ref.shape, f32)

    kept = pltpu.make_async_copy(start_ref, kept_ref, sem)
    kept.start()
    chunks = angles // chunk

    def cycle(index, carry):
        for step in range(CYCLE):
            q = index * CYCLE + step
            operands = row_operands(start_ref[q], True)
            for c in range(chunks):
                more = jnp.minimum(q + (c + 1) // chunks, pairs - 1)
                after = (step * chunks + c + 1) % CYCLE
                weights.make(more, (c + 1) % chunks, held_refs[after])
                here = held_refs[(step * chunks + c) % CYCLE]
                project_rows(here, operands, q, c, sizes, offset_ref, acc_ref)
        return carry

    weights.make(0, 0, held_refs[0])
    lax.fori_loop(0, pairs // CYCLE, cycle, 0)
    spread_rays(acc_ref, predicted_ref, mirror_ref, gain_ref, slices, chunk)
    direct, mirror, weight_sums = predicted_ref[...], mirror_ref[0:angles], gain_ref[...]
    predicted_ref[...] = direct + turn_rays(mirror, flip)
    turned = turn_rays(weight_sums[:, 0, :], flip)
    total = weight_sums + turned[:, None, :]
    gain_ref[...] = 1.0 / jnp.maximum(total, row_floor)
    kept.wait()


def second_kernel(
    sizes,
    step_size,
    rank_ref,
    offset_ref,
    place_ref,
    tile_ref,
    turn_ref,
    slot_ref,
    cos_ref,
    sin_ref,
    vol_ref,
    predicted_ref,
    gain_ref,
    sino_ref,
    flip_ref,
    shift_x_ref,
    shift_y_ref,
    kept_ref,
    *refs,
):
    angles, chunk, slots = sizes
    rays = vol_ref.shape[0]
    out_refs, refs = refs[:rays], refs[rays:]
    held_refs = refs[:CYCLE]
    acc_ref, along_ref, direct_ref, mirror_ref, window_ref, update_ref, half_ref = refs[
        CYCLE:-2
    ]
    start_ref, sem = refs[-2:]
    kept = pltpu.make_async_copy(kept_ref, start_ref, sem)
    kept.start()
    patches = slot_ref.shape[0]
    pairs, both, _ = start_ref.shape
    slices = both // 2
    flip = flip_ref[...]
    weights = Weights(along_ref, place_ref, angles, chunk)
    weights.prepare(shift_x_ref, shift_y_ref, cos_ref, sin_ref)
    chunks = angles // chunk
    windows = (sizes, window_ref, tile_ref, turn_ref)
    rest = (sizes, offset_ref, acc_ref)
    fill_windows(
        (sino_ref[...] - predicted_ref[...]) * gain_ref[...] * (1.0 / ROI), flip, window_ref
    )
    acc_ref[...] = jnp.zeros(acc_ref.shape, f32)
    kept.wait()

    def advance(q, operand, held):
        total = update_pair(operand, held)
        update_ref[q] = total
        return start_ref[q] + step_size * total

    def forward(values, q, held):
        project_rows(held, row_operands(values, False), q, 0, *rest)

    def cycle(index, carry):
        values, operand = carry
        for step in range(CYCLE):
            q = index * CYCLE + step
            after = (step + 1) % CYCLE
            before = (step - 1) % CYCLE
            later = index + (step + 1) // CYCLE
            earlier = index if step else jnp.maximum(index - 1, 0)
            following = jnp.minimum(q + 1, pairs - 1)
            next_operand = window_operand(following, 0, *windows)
            weights.make(following, 0, held_refs[after].at[later])
            new_values = advance(q, operand, held_refs[step][index])
            forward(values, jnp.maximum(q - 1, 0), held_refs[before].at[earlier])
            values, operand = new_values, next_operand
        return values, operand

    def all_chunks(q, body):
        for c in range(chunks):
            weights.make(q, c, held_refs[0].at[0])
            body(c, held_refs[0].at[0])

    def plain_update(q, carry):
        update_ref[q] = jnp.zeros(update_ref.shape[1:], f32)

        def add(c, held):
            operand = window_operand(q, c, *windows)
            update_ref[q] = update_ref[q] + update_pair(operand, held[...])

        all_chunks(q, add)
        return carry

    def plain_forward(q, carry):
        operands = row_operands(start_ref[q] + step_size * update_ref[q], False)
        all_chunks(q, lambda c, held: project_rows(held, operands, q, c, *rest))
        return carry

    if chunks == 1:
        held_refs[CYCLE - 1][0] = jnp.zeros(held_refs[CYCLE - 1].shape[1:], bf16)
        weights.make(0, 0, held_refs[0].at[0])
        begin = (jnp.zeros((both, VOX), f32), window_operand(0, 0, *windows))
        values, _ = lax.fori_loop(0, pairs // CYCLE, cycle, begin)
        forward(values, pairs - 1, held_refs[CYCLE - 1].at[pairs // CYCLE - 1])
    else:
        lax.fori_loop(0, pairs, plain_update, 0)
        lax.fori_loop(0, pairs, plain_forward, 0)

    spread_rays(acc_ref, direct_ref, mirror_ref, None, slices, chunk)
    turned = turn_rays(mirror_ref[0:angles], flip)
    direct_ref[...] = sino_ref[...] - direct_ref[...] - turned
    fill_windows(direct_ref[...] * gain_ref[...] * (1.0 / ROI), flip, window_ref)

    def last_cycle(index, operand):
        for step in range(CYCLE):
            q = index * CYCLE + step
            next_operand = window_operand(jnp.minimum(q + 1, pairs - 1), 0, *windows)
            total = update_pair(operand, held_refs[step][index])
            update_ref[q] = (update_ref[q] + total) * step_size
            operand = next_operand
        return operand

    def plain_last(q, carry):
        def add(c, held):
            operand = window_operand(q, c, *windows)
            update_ref[q] = update_ref[q] + update_pair(operand, held[...])

        all_chunks(q, add)
        update_ref[q] = update_ref[q] * step_size
        return carry

    if chunks == 1:
        lax.fori_loop(0, pairs // CYCLE, last_cycle, window_operand(0, 0, *windows))
    else:
        lax.fori_loop(0, pairs, plain_last, 0)

    mirror_ref[0:pairs] = turn_rays(update_ref[:, slices:both, :], flip)
    for part in range(2):
        half_ref[part] = vol_ref[:, :, part * LANES : (part + 1) * LANES]

    def finish(q):
        for patch, update in (
            (q, update_ref[q, 0:slices, :]),
            (patches - 1 - q, mirror_ref[q]),
        ):
            slot = slot_ref[patch]
            rows = pl.ds(slot % slots, slices, stride=slots)
            for part in range(2):
                half_ref[part, slot // slots, rows, :] = (
                    half_ref[part, slot // slots, rows, :]
                    + update[:, part * LANES : (part + 1) * LANES]
                )

    repeat(pairs, finish, 8)
    lead = slices * slots
    lane = lax.broadcasted_iota(jnp.int32, (slices, LANES), 1)
    for d, out_ref in enumerate(out_refs):
        ray = rank_ref[0] ^ d
        for part in range(2):
            out_ref[0:lead, part * LANES : (part + 1) * LANES] = half_ref[part, ray]
        for k in range(0, angles // rays, 4):
            begin = lead + k // 4 * 3 * slices
            live = [
                pltpu.roll(direct_ref[(k + i) * rays + ray], ACTIVE - EDGE, 1)
                for i in range(4)
            ]
            rest = [part[:, LANES:] for part in live]
            for i in range(2):
                here = begin + i * slices
                out_ref[here : here + slices, 0:LANES] = live[2 * i][:, 0:LANES]
                out_ref[here : here + slices, LANES:] = live[2 * i + 1][:, 0:LANES]
                here = begin + 2 * slices
                out_ref[here : here + slices, i * LANES : (i + 1) * LANES] = jnp.where(
                    lane < SPLIT, rest[2 * i], pltpu.roll(rest[2 * i + 1], SPLIT, 1)
                )


def call(kernel, name, inputs, held_in, held_out, outputs, scratch, micros):
    smem = pl.BlockSpec(memory_space=pltpu.SMEM)
    vmem = pl.BlockSpec(memory_space=pltpu.VMEM)
    hbm = pl.BlockSpec(memory_space=pltpu.HBM)
    return pl.pallas_call(
        kernel,
        out_shape=[jax.ShapeDtypeStruct(*value) for value in held_out + outputs],
        in_specs=[smem if value.ndim == 1 else vmem for value in inputs] + [hbm] * len(held_in),
        out_specs=[hbm] * len(held_out) + [vmem] * len(outputs),
        scratch_shapes=[pltpu.VMEM(*value) for value in scratch]
        + [pltpu.SemaphoreType.DMA],
        compiler_params=pltpu.CompilerParams(vmem_limit_bytes=52 * 2**20),
        cost_estimate=pl.CostEstimate(
            flops=int(micros * 1e9), bytes_accessed=4 * 2**20, transcendentals=0
        ),
        name=name,
    )(*inputs, *held_in)


class Sirt:
    def __init__(self, theta, vol_list, slices, slots, rays, step_size):
        angles = theta.shape[0]
        patches = vol_list.shape[0]
        pairs = patches // 2
        both = 2 * slices
        chunk = math.gcd(angles, 32)
        self.sizes = (angles, chunk, slots)
        self.step_size = step_size
        self.rays = rays
        self.patches = patches
        centre = (ROI - 1) / 2.0
        ids = np.arange(pairs)
        centre_x = (ids // PGRID * float(SIDE) + (SIDE - 1) / 2.0 - centre).astype(np.float32)
        centre_y = (ids % PGRID * float(SIDE) + (SIDE - 1) / 2.0 - centre).astype(np.float32)
        self.cosine = jnp.cos(theta)
        self.sine = jnp.sin(theta)
        along = (
            centre_x[:, None] * self.cosine[None, :]
            + centre_y[:, None] * self.sine[None, :]
            + 0.5
        )
        whole = jnp.floor(along)
        lead = WIN // 2 - 1
        place = along - whole + float(lead)
        offset = whole.astype(jnp.int32) + (ACTIVE // 2 - 1 - lead)
        tile = jnp.minimum(offset // SPLIT, 2)
        local = jnp.arange(angles, dtype=jnp.int32) % chunk * WIN
        turn = (local[None, :] - offset + tile * SPLIT) % LANES
        self.offset = offset.reshape(-1)
        self.place = place.reshape(-1)
        self.tile = tile.reshape(-1)
        self.turn = turn.reshape(-1)
        ids = jnp.arange(patches, dtype=jnp.int32)
        self.slot = jnp.sum(
            jnp.where(vol_list[None, :] == ids[:, None], ids[None, :], 0), axis=1
        )
        voxel = np.arange(VOX)
        shift_x = np.repeat((voxel // SIDE - (SIDE - 1) / 2.0)[None, :], ROWS, axis=0)
        shift_y = np.repeat((voxel % SIDE - (SIDE - 1) / 2.0)[None, :], ROWS, axis=0)
        flip = np.eye(ACTIVE)[::-1].astype(ml_dtypes.bfloat16)
        self.fixed = [jnp.asarray(flip), jnp.asarray(shift_x, f32), jnp.asarray(shift_y, f32)]
        self.weight = ((chunk * WIN, 2 * VOX), bf16)
        self.held = (pairs // CYCLE + 1 if angles == chunk else 1,) + self.weight[0]
        self.acc_rows = ((angles // 2, ACTIVE, LANES), f32)
        self.along = ((angles, ROWS, VOX), f32)
        self.by_ray = ((angles, slices, ACTIVE), f32)
        self.by_pair = ((pairs, both, VOX), f32)
        self.window = ((angles, 3, both, LANES), f32)
        self.half = ((2, rays, slices * slots, LANES), f32)
        self.mirror = ((max(pairs, angles), slices, ACTIVE), f32)
        self.sent = [((slices * (slots + angles // rays * 3 // 4), ACTIVE), f32)] * rays

    def first(self, volume):
        inputs = [self.place, self.offset, self.slot, self.cosine, self.sine, volume]
        return call(
            functools.partial(first_kernel, self.sizes),
            "first",
            inputs + self.fixed,
            [],
            [self.by_pair],
            [self.by_ray, self.by_ray],
            [self.weight] * CYCLE
            + [self.acc_rows, self.along, self.half, self.mirror, self.by_pair],
            14,
        )

    def second(self, rank, volume, start, predicted, gain, sino):
        inputs = [rank.reshape(1), self.offset, self.place, self.tile, self.turn, self.slot]
        inputs += [self.cosine, self.sine, volume, predicted, gain, sino]
        scratch = [(self.held, bf16)] * CYCLE
        scratch += [self.acc_rows, self.along, self.by_ray, self.mirror, self.window]
        return call(
            functools.partial(second_kernel, self.sizes, self.step_size),
            "second",
            inputs + self.fixed,
            [start],
            [],
            self.sent,
            scratch + [self.by_pair, self.half, self.by_pair],
            26,
        )


def gather_kernel(rank_ref, *refs):
    *part_refs, out_ref, active_ref, sems = refs
    rank = rank_ref[0]
    copies = [
        pltpu.make_async_copy(part_ref, out_ref.at[rank ^ d], sems.at[d])
        for d, part_ref in enumerate(part_refs)
    ]
    for copy in copies:
        copy.start()
    offset = (out_ref.shape[2] - ACTIVE) // 2
    for d, part_ref in enumerate(part_refs):
        active_ref[rank ^ d] = part_ref[:, offset : offset + ACTIVE]
    for copy in copies:
        copy.wait()


def gather_parts(parts, rank):
    count = len(parts)
    rows = parts[0].shape[0]
    vmem = pl.BlockSpec(memory_space=pltpu.VMEM)
    return pl.pallas_call(
        gather_kernel,
        out_shape=(
            jax.ShapeDtypeStruct((count,) + parts[0].shape, f32),
            jax.ShapeDtypeStruct((count, rows, ACTIVE), f32),
        ),
        in_specs=[pl.BlockSpec(memory_space=pltpu.SMEM)] + [vmem] * count,
        out_specs=(pl.BlockSpec(memory_space=pltpu.HBM), vmem),
        scratch_shapes=[pltpu.SemaphoreType.DMA((count,))],
        compiler_params=pltpu.CompilerParams(vmem_limit_bytes=8 * 2**20),
        cost_estimate=pl.CostEstimate(
            flops=0, bytes_accessed=8 * count * parts[0].size, transcendentals=0
        ),
        name="gather_parts",
    )(rank.reshape(1), *parts)


def message_order(count):
    near = [d for d in (1, 2) if d < count // 2]
    far = list(range(count - 1, count // 2 - 1, -1))
    return near + far + [d for d in range(count // 2 - 1, -1, -1) if d not in near]


def finish_kernel(rank_ref, *refs):
    *got_refs, given_ref, _, rec_ref, out_ref, values_ref, active_ref, sems = refs
    rays = len(got_refs)
    slots = values_ref.shape[1]
    slabs = active_ref.shape[0]
    slices = values_ref.shape[0] // rays
    lead = slices * slots
    lane = lax.broadcasted_iota(jnp.int32, (slices, ACTIVE), 1)
    live = (lane >= EDGE) & (lane < ACTIVE - EDGE)
    for d, got_ref in zip(message_order(rays), got_refs):
        rows = pl.ds(pl.multiple_of((rank_ref[0] ^ d) * slices, slices), slices)
        values_ref[rows] = got_ref[0:lead, :].reshape(slices, slots, VOX)
        for k in range(slabs):
            begin = lead + k // 4 * 3 * slices
            pair, side = k % 4 // 2, k % 2
            here = begin + pair * slices
            left = got_ref[here : here + slices, side * LANES : (side + 1) * LANES]
            here = begin + 2 * slices
            rest = got_ref[here : here + slices, pair * LANES : (pair + 1) * LANES]
            if side:
                rest = pltpu.roll(rest, SPLIT, 1)
            whole = pltpu.roll(jnp.concatenate([left, rest], axis=1), EDGE, 1)
            active_ref[k, rows, :] = jnp.where(live, whole, given_ref[k, rows, :])
    offset = (out_ref.shape[2] - ACTIVE) // 2
    copies = [
        pltpu.make_async_copy(values_ref, rec_ref, sems.at[0]),
        pltpu.make_async_copy(
            active_ref, out_ref.at[:, :, offset : offset + ACTIVE], sems.at[1]
        ),
    ]
    for copy in copies:
        copy.start()
    for copy in copies:
        copy.wait()


def finish(pieces, given, sinogram, rank, shape):
    slabs, slab_rows, _ = sinogram.shape
    hbm = pl.BlockSpec(memory_space=pltpu.HBM)
    vmem = pl.BlockSpec(memory_space=pltpu.VMEM)
    return pl.pallas_call(
        finish_kernel,
        out_shape=(
            jax.ShapeDtypeStruct(shape, f32),
            jax.ShapeDtypeStruct(sinogram.shape, f32),
        ),
        in_specs=[pl.BlockSpec(memory_space=pltpu.SMEM)]
        + [vmem] * (len(pieces) + 1)
        + [hbm],
        out_specs=[hbm, hbm],
        scratch_shapes=[
            pltpu.VMEM(shape, f32),
            pltpu.VMEM((slabs, slab_rows, ACTIVE), f32),
            pltpu.SemaphoreType.DMA((2,)),
        ],
        input_output_aliases={len(pieces) + 2: 1},
        compiler_params=pltpu.CompilerParams(vmem_limit_bytes=8 * 2**20),
        cost_estimate=pl.CostEstimate(
            flops=0, bytes_accessed=8 * len(pieces) * pieces[0].size, transcendentals=0
        ),
        name="finish",
    )(rank.reshape(1), *[pieces[d] for d in message_order(len(pieces))], given, sinogram)


def exchange(pieces, axis):
    count = len(pieces)
    results = list(pieces)
    for d in range(count - 1, 0, -1):
        results[d] = lax.ppermute(pieces[d], axis, [(i, i ^ d) for i in range(count)])
    return results


def local(intensity, angles, volume, vol_list):
    n_slab = lax.axis_size("slab")
    n_ray = lax.axis_size("ray")
    devices = n_slab * n_ray
    height, band = intensity.shape[2:]
    slices = height // devices
    slots = volume.shape[1]
    count = angles.shape[0] * angles.shape[1]
    step_size = relax * ROI / count
    rank = lax.axis_index("slab")
    ray_rank = lax.axis_index("ray")
    padded = -(-slices // ROWS) * ROWS

    def to_all(values, axes):
        return lax.all_to_all(values, axes, split_axis=0, concat_axis=0, tiled=True)

    own_volume = to_all(volume.reshape(n_ray, slices * slots, VOX), "ray")
    *parts, active = paganin(intensity.reshape(height, band), rank, n_slab)
    active, own_volume = lax.optimization_barrier((active, own_volume))
    own_rays = to_all(active.reshape(devices, slices, ACTIVE), ("slab", "ray"))
    if padded != slices:
        more = padded - slices
        own_volume = jnp.pad(own_volume, ((0, 0), (0, more * slots), (0, 0)))
        own_rays = jnp.pad(own_rays, ((0, 0), (0, more), (0, 0)))

    angles, vol_list, own_volume, parts = lax.optimization_barrier(
        (angles, vol_list, own_volume, parts)
    )
    sirt = Sirt(angles.reshape(-1), vol_list, padded, slots, n_ray, step_size)
    start, predicted, gain = sirt.first(own_volume)
    own_rays, parts, start = lax.optimization_barrier((own_rays, parts, start))
    parts = exchange(parts, "slab")
    pieces = sirt.second(ray_rank, own_volume, start, predicted, gain, own_rays)
    pieces, parts = lax.optimization_barrier((pieces, parts))
    if padded != slices:
        narrow = []
        for piece in pieces:
            lower = piece[padded * slots :].reshape(-1, padded, ACTIVE)[:, :slices]
            lower = lower.reshape(-1, ACTIVE)
            narrow.append(jnp.concatenate([piece[: slices * slots], lower], axis=0))
        pieces = narrow
    pieces = exchange(pieces, "ray")
    sinogram, given = gather_parts(parts, rank)
    if padded == slices:
        reconstruction, residual = finish(pieces, given, sinogram, ray_rank, volume.shape)
    else:
        order = ray_rank ^ jnp.arange(n_ray, dtype=jnp.int32)
        pieces = jnp.take(jnp.stack(pieces), order, axis=0)
        reconstruction = pieces[:, : slices * slots].reshape(volume.shape)
        lower = pieces[:, slices * slots :].reshape(n_ray, -1, 3, slices, ACTIVE)
        left = lower[:, :, :2].reshape(n_ray, -1, 2, slices, 2, LANES)
        left = jnp.transpose(left, (1, 2, 4, 0, 3, 5)).reshape(n_slab, n_ray * slices, LANES)
        rest = lower[:, :, 2].reshape(n_ray, -1, slices, 4, SPLIT)
        rest = jnp.transpose(rest, (1, 3, 0, 2, 4)).reshape(n_slab, n_ray * slices, SPLIT)
        begin = (band - ACTIVE) // 2 + EDGE
        live = jnp.concatenate([left, rest], axis=2)
        residual = lax.dynamic_update_slice(sinogram, live, (0, 0, begin))
    return (reconstruction, residual[:, None])


def solution(mesh):
    placed = (P("slab", "ray", None, None), P(), P("slab", "ray", None), P())
    return jax.shard_map(
        local,
        mesh=mesh,
        in_specs=placed,
        out_specs=(P("slab", "ray", None), P(None, "ray", "slab", None)),
        check_vma=False,
    )
```

```python
import functools
import math

import jax
import jax.numpy as jnp
import ml_dtypes
import numpy as np
from jax import lax
from jax.experimental import pallas as pl
from jax.experimental.pallas import tpu as pltpu
from jax.sharding import PartitionSpec as P

BAND = 2048
PGRID = 8
ROI = 128
SIDE = 16
VOX = SIDE * SIDE
WIN = 24
ACTIVE = 256
LANES = 128
ROWS = 8
SPLIT = 64
EDGE = 32
GROUP = 8
CYCLE = 16

paganin_strength = 10.0
relax = 1.8
row_floor = 0.25

bf16 = jnp.bfloat16
f32 = jnp.float32


def halves(values):
    high = values.astype(bf16)
    low = (values - high.astype(f32)).astype(bf16)
    return high, low


def thirds(values):
    high = values.astype(bf16)
    rest = values - high.astype(f32)
    middle = rest.astype(bf16)
    low = (rest - middle.astype(f32)).astype(bf16)
    return high, middle, low


def dot(left, right):
    return jnp.dot(left, right, preferred_element_type=f32)


def repeat(count, body, unroll):
    unroll = math.gcd(count, unroll)

    def several(index, carry):
        for step in range(unroll):
            body(index * unroll + step)
        return carry

    lax.fori_loop(0, count // unroll, several, 0)


def filter_tables(height):
    index = np.arange(height)
    phase = 2.0 * np.pi * (np.outer(index, index) % height) / height
    cas = (np.cos(phase) + np.sin(phase)) / math.sqrt(height)
    row_freq = 2.0 - 2.0 * np.cos(2.0 * np.pi * index / height)
    middle = (1.0 + paganin_strength * row_freq) / paganin_strength + 2.0
    rho = (middle - np.sqrt(middle * middle - 4.0)) / 2.0
    return np.concatenate([cas, np.repeat(rho[None, :], ROWS, axis=0)], axis=0).astype(np.float32)


def chunk_carry(ends, power, forward):
    shift = 1
    for _ in range(3):
        ends = ends + power * pltpu.roll(ends, shift if forward else ROWS - shift, 0)
        power = power * power
        shift *= 2
    return pltpu.roll(ends, 1 if forward else ROWS - 1, 0) / (1.0 - power)


def filter_kernel(rank_ref, source_ref, given_ref, *refs):
    *part_refs, active_ref, image_ref, table_ref, out_ref, spec_ref, up_ref, down_ref = refs[:-2]
    sems, out_sems = refs[-2:]
    height, width = image_ref.shape
    rank = rank_ref[0]
    share = height // len(part_refs)
    length = width // ROWS
    blocks = height // LANES
    unroll = 8
    copies = []
    for c in range(ROWS):
        columns = slice(c * length, (c + 1) * length)
        copies.append(
            pltpu.make_async_copy(
                source_ref.at[:, columns], image_ref.at[:, columns], sems.at[c]
            )
        )
    given = pltpu.make_async_copy(given_ref, table_ref, sems.at[ROWS])
    given.start()
    for copy in copies:
        copy.start()
    given.wait()
    cas_high, cas_low = halves(table_ref[0:height, :])
    rho_all = table_ref[height : height + ROWS, :]
    rhos = [rho_all[:, b * LANES : (b + 1) * LANES] for b in range(blocks)]
    zeros = [jnp.zeros((ROWS, LANES), f32)] * blocks

    def transform(values):
        high, low = halves(values)
        return dot(high, cas_high) + dot(low, cas_high) + dot(high, cas_low)

    for c in range(ROWS):
        copies[c].wait()
        image = 1.0 - image_ref[:, c * length : (c + 1) * length]
        spectrum = transform(jnp.transpose(image))
        for b in range(blocks):
            spec_ref[b, pl.ds(c, length, stride=ROWS), :] = spectrum[
                :, b * LANES : (b + 1) * LANES
            ]

    def rows(position):
        return pl.ds(pl.multiple_of(position * ROWS, ROWS), ROWS)

    def advance(position, ups, downs):
        ups = [spec_ref[b, rows(position), :] + rhos[b] * ups[b] for b in range(blocks)]
        back = length - 1 - position
        downs = [spec_ref[b, rows(back), :] + rhos[b] * downs[b] for b in range(blocks)]
        return ups, downs

    def sweep(index, carry):
        ups, downs = carry
        for step in range(unroll):
            ups, downs = advance(index * unroll + step, ups, downs)
        return ups, downs

    ups, downs = lax.fori_loop(0, length // unroll, sweep, (zeros, zeros))
    powers = list(rhos)
    for _ in range(int(math.log2(length))):
        powers = [power * power for power in powers]
    ups = [chunk_carry(ups[b], powers[b], True) for b in range(blocks)]
    downs = [chunk_carry(downs[b], powers[b], False) for b in range(blocks)]
    scales = [rho / (paganin_strength * (1.0 - rho * rho)) for rho in rhos]

    def outer(index, carry):
        ups, downs = carry
        for step in range(unroll):
            position = index * unroll + step
            ups, downs = advance(position, ups, downs)
            for b in range(blocks):
                up_ref[b, rows(position), :] = ups[b]
                down_ref[b, rows(position), :] = downs[b]
        return ups, downs

    def inner(index, carry):
        ups, downs = carry
        for step in range(unroll):
            position = index * unroll + step
            back = length - 1 - position
            ups, downs = advance(position, ups, downs)
            for b in range(blocks):
                here = ups[b] + down_ref[b, rows(back), :] - spec_ref[b, rows(position), :]
                there = downs[b] + up_ref[b, rows(back), :] - spec_ref[b, rows(back), :]
                up_ref[b, rows(position), :] = here * scales[b]
                up_ref[b, rows(back), :] = there * scales[b]
        return ups, downs

    half = length // 2 // unroll
    carry = lax.fori_loop(0, half, outer, (ups, downs))
    lax.fori_loop(half, 2 * half, inner, carry)

    offset = (width - ACTIVE) // 2
    sent = []
    for c in range(ROWS):
        spectrum = jnp.concatenate(
            [up_ref[b, pl.ds(c, length, stride=ROWS), :] for b in range(blocks)], axis=1
        )
        filtered = 1.0 - jnp.transpose(transform(spectrum))
        columns = slice(c * length, (c + 1) * length)
        out_ref[:, columns] = -jnp.log(filtered)
        for d, part_ref in enumerate(part_refs):
            rows = pl.ds(pl.multiple_of((rank ^ d) * share, share), share)
            sent.append(
                pltpu.make_async_copy(
                    out_ref.at[rows, columns], part_ref.at[:, columns], out_sems.at[c, d]
                )
            )
            sent[-1].start()
        if c == (offset + ACTIVE - 1) // length:
            columns = slice(offset, offset + ACTIVE)
            sent.append(
                pltpu.make_async_copy(out_ref.at[:, columns], active_ref, sems.at[0])
            )
            sent[-1].start()
    for copy in sent:
        copy.wait()


def paganin(image, rank, parts):
    height, width = image.shape
    blocks = height // LANES
    return pl.pallas_call(
        filter_kernel,
        out_shape=[jax.ShapeDtypeStruct((height // parts, width), f32)] * parts
        + [jax.ShapeDtypeStruct((height, ACTIVE), f32)],
        in_specs=[pl.BlockSpec(memory_space=pltpu.SMEM)]
        + [pl.BlockSpec(memory_space=pltpu.HBM)] * 2,
        out_specs=[pl.BlockSpec(memory_space=pltpu.HBM)] * (parts + 1),
        scratch_shapes=[
            pltpu.VMEM((height, width), f32),
            pltpu.VMEM((height + ROWS, height), f32),
            pltpu.VMEM((height, width), f32),
            pltpu.VMEM((blocks, width, LANES), f32),
            pltpu.VMEM((blocks, width, LANES), f32),
            pltpu.VMEM((blocks, width // 2, LANES), f32),
            pltpu.SemaphoreType.DMA((ROWS + 1,)),
            pltpu.SemaphoreType.DMA((ROWS, parts)),
        ],
        compiler_params=pltpu.CompilerParams(vmem_limit_bytes=58 * 2**20),
        cost_estimate=pl.CostEstimate(
            flops=64 * height * height * width,
            bytes_accessed=8 * height * width,
            transcendentals=height * width,
        ),
        name="paganin",
    )(rank.reshape(1), image, jnp.asarray(filter_tables(height)))


def reversed_exact(values, flip):
    return sum(dot(part, flip) for part in thirds(values))


class Weights:
    def __init__(self, along_ref, place_ref, angles, chunk):
        self.along_ref = along_ref
        self.place_ref = place_ref
        self.angles = angles
        self.chunk = chunk
        self.ray = lax.broadcasted_iota(jnp.int32, (ROWS, VOX), 0).astype(f32)

    def prepare(self, shift_x_ref, shift_y_ref, cos_ref, sin_ref):
        def along_angle(t):
            along = shift_x_ref[...] * cos_ref[t] + shift_y_ref[...] * sin_ref[t]
            self.along_ref[t] = self.ray - along

        repeat(self.angles, along_angle, 8)

    def make(self, q, c, ref):
        for two in range(self.chunk // 2):
            pieces = []
            for t in (2 * two, 2 * two + 1):
                angle = c * self.chunk + t
                base = self.along_ref[angle] - self.place_ref[q * self.angles + angle]
                for group in range(WIN // ROWS):
                    distance = base + float(group * ROWS)
                    pieces.append(jnp.maximum(0.0, 1.0 - jnp.abs(distance)))
            high, low = halves(jnp.concatenate(pieces, axis=0))
            ref[2 * two * WIN : (2 * two + 2) * WIN, 0:VOX] = high
            ref[2 * two * WIN : (2 * two + 2) * WIN, VOX : 2 * VOX] = low


def ray_operand(values, sums_too):
    high, low = halves(values)
    rows = [
        jnp.concatenate([high, high], axis=1),
        jnp.concatenate([low, jnp.zeros_like(low)], axis=1),
    ]
    if sums_too:
        rows.append(jnp.ones((values.shape[0], 2 * VOX), bf16))
    return jnp.concatenate(rows, axis=0)


def row_operands(values, sums_too):
    rows = ray_operand(values, sums_too)
    count, width = rows.shape
    spare = jnp.zeros((SPLIT - count, width), bf16)
    empty = jnp.zeros((SPLIT, width), bf16)
    return (
        jnp.concatenate([rows, spare, empty], axis=0),
        jnp.concatenate([empty, rows, spare], axis=0),
    )


def project_rows(held_ref, operands, q, c, sizes, offset_ref, acc_ref):
    angles, chunk = sizes[:2]
    half = chunk // 2
    for side in range(2):
        sums = lax.dot_general(
            held_ref[side * half * WIN : (side + 1) * half * WIN, :],
            operands[side],
            (((1,), (1,)), ((), ())),
            preferred_element_type=f32,
        )
        for begin in range(0, half, GROUP):
            places = []
            for i in range(begin, begin + GROUP):
                t = side * half + i
                rows = pl.ds(offset_ref[q * angles + c * chunk + t], WIN)
                index = c * half + i
                piece = sums[i * WIN : (i + 1) * WIN, :]
                places.append((index, rows, acc_ref[index, rows, :] + piece))
            for index, rows, values in places:
                acc_ref[index, rows, :] = values


def spread_rays(acc_ref, direct_ref, mirror_ref, total_ref, slices, chunk):
    both = 2 * slices
    half = chunk // 2

    def spread(index):
        turned = jnp.transpose(acc_ref[index]) * (1.0 / ROI)
        for part in range(2):
            rows = turned[part * SPLIT : (part + 1) * SPLIT]
            t = index // half * chunk + part * half + index % half
            direct_ref[t] = rows[0:slices] + rows[both : both + slices]
            mirror_ref[t] = rows[slices:both] + rows[both + slices : 2 * both]
            if total_ref is not None:
                total_ref[t] = rows[2 * both : 2 * both + slices]

    repeat(acc_ref.shape[0], spread, 8)


def turn_rays(values, flip):
    shape = values.shape
    return reversed_exact(values.reshape(-1, shape[-1]), flip).reshape(shape)


def fill_windows(weighted, flip, window_ref):
    angles, slices, _ = weighted.shape
    high, low = halves(weighted.reshape(angles * slices, ACTIVE))
    mirrored = (dot(high, flip) + dot(low, flip)).reshape(weighted.shape)
    lane = lax.broadcasted_iota(jnp.int32, (angles, slices, LANES), 2)
    for part, source in enumerate((weighted, mirrored)):
        rows = slice(part * slices, (part + 1) * slices)
        left = source[:, :, 0:LANES]
        right = source[:, :, LANES : 2 * LANES]
        window_ref[:, 0, rows, :] = left
        window_ref[:, 2, rows, :] = right
        mixed = jnp.where(lane >= SPLIT, left, right)
        window_ref[:, 1, rows, :] = pltpu.roll(mixed, SPLIT, 2)


def window_operand(q, c, sizes, window_ref, tile_ref, turn_ref):
    angles, chunk = sizes[:2]
    both = window_ref.shape[2]
    lane_rows = lax.broadcasted_iota(jnp.int32, (both, LANES), 1)
    tiles = [None] * (-(-chunk * WIN // LANES))
    for t in range(chunk):
        index = q * angles + c * chunk + t
        piece = pltpu.roll(window_ref[c * chunk + t, tile_ref[index]], turn_ref[index], 1)
        begin = t * WIN
        for place in range(begin // LANES, (begin + WIN - 1) // LANES + 1):
            if tiles[place] is None:
                tiles[place] = piece
            else:
                tiles[place] = jnp.where(
                    lane_rows >= begin - place * LANES, piece, tiles[place]
                )
    high, low = halves(jnp.concatenate(tiles, axis=1))
    return jnp.concatenate([high, low], axis=0)


def update_pair(operand, held):
    both = operand.shape[0] // 2
    sums = dot(operand, held)
    return sums[0:both, 0:VOX] + sums[both:, 0:VOX] + sums[0:both, VOX:]


def first_kernel(
    sizes,
    place_ref,
    offset_ref,
    slot_ref,
    cos_ref,
    sin_ref,
    vol_ref,
    flip_ref,
    shift_x_ref,
    shift_y_ref,
    kept_ref,
    predicted_ref,
    gain_ref,
    *refs,
):
    held_refs = refs[:CYCLE]
    acc_ref, along_ref, half_ref, mirror_ref, start_ref, sem = refs[CYCLE:]
    angles, chunk, slots = sizes
    patches = slot_ref.shape[0]
    pairs, both, _ = start_ref.shape
    slices = both // 2
    flip = flip_ref[...]

    def slot_values(patch):
        slot = slot_ref[patch]
        rows = pl.ds(slot % slots, slices, stride=slots)
        return jnp.concatenate(
            [half_ref[part, slot // slots, rows, :] for part in range(2)], axis=1
        )

    for part in range(2):
        half_ref[part] = vol_ref[:, :, part * LANES : (part + 1) * LANES]

    def order(q):
        start_ref[q, 0:slices, :] = slot_values(q)
        mirror_ref[q] = slot_values(patches - 1 - q)

    repeat(pairs, order, 8)
    start_ref[:, slices:both, :] = turn_rays(mirror_ref[0:pairs], flip)
    weights = Weights(along_ref, place_ref, angles, chunk)
    weights.prepare(shift_x_ref, shift_y_ref, cos_ref, sin_ref)
    acc_ref[...] = jnp.zeros(acc_ref.shape, f32)

    kept = pltpu.make_async_copy(start_ref, kept_ref, sem)
    kept.start()
    chunks = angles // chunk

    def cycle(index, carry):
        for step in range(CYCLE):
            q = index * CYCLE + step
            operands = row_operands(start_ref[q], True)
            for c in range(chunks):
                more = jnp.minimum(q + (c + 1) // chunks, pairs - 1)
                after = (step * chunks + c + 1) % CYCLE
                weights.make(more, (c + 1) % chunks, held_refs[after])
                here = held_refs[(step * chunks + c) % CYCLE]
                project_rows(here, operands, q, c, sizes, offset_ref, acc_ref)
        return carry

    weights.make(0, 0, held_refs[0])
    lax.fori_loop(0, pairs // CYCLE, cycle, 0)
    spread_rays(acc_ref, predicted_ref, mirror_ref, gain_ref, slices, chunk)
    direct, mirror, weight_sums = predicted_ref[...], mirror_ref[0:angles], gain_ref[...]
    predicted_ref[...] = direct + turn_rays(mirror, flip)
    turned = turn_rays(weight_sums[:, 0, :], flip)
    total = weight_sums + turned[:, None, :]
    gain_ref[...] = 1.0 / jnp.maximum(total, row_floor)
    kept.wait()


def second_kernel(
    sizes,
    step_size,
    rank_ref,
    offset_ref,
    place_ref,
    tile_ref,
    turn_ref,
    slot_ref,
    cos_ref,
    sin_ref,
    vol_ref,
    predicted_ref,
    gain_ref,
    sino_ref,
    flip_ref,
    shift_x_ref,
    shift_y_ref,
    kept_ref,
    *refs,
):
    angles, chunk, slots = sizes
    rays = vol_ref.shape[0]
    out_refs, refs = refs[:rays], refs[rays:]
    held_refs = refs[:CYCLE]
    acc_ref, along_ref, direct_ref, mirror_ref, window_ref, update_ref, half_ref = refs[
        CYCLE:-2
    ]
    start_ref, sem = refs[-2:]
    kept = pltpu.make_async_copy(kept_ref, start_ref, sem)
    kept.start()
    patches = slot_ref.shape[0]
    pairs, both, _ = start_ref.shape
    slices = both // 2
    flip = flip_ref[...]
    weights = Weights(along_ref, place_ref, angles, chunk)
    weights.prepare(shift_x_ref, shift_y_ref, cos_ref, sin_ref)
    chunks = angles // chunk
    windows = (sizes, window_ref, tile_ref, turn_ref)
    rest = (sizes, offset_ref, acc_ref)
    fill_windows(
        (sino_ref[...] - predicted_ref[...]) * gain_ref[...] * (1.0 / ROI), flip, window_ref
    )
    acc_ref[...] = jnp.zeros(acc_ref.shape, f32)
    kept.wait()

    def advance(q, operand, held):
        total = update_pair(operand, held)
        update_ref[q] = total
        return start_ref[q] + step_size * total

    def forward(values, q, held):
        project_rows(held, row_operands(values, False), q, 0, *rest)

    def cycle(index, carry):
        values, operand = carry
        for step in range(CYCLE):
            q = index * CYCLE + step
            after = (step + 1) % CYCLE
            before = (step - 1) % CYCLE
            later = index + (step + 1) // CYCLE
            earlier = index if step else jnp.maximum(index - 1, 0)
            following = jnp.minimum(q + 1, pairs - 1)
            next_operand = window_operand(following, 0, *windows)
            weights.make(following, 0, held_refs[after].at[later])
            new_values = advance(q, operand, held_refs[step][index])
            forward(values, jnp.maximum(q - 1, 0), held_refs[before].at[earlier])
            values, operand = new_values, next_operand
        return values, operand

    def all_chunks(q, body):
        for c in range(chunks):
            weights.make(q, c, held_refs[0].at[0])
            body(c, held_refs[0].at[0])

    def plain_update(q, carry):
        update_ref[q] = jnp.zeros(update_ref.shape[1:], f32)

        def add(c, held):
            operand = window_operand(q, c, *windows)
            update_ref[q] = update_ref[q] + update_pair(operand, held[...])

        all_chunks(q, add)
        return carry

    def plain_forward(q, carry):
        operands = row_operands(start_ref[q] + step_size * update_ref[q], False)
        all_chunks(q, lambda c, held: project_rows(held, operands, q, c, *rest))
        return carry

    if chunks == 1:
        held_refs[CYCLE - 1][0] = jnp.zeros(held_refs[CYCLE - 1].shape[1:], bf16)
        weights.make(0, 0, held_refs[0].at[0])
        begin = (jnp.zeros((both, VOX), f32), window_operand(0, 0, *windows))
        values, _ = lax.fori_loop(0, pairs // CYCLE, cycle, begin)
        forward(values, pairs - 1, held_refs[CYCLE - 1].at[pairs // CYCLE - 1])
    else:
        lax.fori_loop(0, pairs, plain_update, 0)
        lax.fori_loop(0, pairs, plain_forward, 0)

    spread_rays(acc_ref, direct_ref, mirror_ref, None, slices, chunk)
    turned = turn_rays(mirror_ref[0:angles], flip)
    direct_ref[...] = sino_ref[...] - direct_ref[...] - turned
    fill_windows(direct_ref[...] * gain_ref[...] * (1.0 / ROI), flip, window_ref)

    def last_cycle(index, operand):
        for step in range(CYCLE):
            q = index * CYCLE + step
            next_operand = window_operand(jnp.minimum(q + 1, pairs - 1), 0, *windows)
            total = update_pair(operand, held_refs[step][index])
            update_ref[q] = (update_ref[q] + total) * step_size
            operand = next_operand
        return operand

    def plain_last(q, carry):
        def add(c, held):
            operand = window_operand(q, c, *windows)
            update_ref[q] = update_ref[q] + update_pair(operand, held[...])

        all_chunks(q, add)
        update_ref[q] = update_ref[q] * step_size
        return carry

    if chunks == 1:
        lax.fori_loop(0, pairs // CYCLE, last_cycle, window_operand(0, 0, *windows))
    else:
        lax.fori_loop(0, pairs, plain_last, 0)

    mirror_ref[0:pairs] = turn_rays(update_ref[:, slices:both, :], flip)
    for part in range(2):
        half_ref[part] = vol_ref[:, :, part * LANES : (part + 1) * LANES]

    def finish(q):
        for patch, update in (
            (q, update_ref[q, 0:slices, :]),
            (patches - 1 - q, mirror_ref[q]),
        ):
            slot = slot_ref[patch]
            rows = pl.ds(slot % slots, slices, stride=slots)
            for part in range(2):
                half_ref[part, slot // slots, rows, :] = (
                    half_ref[part, slot // slots, rows, :]
                    + update[:, part * LANES : (part + 1) * LANES]
                )

    repeat(pairs, finish, 8)
    lead = slices * slots
    lane = lax.broadcasted_iota(jnp.int32, (slices, LANES), 1)
    for d, out_ref in enumerate(out_refs):
        ray = rank_ref[0] ^ d
        for part in range(2):
            out_ref[0:lead, part * LANES : (part + 1) * LANES] = half_ref[part, ray]
        for k in range(0, angles // rays, 4):
            begin = lead + k // 4 * 3 * slices
            live = [
                pltpu.roll(direct_ref[(k + i) * rays + ray], ACTIVE - EDGE, 1)
                for i in range(4)
            ]
            rest = [part[:, LANES:] for part in live]
            for i in range(2):
                here = begin + i * slices
                out_ref[here : here + slices, 0:LANES] = live[2 * i][:, 0:LANES]
                out_ref[here : here + slices, LANES:] = live[2 * i + 1][:, 0:LANES]
                here = begin + 2 * slices
                out_ref[here : here + slices, i * LANES : (i + 1) * LANES] = jnp.where(
                    lane < SPLIT, rest[2 * i], pltpu.roll(rest[2 * i + 1], SPLIT, 1)
                )


def call(kernel, name, inputs, held_in, held_out, outputs, scratch, micros):
    smem = pl.BlockSpec(memory_space=pltpu.SMEM)
    vmem = pl.BlockSpec(memory_space=pltpu.VMEM)
    hbm = pl.BlockSpec(memory_space=pltpu.HBM)
    return pl.pallas_call(
        kernel,
        out_shape=[jax.ShapeDtypeStruct(*value) for value in held_out + outputs],
        in_specs=[smem if value.ndim == 1 else vmem for value in inputs] + [hbm] * len(held_in),
        out_specs=[hbm] * len(held_out) + [vmem] * len(outputs),
        scratch_shapes=[pltpu.VMEM(*value) for value in scratch]
        + [pltpu.SemaphoreType.DMA],
        compiler_params=pltpu.CompilerParams(vmem_limit_bytes=52 * 2**20),
        cost_estimate=pl.CostEstimate(
            flops=int(micros * 1e9), bytes_accessed=4 * 2**20, transcendentals=0
        ),
        name=name,
    )(*inputs, *held_in)


class Sirt:
    def __init__(self, theta, vol_list, slices, slots, rays, step_size):
        angles = theta.shape[0]
        patches = vol_list.shape[0]
        pairs = patches // 2
        both = 2 * slices
        chunk = math.gcd(angles, 32)
        self.sizes = (angles, chunk, slots)
        self.step_size = step_size
        self.rays = rays
        self.patches = patches
        centre = (ROI - 1) / 2.0
        ids = np.arange(pairs)
        centre_x = (ids // PGRID * float(SIDE) + (SIDE - 1) / 2.0 - centre).astype(np.float32)
        centre_y = (ids % PGRID * float(SIDE) + (SIDE - 1) / 2.0 - centre).astype(np.float32)
        self.cosine = jnp.cos(theta)
        self.sine = jnp.sin(theta)
        along = (
            centre_x[:, None] * self.cosine[None, :]
            + centre_y[:, None] * self.sine[None, :]
            + 0.5
        )
        whole = jnp.floor(along)
        lead = WIN // 2 - 1
        place = along - whole + float(lead)
        offset = whole.astype(jnp.int32) + (ACTIVE // 2 - 1 - lead)
        tile = jnp.minimum(offset // SPLIT, 2)
        local = jnp.arange(angles, dtype=jnp.int32) % chunk * WIN
        turn = (local[None, :] - offset + tile * SPLIT) % LANES
        self.offset = offset.reshape(-1)
        self.place = place.reshape(-1)
        self.tile = tile.reshape(-1)
        self.turn = turn.reshape(-1)
        ids = jnp.arange(patches, dtype=jnp.int32)
        self.slot = jnp.sum(
            jnp.where(vol_list[None, :] == ids[:, None], ids[None, :], 0), axis=1
        )
        voxel = np.arange(VOX)
        shift_x = np.repeat((voxel // SIDE - (SIDE - 1) / 2.0)[None, :], ROWS, axis=0)
        shift_y = np.repeat((voxel % SIDE - (SIDE - 1) / 2.0)[None, :], ROWS, axis=0)
        flip = np.eye(ACTIVE)[::-1].astype(ml_dtypes.bfloat16)
        self.fixed = [jnp.asarray(flip), jnp.asarray(shift_x, f32), jnp.asarray(shift_y, f32)]
        self.weight = ((chunk * WIN, 2 * VOX), bf16)
        self.held = (pairs // CYCLE + 1 if angles == chunk else 1,) + self.weight[0]
        self.acc_rows = ((angles // 2, ACTIVE, LANES), f32)
        self.along = ((angles, ROWS, VOX), f32)
        self.by_ray = ((angles, slices, ACTIVE), f32)
        self.by_pair = ((pairs, both, VOX), f32)
        self.window = ((angles, 3, both, LANES), f32)
        self.half = ((2, rays, slices * slots, LANES), f32)
        self.mirror = ((max(pairs, angles), slices, ACTIVE), f32)
        self.sent = [((slices * (slots + angles // rays * 3 // 4), ACTIVE), f32)] * rays

    def first(self, volume):
        inputs = [self.place, self.offset, self.slot, self.cosine, self.sine, volume]
        return call(
            functools.partial(first_kernel, self.sizes),
            "first",
            inputs + self.fixed,
            [],
            [self.by_pair],
            [self.by_ray, self.by_ray],
            [self.weight] * CYCLE
            + [self.acc_rows, self.along, self.half, self.mirror, self.by_pair],
            14,
        )

    def second(self, rank, volume, start, predicted, gain, sino):
        inputs = [rank.reshape(1), self.offset, self.place, self.tile, self.turn, self.slot]
        inputs += [self.cosine, self.sine, volume, predicted, gain, sino]
        scratch = [(self.held, bf16)] * CYCLE
        scratch += [self.acc_rows, self.along, self.by_ray, self.mirror, self.window]
        return call(
            functools.partial(second_kernel, self.sizes, self.step_size),
            "second",
            inputs + self.fixed,
            [start],
            [],
            self.sent,
            scratch + [self.by_pair, self.half, self.by_pair],
            26,
        )


def gather_kernel(rank_ref, *refs):
    *part_refs, out_ref, active_ref, sems = refs
    rank = rank_ref[0]
    copies = [
        pltpu.make_async_copy(part_ref, out_ref.at[rank ^ d], sems.at[d])
        for d, part_ref in enumerate(part_refs)
    ]
    for copy in copies:
        copy.start()
    offset = (out_ref.shape[2] - ACTIVE) // 2
    for d, part_ref in enumerate(part_refs):
        active_ref[rank ^ d] = part_ref[:, offset : offset + ACTIVE]
    for copy in copies:
        copy.wait()


def gather_parts(parts, rank):
    count = len(parts)
    rows = parts[0].shape[0]
    vmem = pl.BlockSpec(memory_space=pltpu.VMEM)
    return pl.pallas_call(
        gather_kernel,
        out_shape=(
            jax.ShapeDtypeStruct((count,) + parts[0].shape, f32),
            jax.ShapeDtypeStruct((count, rows, ACTIVE), f32),
        ),
        in_specs=[pl.BlockSpec(memory_space=pltpu.SMEM)] + [vmem] * count,
        out_specs=(pl.BlockSpec(memory_space=pltpu.HBM), vmem),
        scratch_shapes=[pltpu.SemaphoreType.DMA((count,))],
        compiler_params=pltpu.CompilerParams(vmem_limit_bytes=8 * 2**20),
        cost_estimate=pl.CostEstimate(
            flops=0, bytes_accessed=8 * count * parts[0].size, transcendentals=0
        ),
        name="gather_parts",
    )(rank.reshape(1), *parts)


def message_order(count):
    near = [d for d in (1, 2) if d < count // 2]
    far = list(range(count - 1, count // 2 - 1, -1))
    return near + far + [d for d in range(count // 2 - 1, -1, -1) if d not in near]


def finish_kernel(rank_ref, *refs):
    *got_refs, given_ref, _, rec_ref, out_ref, values_ref, active_ref, sems = refs
    rays = len(got_refs)
    slots = values_ref.shape[1]
    slabs = active_ref.shape[0]
    slices = values_ref.shape[0] // rays
    lead = slices * slots
    lane = lax.broadcasted_iota(jnp.int32, (slices, ACTIVE), 1)
    live = (lane >= EDGE) & (lane < ACTIVE - EDGE)
    for d, got_ref in zip(message_order(rays), got_refs):
        rows = pl.ds(pl.multiple_of((rank_ref[0] ^ d) * slices, slices), slices)
        values_ref[rows] = got_ref[0:lead, :].reshape(slices, slots, VOX)
        for k in range(slabs):
            begin = lead + k // 4 * 3 * slices
            pair, side = k % 4 // 2, k % 2
            here = begin + pair * slices
            left = got_ref[here : here + slices, side * LANES : (side + 1) * LANES]
            here = begin + 2 * slices
            rest = got_ref[here : here + slices, pair * LANES : (pair + 1) * LANES]
            if side:
                rest = pltpu.roll(rest, SPLIT, 1)
            whole = pltpu.roll(jnp.concatenate([left, rest], axis=1), EDGE, 1)
            active_ref[k, rows, :] = jnp.where(live, whole, given_ref[k, rows, :])
    offset = (out_ref.shape[2] - ACTIVE) // 2
    copies = [
        pltpu.make_async_copy(values_ref, rec_ref, sems.at[0]),
        pltpu.make_async_copy(
            active_ref, out_ref.at[:, :, offset : offset + ACTIVE], sems.at[1]
        ),
    ]
    for copy in copies:
        copy.start()
    for copy in copies:
        copy.wait()


def finish(pieces, given, sinogram, rank, shape):
    slabs, slab_rows, _ = sinogram.shape
    hbm = pl.BlockSpec(memory_space=pltpu.HBM)
    vmem = pl.BlockSpec(memory_space=pltpu.VMEM)
    return pl.pallas_call(
        finish_kernel,
        out_shape=(
            jax.ShapeDtypeStruct(shape, f32),
            jax.ShapeDtypeStruct(sinogram.shape, f32),
        ),
        in_specs=[pl.BlockSpec(memory_space=pltpu.SMEM)]
        + [vmem] * (len(pieces) + 1)
        + [hbm],
        out_specs=[hbm, hbm],
        scratch_shapes=[
            pltpu.VMEM(shape, f32),
            pltpu.VMEM((slabs, slab_rows, ACTIVE), f32),
            pltpu.SemaphoreType.DMA((2,)),
        ],
        input_output_aliases={len(pieces) + 2: 1},
        compiler_params=pltpu.CompilerParams(vmem_limit_bytes=8 * 2**20),
        cost_estimate=pl.CostEstimate(
            flops=0, bytes_accessed=8 * len(pieces) * pieces[0].size, transcendentals=0
        ),
        name="finish",
    )(rank.reshape(1), *[pieces[d] for d in message_order(len(pieces))], given, sinogram)


def exchange(pieces, axis):
    count = len(pieces)
    results = list(pieces)
    for d in range(count - 1, 0, -1):
        results[d] = lax.ppermute(pieces[d], axis, [(i, i ^ d) for i in range(count)])
    return results


def local(intensity, angles, volume, vol_list):
    n_slab = lax.axis_size("slab")
    n_ray = lax.axis_size("ray")
    devices = n_slab * n_ray
    height, band = intensity.shape[2:]
    slices = height // devices
    slots = volume.shape[1]
    count = angles.shape[0] * angles.shape[1]
    step_size = relax * ROI / count
    rank = lax.axis_index("slab")
    ray_rank = lax.axis_index("ray")
    padded = -(-slices // ROWS) * ROWS

    def to_all(values, axes):
        return lax.all_to_all(values, axes, split_axis=0, concat_axis=0, tiled=True)

    own_volume = to_all(volume.reshape(n_ray, slices * slots, VOX), "ray")
    *parts, active = paganin(intensity.reshape(height, band), rank, n_slab)
    active, own_volume = lax.optimization_barrier((active, own_volume))
    own_rays = to_all(active.reshape(devices, slices, ACTIVE), ("slab", "ray"))
    if padded != slices:
        more = padded - slices
        own_volume = jnp.pad(own_volume, ((0, 0), (0, more * slots), (0, 0)))
        own_rays = jnp.pad(own_rays, ((0, 0), (0, more), (0, 0)))

    angles, vol_list, own_volume, parts = lax.optimization_barrier(
        (angles, vol_list, own_volume, parts)
    )
    sirt = Sirt(angles.reshape(-1), vol_list, padded, slots, n_ray, step_size)
    start, predicted, gain = sirt.first(own_volume)
    own_rays, parts, start = lax.optimization_barrier((own_rays, parts, start))
    parts = exchange(parts, "slab")
    pieces = sirt.second(ray_rank, own_volume, start, predicted, gain, own_rays)
    pieces, parts = lax.optimization_barrier((pieces, parts))
    if padded != slices:
        narrow = []
        for piece in pieces:
            lower = piece[padded * slots :].reshape(-1, padded, ACTIVE)[:, :slices]
            lower = lower.reshape(-1, ACTIVE)
            narrow.append(jnp.concatenate([piece[: slices * slots], lower], axis=0))
        pieces = narrow
    pieces = exchange(pieces, "ray")
    sinogram, given = gather_parts(parts, rank)
    if padded == slices:
        reconstruction, residual = finish(pieces, given, sinogram, ray_rank, volume.shape)
    else:
        order = ray_rank ^ jnp.arange(n_ray, dtype=jnp.int32)
        pieces = jnp.take(jnp.stack(pieces), order, axis=0)
        reconstruction = pieces[:, : slices * slots].reshape(volume.shape)
        lower = pieces[:, slices * slots :].reshape(n_ray, -1, 3, slices, ACTIVE)
        left = lower[:, :, :2].reshape(n_ray, -1, 2, slices, 2, LANES)
        left = jnp.transpose(left, (1, 2, 4, 0, 3, 5)).reshape(n_slab, n_ray * slices, LANES)
        rest = lower[:, :, 2].reshape(n_ray, -1, slices, 4, SPLIT)
        rest = jnp.transpose(rest, (1, 3, 0, 2, 4)).reshape(n_slab, n_ray * slices, SPLIT)
        begin = (band - ACTIVE) // 2 + EDGE
        live = jnp.concatenate([left, rest], axis=2)
        residual = lax.dynamic_update_slice(sinogram, live, (0, 0, begin))
    return (reconstruction, residual[:, None])


def solution(mesh):
    placed = (P("slab", "ray", None, None), P(), P("slab", "ray", None), P())
    return jax.shard_map(
        local,
        mesh=mesh,
        in_specs=placed,
        out_specs=(P("slab", "ray", None), P(None, "ray", "slab", None)),
        check_vma=False,
    )
```

```python
import functools
import math

import jax
import jax.numpy as jnp
import ml_dtypes
import numpy as np
from jax import lax
from jax.experimental import pallas as pl
from jax.experimental.pallas import tpu as pltpu
from jax.sharding import PartitionSpec as P

BAND = 2048
PGRID = 8
ROI = 128
SIDE = 16
VOX = SIDE * SIDE
WIN = 24
ACTIVE = 256
LANES = 128
ROWS = 8
SPLIT = 64
EDGE = 32
GROUP = 8
CYCLE = 16

paganin_strength = 10.0
relax = 1.8
row_floor = 0.25

bf16 = jnp.bfloat16
f32 = jnp.float32


def halves(values):
    high = values.astype(bf16)
    low = (values - high.astype(f32)).astype(bf16)
    return high, low


def dot(left, right):
    return jnp.dot(left, right, preferred_element_type=f32)


def repeat(count, body, unroll):
    unroll = math.gcd(count, unroll)

    def several(index, carry):
        for step in range(unroll):
            body(index * unroll + step)
        return carry

    lax.fori_loop(0, count // unroll, several, 0)


def filter_tables(height):
    index = np.arange(height)
    phase = 2.0 * np.pi * (np.outer(index, index) % height) / height
    cas = (np.cos(phase) + np.sin(phase)) / math.sqrt(height)
    row_freq = 2.0 - 2.0 * np.cos(2.0 * np.pi * index / height)
    middle = (1.0 + paganin_strength * row_freq) / paganin_strength + 2.0
    rho = (middle - np.sqrt(middle * middle - 4.0)) / 2.0
    return np.concatenate([cas, np.repeat(rho[None, :], ROWS, axis=0)], axis=0).astype(np.float32)


def chunk_carry(ends, power, forward):
    shift = 1
    for _ in range(3):
        ends = ends + power * pltpu.roll(ends, shift if forward else ROWS - shift, 0)
        power = power * power
        shift *= 2
    return pltpu.roll(ends, 1 if forward else ROWS - 1, 0) / (1.0 - power)


def filter_kernel(rank_ref, source_ref, given_ref, *refs):
    *part_refs, active_ref, image_ref, table_ref, out_ref, spec_ref, up_ref, down_ref = refs[:-2]
    sems, out_sems = refs[-2:]
    height, width = image_ref.shape
    rank = rank_ref[0]
    share = height // (2 * len(part_refs))
    length = width // ROWS
    blocks = height // LANES
    unroll = 8
    copies = []
    for c in range(ROWS):
        columns = slice(c * length, (c + 1) * length)
        copies.append(
            pltpu.make_async_copy(
                source_ref.at[:, columns], image_ref.at[:, columns], sems.at[c]
            )
        )
    given = pltpu.make_async_copy(given_ref, table_ref, sems.at[ROWS])
    given.start()
    for copy in copies:
        copy.start()
    given.wait()
    cas_high, cas_low = halves(table_ref[0:height, :])
    rho_all = table_ref[height : height + ROWS, :]
    rhos = [rho_all[:, b * LANES : (b + 1) * LANES] for b in range(blocks)]
    zeros = [jnp.zeros((ROWS, LANES), f32)] * blocks

    def transform(values):
        high, low = halves(values)
        return dot(high, cas_high) + dot(low, cas_high) + dot(high, cas_low)

    for c in range(ROWS):
        copies[c].wait()
        image = 1.0 - image_ref[:, c * length : (c + 1) * length]
        spectrum = transform(jnp.transpose(image))
        for b in range(blocks):
            spec_ref[b, pl.ds(c, length, stride=ROWS), :] = spectrum[
                :, b * LANES : (b + 1) * LANES
            ]

    def rows(position):
        return pl.ds(pl.multiple_of(position * ROWS, ROWS), ROWS)

    def advance(position, ups, downs):
        ups = [spec_ref[b, rows(position), :] + rhos[b] * ups[b] for b in range(blocks)]
        back = length - 1 - position
        downs = [spec_ref[b, rows(back), :] + rhos[b] * downs[b] for b in range(blocks)]
        return ups, downs

    def sweep(index, carry):
        ups, downs = carry
        for step in range(unroll):
            ups, downs = advance(index * unroll + step, ups, downs)
        return ups, downs

    ups, downs = lax.fori_loop(0, length // unroll, sweep, (zeros, zeros))
    powers = list(rhos)
    for _ in range(int(math.log2(length))):
        powers = [power * power for power in powers]
    ups = [chunk_carry(ups[b], powers[b], True) for b in range(blocks)]
    downs = [chunk_carry(downs[b], powers[b], False) for b in range(blocks)]
    scales = [rho / (paganin_strength * (1.0 - rho * rho)) for rho in rhos]

    def outer(index, carry):
        ups, downs = carry
        for step in range(unroll):
            position = index * unroll + step
            ups, downs = advance(position, ups, downs)
            for b in range(blocks):
                up_ref[b, rows(position), :] = ups[b]
                down_ref[b, rows(position), :] = downs[b]
        return ups, downs

    def inner(index, carry):
        ups, downs = carry
        for step in range(unroll):
            position = index * unroll + step
            back = length - 1 - position
            ups, downs = advance(position, ups, downs)
            for b in range(blocks):
                here = ups[b] + down_ref[b, rows(back), :] - spec_ref[b, rows(position), :]
                there = downs[b] + up_ref[b, rows(back), :] - spec_ref[b, rows(back), :]
                up_ref[b, rows(position), :] = here * scales[b]
                up_ref[b, rows(back), :] = there * scales[b]
        return ups, downs

    half = length // 2 // unroll
    carry = lax.fori_loop(0, half, outer, (ups, downs))
    lax.fori_loop(half, 2 * half, inner, carry)

    offset = (width - ACTIVE) // 2
    sent = []
    for c in range(ROWS):
        spectrum = jnp.concatenate(
            [up_ref[b, pl.ds(c, length, stride=ROWS), :] for b in range(blocks)], axis=1
        )
        filtered = 1.0 - jnp.transpose(transform(spectrum))
        columns = slice(c * length, (c + 1) * length)
        out_ref[:, columns] = -jnp.log(filtered)
        for d in range(2 * len(part_refs)):
            rows = pl.ds(pl.multiple_of((rank ^ d) * share, share), share)
            there = part_refs[d // 2].at[d % 2 * share : (d % 2 + 1) * share, columns]
            sent.append(
                pltpu.make_async_copy(out_ref.at[rows, columns], there, out_sems.at[c, d])
            )
            sent[-1].start()
        if c == (offset + ACTIVE - 1) // length:
            columns = slice(offset, offset + ACTIVE)
            sent.append(
                pltpu.make_async_copy(out_ref.at[:, columns], active_ref, sems.at[0])
            )
            sent[-1].start()
    for copy in sent:
        copy.wait()


def paganin(image, rank, parts):
    height, width = image.shape
    blocks = height // LANES
    return pl.pallas_call(
        filter_kernel,
        out_shape=[jax.ShapeDtypeStruct((2 * height // parts, width), f32)] * (parts // 2)
        + [jax.ShapeDtypeStruct((height, ACTIVE), f32)],
        in_specs=[pl.BlockSpec(memory_space=pltpu.SMEM)]
        + [pl.BlockSpec(memory_space=pltpu.HBM)] * 2,
        out_specs=[pl.BlockSpec(memory_space=pltpu.HBM)] * (parts // 2 + 1),
        scratch_shapes=[
            pltpu.VMEM((height, width), f32),
            pltpu.VMEM((height + ROWS, height), f32),
            pltpu.VMEM((height, width), f32),
            pltpu.VMEM((blocks, width, LANES), f32),
            pltpu.VMEM((blocks, width, LANES), f32),
            pltpu.VMEM((blocks, width // 2, LANES), f32),
            pltpu.SemaphoreType.DMA((ROWS + 1,)),
            pltpu.SemaphoreType.DMA((ROWS, parts)),
        ],
        compiler_params=pltpu.CompilerParams(vmem_limit_bytes=58 * 2**20),
        cost_estimate=pl.CostEstimate(
            flops=64 * height * height * width,
            bytes_accessed=8 * height * width,
            transcendentals=height * width,
        ),
        name="paganin",
    )(rank.reshape(1), image, jnp.asarray(filter_tables(height)))


def reversed_exact(values, flip):
    return sum(dot(part, flip) for part in halves(values))


class Weights:
    def __init__(self, along_ref, place_ref, angles, chunk):
        self.along_ref = along_ref
        self.place_ref = place_ref
        self.angles = angles
        self.chunk = chunk
        self.ray = lax.broadcasted_iota(jnp.int32, (ROWS, VOX), 0).astype(f32)

    def prepare(self, shift_x_ref, shift_y_ref, cos_ref, sin_ref):
        def along_angle(t):
            along = shift_x_ref[...] * cos_ref[t] + shift_y_ref[...] * sin_ref[t]
            self.along_ref[t] = self.ray - along

        repeat(self.angles, along_angle, 8)

    def make(self, q, c, ref):
        for two in range(self.chunk // 2):
            pieces = []
            for t in (2 * two, 2 * two + 1):
                angle = c * self.chunk + t
                base = self.along_ref[angle] - self.place_ref[q * self.angles + angle]
                for group in range(WIN // ROWS):
                    distance = base + float(group * ROWS)
                    pieces.append(jnp.maximum(0.0, 1.0 - jnp.abs(distance)))
            high, low = halves(jnp.concatenate(pieces, axis=0))
            ref[2 * two * WIN : (2 * two + 2) * WIN, 0:VOX] = high
            ref[2 * two * WIN : (2 * two + 2) * WIN, VOX : 2 * VOX] = low


def ray_operand(values, sums_too):
    high, low = halves(values)
    rows = [
        jnp.concatenate([high, high], axis=1),
        jnp.concatenate([low, jnp.zeros_like(low)], axis=1),
    ]
    if sums_too:
        rows.append(jnp.ones((values.shape[0], 2 * VOX), bf16))
    return jnp.concatenate(rows, axis=0)


def row_operands(values, sums_too):
    rows = ray_operand(values, sums_too)
    count, width = rows.shape
    spare = jnp.zeros((SPLIT - count, width), bf16)
    empty = jnp.zeros((SPLIT, width), bf16)
    return (
        jnp.concatenate([rows, spare, empty], axis=0),
        jnp.concatenate([empty, rows, spare], axis=0),
    )


def project_rows(held_ref, operands, q, c, sizes, offset_ref, acc_ref):
    angles, chunk = sizes[:2]
    half = chunk // 2
    for side in range(2):
        sums = lax.dot_general(
            held_ref[side * half * WIN : (side + 1) * half * WIN, :],
            operands[side],
            (((1,), (1,)), ((), ())),
            preferred_element_type=f32,
        )
        for begin in range(0, half, GROUP):
            places = []
            for i in range(begin, begin + GROUP):
                t = side * half + i
                rows = pl.ds(offset_ref[q * angles + c * chunk + t], WIN)
                index = c * half + i
                piece = sums[i * WIN : (i + 1) * WIN, :]
                places.append((index, rows, acc_ref[index, rows, :] + piece))
            for index, rows, values in places:
                acc_ref[index, rows, :] = values


def spread_rays(acc_ref, direct_ref, mirror_ref, total_ref, slices, chunk):
    both = 2 * slices
    half = chunk // 2

    def spread(index):
        turned = jnp.transpose(acc_ref[index]) * (1.0 / ROI)
        for part in range(2):
            rows = turned[part * SPLIT : (part + 1) * SPLIT]
            t = index // half * chunk + part * half + index % half
            direct_ref[t] = rows[0:slices] + rows[both : both + slices]
            mirror_ref[t] = rows[slices:both] + rows[both + slices : 2 * both]
            if total_ref is not None:
                total_ref[t] = rows[2 * both : 2 * both + slices]

    repeat(acc_ref.shape[0], spread, 8)


def turn_rays(values, flip):
    shape = values.shape
    return reversed_exact(values.reshape(-1, shape[-1]), flip).reshape(shape)


def fill_windows(weighted, flip, window_ref):
    angles, slices, _ = weighted.shape
    high, low = halves(weighted.reshape(angles * slices, ACTIVE))
    mirrored = (dot(high, flip) + dot(low, flip)).reshape(weighted.shape)
    lane = lax.broadcasted_iota(jnp.int32, (angles, slices, LANES), 2)
    for part, source in enumerate((weighted, mirrored)):
        rows = slice(part * slices, (part + 1) * slices)
        left = source[:, :, 0:LANES]
        right = source[:, :, LANES : 2 * LANES]
        window_ref[:, 0, rows, :] = left
        window_ref[:, 2, rows, :] = right
        mixed = jnp.where(lane >= SPLIT, left, right)
        window_ref[:, 1, rows, :] = pltpu.roll(mixed, SPLIT, 2)


def window_operand(q, c, sizes, window_ref, tile_ref, turn_ref):
    angles, chunk = sizes[:2]
    both = window_ref.shape[2]
    lane_rows = lax.broadcasted_iota(jnp.int32, (both, LANES), 1)
    tiles = [None] * (-(-chunk * WIN // LANES))
    for t in range(chunk):
        index = q * angles + c * chunk + t
        piece = pltpu.roll(window_ref[c * chunk + t, tile_ref[index]], turn_ref[index], 1)
        begin = t * WIN
        for place in range(begin // LANES, (begin + WIN - 1) // LANES + 1):
            if tiles[place] is None:
                tiles[place] = piece
            else:
                tiles[place] = jnp.where(
                    lane_rows >= begin - place * LANES, piece, tiles[place]
                )
    high, low = halves(jnp.concatenate(tiles, axis=1))
    return jnp.concatenate([high, low], axis=0)


def update_pair(operand, held):
    both = operand.shape[0] // 2
    sums = dot(operand, held)
    return sums[0:both, 0:VOX] + sums[both:, 0:VOX] + sums[0:both, VOX:]


def first_kernel(
    sizes,
    place_ref,
    offset_ref,
    slot_ref,
    cos_ref,
    sin_ref,
    vol_ref,
    flip_ref,
    shift_x_ref,
    shift_y_ref,
    kept_ref,
    predicted_ref,
    gain_ref,
    *refs,
):
    held_refs = refs[:CYCLE]
    acc_ref, along_ref, half_ref, mirror_ref, start_ref, sem = refs[CYCLE:]
    angles, chunk, slots = sizes
    patches = slot_ref.shape[0]
    pairs, both, _ = start_ref.shape
    slices = both // 2
    flip = flip_ref[...]

    def slot_values(patch):
        slot = slot_ref[patch]
        rows = pl.ds(slot % slots, slices, stride=slots)
        return jnp.concatenate(
            [half_ref[part, slot // slots, rows, :] for part in range(2)], axis=1
        )

    for part in range(2):
        half_ref[part] = vol_ref[:, :, part * LANES : (part + 1) * LANES]

    def order(q):
        start_ref[q, 0:slices, :] = slot_values(q)
        mirror_ref[q] = slot_values(patches - 1 - q)

    repeat(pairs, order, 8)
    start_ref[:, slices:both, :] = turn_rays(mirror_ref[0:pairs], flip)
    weights = Weights(along_ref, place_ref, angles, chunk)
    weights.prepare(shift_x_ref, shift_y_ref, cos_ref, sin_ref)
    acc_ref[...] = jnp.zeros(acc_ref.shape, f32)

    kept = pltpu.make_async_copy(start_ref, kept_ref, sem)
    kept.start()
    chunks = angles // chunk

    def cycle(index, carry):
        for step in range(CYCLE):
            q = index * CYCLE + step
            operands = row_operands(start_ref[q], True)
            for c in range(chunks):
                more = jnp.minimum(q + (c + 1) // chunks, pairs - 1)
                after = (step * chunks + c + 1) % CYCLE
                weights.make(more, (c + 1) % chunks, held_refs[after])
                here = held_refs[(step * chunks + c) % CYCLE]
                project_rows(here, operands, q, c, sizes, offset_ref, acc_ref)
        return carry

    weights.make(0, 0, held_refs[0])
    lax.fori_loop(0, pairs // CYCLE, cycle, 0)
    spread_rays(acc_ref, predicted_ref, mirror_ref, gain_ref, slices, chunk)
    direct, mirror, weight_sums = predicted_ref[...], mirror_ref[0:angles], gain_ref[...]
    predicted_ref[...] = direct + turn_rays(mirror, flip)
    turned = turn_rays(weight_sums[:, 0, :], flip)
    total = weight_sums + turned[:, None, :]
    gain_ref[...] = 1.0 / jnp.maximum(total, row_floor)
    kept.wait()


def second_kernel(
    sizes,
    step_size,
    rank_ref,
    offset_ref,
    place_ref,
    tile_ref,
    turn_ref,
    slot_ref,
    cos_ref,
    sin_ref,
    vol_ref,
    predicted_ref,
    gain_ref,
    sino_ref,
    flip_ref,
    shift_x_ref,
    shift_y_ref,
    kept_ref,
    *refs,
):
    angles, chunk, slots = sizes
    rays = vol_ref.shape[0]
    out_refs, refs = refs[:rays], refs[rays:]
    held_refs = refs[:CYCLE]
    acc_ref, along_ref, direct_ref, mirror_ref, window_ref, update_ref, half_ref = refs[
        CYCLE:-2
    ]
    start_ref, sem = refs[-2:]
    kept = pltpu.make_async_copy(kept_ref, start_ref, sem)
    kept.start()
    patches = slot_ref.shape[0]
    pairs, both, _ = start_ref.shape
    slices = both // 2
    flip = flip_ref[...]
    weights = Weights(along_ref, place_ref, angles, chunk)
    weights.prepare(shift_x_ref, shift_y_ref, cos_ref, sin_ref)
    chunks = angles // chunk
    windows = (sizes, window_ref, tile_ref, turn_ref)
    rest = (sizes, offset_ref, acc_ref)
    fill_windows(
        (sino_ref[...] - predicted_ref[...]) * gain_ref[...] * (1.0 / ROI), flip, window_ref
    )
    acc_ref[...] = jnp.zeros(acc_ref.shape, f32)
    kept.wait()

    def advance(q, operand, held):
        total = update_pair(operand, held)
        update_ref[q] = total
        return start_ref[q] + step_size * total

    def forward(values, q, held):
        project_rows(held, row_operands(values, False), q, 0, *rest)

    def cycle(index, carry):
        values, operand = carry
        for step in range(CYCLE):
            q = index * CYCLE + step
            after = (step + 1) % CYCLE
            before = (step - 1) % CYCLE
            later = index + (step + 1) // CYCLE
            earlier = index if step else jnp.maximum(index - 1, 0)
            following = jnp.minimum(q + 1, pairs - 1)
            next_operand = window_operand(following, 0, *windows)
            weights.make(following, 0, held_refs[after].at[later])
            new_values = advance(q, operand, held_refs[step][index])
            forward(values, jnp.maximum(q - 1, 0), held_refs[before].at[earlier])
            values, operand = new_values, next_operand
        return values, operand

    def all_chunks(q, body):
        for c in range(chunks):
            weights.make(q, c, held_refs[0].at[0])
            body(c, held_refs[0].at[0])

    def plain_update(q, carry):
        update_ref[q] = jnp.zeros(update_ref.shape[1:], f32)

        def add(c, held):
            operand = window_operand(q, c, *windows)
            update_ref[q] = update_ref[q] + update_pair(operand, held[...])

        all_chunks(q, add)
        return carry

    def plain_forward(q, carry):
        operands = row_operands(start_ref[q] + step_size * update_ref[q], False)
        all_chunks(q, lambda c, held: project_rows(held, operands, q, c, *rest))
        return carry

    if chunks == 1:
        held_refs[CYCLE - 1][0] = jnp.zeros(held_refs[CYCLE - 1].shape[1:], bf16)
        weights.make(0, 0, held_refs[0].at[0])
        begin = (jnp.zeros((both, VOX), f32), window_operand(0, 0, *windows))
        values, _ = lax.fori_loop(0, pairs // CYCLE, cycle, begin)
        forward(values, pairs - 1, held_refs[CYCLE - 1].at[pairs // CYCLE - 1])
    else:
        lax.fori_loop(0, pairs, plain_update, 0)
        lax.fori_loop(0, pairs, plain_forward, 0)

    spread_rays(acc_ref, direct_ref, mirror_ref, None, slices, chunk)
    turned = turn_rays(mirror_ref[0:angles], flip)
    direct_ref[...] = sino_ref[...] - direct_ref[...] - turned
    fill_windows(direct_ref[...] * gain_ref[...] * (1.0 / ROI), flip, window_ref)

    def last_cycle(index, operand):
        for step in range(CYCLE):
            q = index * CYCLE + step
            next_operand = window_operand(jnp.minimum(q + 1, pairs - 1), 0, *windows)
            total = update_pair(operand, held_refs[step][index])
            update_ref[q] = (update_ref[q] + total) * step_size
            operand = next_operand
        return operand

    def plain_last(q, carry):
        def add(c, held):
            operand = window_operand(q, c, *windows)
            update_ref[q] = update_ref[q] + update_pair(operand, held[...])

        all_chunks(q, add)
        update_ref[q] = update_ref[q] * step_size
        return carry

    if chunks == 1:
        lax.fori_loop(0, pairs // CYCLE, last_cycle, window_operand(0, 0, *windows))
    else:
        lax.fori_loop(0, pairs, plain_last, 0)

    mirror_ref[0:pairs] = turn_rays(update_ref[:, slices:both, :], flip)
    for part in range(2):
        half_ref[part] = vol_ref[:, :, part * LANES : (part + 1) * LANES]

    def finish(q):
        for patch, update in (
            (q, update_ref[q, 0:slices, :]),
            (patches - 1 - q, mirror_ref[q]),
        ):
            slot = slot_ref[patch]
            rows = pl.ds(slot % slots, slices, stride=slots)
            for part in range(2):
                half_ref[part, slot // slots, rows, :] = (
                    half_ref[part, slot // slots, rows, :]
                    + update[:, part * LANES : (part + 1) * LANES]
                )

    repeat(pairs, finish, 8)
    lead = slices * slots
    lane = lax.broadcasted_iota(jnp.int32, (slices, LANES), 1)
    for d, out_ref in enumerate(out_refs):
        ray = rank_ref[0] ^ d
        for part in range(2):
            out_ref[0:lead, part * LANES : (part + 1) * LANES] = half_ref[part, ray]
        for k in range(0, angles // rays, 4):
            begin = lead + k // 4 * 3 * slices
            live = [
                pltpu.roll(direct_ref[(k + i) * rays + ray], ACTIVE - EDGE, 1)
                for i in range(4)
            ]
            rest = [part[:, LANES:] for part in live]
            for i in range(2):
                here = begin + i * slices
                out_ref[here : here + slices, 0:LANES] = live[2 * i][:, 0:LANES]
                out_ref[here : here + slices, LANES:] = live[2 * i + 1][:, 0:LANES]
                here = begin + 2 * slices
                out_ref[here : here + slices, i * LANES : (i + 1) * LANES] = jnp.where(
                    lane < SPLIT, rest[2 * i], pltpu.roll(rest[2 * i + 1], SPLIT, 1)
                )


def call(kernel, name, inputs, held_in, held_out, outputs, scratch, micros):
    smem = pl.BlockSpec(memory_space=pltpu.SMEM)
    vmem = pl.BlockSpec(memory_space=pltpu.VMEM)
    hbm = pl.BlockSpec(memory_space=pltpu.HBM)
    return pl.pallas_call(
        kernel,
        out_shape=[jax.ShapeDtypeStruct(*value) for value in held_out + outputs],
        in_specs=[smem if value.ndim == 1 else vmem for value in inputs] + [hbm] * len(held_in),
        out_specs=[hbm] * len(held_out) + [vmem] * len(outputs),
        scratch_shapes=[pltpu.VMEM(*value) for value in scratch]
        + [pltpu.SemaphoreType.DMA],
        compiler_params=pltpu.CompilerParams(vmem_limit_bytes=52 * 2**20),
        cost_estimate=pl.CostEstimate(
            flops=int(micros * 1e9), bytes_accessed=4 * 2**20, transcendentals=0
        ),
        name=name,
    )(*inputs, *held_in)


class Sirt:
    def __init__(self, theta, vol_list, slices, slots, rays, step_size):
        angles = theta.shape[0]
        patches = vol_list.shape[0]
        pairs = patches // 2
        both = 2 * slices
        chunk = math.gcd(angles, 32)
        self.sizes = (angles, chunk, slots)
        self.step_size = step_size
        self.rays = rays
        self.patches = patches
        centre = (ROI - 1) / 2.0
        ids = np.arange(pairs)
        centre_x = (ids // PGRID * float(SIDE) + (SIDE - 1) / 2.0 - centre).astype(np.float32)
        centre_y = (ids % PGRID * float(SIDE) + (SIDE - 1) / 2.0 - centre).astype(np.float32)
        self.cosine = jnp.cos(theta)
        self.sine = jnp.sin(theta)
        along = (
            centre_x[:, None] * self.cosine[None, :]
            + centre_y[:, None] * self.sine[None, :]
            + 0.5
        )
        whole = jnp.floor(along)
        lead = WIN // 2 - 1
        place = along - whole + float(lead)
        offset = whole.astype(jnp.int32) + (ACTIVE // 2 - 1 - lead)
        tile = jnp.minimum(offset // SPLIT, 2)
        local = jnp.arange(angles, dtype=jnp.int32) % chunk * WIN
        turn = (local[None, :] - offset + tile * SPLIT) % LANES
        self.offset = offset.reshape(-1)
        self.place = place.reshape(-1)
        self.tile = tile.reshape(-1)
        self.turn = turn.reshape(-1)
        ids = jnp.arange(patches, dtype=jnp.int32)
        self.slot = jnp.sum(
            jnp.where(vol_list[None, :] == ids[:, None], ids[None, :], 0), axis=1
        )
        voxel = np.arange(VOX)
        shift_x = np.repeat((voxel // SIDE - (SIDE - 1) / 2.0)[None, :], ROWS, axis=0)
        shift_y = np.repeat((voxel % SIDE - (SIDE - 1) / 2.0)[None, :], ROWS, axis=0)
        flip = np.eye(ACTIVE)[::-1].astype(ml_dtypes.bfloat16)
        self.fixed = [jnp.asarray(flip), jnp.asarray(shift_x, f32), jnp.asarray(shift_y, f32)]
        self.weight = ((chunk * WIN, 2 * VOX), bf16)
        self.held = (pairs // CYCLE + 1 if angles == chunk else 1,) + self.weight[0]
        self.acc_rows = ((angles // 2, ACTIVE, LANES), f32)
        self.along = ((angles, ROWS, VOX), f32)
        self.by_ray = ((angles, slices, ACTIVE), f32)
        self.by_pair = ((pairs, both, VOX), f32)
        self.window = ((angles, 3, both, LANES), f32)
        self.half = ((2, rays, slices * slots, LANES), f32)
        self.mirror = ((max(pairs, angles), slices, ACTIVE), f32)
        self.sent = [((slices * (slots + angles // rays * 3 // 4), ACTIVE), f32)] * rays

    def first(self, volume):
        inputs = [self.place, self.offset, self.slot, self.cosine, self.sine, volume]
        return call(
            functools.partial(first_kernel, self.sizes),
            "first",
            inputs + self.fixed,
            [],
            [self.by_pair],
            [self.by_ray, self.by_ray],
            [self.weight] * CYCLE
            + [self.acc_rows, self.along, self.half, self.mirror, self.by_pair],
            14,
        )

    def second(self, rank, volume, start, predicted, gain, sino):
        inputs = [rank.reshape(1), self.offset, self.place, self.tile, self.turn, self.slot]
        inputs += [self.cosine, self.sine, volume, predicted, gain, sino]
        scratch = [(self.held, bf16)] * CYCLE
        scratch += [self.acc_rows, self.along, self.by_ray, self.mirror, self.window]
        return call(
            functools.partial(second_kernel, self.sizes, self.step_size),
            "second",
            inputs + self.fixed,
            [start],
            [],
            self.sent,
            scratch + [self.by_pair, self.half, self.by_pair],
            26,
        )


def gather_kernel(rank_ref, *refs):
    *part_refs, out_ref, active_ref, sems = refs
    rank = rank_ref[0]
    rows = out_ref.shape[1]
    copies = [
        pltpu.make_async_copy(part_ref.at[0:rows], out_ref.at[rank ^ d], sems.at[d])
        for d, part_ref in enumerate(part_refs)
    ]
    for copy in copies:
        copy.start()
    offset = (out_ref.shape[2] - ACTIVE) // 2
    for d, part_ref in enumerate(part_refs):
        active_ref[rank ^ d] = part_ref[0:rows, offset : offset + ACTIVE]
    for copy in copies:
        copy.wait()


def gather_parts(parts, rank):
    count = len(parts)
    rows, width = parts[1].shape
    vmem = pl.BlockSpec(memory_space=pltpu.VMEM)
    return pl.pallas_call(
        gather_kernel,
        out_shape=(
            jax.ShapeDtypeStruct((count, rows, width), f32),
            jax.ShapeDtypeStruct((count, rows, ACTIVE), f32),
        ),
        in_specs=[pl.BlockSpec(memory_space=pltpu.SMEM)] + [vmem] * count,
        out_specs=(pl.BlockSpec(memory_space=pltpu.HBM), vmem),
        scratch_shapes=[pltpu.SemaphoreType.DMA((count,))],
        compiler_params=pltpu.CompilerParams(vmem_limit_bytes=12 * 2**20),
        cost_estimate=pl.CostEstimate(
            flops=0, bytes_accessed=8 * count * rows * width, transcendentals=0
        ),
        name="gather_parts",
    )(rank.reshape(1), *parts)


def message_order(count):
    near = [d for d in (1, 2) if d < count // 2]
    far = list(range(count - 1, count // 2 - 1, -1))
    return near + far + [d for d in range(count // 2 - 1, -1, -1) if d not in near]


def finish_kernel(rank_ref, *refs):
    *got_refs, given_ref, _, rec_ref, out_ref, values_ref, active_ref, sems = refs
    rays = len(got_refs)
    slots = values_ref.shape[1]
    slabs = active_ref.shape[0]
    slices = values_ref.shape[0] // rays
    lead = slices * slots
    lane = lax.broadcasted_iota(jnp.int32, (slices, ACTIVE), 1)
    live = (lane >= EDGE) & (lane < ACTIVE - EDGE)
    for d, got_ref in zip(message_order(rays), got_refs):
        rows = pl.ds(pl.multiple_of((rank_ref[0] ^ d) * slices, slices), slices)
        values_ref[rows] = got_ref[0:lead, :].reshape(slices, slots, VOX)
        for k in range(slabs):
            begin = lead + k // 4 * 3 * slices
            pair, side = k % 4 // 2, k % 2
            here = begin + pair * slices
            left = got_ref[here : here + slices, side * LANES : (side + 1) * LANES]
            here = begin + 2 * slices
            rest = got_ref[here : here + slices, pair * LANES : (pair + 1) * LANES]
            if side:
                rest = pltpu.roll(rest, SPLIT, 1)
            whole = pltpu.roll(jnp.concatenate([left, rest], axis=1), EDGE, 1)
            active_ref[k, rows, :] = jnp.where(live, whole, given_ref[k, rows, :])
    offset = (out_ref.shape[2] - ACTIVE) // 2
    copies = [
        pltpu.make_async_copy(values_ref, rec_ref, sems.at[0]),
        pltpu.make_async_copy(
            active_ref, out_ref.at[:, :, offset : offset + ACTIVE], sems.at[1]
        ),
    ]
    for copy in copies:
        copy.start()
    for copy in copies:
        copy.wait()


def finish(pieces, given, sinogram, rank, shape):
    slabs, slab_rows, _ = sinogram.shape
    hbm = pl.BlockSpec(memory_space=pltpu.HBM)
    vmem = pl.BlockSpec(memory_space=pltpu.VMEM)
    return pl.pallas_call(
        finish_kernel,
        out_shape=(
            jax.ShapeDtypeStruct(shape, f32),
            jax.ShapeDtypeStruct(sinogram.shape, f32),
        ),
        in_specs=[pl.BlockSpec(memory_space=pltpu.SMEM)]
        + [vmem] * (len(pieces) + 1)
        + [hbm],
        out_specs=[hbm, hbm],
        scratch_shapes=[
            pltpu.VMEM(shape, f32),
            pltpu.VMEM((slabs, slab_rows, ACTIVE), f32),
            pltpu.SemaphoreType.DMA((2,)),
        ],
        input_output_aliases={len(pieces) + 2: 1},
        compiler_params=pltpu.CompilerParams(vmem_limit_bytes=8 * 2**20),
        cost_estimate=pl.CostEstimate(
            flops=0, bytes_accessed=8 * len(pieces) * pieces[0].size, transcendentals=0
        ),
        name="finish",
    )(rank.reshape(1), *[pieces[d] for d in message_order(len(pieces))], given, sinogram)


def partner(values, axis, d):
    count = lax.axis_size(axis)
    return lax.ppermute(values, axis, [(i, i ^ d) for i in range(count)])


def exchange(pieces, axis):
    count = len(pieces)
    results = list(pieces)
    for d in range(count - 1, 0, -1):
        results[d] = partner(pieces[d], axis, d)
    return results


def local(intensity, angles, volume, vol_list):
    n_slab = lax.axis_size("slab")
    n_ray = lax.axis_size("ray")
    devices = n_slab * n_ray
    height, band = intensity.shape[2:]
    slices = height // devices
    slots = volume.shape[1]
    count = angles.shape[0] * angles.shape[1]
    step_size = relax * ROI / count
    rank = lax.axis_index("slab")
    ray_rank = lax.axis_index("ray")
    padded = -(-slices // ROWS) * ROWS

    def to_all(values, axes):
        return lax.all_to_all(values, axes, split_axis=0, concat_axis=0, tiled=True)

    own_volume = to_all(volume.reshape(n_ray, slices * slots, VOX), "ray")
    *parts, active = paganin(intensity.reshape(height, band), rank, n_slab)
    active, own_volume = lax.optimization_barrier((active, own_volume))
    own_rays = to_all(active.reshape(devices, slices, ACTIVE), ("slab", "ray"))
    if padded != slices:
        more = padded - slices
        own_volume = jnp.pad(own_volume, ((0, 0), (0, more * slots), (0, 0)))
        own_rays = jnp.pad(own_rays, ((0, 0), (0, more), (0, 0)))

    angles, vol_list, own_volume, parts = lax.optimization_barrier(
        (angles, vol_list, own_volume, parts)
    )
    sirt = Sirt(angles.reshape(-1), vol_list, padded, slots, n_ray, step_size)
    start, predicted, gain = sirt.first(own_volume)
    own_rays, parts, start = lax.optimization_barrier((own_rays, parts, start))
    share = parts[0].shape[0] // 2
    parts = [partner(part, "slab", 2 * j) if j else part for j, part in enumerate(parts)]
    swapped = [partner(parts[0][share:], "slab", 1)]
    pieces = sirt.second(ray_rank, own_volume, start, predicted, gain, own_rays)
    pieces, parts, swapped = lax.optimization_barrier((pieces, parts, swapped))
    if padded != slices:
        narrow = []
        for piece in pieces:
            lower = piece[padded * slots :].reshape(-1, padded, ACTIVE)[:, :slices]
            lower = lower.reshape(-1, ACTIVE)
            narrow.append(jnp.concatenate([piece[: slices * slots], lower], axis=0))
        pieces = narrow
    pieces = exchange(pieces, "ray")
    swapped += [partner(part[share:], "slab", 1) for part in parts[1:]]
    parts = [part for two in zip(parts, swapped) for part in two]
    sinogram, given = gather_parts(parts, rank)
    if padded == slices:
        reconstruction, residual = finish(pieces, given, sinogram, ray_rank, volume.shape)
    else:
        order = ray_rank ^ jnp.arange(n_ray, dtype=jnp.int32)
        pieces = jnp.take(jnp.stack(pieces), order, axis=0)
        reconstruction = pieces[:, : slices * slots].reshape(volume.shape)
        lower = pieces[:, slices * slots :].reshape(n_ray, -1, 3, slices, ACTIVE)
        left = lower[:, :, :2].reshape(n_ray, -1, 2, slices, 2, LANES)
        left = jnp.transpose(left, (1, 2, 4, 0, 3, 5)).reshape(n_slab, n_ray * slices, LANES)
        rest = lower[:, :, 2].reshape(n_ray, -1, slices, 4, SPLIT)
        rest = jnp.transpose(rest, (1, 3, 0, 2, 4)).reshape(n_slab, n_ray * slices, SPLIT)
        begin = (band - ACTIVE) // 2 + EDGE
        live = jnp.concatenate([left, rest], axis=2)
        residual = lax.dynamic_update_slice(sinogram, live, (0, 0, begin))
    return (reconstruction, residual[:, None])


def solution(mesh):
    placed = (P("slab", "ray", None, None), P(), P("slab", "ray", None), P())
    return jax.shard_map(
        local,
        mesh=mesh,
        in_specs=placed,
        out_specs=(P("slab", "ray", None), P(None, "ray", "slab", None)),
        check_vma=False,
    )
```
